32 devices in a mesh: runs: 2 (over y), gx: 4 (over z), gy: 4 (over x, core).
Axes of the slice: x: 2, y: 2, z: 4, core: 2. Of those that a mesh axis runs over, the one named last changes fastest.
Arguments:
- melt_flow: float32 [3, 32, 512, 128], P(None, ('runs', 'gx'), 'gy'), parts along dimension 1, may hold values from -6 to 6
- thermal_state: float32 [32, 512, 128], P(('runs', 'gx'), 'gy'), parts along dimension 0, may hold values from -6 to 6
- powder_flag: int32 [32, 512, 128], P(('runs', 'gx'), 'gy'), parts along dimension 0, may hold values 0 or 1
- spot_lateral_a_cell: int32 [16], P('runs'), parts along dimension 0, may hold values from 0 to 15
- spot_lateral_b_cell: int32 [16], P('runs'), parts along dimension 0, may hold values from 0 to 511
Outputs:
- corrected_flow: float32 [3, 32, 512, 128], P(None, ('runs', 'gx'), 'gy'), parts along dimension 1
- advected_thermal_state: float32 [32, 512, 128], P(('runs', 'gx'), 'gy'), parts along dimension 0
- pressure_iterate: float32 [32, 512, 128], P(('runs', 'gx'), 'gy'), parts along dimension 0
The draws below stay inside these ranges and needn't reach their ends.
There are 2 independent parts, one for each index of `runs`. The reference program is written for one: setup_inputs(seed, part) draws one part's arguments, and reference() takes and returns one part's arrays. A program takes and returns all parts, laid end to end along the dimension named above; each array names one. Nothing has to cross between parts.
All inputs are finite; a program needn't handle non-finite values. No bound on the sum of `powder_flag` on one device may be relied on, other than what follows from the above.
Results may differ from the reference program's by a relative error of at most 0.0003.
Values sent between devices are 32-bit elements; how exact they have to be, the bound alone decides.
No kernel may reach another device: no remote copies, remote signals or barrier semaphores. Data moves between devices by JAX's collectives and lax.ppermute only.
A program may use at most 64 MiB of HBM per device.

```python
import math
import jax
import jax.numpy as jnp
from jax import lax

CY = 128
NUM_VERTICAL = 128
ITERS = 2
LASER = 8
BX = 16
NUM_LATERAL_A = 16
NUM_LATERAL_B = 512


def place_ends(result, key, least, high):
    shape = result.shape
    spot = [jax.random.randint(jax.random.fold_in(key, axis), (), 0, shape[axis]) for axis in range(len(shape))]
    result = result.at[tuple(spot)].set(least)
    longest = shape.index(max(shape))
    spot[longest] = (spot[longest] + 1) % shape[longest]
    return result.at[tuple(spot)].set(high)


def shard_levels(stream_key, shape, cuts, low, high):
    def one(position, blocks):
        heights = jax.random.uniform(jax.random.fold_in(jax.random.fold_in(stream_key, 6), position), (blocks,), jnp.float32, low / len(cuts), high / len(cuts))
        return jnp.repeat(jnp.exp(heights), shape[position] // blocks).reshape((-1,) + (1,) * (len(shape) - position - 1))

    factor_of = one(*cuts[0])
    for cut in cuts[1:]:
        factor_of = factor_of * one(*cut)
    return factor_of


def scatter_about(key, extent, spread, most, pieces=(), kind=jnp.bfloat16):
    loudness = shard_levels(key, extent, pieces, -0.22, 0.18) if pieces else 1.0
    drawn = jax.random.normal(key, extent, jnp.float32) * spread * loudness
    return jnp.minimum(jnp.maximum(drawn, -most), most).astype(kind)


def setup_inputs(seed: int = 0, part: int = 0) -> dict:
    arg_keys = jax.random.split(jax.random.key(seed), 6)
    part_splits = jax.random.split(jax.random.fold_in(arg_keys[5], part), 6)
    return {
        "melt_flow": scatter_about(part_splits[0], (3, NUM_LATERAL_A, NUM_LATERAL_B, NUM_VERTICAL), 1.0, 6.0, ((1, 4), (2, 4)), jnp.float32),
        "thermal_state": scatter_about(part_splits[1], (NUM_LATERAL_A, NUM_LATERAL_B, NUM_VERTICAL), 1.0, 6.0, ((0, 4), (1, 4)), jnp.float32),
        "powder_flag": place_ends((jax.random.randint(part_splits[2], (NUM_LATERAL_A, NUM_LATERAL_B, NUM_VERTICAL), 0, 2) < 1).astype(jnp.int32), jax.random.fold_in(part_splits[2], 1), 0, 1),
        "spot_lateral_a_cell": place_ends(jax.random.randint(part_splits[3], (LASER,), 0, NUM_LATERAL_A), jax.random.fold_in(part_splits[3], 1), 0, NUM_LATERAL_A - 1).astype(jnp.int32),
        "spot_lateral_b_cell": place_ends(jax.random.randint(part_splits[4], (LASER,), 0, NUM_LATERAL_B), jax.random.fold_in(part_splits[4], 1), 0, NUM_LATERAL_B - 1).astype(jnp.int32),
    }


TIME_INCREMENT = 0.2
MARANGONI = 1.5
DRAG_RATE = 4.0
LASER_POWER = 3.0
SPOT_RADIUS = 5.0

def sine_table(length):
    positions = jnp.arange(length, dtype=jnp.float32) + 1.0
    phase_step = math.pi / (length + 1)
    sine_rows = jnp.sqrt(2.0 / (length + 1)) * jnp.sin(phase_step * positions[:, None] * positions[None, :])
    eigen_values = 2.0 - 2.0 * jnp.cos(phase_step * positions)
    return (sine_rows, eigen_values)

def depth_shift(source, offset):
    vertical_plane_number = source.shape[-1]
    padded = jnp.pad(source, [(0, 0)] * (source.ndim - 1) + [(2, 2)])
    return padded[..., 2 + offset:2 + offset + vertical_plane_number]

def laser_heat(start_x, start_y, span_lateral_a, span_lateral_b, total_x, total_y, spot_lateral_a_cell, spot_lateral_b_cell):
    cells_x = start_x + jnp.arange(span_lateral_a, dtype=jnp.int32)
    cells_y = start_y + jnp.arange(span_lateral_b, dtype=jnp.int32)
    dist_x = ((cells_x[:, None] - spot_lateral_a_cell[None, :] + total_x // 2) % total_x - total_x // 2).astype(jnp.float32)
    dist_y = ((cells_y[:, None] - spot_lateral_b_cell[None, :] + total_y // 2) % total_y - total_y // 2).astype(jnp.float32)
    spot_x = jnp.exp(-(dist_x * dist_x) / (SPOT_RADIUS * SPOT_RADIUS))
    spot_y = jnp.exp(-(dist_y * dist_y) / (SPOT_RADIUS * SPOT_RADIUS))
    return LASER_POWER * jnp.dot(spot_x, spot_y.T, precision=lax.Precision.HIGHEST)

def upwind_lateral(source, speed, axis):
    behind = 1.5 * source - 2.0 * jnp.roll(source, 1, axis) + 0.5 * jnp.roll(source, 2, axis)
    forward = -1.5 * source + 2.0 * jnp.roll(source, -1, axis) - 0.5 * jnp.roll(source, -2, axis)
    return jnp.where(speed >= 0.0, behind, forward)

def upwind_depth(source, speed):
    behind = 1.5 * source - 2.0 * depth_shift(source, -1) + 0.5 * depth_shift(source, -2)
    forward = -1.5 * source + 2.0 * depth_shift(source, 1) - 0.5 * depth_shift(source, 2)
    return jnp.where(speed >= 0.0, behind, forward)

def operate(source):
    beside = jnp.roll(source, -1, 0) + jnp.roll(source, 1, 0)
    beside = beside + jnp.roll(source, -1, 1) + jnp.roll(source, 1, 1)
    beside = beside + depth_shift(source, 1) + depth_shift(source, -1)
    return 6.0 * source - beside

def block_solve(source):
    highest = lax.Precision.HIGHEST
    table_x, values_x = sine_table(BX)
    table_y, values_y = sine_table(CY)
    table_z, values_z = sine_table(NUM_VERTICAL)
    blocks_view = source.reshape(NUM_LATERAL_A // BX, BX, NUM_LATERAL_B // CY, CY, NUM_VERTICAL)

    def transform(spectrum):
        spectrum = jnp.einsum('ia,gihjk->gahjk', table_x, spectrum, precision=highest)
        spectrum = jnp.einsum('jb,gahjk->gahbk', table_y, spectrum, precision=highest)
        return jnp.einsum('kc,gahbk->gahbc', table_z, spectrum, precision=highest)
    spectrum = transform(blocks_view)
    denominator = values_x[None, :, None, None, None] + values_y[None, None, None, :, None] + values_z[None, None, None, None, :]
    spectrum = spectrum / denominator
    return transform(spectrum).reshape(NUM_LATERAL_A, NUM_LATERAL_B, NUM_VERTICAL)

def reference(melt_flow, thermal_state, powder_flag, spot_lateral_a_cell, spot_lateral_b_cell):
    state_tensors = jnp.concatenate([melt_flow, thermal_state[None]], 0)
    speed_x = melt_flow[0][None]
    speed_y = melt_flow[1][None]
    speed_z = melt_flow[2][None]
    time_derivative = speed_x * upwind_lateral(state_tensors, speed_x, 1) + speed_y * upwind_lateral(state_tensors, speed_y, 2) + speed_z * upwind_depth(state_tensors, speed_z)
    upper_boundary = (jnp.arange(NUM_VERTICAL) == NUM_VERTICAL - 1).astype(jnp.float32)
    slope_lateral_a = 0.5 * (jnp.roll(thermal_state, -1, 0) - jnp.roll(thermal_state, 1, 0))
    slope_lateral_b = 0.5 * (jnp.roll(thermal_state, -1, 1) - jnp.roll(thermal_state, 1, 1))
    traction = jnp.stack([-MARANGONI * slope_lateral_a * upper_boundary, -MARANGONI * slope_lateral_b * upper_boundary, jnp.zeros_like(slope_lateral_a)])
    solid_fraction = powder_flag.astype(jnp.float32)
    provisional_flow = (melt_flow - TIME_INCREMENT * time_derivative[:3] + TIME_INCREMENT * traction) / (1.0 + TIME_INCREMENT * DRAG_RATE * solid_fraction)[None]
    laser_power_input = laser_heat(0, 0, NUM_LATERAL_A, NUM_LATERAL_B, NUM_LATERAL_A, NUM_LATERAL_B, spot_lateral_a_cell, spot_lateral_b_cell)
    advected_thermal_state = thermal_state - TIME_INCREMENT * time_derivative[3] + TIME_INCREMENT * laser_power_input[:, :, None] * upper_boundary
    divergence = provisional_flow[0] - jnp.roll(provisional_flow[0], 1, 0) + (provisional_flow[1] - jnp.roll(provisional_flow[1], 1, 1)) + (provisional_flow[2] - depth_shift(provisional_flow[2], -1))
    residual = -divergence
    pressure_iterate = jnp.zeros_like(residual)
    precond = block_solve(residual)
    direction = precond
    energy_now = jnp.sum(residual * precond)
    for iteration in range(ITERS):
        applied = operate(direction)
        step_size = energy_now / jnp.sum(direction * applied)
        pressure_iterate = pressure_iterate + step_size * direction
        residual = residual - step_size * applied
        if iteration + 1 < ITERS:
            precond = block_solve(residual)
            energy_next = jnp.sum(residual * precond)
            direction = precond + energy_next / energy_now * direction
            energy_now = energy_next
    gradient = jnp.stack([jnp.roll(pressure_iterate, -1, 0) - pressure_iterate, jnp.roll(pressure_iterate, -1, 1) - pressure_iterate, depth_shift(pressure_iterate, 1) - pressure_iterate])
    corrected_flow = provisional_flow - gradient
    return (corrected_flow, advected_thermal_state, pressure_iterate)
```

```python
import functools
import math

import jax
import jax.numpy as jnp
import numpy as np
from jax import lax
from jax.experimental import pallas as pl
from jax.experimental.pallas import tpu as pltpu
from jax.sharding import PartitionSpec as P

BLOCK = 128

TIME_INCREMENT = 0.2
MARANGONI = 1.5
DRAG_RATE = 4.0
LASER_POWER = 3.0
SPOT_RADIUS = 5.0

F32 = jnp.float32
VMEM = pl.BlockSpec(memory_space=pltpu.VMEM)
SMEM = pl.BlockSpec(memory_space=pltpu.SMEM)


def call(body, operands, shapes, scratch=(), scalars=1, flops=1 << 20):
    out_shape = [jax.ShapeDtypeStruct(shape, F32) for shape in shapes]
    moved = 4 * sum(math.prod(shape) for shape in shapes)
    return pl.pallas_call(
        body,
        out_shape=out_shape,
        in_specs=[SMEM] * scalars + [VMEM] * (len(operands) - scalars),
        out_specs=[VMEM] * len(shapes),
        scratch_shapes=list(scratch),
        compiler_params=pltpu.CompilerParams(vmem_limit_bytes=44 << 20),
        cost_estimate=pl.CostEstimate(flops=flops, bytes_accessed=2 * moved, transcendentals=0),
    )(*operands)


def dot(left, right):
    return jnp.dot(left, right, precision=lax.Precision.HIGHEST, preferred_element_type=F32)


def total(cells):
    return jnp.sum(jnp.sum(cells, axis=0, keepdims=True), axis=1, keepdims=True)


def loop(low, high, body, start):
    if isinstance(high, int) and isinstance(low, int) and high - low <= 24:
        carry = start
        for index in range(low, high):
            carry = body(index, carry)
        return carry
    return lax.fori_loop(low, high, body, start)


def sines(length):
    positions = np.arange(length) + 1.0
    step = math.pi / (length + 1)
    table = np.sqrt(2.0 / (length + 1)) * np.sin(step * positions[:, None] * positions[None, :])
    return table, 2.0 - 2.0 * np.cos(step * positions)


def lane_shift(cells, offset):
    width = cells.shape[1]
    lane = lax.broadcasted_iota(jnp.int32, cells.shape, 1)
    moved = pltpu.roll(cells, (-offset) % width, 1)
    keep = lane < width - offset if offset > 0 else lane >= -offset
    return jnp.where(keep, moved, 0.0)


def column(row):
    length = row.shape[1]
    shape = (length, length)
    same = lax.broadcasted_iota(jnp.int32, shape, 0) == lax.broadcasted_iota(jnp.int32, shape, 1)
    return jnp.sum(jnp.where(same, row, 0.0), axis=1, keepdims=True)


def advance(layers, padded, index, speed):
    middle = layers[2]
    rows = middle.shape[0]
    speed_x, speed_y, speed_z = speed
    ahead = speed_x >= 0.0
    near = jnp.where(ahead, layers[1], layers[3])
    far = jnp.where(ahead, layers[0], layers[4])
    rate = jnp.abs(speed_x) * (1.5 * middle - 2.0 * near + 0.5 * far)
    ahead = speed_y >= 0.0
    near = jnp.where(ahead, padded[index, pl.ds(7, rows), :], padded[index, pl.ds(9, rows), :])
    far = jnp.where(ahead, padded[index, pl.ds(6, rows), :], padded[index, pl.ds(10, rows), :])
    rate = rate + jnp.abs(speed_y) * (1.5 * middle - 2.0 * near + 0.5 * far)
    ahead = speed_z >= 0.0
    near = jnp.where(ahead, lane_shift(middle, -1), lane_shift(middle, 1))
    far = jnp.where(ahead, lane_shift(middle, -2), lane_shift(middle, 2))
    rate = rate + jnp.abs(speed_z) * (1.5 * middle - 2.0 * near + 0.5 * far)
    return middle - TIME_INCREMENT * rate


def pad_rows(padded, index, before, middle, after):
    rows = middle.shape[0]
    padded[index, pl.ds(8, rows), :] = middle
    padded[index, pl.ds(6, 2), :] = before
    padded[index, pl.ds(8 + rows, 2), :] = after


def march_kernel(flow, low_x, high_x, low_y, high_y, thermal, low_t, high_t, flag, star, padded):
    _, layers, rows, depth = flow.shape
    top = lax.broadcasted_iota(jnp.int32, (rows, depth), 1) == depth - 1
    for index in range(layers):
        for part in range(3):
            pad_rows(
                padded, part, low_y[part, index], flow[part, index], high_y[part, index]
            )
        pad_rows(padded, 3, low_y[3, index], thermal[index], high_y[3, index])
        speed = [flow[part, index] for part in range(3)]
        behind = thermal[index - 1] if index > 0 else column(low_t[...])
        before = thermal[index + 1] if index + 1 < layers else column(high_t[...])
        pull = -MARANGONI * 0.5 * TIME_INCREMENT
        drive_x = jnp.where(top, pull * (before - behind), 0.0)
        drive_y = jnp.where(
            top, pull * (padded[3, pl.ds(9, rows), :] - padded[3, pl.ds(7, rows), :]), 0.0
        )
        drag = 1.0 / (1.0 + TIME_INCREMENT * DRAG_RATE * flag[index].astype(F32))
        for part in range(3):
            around = []
            for other in range(index - 2, index + 3):
                if other < 0:
                    around.append(low_x[part, other + 2])
                elif other >= layers:
                    around.append(high_x[part, other - layers])
                else:
                    around.append(flow[part, other])
            moved = advance(around, padded, part, speed)
            if part == 0:
                moved = moved + drive_x
            if part == 1:
                moved = moved + drive_y
            star[part, index] = moved * drag


def heat_kernel(thermal, low_x, high_x, low_y, high_y, flow, heat, warmed, padded):
    layers, rows, depth = thermal.shape
    top = lax.broadcasted_iota(jnp.int32, (rows, depth), 1) == depth - 1
    for index in range(layers):
        pad_rows(padded, 0, low_y[index], thermal[index], high_y[index])
        around = []
        for other in range(index - 2, index + 3):
            if other < 0:
                around.append(low_x[other + 2])
            elif other >= layers:
                around.append(high_x[other - layers])
            else:
                around.append(thermal[other])
        speed = [flow[part, index] for part in range(3)]
        gain = TIME_INCREMENT * column(heat[pl.ds(index, 1), :])
        warmed[index] = advance(around, padded, 0, speed) + jnp.where(top, gain, 0.0)


def laser_heat(start_x, start_y, span_x, span_y, total_x, total_y, spots_a, spots_b):
    cells_x = start_x + jnp.arange(span_x, dtype=jnp.int32)
    cells_y = start_y + jnp.arange(span_y, dtype=jnp.int32)
    dist_x = (
        (cells_x[:, None] - spots_a[None, :] + total_x // 2) % total_x - total_x // 2
    ).astype(F32)
    dist_y = (
        (cells_y[:, None] - spots_b[None, :] + total_y // 2) % total_y - total_y // 2
    ).astype(F32)
    spot_x = jnp.exp(-(dist_x * dist_x) / (SPOT_RADIUS * SPOT_RADIUS))
    spot_y = jnp.exp(-(dist_y * dist_y) / (SPOT_RADIUS * SPOT_RADIUS))
    return LASER_POWER * jnp.dot(spot_x, spot_y.T, precision=lax.Precision.HIGHEST)


def tables_kernel(group, layers, place, diagonal, ratio, weight):
    length = group * layers
    mine = place[0]
    first = mine * layers
    diag = diagonal[...]
    ratio[0] = jnp.zeros_like(diag)

    def step(index, previous):
        current = 1.0 / (diag - previous)
        ratio[index] = current
        return current

    loop(1, length + 1, step, jnp.zeros_like(diag))

    def decay(low, high):
        return lax.fori_loop(
            low + 1, high + 1, lambda index, value: value * ratio[index], jnp.ones_like(diag)
        )

    def green(index):
        return 1.0 / (diag - ratio[index] - ratio[jnp.maximum(length - 1 - index, 0)])

    rounds = group.bit_length() - 1
    for turn in range(rounds):
        half = 1 << turn
        right = ((mine >> turn) & 1) == 1
        start = (mine >> (turn + 1)) << (turn + 1)
        cut = (start + half) * layers
        end = (start + 2 * half) * layers
        weight[4 * turn] = decay(cut - 1, end - 1)
        weight[4 * turn + 1] = decay(length - 1 - cut, length - 1 - start * layers)
        low = jnp.where(right, cut - 1, length - 1 - cut)
        high = jnp.where(right, first - 1, length - 1 - first - layers)
        weight[4 * turn + 2] = decay(low, high)
        weight[4 * turn + 3] = green(cut) * ratio[cut]
    inner = jnp.where(mine == group - 1, 0.0, 1.0)
    weight[4 * rounds] = inner * green(first + layers)


def source_kernel(
    length, place, star, before_x, before_y, table_y, table_z, ratio, source, ends, rows_
):
    _, layers, rows, depth = star.shape
    first = place[0] * layers
    for index in range(layers):
        rows_[pl.ds(8, rows), :] = star[1, index]
        rows_[pl.ds(7, 1), :] = before_y[pl.ds(index, 1), :]
        behind = star[0, index - 1] if index > 0 else before_x[...]
        sink = star[0, index] - behind
        sink = sink + (star[1, index] - rows_[pl.ds(7, rows), :])
        sink = sink + (star[2, index] - lane_shift(star[2, index], -1))
        source[index] = dot(dot(table_y[...], -sink), table_z[...])
    forward = source[0]
    for index in range(1, layers):
        forward = source[index] + ratio[first + index] * forward
    ends[0] = forward
    backward = source[layers - 1]
    for index in range(layers - 2, -1, -1):
        backward = source[index] + ratio[length - 1 - first - index] * backward
    ends[1] = backward


def face_rows(plane, edge):
    return (
        jnp.sum(plane * edge[0], axis=0, keepdims=True),
        jnp.sum(plane * edge[1], axis=0, keepdims=True),
    )


def faces_kernel(length, place, source, ratio, edge, faces, sweep):
    layers, rows, depth = source.shape
    first = place[0] * layers
    inside = lambda index: (index >= first) & (index < first + layers)
    zero = jnp.zeros((rows, depth), F32)

    def own(index):
        value = source[jnp.clip(index - first, 0, layers - 1)]
        return jnp.where(inside(index), value, 0.0)

    def down(index, previous):
        current = own(index) + ratio[index] * previous
        sweep[index] = current
        return current

    loop(0, length, down, zero)

    def up(back, carry):
        following, energy = carry
        index = length - 1 - back
        value = ratio[index + 1] * (sweep[index] + following)
        low, high = face_rows(value, edge)
        faces[pl.ds(index, 1), :] = low
        faces[pl.ds(length + index, 1), :] = high
        return value, energy + own(index) * value

    _, energy = loop(0, length, up, (zero, zero))
    faces[pl.ds(2 * length, 8), :] = jnp.broadcast_to(total(energy), (8, depth))


def merge_kernel(
    turn, last, length, place, ends, other, sums, faces, other_faces, weight, ratio,
    new_ends, new_sums, new_faces,
):
    count = faces.shape[0] - 8
    right = ((place[0] >> turn) & 1) == 1
    left_s = jnp.where(right, other[0], ends[0])
    right_s = jnp.where(right, ends[0], other[0])
    left_t = jnp.where(right, other[1], ends[1])
    right_t = jnp.where(right, ends[1], other[1])
    own = weight[4 * turn + 2]
    new_sums[0] = sums[0] + jnp.where(right, left_s * own, 0.0)
    new_sums[1] = sums[1] + jnp.where(right, 0.0, right_t * own)
    scale = ratio[length] if last else 1.0
    new_ends[0] = scale * (right_s + left_s * weight[4 * turn])
    new_ends[1] = scale * (left_t + right_t * weight[4 * turn + 1])
    new_faces[...] = faces[...] + other_faces[...]
    cross = 2.0 * total(left_s * right_t * weight[4 * turn + 3])
    new_faces[pl.ds(count, 8), :] = new_faces[pl.ds(count, 8), :] + cross


def coarse_kernel(
    length, place, source, ends, beyond, sums, faces, weight, ratio, edge,
    precond, image, report, sweep,
):
    layers, rows, depth = source.shape
    mine = place[0]
    first = mine * layers
    lone = weight.shape[0] - 1
    count = faces.shape[0] - 8
    forward = sums[0]
    for index in range(layers):
        forward = source[index] + ratio[first + index] * forward
        sweep[index] = forward
    value = weight[lone] * (sums[1] + ratio[first + layers] * forward)
    is_last = first + layers == length
    precond[layers] = jnp.where(is_last, beyond[1], value)
    for index in range(layers - 1, -1, -1):
        value = ratio[first + index + 1] * (sweep[index] + value)
        precond[index] = value
    lead, trail = edge[0], edge[1]

    def pull(index):
        below = faces[pl.ds(length + index, 1), :]
        above = faces[pl.ds(2 * length + index, 1), :]
        return below, above

    def down(index, previous):
        below, above = pull(index)
        current = lead * below + trail * above + ratio[index] * previous
        if isinstance(index, int):
            if index == 0:
                current = current + beyond[0]
            if index == length - 1:
                current = current + beyond[1]
        else:
            current = current + jnp.where(index == 0, beyond[0], 0.0)
            current = current + jnp.where(index == length - 1, beyond[1], 0.0)
        sweep[index] = current
        return current

    zero = jnp.zeros((rows, depth), F32)
    loop(0, length, down, zero)
    line = jnp.zeros((1, depth), F32)

    def up(back, carry):
        following, linked, squared = carry
        index = length - 1 - back
        value = ratio[index + 1] * (sweep[index] + following)
        sweep[index] = value
        low, high = face_rows(value, edge)
        report[pl.ds(index, 1), :] = low
        report[pl.ds(length + index, 1), :] = high
        below, above = pull(index)
        linked = linked + faces[pl.ds(index, 1), :] * below
        squared = squared + low * below + high * above
        return value, linked, squared

    _, linked, squared = loop(0, length, up, (zero, line, line))
    sweep[length] = sweep[0]
    for index in range(layers + 1):
        image[index] = sweep[first + index]
    head, tail = sweep[0], sweep[length - 1]
    linked = 2.0 * total(linked) + total(ends[1] * beyond[0] + ends[0] * beyond[1])
    squared = total(squared) + total(head * beyond[0] + tail * beyond[1])
    crossing = 2.0 * total(head * tail)
    where = 2 * length
    report[pl.ds(where, 1), :] = faces[pl.ds(count, 1), :]
    report[pl.ds(where + 1, 1), :] = jnp.broadcast_to(linked, (1, depth))
    report[pl.ds(where + 2, 1), :] = jnp.broadcast_to(squared, (1, depth))
    report[pl.ds(where + 3, 1), :] = jnp.broadcast_to(crossing, (1, depth))
    report[pl.ds(where + 4, 4), :] = jnp.zeros((4, depth), F32)


def physical_kernel(precond, image, table_y, table_z, precond_out, image_out):
    for index in range(precond.shape[0]):
        precond_out[index] = dot(dot(table_y[...], precond[index]), table_z[...])
        image_out[index] = dot(dot(table_y[...], image[index]), table_z[...])


def project_kernel(
    length, paired, place, star, precond, image, faces, table_z, *refs
):
    reports, (flow, pressure, field, rows_) = refs[:-4], refs[-4:]
    _, layers, rows, depth = star.shape
    first = place[0] * layers
    where = 2 * length
    sums = reports[0][pl.ds(where, 8), :]
    for other in reports[1:]:
        sums = sums + other[pl.ds(where, 8), :]
    pairs = jnp.zeros((1, depth), F32)
    for index in range(len(reports)):
        upper, lower = reports[index], reports[(index + 1) % len(reports)]
        pairs = pairs + jnp.sum(
            upper[pl.ds(0, length), :] * lower[pl.ds(length, length), :], axis=0, keepdims=True
        )
    energy, linked, squared, crossing = (sums[k : k + 1, 0:1] for k in range(4))
    if not paired:
        crossing = crossing + 2.0 * total(pairs)
    first_image = energy - linked
    step = energy / first_image
    beta = (energy * squared - linked * linked) / (first_image * first_image)
    rest = -linked / first_image
    second_image = (
        rest * rest * first_image
        + 2.0 * rest * step * (linked - squared)
        + step * step * (squared - crossing)
        - beta * beta * first_image
    )
    second_step = beta * energy / second_image
    alpha = step + second_step * (rest + beta)
    gamma = second_step * step
    for index in range(layers + 1):
        field[index] = alpha * precond[index] + gamma * image[index]
    own = pl.ds(2 * length + first, layers)
    following = alpha * faces[own, :] + gamma * reports[-1][pl.ds(first, layers), :]
    following = dot(following, table_z[...])
    for index in range(layers):
        value = field[index]
        pressure[index] = value
        rows_[pl.ds(0, rows), :] = value
        rows_[pl.ds(rows, 1), :] = following[index : index + 1]
        flow[0, index] = star[0, index] - (field[index + 1] - value)
        flow[1, index] = star[1, index] - (rows_[pl.ds(1, rows), :] - value)
        flow[2, index] = star[2, index] - (lane_shift(value, 1) - value)


def along(array, axis, by):
    length = lax.axis_size(axis)
    return lax.ppermute(array, axis, [(i, (i + by) % length) for i in range(length)])


def swapped(array, axis, bit):
    return lax.ppermute(array, axis, [(i, i ^ bit) for i in range(lax.axis_size(axis))])


def per_device(melt_flow, thermal_state, powder_flag, spot_lateral_a_cell, spot_lateral_b_cell):
    layers, rows, depth = thermal_state.shape
    count_x, count_y = lax.axis_size("gx"), lax.axis_size("gy")
    group = min(count_x, BLOCK // layers)
    blocks = count_x // group
    length = group * layers
    rounds = group.bit_length() - 1
    sine_y, values_y = sines(rows)
    sine_z, values_z = sines(depth)
    table_y = jnp.asarray(sine_y, F32)
    table_z = jnp.asarray(sine_z, F32)
    edge = jnp.asarray(
        np.broadcast_to(sine_y[[0, rows - 1]][:, :, None], (2, rows, depth)), F32
    )
    diagonal = jnp.asarray(2.0 + values_y[:, None] + values_z[None, :], F32)
    place = (lax.axis_index("gx") % group).astype(jnp.int32).reshape(1)
    plane = (rows, depth)

    states = jnp.concatenate([melt_flow, thermal_state[None]], 0)
    low_x = along(melt_flow[:, -2:], "gx", 1)
    high_x = along(melt_flow[:, :2], "gx", -1)
    low_t = along(thermal_state[-1, :, -1].reshape(1, rows), "gx", 1)
    high_t = along(thermal_state[0, :, -1].reshape(1, rows), "gx", -1)
    low_y = along(states[:, :, -2:], "gy", 1)
    high_y = along(states[:, :, :2], "gy", -1)
    far_low = along(thermal_state[-2:], "gx", 1)
    far_high = along(thermal_state[:2], "gx", -1)

    ratio, weight = call(
        functools.partial(tables_kernel, group, layers),
        [place, diagonal],
        [(length + 1,) + plane, (4 * rounds + 1,) + plane],
    )
    (star,) = call(
        march_kernel,
        [
            melt_flow, low_x, high_x, low_y, high_y, thermal_state, low_t, high_t,
            powder_flag.astype(jnp.int32),
        ],
        [(3, layers) + plane],
        [pltpu.VMEM((4, rows + 16, depth), F32)],
        scalars=0,
    )
    before_x = along(star[0, -1], "gx", 1)
    before_y = along(star[1, :, -1], "gy", 1)
    source, ends = call(
        functools.partial(source_kernel, length),
        [place, star, before_x, before_y, table_y, table_z, ratio],
        [(layers,) + plane, (2,) + plane],
        [pltpu.VMEM((rows + 16, depth), F32)],
    )
    (faces,) = call(
        functools.partial(faces_kernel, length),
        [place, source, ratio, edge],
        [(2 * length + 8, depth)],
        [pltpu.VMEM((length,) + plane, F32)],
    )
    below = along(faces[length : 2 * length], "gy", 1)
    above = along(faces[:length], "gy", -1)
    faces = jnp.concatenate([faces[:length], below, above, faces[2 * length :]], 0)
    sums = jnp.zeros((2,) + plane, F32)
    for turn in range(rounds):
        other = swapped(ends, "gx", 1 << turn)
        other_faces = swapped(faces, "gx", 1 << turn)
        ends, sums, faces = call(
            functools.partial(merge_kernel, turn, turn + 1 == rounds, length),
            [place, ends, other, sums, faces, other_faces, weight, ratio],
            [(2,) + plane, (2,) + plane, faces.shape],
        )
    if blocks == 1:
        beyond = ends
    else:
        beyond = jnp.stack([along(ends[0], "gx", group), along(ends[1], "gx", -group)])
    precond, image, report = call(
        functools.partial(coarse_kernel, length),
        [place, source, ends, beyond, sums, faces, weight, ratio, edge],
        [(layers + 1,) + plane, (layers + 1,) + plane, (2 * length + 8, depth)],
        [pltpu.VMEM((length + 1,) + plane, F32)],
    )
    if blocks > 1:
        ahead = along(image[0], "gx", -1)
        tail = place[0] == group - 1
        image = image.at[layers].set(jnp.where(tail, ahead, image[layers]))
        upper = along(report[:length], "gy", -1)
        crossing = jnp.sum(ahead * image[layers - 1]) + jnp.sum(upper * report[length : 2 * length])
        crossing = jnp.where(tail, 2.0 * crossing, 0.0)
        numbers = report[2 * length :]
        numbers = jnp.where(place[0] == group - 1, numbers, 0.0).at[3].set(crossing)
        report = report.at[2 * length :].set(lax.psum(numbers, "gx"))
    reports = [report] + [along(report, "gy", by) for by in range(1, count_y)]
    precond, image = call(
        physical_kernel,
        [precond, image, table_y, table_z],
        [(layers + 1,) + plane, (layers + 1,) + plane],
        scalars=0,
    )
    heat = laser_heat(
        lax.axis_index("gx") * layers,
        lax.axis_index("gy") * rows,
        layers,
        rows,
        layers * count_x,
        rows * count_y,
        spot_lateral_a_cell,
        spot_lateral_b_cell,
    )
    (warmed,) = call(
        heat_kernel,
        [thermal_state, far_low, far_high, low_y[3], high_y[3], melt_flow, heat],
        [(layers,) + plane],
        [pltpu.VMEM((1, rows + 16, depth), F32)],
        scalars=0,
    )
    flow, pressure = call(
        functools.partial(project_kernel, length, blocks > 1),
        [place, star, precond, image, faces, table_z] + reports,
        [(3, layers) + plane, (layers,) + plane],
        [pltpu.VMEM((layers + 1,) + plane, F32), pltpu.VMEM((rows + 16, depth), F32)],
    )
    return (flow, warmed, pressure)


def solution(mesh):
    placed = (
        P(None, ("runs", "gx"), "gy", None),
        P(("runs", "gx"), "gy", None),
        P(("runs", "gx"), "gy", None),
        P("runs"),
        P("runs"),
    )
    return jax.shard_map(
        per_device,
        mesh=mesh,
        in_specs=placed,
        out_specs=(
            P(None, ("runs", "gx"), "gy", None),
            P(("runs", "gx"), "gy", None),
            P(("runs", "gx"), "gy", None),
        ),
        check_vma=False,
    )
```

```python
import functools
import math

import jax
import jax.numpy as jnp
import numpy as np
from jax import lax
from jax.experimental import pallas as pl
from jax.experimental.pallas import tpu as pltpu
from jax.sharding import PartitionSpec as P

BLOCK = 128

TIME_INCREMENT = 0.2
MARANGONI = 1.5
DRAG_RATE = 4.0
LASER_POWER = 3.0
SPOT_RADIUS = 5.0

F32 = jnp.float32
VMEM = pl.BlockSpec(memory_space=pltpu.VMEM)
SMEM = pl.BlockSpec(memory_space=pltpu.SMEM)


def call(body, operands, shapes, scratch=(), scalars=1, flops=1 << 20):
    out_shape = [jax.ShapeDtypeStruct(shape, F32) for shape in shapes]
    moved = 4 * sum(math.prod(shape) for shape in shapes)
    return pl.pallas_call(
        body,
        out_shape=out_shape,
        in_specs=[SMEM] * scalars + [VMEM] * (len(operands) - scalars),
        out_specs=[VMEM] * len(shapes),
        scratch_shapes=list(scratch),
        compiler_params=pltpu.CompilerParams(vmem_limit_bytes=44 << 20),
        cost_estimate=pl.CostEstimate(flops=flops, bytes_accessed=2 * moved, transcendentals=0),
    )(*operands)


def dot(left, right):
    return jnp.dot(left, right, precision=lax.Precision.HIGHEST, preferred_element_type=F32)


def total(cells):
    return jnp.sum(jnp.sum(cells, axis=0, keepdims=True), axis=1, keepdims=True)


def loop(low, high, body, start):
    if isinstance(high, int) and isinstance(low, int) and high - low <= 24:
        carry = start
        for index in range(low, high):
            carry = body(index, carry)
        return carry
    return lax.fori_loop(low, high, body, start)


def sines(length):
    positions = np.arange(length) + 1.0
    step = math.pi / (length + 1)
    table = np.sqrt(2.0 / (length + 1)) * np.sin(step * positions[:, None] * positions[None, :])
    return table, 2.0 - 2.0 * np.cos(step * positions)


def lane_shift(cells, offset):
    width = cells.shape[1]
    lane = lax.broadcasted_iota(jnp.int32, cells.shape, 1)
    moved = pltpu.roll(cells, (-offset) % width, 1)
    keep = lane < width - offset if offset > 0 else lane >= -offset
    return jnp.where(keep, moved, 0.0)


def column(row):
    length = row.shape[1]
    shape = (length, length)
    same = lax.broadcasted_iota(jnp.int32, shape, 0) == lax.broadcasted_iota(jnp.int32, shape, 1)
    return jnp.sum(jnp.where(same, row, 0.0), axis=1, keepdims=True)


def advance(layers, padded, index, speed, start=0):
    middle = layers[2]
    rows = middle.shape[0]
    speed_x, speed_y, speed_z = speed
    ahead = speed_x >= 0.0
    near = jnp.where(ahead, layers[1], layers[3])
    far = jnp.where(ahead, layers[0], layers[4])
    rate = jnp.abs(speed_x) * (1.5 * middle - 2.0 * near + 0.5 * far)
    ahead = speed_y >= 0.0
    near = jnp.where(ahead, padded[index, pl.ds(7 + start, rows), :], padded[index, pl.ds(9 + start, rows), :])
    far = jnp.where(ahead, padded[index, pl.ds(6 + start, rows), :], padded[index, pl.ds(10 + start, rows), :])
    rate = rate + jnp.abs(speed_y) * (1.5 * middle - 2.0 * near + 0.5 * far)
    ahead = speed_z >= 0.0
    near = jnp.where(ahead, lane_shift(middle, -1), lane_shift(middle, 1))
    far = jnp.where(ahead, lane_shift(middle, -2), lane_shift(middle, 2))
    rate = rate + jnp.abs(speed_z) * (1.5 * middle - 2.0 * near + 0.5 * far)
    return middle - TIME_INCREMENT * rate


def pad_rows(padded, index, before, middle, after):
    rows = middle.shape[0]
    padded[index, pl.ds(8, rows), :] = middle
    padded[index, pl.ds(6, 2), :] = before
    padded[index, pl.ds(8 + rows, 2), :] = after


def march_layer(refs, padded, index, parts, start, count):
    flow, low_x, high_x, thermal, flag = refs
    _, layers, rows, depth = flow.shape
    span = pl.ds(start, count)
    surface = 6 * rows
    speed = [flow[part, index, span, :] for part in range(3)]
    drag = 1.0 / (1.0 + TIME_INCREMENT * DRAG_RATE * flag[index, span, :].astype(F32))
    top = lax.broadcasted_iota(jnp.int32, (count, depth), 1) == depth - 1
    pull = -MARANGONI * 0.5 * TIME_INCREMENT
    out = []
    for part in parts:
        around = []
        for other in range(index - 2, index + 3):
            if other < 0:
                first = (2 * part + other + 2) * rows + start
                around.append(low_x[pl.ds(first, count), :])
            elif other >= layers:
                first = (2 * part + other - layers) * rows + start
                around.append(high_x[pl.ds(first, count), :])
            else:
                around.append(flow[part, other, span, :])
        moved = advance(around, padded, part, speed, start)
        if part == 0:
            edge = lambda halo: column(halo[pl.ds(surface, 1), pl.ds(0, rows)])
            behind = thermal[index - 1] if index > 0 else edge(low_x)
            before = thermal[index + 1] if index + 1 < layers else edge(high_x)
            moved = moved + jnp.where(top, pull * (before - behind), 0.0)
        if part == 1:
            slope = padded[3, pl.ds(9 + start, count), :] - padded[3, pl.ds(7 + start, count), :]
            moved = moved + jnp.where(top, pull * slope, 0.0)
        out.append(moved * drag)
    return out


def pad_layer(refs, low_y, high_y, padded, index):
    flow, _, _, thermal, _ = refs
    for part in range(3):
        pad_rows(padded, part, low_y[part, index], flow[part, index], high_y[part, index])
    pad_rows(padded, 3, low_y[3, index], thermal[index], high_y[3, index])


def rim_kernel(
    flow, low_x, high_x, thermal, flag, low_y, high_y, weight, star, side_x, side_y, padded
):
    refs = (flow, low_x, high_x, thermal, flag)
    _, layers, rows, depth = flow.shape
    for index in range(layers):
        pad_layer(refs, low_y, high_y, padded, index)
        if index == layers - 1:
            for part, value in enumerate(march_layer(refs, padded, index, range(3), 0, rows)):
                star[part] = value
                if part == 0:
                    side_x[...] = value
                if part == 1:
                    side_y[pl.ds(index, 1), :] = value[rows - 1 :, :]
        else:
            (value,) = march_layer(refs, padded, index, [1], rows - 8, 8)
            side_y[pl.ds(index, 1), :] = value[7:, :]


def march_kernel(
    flow, low_x, high_x, thermal, flag, low_y, high_y, rim, table_y, table_z,
    star, source, padded,
):
    refs = (flow, low_x, high_x, thermal, flag)
    _, layers, rows, depth = flow.shape
    top = lax.broadcasted_iota(jnp.int32, (rows, depth), 0) == 0
    for index in range(layers):
        if index == layers - 1:
            value = [rim[part] for part in range(3)]
        else:
            pad_layer(refs, low_y, high_y, padded, index)
            value = march_layer(refs, padded, index, range(3), 0, rows)
        for part in range(3):
            star[part, index] = value[part]
        sink = value[0]
        if index > 0:
            sink = sink - star[0, index - 1]
        sink = sink + (value[1] - jnp.where(top, 0.0, pltpu.roll(value[1], 1, 0)))
        sink = sink + (value[2] - lane_shift(value[2], -1))
        source[index] = dot(dot(table_y[...], -sink), table_z[...])


def pack_kernel(flow, thermal, ahead, behind, planes, sems):
    parts, layers, rows, depth = flow.shape
    copies = []
    for part in range(parts):
        for layer in range(2):
            for target, source in ((ahead, layers - 2 + layer), (behind, layer)):
                copies.append(
                    (flow.at[part, source], target.at[pl.ds((2 * part + layer) * rows, rows), :])
                )
    copies.append((thermal.at[layers - 1], planes.at[0]))
    copies.append((thermal.at[0], planes.at[1]))
    copies = [
        pltpu.make_async_copy(source, target, sems.at[index])
        for index, (source, target) in enumerate(copies)
    ]
    for copy in copies:
        copy.start()
    shape = (rows, rows)
    same = lax.broadcasted_iota(jnp.int32, shape, 0) == lax.broadcasted_iota(jnp.int32, shape, 1)
    for copy in copies[-2:]:
        copy.wait()
    for side, target in enumerate((ahead, behind)):
        tops = planes[side][:, depth - 1 :]
        row = jnp.sum(jnp.where(same, tops, 0.0), axis=0, keepdims=True)
        target[pl.ds(2 * parts * rows, 8), pl.ds(0, rows)] = jnp.broadcast_to(row, (8, rows))
    for copy in copies[:-2]:
        copy.wait()


def heat_kernel(span, thermal, halo, low_y, high_y, flow, heat, warmed, padded):
    layers, rows, depth = thermal.shape
    top = lax.broadcasted_iota(jnp.int32, (rows, depth), 1) == depth - 1
    for index in span:
        pad_rows(padded, 0, low_y[3, index], thermal[index], high_y[3, index])
        around = []
        for other in range(index - 2, index + 3):
            if other < 0:
                around.append(halo[other + 2])
            elif other >= layers:
                around.append(halo[other - layers])
            else:
                around.append(thermal[other])
        speed = [flow[part, index] for part in range(3)]
        gain = TIME_INCREMENT * column(heat[pl.ds(index, 1), :])
        moved = advance(around, padded, 0, speed) + jnp.where(top, gain, 0.0)
        warmed[index - span[0]] = moved


def laser_heat(start_x, start_y, span_x, span_y, total_x, total_y, spots_a, spots_b):
    cells_x = start_x + jnp.arange(span_x, dtype=jnp.int32)
    cells_y = start_y + jnp.arange(span_y, dtype=jnp.int32)
    dist_x = (
        (cells_x[:, None] - spots_a[None, :] + total_x // 2) % total_x - total_x // 2
    ).astype(F32)
    dist_y = (
        (cells_y[:, None] - spots_b[None, :] + total_y // 2) % total_y - total_y // 2
    ).astype(F32)
    spot_x = jnp.exp(-(dist_x * dist_x) / (SPOT_RADIUS * SPOT_RADIUS))
    spot_y = jnp.exp(-(dist_y * dist_y) / (SPOT_RADIUS * SPOT_RADIUS))
    return LASER_POWER * jnp.dot(spot_x, spot_y.T, precision=lax.Precision.HIGHEST)


def tables_kernel(group, layers, place, diagonal, ratio, weight):
    length = group * layers
    mine = place[0]
    first = mine * layers
    diag = diagonal[...]
    ratio[0] = jnp.zeros_like(diag)

    def step(index, previous):
        current = 1.0 / (diag - previous)
        ratio[index] = current
        return current

    loop(1, length + 1, step, jnp.zeros_like(diag))

    def decay(low, high):
        return lax.fori_loop(
            low + 1, high + 1, lambda index, value: value * ratio[index], jnp.ones_like(diag)
        )

    def green(index):
        return 1.0 / (diag - ratio[index] - ratio[jnp.maximum(length - 1 - index, 0)])

    rounds = group.bit_length() - 1
    for turn in range(rounds):
        half = 1 << turn
        right = ((mine >> turn) & 1) == 1
        start = (mine >> (turn + 1)) << (turn + 1)
        cut = (start + half) * layers
        end = (start + 2 * half) * layers
        weight[4 * turn] = decay(cut - 1, end - 1)
        weight[4 * turn + 1] = decay(length - 1 - cut, length - 1 - start * layers)
        low = jnp.where(right, cut - 1, length - 1 - cut)
        high = jnp.where(right, first - 1, length - 1 - first - layers)
        weight[4 * turn + 2] = decay(low, high)
        weight[4 * turn + 3] = green(cut) * ratio[cut]
    inner = jnp.where(mine == group - 1, 0.0, 1.0)
    weight[4 * rounds] = inner * green(first + layers)


def face_rows(plane, edge):
    return (
        jnp.sum(plane * edge[0], axis=0, keepdims=True),
        jnp.sum(plane * edge[1], axis=0, keepdims=True),
    )


def source_kernel(
    length, place, partial, before_x, before_y, table_y, table_z, ratio, edge, thermal,
    source, message, head, tail, late, sweep,
):
    layers, rows, depth = partial.shape
    first = place[0] * layers
    inside = lambda index: (index >= first) & (index < first + layers)
    zero = jnp.zeros((rows, depth), F32)
    late[...] = thermal[layers - 2 :]
    extra = dot(before_y[...], table_z[...])
    for index in range(layers):
        value = partial[index] + edge[0] * extra[index : index + 1]
        if index == 0:
            value = value + dot(dot(table_y[...], before_x[...]), table_z[...])
        source[index] = value
    forward = source[0]
    for index in range(1, layers):
        forward = source[index] + ratio[first + index] * forward
    message[pl.ds(0, rows), :] = forward
    backward = source[layers - 1]
    for index in range(layers - 2, -1, -1):
        backward = source[index] + ratio[length - 1 - first - index] * backward
    message[pl.ds(rows, rows), :] = backward

    def own(index):
        value = source[jnp.clip(index - first, 0, layers - 1)]
        return jnp.where(inside(index), value, 0.0)

    def down(index, previous):
        current = own(index) + ratio[index] * previous
        sweep[index] = current
        return current

    loop(0, length, down, zero)

    def up(back, carry):
        following, energy = carry
        index = length - 1 - back
        value = ratio[index + 1] * (sweep[index] + following)
        low, high = face_rows(value, edge)
        head[pl.ds(index, 1), :] = low
        tail[pl.ds(index, 1), :] = high
        return value, energy + own(index) * value

    _, energy = loop(0, length, up, (zero, zero))
    message[pl.ds(2 * rows, length), :] = head[...]
    message[pl.ds(2 * rows + length, length), :] = tail[...]
    energy = jnp.broadcast_to(total(energy), (8, depth))
    message[pl.ds(2 * rows + 2 * length, 8), :] = energy


def joined(turn, place, message, other, sums, weight, new_sums):
    rows, depth = weight.shape[1:]
    right = ((place[0] >> turn) & 1) == 1
    upper, lower = pl.ds(0, rows), pl.ds(rows, rows)
    left_s = jnp.where(right, other[upper, :], message[upper, :])
    right_s = jnp.where(right, message[upper, :], other[upper, :])
    left_t = jnp.where(right, other[lower, :], message[lower, :])
    right_t = jnp.where(right, message[lower, :], other[lower, :])
    own = weight[4 * turn + 2]
    new_sums[0] = sums[0] + jnp.where(right, left_s * own, 0.0)
    new_sums[1] = sums[1] + jnp.where(right, 0.0, right_t * own)
    forward = right_s + left_s * weight[4 * turn]
    backward = left_t + right_t * weight[4 * turn + 1]
    energy = 2.0 * total(left_s * right_t * weight[4 * turn + 3])
    where = pl.ds(message.shape[0] - 8, 8)
    return forward, backward, message[where, :] + other[where, :] + energy


def merge_kernel(
    turn, length, place, message, other, sums, weight, thermal,
    new_message, new_sums, head, tail, late,
):
    rows, depth = weight.shape[1:]
    late[...] = thermal[:2]
    forward, backward, energy = joined(turn, place, message, other, sums, weight, new_sums)
    new_message[pl.ds(0, rows), :] = forward
    new_message[pl.ds(rows, rows), :] = backward
    both = pl.ds(2 * rows, 2 * length)
    new_message[both, :] = message[both, :] + other[both, :]
    new_message[pl.ds(2 * rows + 2 * length, 8), :] = energy
    head[...] = new_message[pl.ds(2 * rows, length), :]
    tail[...] = new_message[pl.ds(2 * rows + length, length), :]


def close_kernel(
    turn, length, place, message, other, sums, weight, ratio, below, below_far, above, above_far,
    ends, new_sums, faces,
):
    rows, depth = weight.shape[1:]
    forward, backward, energy = joined(turn, place, message, other, sums, weight, new_sums)
    ends[0] = ratio[length] * forward
    ends[1] = ratio[length] * backward
    own = pl.ds(2 * rows, length)
    faces[pl.ds(0, length), :] = message[own, :] + other[own, :]
    faces[pl.ds(length, length), :] = below[...] + below_far[...]
    faces[pl.ds(2 * length, length), :] = above[...] + above_far[...]
    faces[pl.ds(3 * length, 8), :] = energy


def coarse_kernel(
    length, place, source, ends, beyond, sums, faces, weight, ratio, edge,
    precond, image, report, sweep,
):
    layers, rows, depth = source.shape
    mine = place[0]
    first = mine * layers
    lone = weight.shape[0] - 1
    count = faces.shape[0] - 8
    forward = sums[0]
    for index in range(layers):
        forward = source[index] + ratio[first + index] * forward
        sweep[index] = forward
    value = weight[lone] * (sums[1] + ratio[first + layers] * forward)
    is_last = first + layers == length
    precond[layers] = jnp.where(is_last, beyond[1], value)
    for index in range(layers - 1, -1, -1):
        value = ratio[first + index + 1] * (sweep[index] + value)
        precond[index] = value
    lead, trail = edge[0], edge[1]

    def pull(index):
        below = faces[pl.ds(length + index, 1), :]
        above = faces[pl.ds(2 * length + index, 1), :]
        return below, above

    def down(index, previous):
        below, above = pull(index)
        current = lead * below + trail * above + ratio[index] * previous
        if isinstance(index, int):
            if index == 0:
                current = current + beyond[0]
            if index == length - 1:
                current = current + beyond[1]
        else:
            current = current + jnp.where(index == 0, beyond[0], 0.0)
            current = current + jnp.where(index == length - 1, beyond[1], 0.0)
        sweep[index] = current
        return current

    zero = jnp.zeros((rows, depth), F32)
    loop(0, length, down, zero)
    line = jnp.zeros((1, depth), F32)

    def up(back, carry):
        following, linked, squared = carry
        index = length - 1 - back
        value = ratio[index + 1] * (sweep[index] + following)
        sweep[index] = value
        low, high = face_rows(value, edge)
        report[pl.ds(index, 1), :] = low
        report[pl.ds(length + index, 1), :] = high
        below, above = pull(index)
        linked = linked + faces[pl.ds(index, 1), :] * below
        squared = squared + low * below + high * above
        return value, linked, squared

    _, linked, squared = loop(0, length, up, (zero, line, line))
    sweep[length] = sweep[0]
    for index in range(layers + 1):
        image[index] = sweep[first + index]
    head, tail = sweep[0], sweep[length - 1]
    linked = 2.0 * total(linked) + total(ends[1] * beyond[0] + ends[0] * beyond[1])
    squared = total(squared) + total(head * beyond[0] + tail * beyond[1])
    crossing = 2.0 * total(head * tail)
    where = 2 * length
    report[pl.ds(where, 1), :] = faces[pl.ds(count, 1), :]
    report[pl.ds(where + 1, 1), :] = jnp.broadcast_to(linked, (1, depth))
    report[pl.ds(where + 2, 1), :] = jnp.broadcast_to(squared, (1, depth))
    report[pl.ds(where + 3, 1), :] = jnp.broadcast_to(crossing, (1, depth))
    report[pl.ds(where + 4, 4), :] = jnp.zeros((4, depth), F32)


def physical_kernel(precond, image, table_y, table_z, precond_out, image_out):
    for index in range(precond.shape[0]):
        precond_out[index] = dot(dot(table_y[...], precond[index]), table_z[...])
        image_out[index] = dot(dot(table_y[...], image[index]), table_z[...])


def project_kernel(
    length, paired, place, star, precond, image, faces, table_z, warm_low, warm_high, *refs
):
    reports, (flow, pressure, warmed, field, rows_) = refs[:-5], refs[-5:]
    warmed[:2] = warm_low[...]
    warmed[2:] = warm_high[...]
    _, layers, rows, depth = star.shape
    first = place[0] * layers
    where = 2 * length
    sums = reports[0][pl.ds(where, 8), :]
    for other in reports[1:]:
        sums = sums + other[pl.ds(where, 8), :]
    pairs = jnp.zeros((1, depth), F32)
    for index in range(len(reports)):
        upper, lower = reports[index], reports[(index + 1) % len(reports)]
        pairs = pairs + jnp.sum(
            upper[pl.ds(0, length), :] * lower[pl.ds(length, length), :], axis=0, keepdims=True
        )
    energy, linked, squared, crossing = (sums[k : k + 1, 0:1] for k in range(4))
    if not paired:
        crossing = crossing + 2.0 * total(pairs)
    first_image = energy - linked
    step = energy / first_image
    beta = (energy * squared - linked * linked) / (first_image * first_image)
    rest = -linked / first_image
    second_image = (
        rest * rest * first_image
        + 2.0 * rest * step * (linked - squared)
        + step * step * (squared - crossing)
        - beta * beta * first_image
    )
    second_step = beta * energy / second_image
    alpha = step + second_step * (rest + beta)
    gamma = second_step * step
    for index in range(layers + 1):
        field[index] = alpha * precond[index] + gamma * image[index]
    own = pl.ds(2 * length + first, layers)
    following = alpha * faces[own, :] + gamma * reports[-1][pl.ds(first, layers), :]
    following = dot(following, table_z[...])
    for index in range(layers):
        value = field[index]
        pressure[index] = value
        rows_[pl.ds(0, rows), :] = value
        rows_[pl.ds(rows, 1), :] = following[index : index + 1]
        flow[0, index] = star[0, index] - (field[index + 1] - value)
        flow[1, index] = star[1, index] - (rows_[pl.ds(1, rows), :] - value)
        flow[2, index] = star[2, index] - (lane_shift(value, 1) - value)


def along(array, axis, by):
    length = lax.axis_size(axis)
    return lax.ppermute(array, axis, [(i, (i + by) % length) for i in range(length)])


def swapped(array, bit, by=0):
    count_x, count_y = lax.axis_size("gx"), lax.axis_size("gy")
    pairs = [
        (x * count_y + y, (x ^ bit) * count_y + (y + by) % count_y)
        for x in range(count_x)
        for y in range(count_y)
    ]
    return lax.ppermute(array, ("gx", "gy"), pairs)


def pack(melt_flow, thermal_state):
    parts, layers, rows, depth = melt_flow.shape
    shape = jax.ShapeDtypeStruct((2 * parts * rows + 8, max(rows, depth)), F32)
    return pl.pallas_call(
        pack_kernel,
        out_shape=[shape, shape],
        in_specs=[pl.BlockSpec(memory_space=pl.ANY)] * 2,
        out_specs=[VMEM, VMEM],
        scratch_shapes=[
            pltpu.VMEM((2, rows, depth), F32),
            pltpu.SemaphoreType.DMA((4 * parts + 2,)),
        ],
    )(melt_flow, thermal_state)


def per_device(melt_flow, thermal_state, powder_flag, spot_lateral_a_cell, spot_lateral_b_cell):
    layers, rows, depth = thermal_state.shape
    count_x, count_y = lax.axis_size("gx"), lax.axis_size("gy")
    group = min(count_x, BLOCK // layers)
    blocks = count_x // group
    length = group * layers
    rounds = group.bit_length() - 1
    sine_y, values_y = sines(rows)
    sine_z, values_z = sines(depth)
    table_y = jnp.asarray(sine_y, F32)
    table_z = jnp.asarray(sine_z, F32)
    edge = jnp.asarray(
        np.broadcast_to(sine_y[[0, rows - 1]][:, :, None], (2, rows, depth)), F32
    )
    diagonal = jnp.asarray(2.0 + values_y[:, None] + values_z[None, :], F32)
    place = (lax.axis_index("gx") % group).astype(jnp.int32).reshape(1)
    plane = (rows, depth)
    line = (length, depth)
    padded = pltpu.VMEM((4, rows + 16, depth), F32)

    ahead, behind = pack(melt_flow, thermal_state)
    low_x = along(ahead, "gx", 1)
    high_x = along(behind, "gx", -1)
    states = jnp.concatenate([melt_flow, thermal_state[None]], 0)
    low_y = along(states[:, :, -2:], "gy", 1)
    high_y = along(states[:, :, :2], "gy", -1)
    ratio, weight = call(
        functools.partial(tables_kernel, group, layers),
        [place, diagonal],
        [(length + 1,) + plane, (4 * rounds + 1,) + plane],
    )
    marched = [melt_flow, low_x, high_x, thermal_state, powder_flag, low_y, high_y]
    rim, side_x, side_y = call(
        rim_kernel, marched + [weight], [(3,) + plane, plane, (layers, depth)], [padded], scalars=0
    )
    before_x = along(side_x, "gx", 1)
    before_y = along(side_y, "gy", 1)
    star, partial = call(
        march_kernel,
        marched + [rim, table_y, table_z],
        [(3, layers) + plane, (layers,) + plane],
        [padded],
        scalars=0,
    )
    tall = (2 * rows + 2 * length + 8, depth)
    source, message, head, tail, late_low = call(
        functools.partial(source_kernel, length),
        [place, partial, before_x, before_y, table_y, table_z, ratio, edge, thermal_state],
        [(layers,) + plane, tall, line, line, (2,) + plane],
        [pltpu.VMEM((length,) + plane, F32)],
    )
    sums = jnp.zeros((2,) + plane, F32)
    late_high = thermal_state[:2]
    for turn in range(rounds - 1):
        other = swapped(message, 1 << turn)
        message, sums, head, tail, late_high = call(
            functools.partial(merge_kernel, turn, length),
            [place, message, other, sums, weight, thermal_state],
            [tall, (2,) + plane, line, line, (2,) + plane],
        )
    bit = group >> 1
    other = swapped(message, bit)
    ends, sums, faces = call(
        functools.partial(close_kernel, rounds - 1, length),
        [
            place, message, other, sums, weight, ratio,
            swapped(tail, 0, 1), swapped(tail, bit, 1),
            swapped(head, 0, -1), swapped(head, bit, -1),
        ],
        [(2,) + plane, (2,) + plane, (3 * length + 8, depth)],
    )
    if blocks == 1:
        beyond = ends
    else:
        beyond = jnp.stack([along(ends[0], "gx", group), along(ends[1], "gx", -group)])
    precond, image, report = call(
        functools.partial(coarse_kernel, length),
        [place, source, ends, beyond, sums, faces, weight, ratio, edge],
        [(layers + 1,) + plane, (layers + 1,) + plane, (2 * length + 8, depth)],
        [pltpu.VMEM((length + 1,) + plane, F32)],
    )
    if blocks > 1:
        onward = along(image[0], "gx", -1)
        at_end = place[0] == group - 1
        image = image.at[layers].set(jnp.where(at_end, onward, image[layers]))
        upper = along(report[:length], "gy", -1)
        crossing = jnp.sum(onward * image[layers - 1])
        crossing = crossing + jnp.sum(upper * report[length : 2 * length])
        numbers = report[2 * length :].at[3].set(2.0 * crossing)
        numbers = lax.psum(jnp.where(at_end, numbers, 0.0), "gx")
        report = report.at[2 * length :].set(numbers)
    reports = [report] + [along(report, "gy", by) for by in range(1, count_y)]
    precond, image = call(
        physical_kernel,
        [precond, image, table_y, table_z],
        [(layers + 1,) + plane, (layers + 1,) + plane],
        scalars=0,
    )
    heat = laser_heat(
        lax.axis_index("gx") * layers,
        lax.axis_index("gy") * rows,
        layers,
        rows,
        layers * count_x,
        rows * count_y,
        spot_lateral_a_cell,
        spot_lateral_b_cell,
    )
    warmed = []
    late = (along(late_low, "gx", 1), along(late_high, "gx", -1))
    for halo, span in zip(late, (range(0, 2), range(2, layers))):
        warmed += call(
            functools.partial(heat_kernel, span),
            [thermal_state, halo, low_y, high_y, melt_flow, heat],
            [(len(span),) + plane],
            [pltpu.VMEM((1, rows + 16, depth), F32)],
            scalars=0,
        )
    flow, pressure, warmed = call(
        functools.partial(project_kernel, length, blocks > 1),
        [place, star, precond, image, faces, table_z] + warmed + reports,
        [(3, layers) + plane, (layers,) + plane, (layers,) + plane],
        [pltpu.VMEM((layers + 1,) + plane, F32), pltpu.VMEM((rows + 16, depth), F32)],
    )
    return (flow, warmed, pressure)


def solution(mesh):
    placed = (
        P(None, ("runs", "gx"), "gy", None),
        P(("runs", "gx"), "gy", None),
        P(("runs", "gx"), "gy", None),
        P("runs"),
        P("runs"),
    )
    return jax.shard_map(
        per_device,
        mesh=mesh,
        in_specs=placed,
        out_specs=(
            P(None, ("runs", "gx"), "gy", None),
            P(("runs", "gx"), "gy", None),
            P(("runs", "gx"), "gy", None),
        ),
        check_vma=False,
    )
```

```python
import functools
import math

import jax
import jax.numpy as jnp
import numpy as np
from jax import lax
from jax.experimental import pallas as pl
from jax.experimental.pallas import tpu as pltpu
from jax.sharding import PartitionSpec as P

BLOCK = 128

TIME_INCREMENT = 0.2
MARANGONI = 1.5
DRAG_RATE = 4.0
LASER_POWER = 3.0
SPOT_RADIUS = 5.0

F32 = jnp.float32
VMEM = pl.BlockSpec(memory_space=pltpu.VMEM)
SMEM = pl.BlockSpec(memory_space=pltpu.SMEM)


def call(body, operands, shapes, scratch=(), scalars=1, flops=1 << 20):
    out_shape = [jax.ShapeDtypeStruct(shape, F32) for shape in shapes]
    moved = 4 * sum(math.prod(shape) for shape in shapes)
    held = moved + 4 * sum(operand.size for operand in operands)
    held += 4 * sum(math.prod(space.shape) for space in scratch)
    return pl.pallas_call(
        body,
        out_shape=out_shape,
        in_specs=[SMEM] * scalars + [VMEM] * (len(operands) - scalars),
        out_specs=[VMEM] * len(shapes),
        scratch_shapes=list(scratch),
        compiler_params=pltpu.CompilerParams(vmem_limit_bytes=held + (4 << 20)),
        cost_estimate=pl.CostEstimate(flops=flops, bytes_accessed=2 * moved, transcendentals=0),
    )(*operands)


def dot(left, right):
    return jnp.dot(left, right, precision=lax.Precision.HIGHEST, preferred_element_type=F32)


def total(cells):
    return jnp.sum(jnp.sum(cells, axis=0, keepdims=True), axis=1, keepdims=True)


def loop(low, high, body, start):
    if isinstance(high, int) and isinstance(low, int) and high - low <= 24:
        carry = start
        for index in range(low, high):
            carry = body(index, carry)
        return carry
    return lax.fori_loop(low, high, body, start)


def sines(length):
    positions = np.arange(length) + 1.0
    step = math.pi / (length + 1)
    table = np.sqrt(2.0 / (length + 1)) * np.sin(step * positions[:, None] * positions[None, :])
    return table, 2.0 - 2.0 * np.cos(step * positions)


def lane_shift(cells, offset):
    width = cells.shape[1]
    lane = lax.broadcasted_iota(jnp.int32, cells.shape, 1)
    moved = pltpu.roll(cells, (-offset) % width, 1)
    keep = lane < width - offset if offset > 0 else lane >= -offset
    return jnp.where(keep, moved, 0.0)


def column(row):
    length = row.shape[1]
    shape = (length, length)
    same = lax.broadcasted_iota(jnp.int32, shape, 0) == lax.broadcasted_iota(jnp.int32, shape, 1)
    return jnp.sum(jnp.where(same, row, 0.0), axis=1, keepdims=True)


def advance(layers, padded, index, speed, start=0):
    middle = layers[2]
    rows = middle.shape[0]
    speed_x, speed_y, speed_z = speed
    ahead = speed_x >= 0.0
    near = jnp.where(ahead, layers[1], layers[3])
    far = jnp.where(ahead, layers[0], layers[4])
    rate = jnp.abs(speed_x) * (1.5 * middle - 2.0 * near + 0.5 * far)
    ahead = speed_y >= 0.0
    near = jnp.where(ahead, padded[index, pl.ds(7 + start, rows), :], padded[index, pl.ds(9 + start, rows), :])
    far = jnp.where(ahead, padded[index, pl.ds(6 + start, rows), :], padded[index, pl.ds(10 + start, rows), :])
    rate = rate + jnp.abs(speed_y) * (1.5 * middle - 2.0 * near + 0.5 * far)
    ahead = speed_z >= 0.0
    near = jnp.where(ahead, lane_shift(middle, -1), lane_shift(middle, 1))
    far = jnp.where(ahead, lane_shift(middle, -2), lane_shift(middle, 2))
    rate = rate + jnp.abs(speed_z) * (1.5 * middle - 2.0 * near + 0.5 * far)
    return middle - TIME_INCREMENT * rate


def pad_rows(padded, index, before, middle, after):
    rows = middle.shape[0]
    padded[index, pl.ds(8, rows), :] = middle
    padded[index, pl.ds(6, 2), :] = before
    padded[index, pl.ds(8 + rows, 2), :] = after


def march_layer(refs, padded, index, parts, start, count):
    flow, low_x, high_x, thermal, flag = refs
    _, layers, rows, depth = flow.shape
    span = pl.ds(start, count)
    surface = 6 * rows
    speed = [flow[part, index, span, :] for part in range(3)]
    drag = 1.0 / (1.0 + TIME_INCREMENT * DRAG_RATE * flag[index, span, :].astype(F32))
    top = lax.broadcasted_iota(jnp.int32, (count, depth), 1) == depth - 1
    pull = -MARANGONI * 0.5 * TIME_INCREMENT
    out = []
    for part in parts:
        around = []
        for other in range(index - 2, index + 3):
            if other < 0:
                first = (2 * part + other + 2) * rows + start
                around.append(low_x[pl.ds(first, count), :])
            elif other >= layers:
                first = (2 * part + other - layers) * rows + start
                around.append(high_x[pl.ds(first, count), :])
            else:
                around.append(flow[part, other, span, :])
        moved = advance(around, padded, part, speed, start)
        if part == 0:
            edge = lambda halo: column(halo[pl.ds(surface, 1), pl.ds(0, rows)])
            behind = thermal[index - 1] if index > 0 else edge(low_x)
            before = thermal[index + 1] if index + 1 < layers else edge(high_x)
            moved = moved + jnp.where(top, pull * (before - behind), 0.0)
        if part == 1:
            slope = padded[3, pl.ds(9 + start, count), :] - padded[3, pl.ds(7 + start, count), :]
            moved = moved + jnp.where(top, pull * slope, 0.0)
        out.append(moved * drag)
    return out


def pad_layer(refs, low_y, high_y, padded, index):
    flow, _, _, thermal, _ = refs
    for part in range(3):
        pad_rows(padded, part, low_y[part, index], flow[part, index], high_y[part, index])
    pad_rows(padded, 3, low_y[3, index], thermal[index], high_y[3, index])


def march_kernel(
    flow, low_x, high_x, thermal, flag, low_y, high_y, weight, star, side_x, side_y, padded
):
    refs = (flow, low_x, high_x, thermal, flag)
    _, layers, rows, depth = flow.shape
    for index in range(layers):
        pad_layer(refs, low_y, high_y, padded, index)
        value = march_layer(refs, padded, index, range(3), 0, rows)
        for part in range(3):
            star[part, index] = value[part]
        side_y[pl.ds(index, 1), :] = value[1][rows - 1 :, :]
        if index == layers - 1:
            side_x[...] = value[0]


def transform_kernel(star, table_y, table_z, source, rows_):
    _, layers, rows, depth = star.shape
    rows_[pl.ds(0, 8), :] = jnp.zeros((8, depth), F32)
    for index in range(layers):
        rows_[pl.ds(8, rows), :] = star[1, index]
        sink = star[0, index]
        if index > 0:
            sink = sink - star[0, index - 1]
        sink = sink + (star[1, index] - rows_[pl.ds(7, rows), :])
        sink = sink + (star[2, index] - lane_shift(star[2, index], -1))
        source[index] = dot(dot(table_y[...], -sink), table_z[...])


def pack_kernel(flow, thermal, ahead, behind, planes, sems):
    parts, layers, rows, depth = flow.shape
    copies = []
    for part in range(parts):
        for layer in range(2):
            for target, source in ((ahead, layers - 2 + layer), (behind, layer)):
                copies.append(
                    (flow.at[part, source], target.at[pl.ds((2 * part + layer) * rows, rows), :])
                )
    copies.append((thermal.at[layers - 1], planes.at[0]))
    copies.append((thermal.at[0], planes.at[1]))
    copies = [
        pltpu.make_async_copy(source, target, sems.at[index])
        for index, (source, target) in enumerate(copies)
    ]
    for copy in copies:
        copy.start()
    shape = (rows, rows)
    same = lax.broadcasted_iota(jnp.int32, shape, 0) == lax.broadcasted_iota(jnp.int32, shape, 1)
    for copy in copies[-2:]:
        copy.wait()
    for side, target in enumerate((ahead, behind)):
        tops = planes[side][:, depth - 1 :]
        row = jnp.sum(jnp.where(same, tops, 0.0), axis=0, keepdims=True)
        target[pl.ds(2 * parts * rows, 8), pl.ds(0, rows)] = jnp.broadcast_to(row, (8, rows))
    for copy in copies[:-2]:
        copy.wait()


def heat_kernel(span, thermal, halo, low_y, high_y, flow, heat, warmed, padded):
    layers, rows, depth = thermal.shape
    top = lax.broadcasted_iota(jnp.int32, (rows, depth), 1) == depth - 1
    for index in span:
        pad_rows(padded, 0, low_y[3, index], thermal[index], high_y[3, index])
        around = []
        for other in range(index - 2, index + 3):
            if other < 0:
                around.append(halo[other + 2])
            elif other >= layers:
                around.append(halo[other - layers])
            else:
                around.append(thermal[other])
        speed = [flow[part, index] for part in range(3)]
        gain = TIME_INCREMENT * column(heat[pl.ds(index, 1), :])
        moved = advance(around, padded, 0, speed) + jnp.where(top, gain, 0.0)
        warmed[index - span[0]] = moved


def laser_heat(start_x, start_y, span_x, span_y, total_x, total_y, spots_a, spots_b):
    cells_x = start_x + jnp.arange(span_x, dtype=jnp.int32)
    cells_y = start_y + jnp.arange(span_y, dtype=jnp.int32)
    dist_x = (
        (cells_x[:, None] - spots_a[None, :] + total_x // 2) % total_x - total_x // 2
    ).astype(F32)
    dist_y = (
        (cells_y[:, None] - spots_b[None, :] + total_y // 2) % total_y - total_y // 2
    ).astype(F32)
    spot_x = jnp.exp(-(dist_x * dist_x) / (SPOT_RADIUS * SPOT_RADIUS))
    spot_y = jnp.exp(-(dist_y * dist_y) / (SPOT_RADIUS * SPOT_RADIUS))
    return LASER_POWER * jnp.dot(spot_x, spot_y.T, precision=lax.Precision.HIGHEST)


def tables_kernel(group, layers, place, diagonal, ratio, weight):
    length = group * layers
    mine = place[0]
    first = mine * layers
    diag = diagonal[...]
    ratio[0] = jnp.zeros_like(diag)

    def step(index, previous):
        current = 1.0 / (diag - previous)
        ratio[index] = current
        return current

    loop(1, length + 1, step, jnp.zeros_like(diag))

    def decay(low, high):
        return lax.fori_loop(
            low + 1, high + 1, lambda index, value: value * ratio[index], jnp.ones_like(diag)
        )

    def green(index):
        return 1.0 / (diag - ratio[index] - ratio[jnp.maximum(length - 1 - index, 0)])

    rounds = group.bit_length() - 1
    for turn in range(rounds):
        half = 1 << turn
        right = ((mine >> turn) & 1) == 1
        start = (mine >> (turn + 1)) << (turn + 1)
        cut = (start + half) * layers
        end = (start + 2 * half) * layers
        weight[4 * turn] = decay(cut - 1, end - 1)
        weight[4 * turn + 1] = decay(length - 1 - cut, length - 1 - start * layers)
        low = jnp.where(right, cut - 1, length - 1 - cut)
        high = jnp.where(right, first - 1, length - 1 - first - layers)
        weight[4 * turn + 2] = decay(low, high)
        weight[4 * turn + 3] = green(cut) * ratio[cut]
    inner = jnp.where(mine == group - 1, 0.0, 1.0)
    weight[4 * rounds] = inner * green(first + layers)


def face_rows(plane, edge):
    return (
        jnp.sum(plane * edge[0], axis=0, keepdims=True),
        jnp.sum(plane * edge[1], axis=0, keepdims=True),
    )


def source_kernel(
    length, place, partial, before_x, before_y, table_y, table_z, ratio, edge, early, thermal,
    source, message, late,
):
    layers, rows, depth = partial.shape
    first = place[0] * layers
    late[...] = thermal[:2]
    extra = dot(before_y[...], table_z[...])
    for index in range(layers):
        value = partial[index] + edge[0] * extra[index : index + 1]
        if index == 0:
            value = value + dot(dot(table_y[...], before_x[...]), table_z[...])
        source[index] = value
    forward = source[0]
    for index in range(1, layers):
        forward = source[index] + ratio[first + index] * forward
    message[pl.ds(0, rows), :] = forward
    backward = source[layers - 1]
    for index in range(layers - 2, -1, -1):
        backward = source[index] + ratio[length - 1 - first - index] * backward
    message[pl.ds(rows, rows), :] = backward


def faces_kernel(length, place, source, ratio, edge, faces, sweep):
    layers, rows, depth = source.shape
    first = place[0] * layers
    inside = lambda index: (index >= first) & (index < first + layers)
    zero = jnp.zeros((rows, depth), F32)

    def own(index):
        value = source[jnp.clip(index - first, 0, layers - 1)]
        return jnp.where(inside(index), value, 0.0)

    def down(index, previous):
        current = own(index) + ratio[index] * previous
        sweep[index] = current
        return current

    loop(0, length, down, zero)

    def up(back, carry):
        following, energy = carry
        index = length - 1 - back
        value = ratio[index + 1] * (sweep[index] + following)
        low, high = face_rows(value, edge)
        faces[pl.ds(index, 1), :] = low
        faces[pl.ds(length + index, 1), :] = high
        return value, energy + own(index) * value

    _, energy = loop(0, length, up, (zero, zero))
    faces[pl.ds(2 * length, 8), :] = jnp.broadcast_to(total(energy), (8, depth))


def joined(turn, place, message, other, sums, weight):
    rows, depth = weight.shape[1:]
    right = ((place[0] >> turn) & 1) == 1
    upper, lower = pl.ds(0, rows), pl.ds(rows, rows)
    left_s = jnp.where(right, other[upper, :], message[upper, :])
    right_s = jnp.where(right, message[upper, :], other[upper, :])
    left_t = jnp.where(right, other[lower, :], message[lower, :])
    right_t = jnp.where(right, message[lower, :], other[lower, :])
    own = weight[4 * turn + 2]
    before = sums[0] + jnp.where(right, left_s * own, 0.0)
    after = sums[1] + jnp.where(right, 0.0, right_t * own)
    forward = right_s + left_s * weight[4 * turn]
    backward = left_t + right_t * weight[4 * turn + 1]
    energy = 2.0 * total(left_s * right_t * weight[4 * turn + 3])
    return forward, backward, before, after, energy


def merge_kernel(
    turn, length, place, message, other, faces, other_faces, sums, weight,
    new_message, new_sums, head, tail,
):
    rows, depth = weight.shape[1:]
    forward, backward, before, after, energy = joined(turn, place, message, other, sums, weight)
    new_sums[0] = before
    new_sums[1] = after
    new_message[pl.ds(0, rows), :] = forward
    new_message[pl.ds(rows, rows), :] = backward
    low, high, number = pl.ds(0, length), pl.ds(length, length), pl.ds(2 * length, 8)
    head[...] = faces[low, :] + other_faces[low, :]
    tail[...] = faces[high, :] + other_faces[high, :]
    new_message[pl.ds(2 * rows, length), :] = head[...]
    new_message[pl.ds(2 * rows + length, 8), :] = faces[number, :] + other_faces[number, :] + energy


def close_kernel(turn, length, place, message, other, sums, weight, ratio, ends, new_sums):
    forward, backward, before, after, energy = joined(turn, place, message, other, sums, weight)
    ends[0] = ratio[length] * forward
    ends[1] = ratio[length] * backward
    new_sums[0] = before
    new_sums[1] = after


def coarse_kernel(
    turn, length, lone, place, source, message, other, sums, faces_in, weight, ratio, edge, *refs
):
    outer, (precond, image, report, faces, sweep, ends) = refs[:-6], refs[-6:]
    layers, rows, depth = source.shape
    mine = place[0]
    first = mine * layers
    below, below_far, above, above_far = faces_in
    forward, backward, before, after, energy = joined(turn, place, message, other, sums, weight)
    ends[0] = ratio[length] * forward
    ends[1] = ratio[length] * backward
    beyond = outer[0] if outer else ends
    own = pl.ds(2 * rows, length)
    faces[pl.ds(0, length), :] = message[own, :] + other[own, :]
    faces[pl.ds(length, length), :] = below[...] + below_far[...]
    faces[pl.ds(2 * length, length), :] = above[...] + above_far[...]
    number = pl.ds(2 * rows + length, 8)
    energy = message[number, :] + other[number, :] + energy
    forward = before
    for index in range(layers):
        forward = source[index] + ratio[first + index] * forward
        sweep[index] = forward
    value = weight[lone] * (after + ratio[first + layers] * forward)
    is_last = first + layers == length
    precond[layers] = jnp.where(is_last, beyond[1], value)
    for index in range(layers - 1, -1, -1):
        value = ratio[first + index + 1] * (sweep[index] + value)
        precond[index] = value
    lead, trail = edge[0], edge[1]

    def pull(index):
        below = faces[pl.ds(length + index, 1), :]
        above = faces[pl.ds(2 * length + index, 1), :]
        return below, above

    def down(index, previous):
        below, above = pull(index)
        current = lead * below + trail * above + ratio[index] * previous
        if isinstance(index, int):
            if index == 0:
                current = current + beyond[0]
            if index == length - 1:
                current = current + beyond[1]
        else:
            current = current + jnp.where(index == 0, beyond[0], 0.0)
            current = current + jnp.where(index == length - 1, beyond[1], 0.0)
        sweep[index] = current
        return current

    zero = jnp.zeros((rows, depth), F32)
    loop(0, length, down, zero)
    line = jnp.zeros((1, depth), F32)

    def up(back, carry):
        following, linked, squared = carry
        index = length - 1 - back
        value = ratio[index + 1] * (sweep[index] + following)
        sweep[index] = value
        low, high = face_rows(value, edge)
        report[pl.ds(index, 1), :] = low
        report[pl.ds(length + index, 1), :] = high
        below, above = pull(index)
        linked = linked + faces[pl.ds(index, 1), :] * below
        squared = squared + low * below + high * above
        return value, linked, squared

    _, linked, squared = loop(0, length, up, (zero, line, line))
    sweep[length] = sweep[0]
    for index in range(layers + 1):
        image[index] = sweep[first + index]
    head, tail = sweep[0], sweep[length - 1]
    linked = 2.0 * total(linked) + total(ends[1] * beyond[0] + ends[0] * beyond[1])
    squared = total(squared) + total(head * beyond[0] + tail * beyond[1])
    crossing = 2.0 * total(head * tail)
    where = 2 * length
    report[pl.ds(where, 1), :] = energy[0:1]
    report[pl.ds(where + 1, 1), :] = jnp.broadcast_to(linked, (1, depth))
    report[pl.ds(where + 2, 1), :] = jnp.broadcast_to(squared, (1, depth))
    report[pl.ds(where + 3, 1), :] = jnp.broadcast_to(crossing, (1, depth))
    report[pl.ds(where + 4, 4), :] = jnp.zeros((4, depth), F32)


def physical_kernel(precond, image, table_y, table_z, precond_out, image_out):
    for index in range(precond.shape[0]):
        precond_out[index] = dot(dot(table_y[...], precond[index]), table_z[...])
        image_out[index] = dot(dot(table_y[...], image[index]), table_z[...])


def project_kernel(
    length, paired, place, star, precond, image, faces, table_z, warm_low, warm_high, *refs
):
    reports, (flow, pressure, warmed, field, rows_) = refs[:-5], refs[-5:]
    warmed[:2] = warm_low[...]
    warmed[2:] = warm_high[...]
    _, layers, rows, depth = star.shape
    first = place[0] * layers
    where = 2 * length
    sums = reports[0][pl.ds(where, 8), :]
    for other in reports[1:]:
        sums = sums + other[pl.ds(where, 8), :]
    pairs = jnp.zeros((1, depth), F32)
    for index in range(len(reports)):
        upper, lower = reports[index], reports[(index + 1) % len(reports)]
        pairs = pairs + jnp.sum(
            upper[pl.ds(0, length), :] * lower[pl.ds(length, length), :], axis=0, keepdims=True
        )
    energy, linked, squared, crossing = (sums[k : k + 1, 0:1] for k in range(4))
    if not paired:
        crossing = crossing + 2.0 * total(pairs)
    first_image = energy - linked
    step = energy / first_image
    beta = (energy * squared - linked * linked) / (first_image * first_image)
    rest = -linked / first_image
    second_image = (
        rest * rest * first_image
        + 2.0 * rest * step * (linked - squared)
        + step * step * (squared - crossing)
        - beta * beta * first_image
    )
    second_step = beta * energy / second_image
    alpha = step + second_step * (rest + beta)
    gamma = second_step * step
    for index in range(layers + 1):
        field[index] = alpha * precond[index] + gamma * image[index]
    own = pl.ds(2 * length + first, layers)
    following = alpha * faces[own, :] + gamma * reports[-1][pl.ds(first, layers), :]
    following = dot(following, table_z[...])
    for index in range(layers):
        value = field[index]
        pressure[index] = value
        rows_[pl.ds(0, rows), :] = value
        rows_[pl.ds(rows, 1), :] = following[index : index + 1]
        flow[0, index] = star[0, index] - (field[index + 1] - value)
        flow[1, index] = star[1, index] - (rows_[pl.ds(1, rows), :] - value)
        flow[2, index] = star[2, index] - (lane_shift(value, 1) - value)


def along(array, axis, by):
    length = lax.axis_size(axis)
    return lax.ppermute(array, axis, [(i, (i + by) % length) for i in range(length)])


def swapped(array, bit, by=0):
    count_x, count_y = lax.axis_size("gx"), lax.axis_size("gy")
    pairs = [
        (x * count_y + y, (x ^ bit) * count_y + (y + by) % count_y)
        for x in range(count_x)
        for y in range(count_y)
    ]
    return lax.ppermute(array, ("gx", "gy"), pairs)


def pack(melt_flow, thermal_state):
    parts, layers, rows, depth = melt_flow.shape
    shape = jax.ShapeDtypeStruct((2 * parts * rows + 8, max(rows, depth)), F32)
    return pl.pallas_call(
        pack_kernel,
        out_shape=[shape, shape],
        in_specs=[pl.BlockSpec(memory_space=pl.ANY)] * 2,
        out_specs=[VMEM, VMEM],
        scratch_shapes=[
            pltpu.VMEM((2, rows, depth), F32),
            pltpu.SemaphoreType.DMA((4 * parts + 2,)),
        ],
        compiler_params=pltpu.CompilerParams(vmem_limit_bytes=4 << 20),
    )(melt_flow, thermal_state)


def per_device(melt_flow, thermal_state, powder_flag, spot_lateral_a_cell, spot_lateral_b_cell):
    layers, rows, depth = thermal_state.shape
    count_x, count_y = lax.axis_size("gx"), lax.axis_size("gy")
    group = min(count_x, BLOCK // layers)
    blocks = count_x // group
    length = group * layers
    rounds = group.bit_length() - 1
    sine_y, values_y = sines(rows)
    sine_z, values_z = sines(depth)
    table_y = jnp.asarray(sine_y, F32)
    table_z = jnp.asarray(sine_z, F32)
    edge = jnp.asarray(
        np.broadcast_to(sine_y[[0, rows - 1]][:, :, None], (2, rows, depth)), F32
    )
    diagonal = jnp.asarray(2.0 + values_y[:, None] + values_z[None, :], F32)
    place = (lax.axis_index("gx") % group).astype(jnp.int32).reshape(1)
    plane = (rows, depth)
    line = (length, depth)

    ahead, behind = pack(melt_flow, thermal_state)
    low_x = along(ahead, "gx", 1)
    high_x = along(behind, "gx", -1)
    states = jnp.concatenate([melt_flow, thermal_state[None]], 0)
    low_y = along(states[:, :, -2:], "gy", 1)
    high_y = along(states[:, :, :2], "gy", -1)
    ratio, weight = call(
        functools.partial(tables_kernel, group, layers),
        [place, diagonal],
        [(length + 1,) + plane, (4 * rounds + 1,) + plane],
    )
    star, side_x, side_y = call(
        march_kernel,
        [melt_flow, low_x, high_x, thermal_state, powder_flag, low_y, high_y, weight],
        [(3, layers) + plane, plane, (layers, depth)],
        [pltpu.VMEM((4, rows + 16, depth), F32)],
        scalars=0,
    )
    before_x = along(side_x, "gx", 1)
    before_y = along(side_y, "gy", 1)
    early = along(thermal_state[-2:], "gx", 1)
    (partial,) = call(
        transform_kernel,
        [star, table_y, table_z],
        [(layers,) + plane],
        [pltpu.VMEM((rows + 16, depth), F32)],
        scalars=0,
    )
    source, message, late = call(
        functools.partial(source_kernel, length),
        [
            place, partial, before_x, before_y, table_y, table_z, ratio, edge, early,
            thermal_state,
        ],
        [(layers,) + plane, (2 * rows, depth), (2,) + plane],
    )
    late = along(late, "gx", -1)
    (faces,) = call(
        functools.partial(faces_kernel, length),
        [place, source, ratio, edge],
        [(2 * length + 8, depth)],
        [pltpu.VMEM((length,) + plane, F32)],
    )
    sums = jnp.zeros((2,) + plane, F32)
    for turn in range(rounds - 1):
        message, sums, head, tail = call(
            functools.partial(merge_kernel, turn, length),
            [
                place, message, swapped(message, 1 << turn), faces, swapped(faces, 1 << turn),
                sums, weight,
            ],
            [(2 * rows + length + 8, depth), (2,) + plane, line, line],
        )
        if turn + 2 < rounds:
            number = message[2 * rows + length :]
            message, faces = message[: 2 * rows], jnp.concatenate([head, tail, number], 0)
    bit = group >> 1
    other = swapped(message, bit)
    rim = [
        swapped(tail, 0, 1), swapped(tail, bit, 1), swapped(head, 0, -1), swapped(head, bit, -1)
    ]
    outer = []
    if blocks > 1:
        ends, _ = call(
            functools.partial(close_kernel, rounds - 1, length),
            [place, message, other, sums, weight, ratio],
            [(2,) + plane, (2,) + plane],
        )
        outer = [jnp.stack([along(ends[0], "gx", group), along(ends[1], "gx", -group)])]
    operands = [place, source, message, other, sums] + rim + [weight, ratio, edge] + outer

    def coarse(*refs):
        return coarse_kernel(
            rounds - 1, length, 4 * rounds, *refs[:5], refs[5:9], *refs[9:]
        )

    precond, image, report, faces = call(
        coarse,
        operands,
        [(layers + 1,) + plane, (layers + 1,) + plane, (2 * length + 8, depth), (3 * length, depth)],
        [pltpu.VMEM((length + 1,) + plane, F32), pltpu.VMEM((2,) + plane, F32)],
    )
    if blocks > 1:
        onward = along(image[0], "gx", -1)
        at_end = place[0] == group - 1
        image = image.at[layers].set(jnp.where(at_end, onward, image[layers]))
        upper = along(report[:length], "gy", -1)
        crossing = jnp.sum(onward * image[layers - 1])
        crossing = crossing + jnp.sum(upper * report[length : 2 * length])
        numbers = report[2 * length :].at[3].set(2.0 * crossing)
        numbers = lax.psum(jnp.where(at_end, numbers, 0.0), "gx")
        report = report.at[2 * length :].set(numbers)
    reports = [report] + [along(report, "gy", by) for by in range(1, count_y)]
    precond, image = call(
        physical_kernel,
        [precond, image, table_y, table_z],
        [(layers + 1,) + plane, (layers + 1,) + plane],
        scalars=0,
    )
    heat = laser_heat(
        lax.axis_index("gx") * layers,
        lax.axis_index("gy") * rows,
        layers,
        rows,
        layers * count_x,
        rows * count_y,
        spot_lateral_a_cell,
        spot_lateral_b_cell,
    )
    warmed = []
    for halo, span in ((early, range(0, 2)), (late, range(2, layers))):
        warmed += call(
            functools.partial(heat_kernel, span),
            [thermal_state, halo, low_y, high_y, melt_flow, heat],
            [(len(span),) + plane],
            [pltpu.VMEM((1, rows + 16, depth), F32)],
            scalars=0,
        )
    flow, pressure, warmed = call(
        functools.partial(project_kernel, length, blocks > 1),
        [place, star, precond, image, faces, table_z] + warmed + reports,
        [(3, layers) + plane, (layers,) + plane, (layers,) + plane],
        [pltpu.VMEM((layers + 1,) + plane, F32), pltpu.VMEM((rows + 16, depth), F32)],
    )
    return (flow, warmed, pressure)


def solution(mesh):
    placed = (
        P(None, ("runs", "gx"), "gy", None),
        P(("runs", "gx"), "gy", None),
        P(("runs", "gx"), "gy", None),
        P("runs"),
        P("runs"),
    )
    return jax.shard_map(
        per_device,
        mesh=mesh,
        in_specs=placed,
        out_specs=(
            P(None, ("runs", "gx"), "gy", None),
            P(("runs", "gx"), "gy", None),
            P(("runs", "gx"), "gy", None),
        ),
        check_vma=False,
    )
```

```python
import functools
import math

import jax
import jax.numpy as jnp
import numpy as np
from jax import lax
from jax.experimental import pallas as pl
from jax.experimental.pallas import tpu as pltpu
from jax.sharding import PartitionSpec as P

BLOCK = 128

TIME_INCREMENT = 0.2
MARANGONI = 1.5
DRAG_RATE = 4.0
LASER_POWER = 3.0
SPOT_RADIUS = 5.0

F32 = jnp.float32
VMEM = pl.BlockSpec(memory_space=pltpu.VMEM)
SMEM = pl.BlockSpec(memory_space=pltpu.SMEM)


def call(body, operands, shapes, scratch=(), scalars=0, flops=1 << 20):
    out_shape = [jax.ShapeDtypeStruct(shape, F32) for shape in shapes]
    moved = 4 * sum(math.prod(shape) for shape in shapes)
    held = moved + 4 * sum(operand.size for operand in operands)
    held += 4 * sum(math.prod(space.shape) for space in scratch)
    return pl.pallas_call(
        body,
        out_shape=out_shape,
        in_specs=[SMEM] * scalars + [VMEM] * (len(operands) - scalars),
        out_specs=[VMEM] * len(shapes),
        scratch_shapes=list(scratch),
        compiler_params=pltpu.CompilerParams(vmem_limit_bytes=held + (4 << 20)),
        cost_estimate=pl.CostEstimate(flops=flops, bytes_accessed=2 * moved, transcendentals=0),
    )(*operands)


def dot(left, right):
    return jnp.dot(left, right, precision=lax.Precision.HIGHEST, preferred_element_type=F32)


def total(cells):
    return jnp.sum(jnp.sum(cells, axis=0, keepdims=True), axis=1, keepdims=True)


def loop(low, high, body, start):
    if isinstance(high, int) and isinstance(low, int) and high - low <= 24:
        carry = start
        for index in range(low, high):
            carry = body(index, carry)
        return carry
    return lax.fori_loop(low, high, body, start)


def position(group):
    return lax.rem(lax.axis_index("gx"), group)


def sines(length):
    positions = np.arange(length) + 1.0
    step = math.pi / (length + 1)
    table = np.sqrt(2.0 / (length + 1)) * np.sin(step * positions[:, None] * positions[None, :])
    return table, 2.0 - 2.0 * np.cos(step * positions)


def lane_shift(cells, offset):
    width = cells.shape[1]
    lane = lax.broadcasted_iota(jnp.int32, cells.shape, 1)
    moved = pltpu.roll(cells, (-offset) % width, 1)
    keep = lane < width - offset if offset > 0 else lane >= -offset
    return jnp.where(keep, moved, 0.0)


def column(row):
    length = row.shape[1]
    shape = (length, length)
    same = lax.broadcasted_iota(jnp.int32, shape, 0) == lax.broadcasted_iota(jnp.int32, shape, 1)
    return jnp.sum(jnp.where(same, row, 0.0), axis=1, keepdims=True)


def advance(layers, padded, index, speed, start=0):
    middle = layers[2]
    rows = middle.shape[0]
    speed_x, speed_y, speed_z = speed
    ahead = speed_x >= 0.0
    near = jnp.where(ahead, layers[1], layers[3])
    far = jnp.where(ahead, layers[0], layers[4])
    rate = jnp.abs(speed_x) * (1.5 * middle - 2.0 * near + 0.5 * far)
    ahead = speed_y >= 0.0
    near = jnp.where(ahead, padded[index, pl.ds(7 + start, rows), :], padded[index, pl.ds(9 + start, rows), :])
    far = jnp.where(ahead, padded[index, pl.ds(6 + start, rows), :], padded[index, pl.ds(10 + start, rows), :])
    rate = rate + jnp.abs(speed_y) * (1.5 * middle - 2.0 * near + 0.5 * far)
    ahead = speed_z >= 0.0
    near = jnp.where(ahead, lane_shift(middle, -1), lane_shift(middle, 1))
    far = jnp.where(ahead, lane_shift(middle, -2), lane_shift(middle, 2))
    rate = rate + jnp.abs(speed_z) * (1.5 * middle - 2.0 * near + 0.5 * far)
    return middle - TIME_INCREMENT * rate


def pad_rows(padded, index, before, middle, after):
    rows = middle.shape[0]
    padded[index, pl.ds(8, rows), :] = middle
    padded[index, pl.ds(6, 2), :] = before
    padded[index, pl.ds(8 + rows, 2), :] = after


def march_layer(refs, padded, index, parts, start, count):
    flow, low_x, high_x, thermal, flag = refs
    _, layers, rows, depth = flow.shape
    span = pl.ds(start, count)
    surface = 6 * rows
    speed = [flow[part, index, span, :] for part in range(3)]
    drag = 1.0 / (1.0 + TIME_INCREMENT * DRAG_RATE * flag[index, span, :].astype(F32))
    top = lax.broadcasted_iota(jnp.int32, (count, depth), 1) == depth - 1
    pull = -MARANGONI * 0.5 * TIME_INCREMENT
    out = []
    for part in parts:
        around = []
        for other in range(index - 2, index + 3):
            if other < 0:
                first = (2 * part + other + 2) * rows + start
                around.append(low_x[pl.ds(first, count), :])
            elif other >= layers:
                first = (2 * part + other - layers) * rows + start
                around.append(high_x[pl.ds(first, count), :])
            else:
                around.append(flow[part, other, span, :])
        moved = advance(around, padded, part, speed, start)
        if part == 0:
            edge = lambda halo: column(halo[pl.ds(surface, 1), pl.ds(0, rows)])
            behind = thermal[index - 1] if index > 0 else edge(low_x)
            before = thermal[index + 1] if index + 1 < layers else edge(high_x)
            moved = moved + jnp.where(top, pull * (before - behind), 0.0)
        if part == 1:
            slope = padded[3, pl.ds(9 + start, count), :] - padded[3, pl.ds(7 + start, count), :]
            moved = moved + jnp.where(top, pull * slope, 0.0)
        out.append(moved * drag)
    return out


def pad_layer(refs, low_y, high_y, padded, index):
    flow, _, _, thermal, _ = refs
    for part in range(3):
        pad_rows(padded, part, low_y[part, index], flow[part, index], high_y[part, index])
    pad_rows(padded, 3, low_y[3, index], thermal[index], high_y[3, index])


def march_kernel(
    flow, low_x, high_x, thermal, flag, low_y, high_y, weight, star, side_x, side_y, padded
):
    refs = (flow, low_x, high_x, thermal, flag)
    _, layers, rows, depth = flow.shape
    for index in range(layers):
        pad_layer(refs, low_y, high_y, padded, index)
        value = march_layer(refs, padded, index, range(3), 0, rows)
        for part in range(3):
            star[part, index] = value[part]
        side_y[pl.ds(index, 1), :] = value[1][rows - 1 :, :]
        if index == layers - 1:
            side_x[...] = value[0]


def transform_kernel(star, table_y, table_z, source, rows_):
    _, layers, rows, depth = star.shape
    rows_[pl.ds(0, 8), :] = jnp.zeros((8, depth), F32)
    for index in range(layers):
        rows_[pl.ds(8, rows), :] = star[1, index]
        sink = star[0, index]
        if index > 0:
            sink = sink - star[0, index - 1]
        sink = sink + (star[1, index] - rows_[pl.ds(7, rows), :])
        sink = sink + (star[2, index] - lane_shift(star[2, index], -1))
        source[index] = dot(dot(table_y[...], -sink), table_z[...])


def pack_kernel(flow, thermal, ahead, behind, planes, sems):
    parts, layers, rows, depth = flow.shape
    copies = []
    for part in range(parts):
        for layer in range(2):
            for target, source in ((ahead, layers - 2 + layer), (behind, layer)):
                copies.append(
                    (flow.at[part, source], target.at[pl.ds((2 * part + layer) * rows, rows), :])
                )
    copies.append((thermal.at[layers - 1], planes.at[0]))
    copies.append((thermal.at[0], planes.at[1]))
    copies = [
        pltpu.make_async_copy(source, target, sems.at[index])
        for index, (source, target) in enumerate(copies)
    ]
    for copy in copies:
        copy.start()
    shape = (rows, rows)
    same = lax.broadcasted_iota(jnp.int32, shape, 0) == lax.broadcasted_iota(jnp.int32, shape, 1)
    for copy in copies[-2:]:
        copy.wait()
    for side, target in enumerate((ahead, behind)):
        tops = planes[side][:, depth - 1 :]
        row = jnp.sum(jnp.where(same, tops, 0.0), axis=0, keepdims=True)
        target[pl.ds(2 * parts * rows, 8), pl.ds(0, rows)] = jnp.broadcast_to(row, (8, rows))
    for copy in copies[:-2]:
        copy.wait()


def wrapped(distance, span):
    moved = distance + span // 2
    moved = jnp.where(moved < 0, moved + span, moved)
    moved = jnp.where(moved >= span, moved - span, moved)
    return (moved - span // 2).astype(F32)


def laser_row(index, layers, rows, spots_a, spots_b):
    total_x = layers * lax.axis_size("gx")
    total_y = rows * lax.axis_size("gy")
    cell_x = lax.axis_index("gx") * layers + index
    cells_y = lax.broadcasted_iota(jnp.int32, (1, rows), 1) + lax.axis_index("gy") * rows
    heat = jnp.zeros((1, rows), F32)
    for spot in range(spots_a.shape[0]):
        dist_x = wrapped(jnp.full((1, rows), cell_x - spots_a[spot], jnp.int32), total_x)
        dist_y = wrapped(cells_y - spots_b[spot], total_y)
        square = dist_x * dist_x + dist_y * dist_y
        heat = heat + jnp.exp(square * (-1.0 / (SPOT_RADIUS * SPOT_RADIUS)))
    return LASER_POWER * heat


def heat_kernel(span, spots_a, spots_b, thermal, halo, low_y, high_y, flow, warmed, padded):
    layers, rows, depth = thermal.shape
    top = lax.broadcasted_iota(jnp.int32, (rows, depth), 1) == depth - 1
    for index in span:
        pad_rows(padded, 0, low_y[3, index], thermal[index], high_y[3, index])
        around = []
        for other in range(index - 2, index + 3):
            if other < 0:
                around.append(halo[other + 2])
            elif other >= layers:
                around.append(halo[other - layers])
            else:
                around.append(thermal[other])
        speed = [flow[part, index] for part in range(3)]
        gain = TIME_INCREMENT * column(laser_row(index, layers, rows, spots_a, spots_b))
        moved = advance(around, padded, 0, speed) + jnp.where(top, gain, 0.0)
        warmed[index - span[0]] = moved


def tables_kernel(group, layers, diagonal, ratio, weight):
    length = group * layers
    mine = position(group)
    first = mine * layers
    diag = diagonal[...]
    ratio[0] = jnp.zeros_like(diag)

    def step(index, previous):
        current = 1.0 / (diag - previous)
        ratio[index] = current
        return current

    loop(1, length + 1, step, jnp.zeros_like(diag))

    def decay(low, high):
        return lax.fori_loop(
            low + 1, high + 1, lambda index, value: value * ratio[index], jnp.ones_like(diag)
        )

    def green(index):
        return 1.0 / (diag - ratio[index] - ratio[jnp.maximum(length - 1 - index, 0)])

    rounds = group.bit_length() - 1
    for turn in range(rounds):
        half = 1 << turn
        right = ((mine >> turn) & 1) == 1
        start = (mine >> (turn + 1)) << (turn + 1)
        cut = (start + half) * layers
        end = (start + 2 * half) * layers
        weight[4 * turn] = decay(cut - 1, end - 1)
        weight[4 * turn + 1] = decay(length - 1 - cut, length - 1 - start * layers)
        low = jnp.where(right, cut - 1, length - 1 - cut)
        high = jnp.where(right, first - 1, length - 1 - first - layers)
        weight[4 * turn + 2] = decay(low, high)
        weight[4 * turn + 3] = green(cut) * ratio[cut]
    inner = jnp.where(mine == group - 1, 0.0, 1.0)
    weight[4 * rounds] = inner * green(first + layers)


def face_rows(plane, edge):
    return (
        jnp.sum(plane * edge[0], axis=0, keepdims=True),
        jnp.sum(plane * edge[1], axis=0, keepdims=True),
    )


def source_kernel(
    group, length, partial, before_x, before_y, table_y, table_z, ratio, edge, early,
    source, message,
):
    layers, rows, depth = partial.shape
    first = position(group) * layers
    extra = dot(before_y[...], table_z[...])
    for index in range(layers):
        value = partial[index] + edge[0] * extra[index : index + 1]
        if index == 0:
            value = value + dot(dot(table_y[...], before_x[...]), table_z[...])
        source[index] = value
    forward = source[0]
    for index in range(1, layers):
        forward = source[index] + ratio[first + index] * forward
    message[pl.ds(0, rows), :] = forward
    backward = source[layers - 1]
    for index in range(layers - 2, -1, -1):
        backward = source[index] + ratio[length - 1 - first - index] * backward
    message[pl.ds(rows, rows), :] = backward


def faces_kernel(group, length, source, ratio, edge, faces, sweep):
    layers, rows, depth = source.shape
    first = position(group) * layers
    inside = lambda index: (index >= first) & (index < first + layers)
    zero = jnp.zeros((rows, depth), F32)

    def own(index):
        value = source[jnp.clip(index - first, 0, layers - 1)]
        return jnp.where(inside(index), value, 0.0)

    def down(index, previous):
        current = own(index) + ratio[index] * previous
        sweep[index] = current
        return current

    loop(0, length, down, zero)

    def up(back, carry):
        following, energy = carry
        index = length - 1 - back
        value = ratio[index + 1] * (sweep[index] + following)
        low, high = face_rows(value, edge)
        faces[pl.ds(index, 1), :] = low
        faces[pl.ds(length + index, 1), :] = high
        return value, energy + own(index) * value

    _, energy = loop(0, length, up, (zero, zero))
    faces[pl.ds(2 * length, 8), :] = jnp.broadcast_to(total(energy), (8, depth))


def joined(turn, group, message, other, sums, weight):
    rows, depth = weight.shape[1:]
    right = ((position(group) >> turn) & 1) == 1
    upper, lower = pl.ds(0, rows), pl.ds(rows, rows)
    left_s = jnp.where(right, other[upper, :], message[upper, :])
    right_s = jnp.where(right, message[upper, :], other[upper, :])
    left_t = jnp.where(right, other[lower, :], message[lower, :])
    right_t = jnp.where(right, message[lower, :], other[lower, :])
    own = weight[4 * turn + 2]
    before = sums[0] + jnp.where(right, left_s * own, 0.0)
    after = sums[1] + jnp.where(right, 0.0, right_t * own)
    forward = right_s + left_s * weight[4 * turn]
    backward = left_t + right_t * weight[4 * turn + 1]
    energy = 2.0 * total(left_s * right_t * weight[4 * turn + 3])
    return forward, backward, before, after, energy


def merge_kernel(
    turn, group, length, message, other, faces, other_faces, sums, weight,
    new_message, new_sums, head, tail,
):
    rows, depth = weight.shape[1:]
    forward, backward, before, after, energy = joined(turn, group, message, other, sums, weight)
    new_sums[0] = before
    new_sums[1] = after
    new_message[pl.ds(0, rows), :] = forward
    new_message[pl.ds(rows, rows), :] = backward
    low, high, number = pl.ds(0, length), pl.ds(length, length), pl.ds(2 * length, 8)
    head[...] = faces[low, :] + other_faces[low, :]
    tail[...] = faces[high, :] + other_faces[high, :]
    new_message[pl.ds(2 * rows, length), :] = head[...]
    new_message[pl.ds(2 * rows + length, 8), :] = faces[number, :] + other_faces[number, :] + energy


def close_kernel(turn, group, length, message, other, sums, weight, ratio, ends, new_sums):
    forward, backward, before, after, energy = joined(turn, group, message, other, sums, weight)
    ends[0] = ratio[length] * forward
    ends[1] = ratio[length] * backward
    new_sums[0] = before
    new_sums[1] = after


def coarse_kernel(
    turn, group, length, lone, source, message, other, sums, faces_in, weight, ratio, edge,
    thermal, *refs
):
    outer, (precond, image, report, faces, late, sweep, ends) = refs[:-7], refs[-7:]
    late[...] = thermal[:2]
    layers, rows, depth = source.shape
    mine = position(group)
    first = mine * layers
    below, below_far, above, above_far = faces_in
    forward, backward, before, after, energy = joined(turn, group, message, other, sums, weight)
    ends[0] = ratio[length] * forward
    ends[1] = ratio[length] * backward
    beyond = outer[0] if outer else ends
    own = pl.ds(2 * rows, length)
    faces[pl.ds(0, length), :] = message[own, :] + other[own, :]
    faces[pl.ds(length, length), :] = below[...] + below_far[...]
    faces[pl.ds(2 * length, length), :] = above[...] + above_far[...]
    number = pl.ds(2 * rows + length, 8)
    energy = message[number, :] + other[number, :] + energy
    forward = before
    for index in range(layers):
        forward = source[index] + ratio[first + index] * forward
        sweep[index] = forward
    value = weight[lone] * (after + ratio[first + layers] * forward)
    is_last = first + layers == length
    precond[layers] = jnp.where(is_last, beyond[1], value)
    for index in range(layers - 1, -1, -1):
        value = ratio[first + index + 1] * (sweep[index] + value)
        precond[index] = value
    lead, trail = edge[0], edge[1]

    def pull(index):
        below = faces[pl.ds(length + index, 1), :]
        above = faces[pl.ds(2 * length + index, 1), :]
        return below, above

    def down(index, previous):
        below, above = pull(index)
        current = lead * below + trail * above + ratio[index] * previous
        if isinstance(index, int):
            if index == 0:
                current = current + beyond[0]
            if index == length - 1:
                current = current + beyond[1]
        else:
            current = current + jnp.where(index == 0, beyond[0], 0.0)
            current = current + jnp.where(index == length - 1, beyond[1], 0.0)
        sweep[index] = current
        return current

    zero = jnp.zeros((rows, depth), F32)
    loop(0, length, down, zero)
    line = jnp.zeros((1, depth), F32)

    def up(back, carry):
        following, linked, squared = carry
        index = length - 1 - back
        value = ratio[index + 1] * (sweep[index] + following)
        sweep[index] = value
        low, high = face_rows(value, edge)
        report[pl.ds(index, 1), :] = low
        report[pl.ds(length + index, 1), :] = high
        below, above = pull(index)
        linked = linked + faces[pl.ds(index, 1), :] * below
        squared = squared + low * below + high * above
        return value, linked, squared

    _, linked, squared = loop(0, length, up, (zero, line, line))
    sweep[length] = sweep[0]
    for index in range(layers + 1):
        image[index] = sweep[first + index]
    head, tail = sweep[0], sweep[length - 1]
    linked = 2.0 * total(linked) + total(ends[1] * beyond[0] + ends[0] * beyond[1])
    squared = total(squared) + total(head * beyond[0] + tail * beyond[1])
    crossing = 2.0 * total(head * tail)
    where = 2 * length
    report[pl.ds(where, 1), :] = energy[0:1]
    report[pl.ds(where + 1, 1), :] = jnp.broadcast_to(linked, (1, depth))
    report[pl.ds(where + 2, 1), :] = jnp.broadcast_to(squared, (1, depth))
    report[pl.ds(where + 3, 1), :] = jnp.broadcast_to(crossing, (1, depth))
    report[pl.ds(where + 4, 4), :] = jnp.zeros((4, depth), F32)


def physical_kernel(precond, image, table_y, table_z, precond_out, image_out):
    for index in range(precond.shape[0]):
        precond_out[index] = dot(dot(table_y[...], precond[index]), table_z[...])
        image_out[index] = dot(dot(table_y[...], image[index]), table_z[...])


def project_kernel(
    group, length, paired, star, precond, image, faces, table_z, warm_low, warm_high, *refs
):
    reports, (flow, pressure, warmed, field, rows_) = refs[:-5], refs[-5:]
    warmed[:2] = warm_low[...]
    warmed[2:] = warm_high[...]
    _, layers, rows, depth = star.shape
    first = position(group) * layers
    where = 2 * length
    sums = reports[0][pl.ds(where, 8), :]
    for other in reports[1:]:
        sums = sums + other[pl.ds(where, 8), :]
    pairs = jnp.zeros((1, depth), F32)
    for index in range(len(reports)):
        upper, lower = reports[index], reports[(index + 1) % len(reports)]
        pairs = pairs + jnp.sum(
            upper[pl.ds(0, length), :] * lower[pl.ds(length, length), :], axis=0, keepdims=True
        )
    energy, linked, squared, crossing = (sums[k : k + 1, 0:1] for k in range(4))
    if not paired:
        crossing = crossing + 2.0 * total(pairs)
    first_image = energy - linked
    step = energy / first_image
    beta = (energy * squared - linked * linked) / (first_image * first_image)
    rest = -linked / first_image
    second_image = (
        rest * rest * first_image
        + 2.0 * rest * step * (linked - squared)
        + step * step * (squared - crossing)
        - beta * beta * first_image
    )
    second_step = beta * energy / second_image
    alpha = step + second_step * (rest + beta)
    gamma = second_step * step
    for index in range(layers + 1):
        field[index] = alpha * precond[index] + gamma * image[index]
    own = pl.ds(2 * length + first, layers)
    following = alpha * faces[own, :] + gamma * reports[-1][pl.ds(first, layers), :]
    following = dot(following, table_z[...])
    for index in range(layers):
        value = field[index]
        pressure[index] = value
        rows_[pl.ds(0, rows), :] = value
        rows_[pl.ds(rows, 1), :] = following[index : index + 1]
        flow[0, index] = star[0, index] - (field[index + 1] - value)
        flow[1, index] = star[1, index] - (rows_[pl.ds(1, rows), :] - value)
        flow[2, index] = star[2, index] - (lane_shift(value, 1) - value)


def along(array, axis, by):
    length = lax.axis_size(axis)
    return lax.ppermute(array, axis, [(i, (i + by) % length) for i in range(length)])


def swapped(array, bit, by=0):
    count_x, count_y = lax.axis_size("gx"), lax.axis_size("gy")
    pairs = [
        (x * count_y + y, (x ^ bit) * count_y + (y + by) % count_y)
        for x in range(count_x)
        for y in range(count_y)
    ]
    return lax.ppermute(array, ("gx", "gy"), pairs)


def pack(melt_flow, thermal_state):
    parts, layers, rows, depth = melt_flow.shape
    shape = jax.ShapeDtypeStruct((2 * parts * rows + 8, max(rows, depth)), F32)
    return pl.pallas_call(
        pack_kernel,
        out_shape=[shape, shape],
        in_specs=[pl.BlockSpec(memory_space=pl.ANY)] * 2,
        out_specs=[VMEM, VMEM],
        scratch_shapes=[
            pltpu.VMEM((2, rows, depth), F32),
            pltpu.SemaphoreType.DMA((4 * parts + 2,)),
        ],
        compiler_params=pltpu.CompilerParams(vmem_limit_bytes=4 << 20),
    )(melt_flow, thermal_state)


def per_device(melt_flow, thermal_state, powder_flag, spot_lateral_a_cell, spot_lateral_b_cell):
    layers, rows, depth = thermal_state.shape
    count_x, count_y = lax.axis_size("gx"), lax.axis_size("gy")
    group = min(count_x, BLOCK // layers)
    blocks = count_x // group
    length = group * layers
    rounds = group.bit_length() - 1
    sine_y, values_y = sines(rows)
    sine_z, values_z = sines(depth)
    table_y = jnp.asarray(sine_y, F32)
    table_z = jnp.asarray(sine_z, F32)
    edge = jnp.asarray(
        np.broadcast_to(sine_y[[0, rows - 1]][:, :, None], (2, rows, depth)), F32
    )
    diagonal = jnp.asarray(2.0 + values_y[:, None] + values_z[None, :], F32)
    plane = (rows, depth)
    line = (length, depth)

    ahead, behind = pack(melt_flow, thermal_state)
    low_x = along(ahead, "gx", 1)
    high_x = along(behind, "gx", -1)
    states = jnp.concatenate([melt_flow, thermal_state[None]], 0)
    low_y = along(states[:, :, -2:], "gy", 1)
    high_y = along(states[:, :, :2], "gy", -1)
    ratio, weight = call(
        functools.partial(tables_kernel, group, layers),
        [diagonal],
        [(length + 1,) + plane, (4 * rounds + 1,) + plane],
    )
    star, side_x, side_y = call(
        march_kernel,
        [melt_flow, low_x, high_x, thermal_state, powder_flag, low_y, high_y, weight],
        [(3, layers) + plane, plane, (layers, depth)],
        [pltpu.VMEM((4, rows + 16, depth), F32)],
    )
    before_x = along(side_x, "gx", 1)
    before_y = along(side_y, "gy", 1)
    early = along(thermal_state[-2:], "gx", 1)
    (partial,) = call(
        transform_kernel,
        [star, table_y, table_z],
        [(layers,) + plane],
        [pltpu.VMEM((rows + 16, depth), F32)],
    )
    source, message = call(
        functools.partial(source_kernel, group, length),
        [
            partial, before_x, before_y, table_y, table_z, ratio, edge, early,
        ],
        [(layers,) + plane, (2 * rows, depth)],
    )
    (faces,) = call(
        functools.partial(faces_kernel, group, length),
        [source, ratio, edge],
        [(2 * length + 8, depth)],
        [pltpu.VMEM((length,) + plane, F32)],
    )
    sums = jnp.zeros((2,) + plane, F32)
    for turn in range(rounds - 1):
        message, sums, head, tail = call(
            functools.partial(merge_kernel, turn, group, length),
            [
                message, swapped(message, 1 << turn), faces, swapped(faces, 1 << turn),
                sums, weight,
            ],
            [(2 * rows + length + 8, depth), (2,) + plane, line, line],
        )
        if turn + 2 < rounds:
            number = message[2 * rows + length :]
            message, faces = message[: 2 * rows], jnp.concatenate([head, tail, number], 0)
    bit = group >> 1
    other = swapped(message, bit)
    rim = [
        swapped(tail, 0, 1), swapped(tail, bit, 1), swapped(head, 0, -1), swapped(head, bit, -1)
    ]
    outer = []
    if blocks > 1:
        ends, _ = call(
            functools.partial(close_kernel, rounds - 1, group, length),
            [message, other, sums, weight, ratio],
            [(2,) + plane, (2,) + plane],
        )
        outer = [jnp.stack([along(ends[0], "gx", group), along(ends[1], "gx", -group)])]
    operands = [source, message, other, sums] + rim + [weight, ratio, edge, thermal_state] + outer

    def coarse(*refs):
        return coarse_kernel(
            rounds - 1, group, length, 4 * rounds, *refs[:4], refs[4:8], *refs[8:]
        )

    precond, image, report, faces, late = call(
        coarse,
        operands,
        [
            (layers + 1,) + plane, (layers + 1,) + plane, (2 * length + 8, depth),
            (3 * length, depth), (2,) + plane,
        ],
        [pltpu.VMEM((length + 1,) + plane, F32), pltpu.VMEM((2,) + plane, F32)],
    )
    if blocks > 1:
        onward = along(image[0], "gx", -1)
        at_end = position(group) == group - 1
        image = image.at[layers].set(jnp.where(at_end, onward, image[layers]))
        upper = along(report[:length], "gy", -1)
        crossing = jnp.sum(onward * image[layers - 1])
        crossing = crossing + jnp.sum(upper * report[length : 2 * length])
        numbers = report[2 * length :].at[3].set(2.0 * crossing)
        numbers = lax.psum(jnp.where(at_end, numbers, 0.0), "gx")
        report = report.at[2 * length :].set(numbers)
    reports = [report] + [along(report, "gy", by) for by in range(1, count_y)]
    precond, image = call(
        physical_kernel,
        [precond, image, table_y, table_z],
        [(layers + 1,) + plane, (layers + 1,) + plane],
    )
    late = along(late, "gx", -1)
    warmed = []
    for halo, span in ((early, range(0, 2)), (late, range(2, layers))):
        warmed += call(
            functools.partial(heat_kernel, span),
            [spot_lateral_a_cell, spot_lateral_b_cell, thermal_state, halo, low_y, high_y, melt_flow],
            [(len(span),) + plane],
            [pltpu.VMEM((1, rows + 16, depth), F32)],
            )
    flow, pressure, warmed = call(
        functools.partial(project_kernel, group, length, blocks > 1),
        [star, precond, image, faces, table_z] + warmed + reports,
        [(3, layers) + plane, (layers,) + plane, (layers,) + plane],
        [pltpu.VMEM((layers + 1,) + plane, F32), pltpu.VMEM((rows + 16, depth), F32)],
    )
    return (flow, warmed, pressure)


def solution(mesh):
    placed = (
        P(None, ("runs", "gx"), "gy", None),
        P(("runs", "gx"), "gy", None),
        P(("runs", "gx"), "gy", None),
        P("runs"),
        P("runs"),
    )
    return jax.shard_map(
        per_device,
        mesh=mesh,
        in_specs=placed,
        out_specs=(
            P(None, ("runs", "gx"), "gy", None),
            P(("runs", "gx"), "gy", None),
            P(("runs", "gx"), "gy", None),
        ),
        check_vma=False,
    )
```

```python
import functools
import math

import jax
import jax.numpy as jnp
import numpy as np
from jax import lax
from jax.experimental import pallas as pl
from jax.experimental.pallas import tpu as pltpu
from jax.sharding import PartitionSpec as P

BLOCK = 128

TIME_INCREMENT = 0.2
MARANGONI = 1.5
DRAG_RATE = 4.0
LASER_POWER = 3.0
SPOT_RADIUS = 5.0

F32 = jnp.float32
VMEM = pl.BlockSpec(memory_space=pltpu.VMEM)
SMEM = pl.BlockSpec(memory_space=pltpu.SMEM)


def call(body, operands, shapes, scratch=(), scalars=0, flops=1 << 20):
    out_shape = [jax.ShapeDtypeStruct(shape, F32) for shape in shapes]
    moved = 4 * sum(math.prod(shape) for shape in shapes)
    held = moved + 4 * sum(operand.size for operand in operands)
    held += 4 * sum(math.prod(space.shape) for space in scratch)
    return pl.pallas_call(
        body,
        out_shape=out_shape,
        in_specs=[SMEM] * scalars + [VMEM] * (len(operands) - scalars),
        out_specs=[VMEM] * len(shapes),
        scratch_shapes=list(scratch),
        compiler_params=pltpu.CompilerParams(vmem_limit_bytes=held + (4 << 20)),
        cost_estimate=pl.CostEstimate(flops=flops, bytes_accessed=2 * moved, transcendentals=0),
    )(*operands)


def dot(left, right):
    return jnp.dot(left, right, precision=lax.Precision.HIGHEST, preferred_element_type=F32)


def total(cells):
    return jnp.sum(jnp.sum(cells, axis=0, keepdims=True), axis=1, keepdims=True)


def loop(low, high, body, start):
    if isinstance(high, int) and isinstance(low, int) and high - low <= 24:
        carry = start
        for index in range(low, high):
            carry = body(index, carry)
        return carry
    return lax.fori_loop(low, high, body, start)


def position(group):
    return lax.rem(lax.axis_index("gx"), group)


def sines(length):
    positions = np.arange(length) + 1.0
    step = math.pi / (length + 1)
    table = np.sqrt(2.0 / (length + 1)) * np.sin(step * positions[:, None] * positions[None, :])
    return table, 2.0 - 2.0 * np.cos(step * positions)


def lane_shift(cells, offset):
    width = cells.shape[1]
    lane = lax.broadcasted_iota(jnp.int32, cells.shape, 1)
    moved = pltpu.roll(cells, (-offset) % width, 1)
    keep = lane < width - offset if offset > 0 else lane >= -offset
    return jnp.where(keep, moved, 0.0)


def column(row):
    length = row.shape[1]
    shape = (length, length)
    same = lax.broadcasted_iota(jnp.int32, shape, 0) == lax.broadcasted_iota(jnp.int32, shape, 1)
    return jnp.sum(jnp.where(same, row, 0.0), axis=1, keepdims=True)


def advance(layers, padded, index, speed, start=0):
    middle = layers[2]
    rows = middle.shape[0]
    speed_x, speed_y, speed_z = speed
    ahead = speed_x >= 0.0
    near = jnp.where(ahead, layers[1], layers[3])
    far = jnp.where(ahead, layers[0], layers[4])
    rate = jnp.abs(speed_x) * (1.5 * middle - 2.0 * near + 0.5 * far)
    ahead = speed_y >= 0.0
    near = jnp.where(ahead, padded[index, pl.ds(7 + start, rows), :], padded[index, pl.ds(9 + start, rows), :])
    far = jnp.where(ahead, padded[index, pl.ds(6 + start, rows), :], padded[index, pl.ds(10 + start, rows), :])
    rate = rate + jnp.abs(speed_y) * (1.5 * middle - 2.0 * near + 0.5 * far)
    ahead = speed_z >= 0.0
    near = jnp.where(ahead, lane_shift(middle, -1), lane_shift(middle, 1))
    far = jnp.where(ahead, lane_shift(middle, -2), lane_shift(middle, 2))
    rate = rate + jnp.abs(speed_z) * (1.5 * middle - 2.0 * near + 0.5 * far)
    return middle - TIME_INCREMENT * rate


def pad_rows(padded, index, before, middle, after):
    rows = middle.shape[0]
    padded[index, pl.ds(8, rows), :] = middle
    padded[index, pl.ds(6, 2), :] = before
    padded[index, pl.ds(8 + rows, 2), :] = after


def march_layer(refs, padded, index, parts, start, count):
    flow, low_x, high_x, thermal, flag = refs
    _, layers, rows, depth = flow.shape
    span = pl.ds(start, count)
    surface = 6 * rows
    speed = [flow[part, index, span, :] for part in range(3)]
    drag = 1.0 / (1.0 + TIME_INCREMENT * DRAG_RATE * flag[index, span, :].astype(F32))
    top = lax.broadcasted_iota(jnp.int32, (count, depth), 1) == depth - 1
    pull = -MARANGONI * 0.5 * TIME_INCREMENT
    out = []
    for part in parts:
        around = []
        for other in range(index - 2, index + 3):
            if other < 0:
                first = (2 * part + other + 2) * rows + start
                around.append(low_x[pl.ds(first, count), :])
            elif other >= layers:
                first = (2 * part + other - layers) * rows + start
                around.append(high_x[pl.ds(first, count), :])
            else:
                around.append(flow[part, other, span, :])
        moved = advance(around, padded, part, speed, start)
        if part == 0:
            edge = lambda halo: column(halo[pl.ds(surface, 1), pl.ds(0, rows)])
            behind = thermal[index - 1] if index > 0 else edge(low_x)
            before = thermal[index + 1] if index + 1 < layers else edge(high_x)
            moved = moved + jnp.where(top, pull * (before - behind), 0.0)
        if part == 1:
            slope = padded[3, pl.ds(9 + start, count), :] - padded[3, pl.ds(7 + start, count), :]
            moved = moved + jnp.where(top, pull * slope, 0.0)
        out.append(moved * drag)
    return out


def pad_layer(refs, low_y, high_y, padded, index):
    flow, _, _, thermal, _ = refs
    for part in range(3):
        pad_rows(padded, part, low_y[part, index], flow[part, index], high_y[part, index])
    pad_rows(padded, 3, low_y[3, index], thermal[index], high_y[3, index])


def march_kernel(
    flow, low_x, high_x, thermal, flag, low_y, high_y, weight, star, side_y, padded
):
    refs = (flow, low_x, high_x, thermal, flag)
    _, layers, rows, depth = flow.shape
    for index in range(layers):
        pad_layer(refs, low_y, high_y, padded, index)
        value = march_layer(refs, padded, index, range(3), 0, rows)
        for part in range(3):
            star[part, index] = value[part]
        side_y[pl.ds(index, 1), :] = value[1][rows - 1 :, :]


def transform_kernel(group, length, star, table_y, table_z, ratio, source, message, side, rows_):
    _, layers, rows, depth = star.shape
    first = position(group) * layers
    inner = jnp.where(first + layers == length, 0.0, 1.0)
    rows_[pl.ds(0, 8), :] = jnp.zeros((8, depth), F32)
    for index in range(layers):
        rows_[pl.ds(8, rows), :] = star[1, index]
        sink = star[0, index]
        if index > 0:
            sink = sink - star[0, index - 1]
        sink = sink + (star[1, index] - rows_[pl.ds(7, rows), :])
        sink = sink + (star[2, index] - lane_shift(star[2, index], -1))
        source[index] = dot(dot(table_y[...], -sink), table_z[...])
    onward = dot(dot(table_y[...], star[0, layers - 1]), table_z[...])
    side[...] = onward
    onward = inner * onward
    source[layers] = onward
    forward = source[0]
    for index in range(1, layers):
        forward = source[index] + ratio[first + index] * forward
    message[pl.ds(0, rows), :] = forward + onward / ratio[first + layers]
    backward = onward
    for index in range(layers - 1, -1, -1):
        backward = source[index] + ratio[length - 1 - first - index] * backward
    message[pl.ds(rows, rows), :] = backward


def pack_kernel(flow, thermal, ahead, behind, planes, sems):
    parts, layers, rows, depth = flow.shape
    copies = []
    for part in range(parts):
        for layer in range(2):
            for target, source in ((ahead, layers - 2 + layer), (behind, layer)):
                copies.append(
                    (flow.at[part, source], target.at[pl.ds((2 * part + layer) * rows, rows), :])
                )
    copies.append((thermal.at[layers - 1], planes.at[0]))
    copies.append((thermal.at[0], planes.at[1]))
    copies = [
        pltpu.make_async_copy(source, target, sems.at[index])
        for index, (source, target) in enumerate(copies)
    ]
    for copy in copies:
        copy.start()
    shape = (rows, rows)
    same = lax.broadcasted_iota(jnp.int32, shape, 0) == lax.broadcasted_iota(jnp.int32, shape, 1)
    for copy in copies[-2:]:
        copy.wait()
    for side, target in enumerate((ahead, behind)):
        tops = planes[side][:, depth - 1 :]
        row = jnp.sum(jnp.where(same, tops, 0.0), axis=0, keepdims=True)
        target[pl.ds(2 * parts * rows, 8), pl.ds(0, rows)] = jnp.broadcast_to(row, (8, rows))
    for copy in copies[:-2]:
        copy.wait()


def wrapped(distance, span):
    moved = distance + span // 2
    moved = jnp.where(moved < 0, moved + span, moved)
    moved = jnp.where(moved >= span, moved - span, moved)
    return (moved - span // 2).astype(F32)


def laser_row(index, layers, rows, spots_a, spots_b):
    total_x = layers * lax.axis_size("gx")
    total_y = rows * lax.axis_size("gy")
    cell_x = lax.axis_index("gx") * layers + index
    cells_y = lax.broadcasted_iota(jnp.int32, (1, rows), 1) + lax.axis_index("gy") * rows
    heat = jnp.zeros((1, rows), F32)
    for spot in range(spots_a.shape[0]):
        dist_x = wrapped(jnp.full((1, rows), cell_x - spots_a[spot], jnp.int32), total_x)
        dist_y = wrapped(cells_y - spots_b[spot], total_y)
        square = dist_x * dist_x + dist_y * dist_y
        heat = heat + jnp.exp(square * (-1.0 / (SPOT_RADIUS * SPOT_RADIUS)))
    return LASER_POWER * heat


def heat_kernel(span, spots_a, spots_b, thermal, halo, low_y, high_y, flow, warmed, padded):
    layers, rows, depth = thermal.shape
    top = lax.broadcasted_iota(jnp.int32, (rows, depth), 1) == depth - 1
    for index in span:
        pad_rows(padded, 0, low_y[3, index], thermal[index], high_y[3, index])
        around = []
        for other in range(index - 2, index + 3):
            if other < 0:
                around.append(halo[other + 2])
            elif other >= layers:
                around.append(halo[other - layers])
            else:
                around.append(thermal[other])
        speed = [flow[part, index] for part in range(3)]
        gain = TIME_INCREMENT * column(laser_row(index, layers, rows, spots_a, spots_b))
        moved = advance(around, padded, 0, speed) + jnp.where(top, gain, 0.0)
        warmed[index - span[0]] = moved


def tables_kernel(group, layers, diagonal, ratio, weight):
    length = group * layers
    mine = position(group)
    first = mine * layers
    diag = diagonal[...]
    ratio[0] = jnp.zeros_like(diag)

    def step(index, previous):
        current = 1.0 / (diag - previous)
        ratio[index] = current
        return current

    loop(1, length + 1, step, jnp.zeros_like(diag))

    def decay(low, high):
        return lax.fori_loop(
            low + 1, high + 1, lambda index, value: value * ratio[index], jnp.ones_like(diag)
        )

    def green(index):
        return 1.0 / (diag - ratio[index] - ratio[jnp.maximum(length - 1 - index, 0)])

    rounds = group.bit_length() - 1
    for turn in range(rounds):
        half = 1 << turn
        right = ((mine >> turn) & 1) == 1
        start = (mine >> (turn + 1)) << (turn + 1)
        cut = (start + half) * layers
        end = (start + 2 * half) * layers
        weight[4 * turn] = decay(cut - 1, end - 1)
        weight[4 * turn + 1] = decay(length - 1 - cut, length - 1 - start * layers)
        low = jnp.where(right, cut - 1, length - 1 - cut)
        high = jnp.where(right, first - 1, length - 1 - first - layers)
        weight[4 * turn + 2] = decay(low, high)
        weight[4 * turn + 3] = green(cut) * ratio[cut]
    inner = jnp.where(mine == group - 1, 0.0, 1.0)
    weight[4 * rounds] = inner * green(first + layers)


def face_rows(plane, edge):
    return (
        jnp.sum(plane * edge[0], axis=0, keepdims=True),
        jnp.sum(plane * edge[1], axis=0, keepdims=True),
    )


def faces_kernel(
    group, length, alone, source, wrap, before_y, table_z, ratio, weight, edge, early,
    faces, sweep,
):
    layers, rows, depth = source.shape[0] - 1, *source.shape[1:]
    mine = position(group)
    first = mine * layers
    zero = jnp.zeros((rows, depth), F32)
    keep = jnp.where(mine == (group - 1 if alone else 0), 1.0, 0.0)
    extra = dot(before_y[...], table_z[...])
    faces[...] = jnp.zeros(faces.shape, F32)
    for index in range(layers):
        faces[pl.ds(2 * length + first + index, 1), :] = extra[index : index + 1]
    forward = zero
    for index in range(layers):
        forward = source[index] + ratio[first + index] * forward
        sweep[index] = forward
    value = weight[weight.shape[0] - 1] * (source[layers] + ratio[first + layers] * forward)
    energy = source[layers] * value
    for index in range(layers - 1, -1, -1):
        value = ratio[first + index + 1] * (sweep[index] + value)
        energy = energy + source[index] * value
    faces[pl.ds(3 * length, 8), :] = jnp.broadcast_to(total(energy), (8, depth))

    def own(index):
        value = source[jnp.clip(index - first, 0, layers)]
        inside = (index >= first) & (index <= first + layers)
        value = jnp.where(inside, value, 0.0) + edge[0] * faces[pl.ds(2 * length + index, 1), :]
        if isinstance(index, int):
            return value + keep * wrap[...] if index == 0 else value
        return value + jnp.where(index == 0, keep * wrap[...], 0.0)

    def down(index, previous):
        current = own(index) + ratio[index] * previous
        sweep[index] = current
        return current

    loop(0, length, down, zero)

    def up(back, following):
        index = length - 1 - back
        value = ratio[index + 1] * (sweep[index] + following)
        low, high = face_rows(value, edge)
        faces[pl.ds(index, 1), :] = low
        faces[pl.ds(length + index, 1), :] = high
        return value

    loop(0, length, up, zero)


def joined(turn, group, message, other, sums, weight):
    rows, depth = weight.shape[1:]
    right = ((position(group) >> turn) & 1) == 1
    upper, lower = pl.ds(0, rows), pl.ds(rows, rows)
    left_s = jnp.where(right, other[upper, :], message[upper, :])
    right_s = jnp.where(right, message[upper, :], other[upper, :])
    left_t = jnp.where(right, other[lower, :], message[lower, :])
    right_t = jnp.where(right, message[lower, :], other[lower, :])
    own = weight[4 * turn + 2]
    before = sums[0] + jnp.where(right, left_s * own, 0.0)
    after = sums[1] + jnp.where(right, 0.0, right_t * own)
    forward = right_s + left_s * weight[4 * turn]
    backward = left_t + right_t * weight[4 * turn + 1]
    energy = 2.0 * total(left_s * right_t * weight[4 * turn + 3])
    return forward, backward, before, after, energy


def merge_kernel(
    turn, group, length, message, other, faces, other_faces, sums, weight,
    new_message, new_sums, head, tail,
):
    rows, depth = weight.shape[1:]
    forward, backward, before, after, energy = joined(turn, group, message, other, sums, weight)
    new_sums[0] = before
    new_sums[1] = after
    new_message[pl.ds(0, rows), :] = forward
    new_message[pl.ds(rows, rows), :] = backward
    low, high = pl.ds(0, length), pl.ds(length, length)
    late, number = pl.ds(2 * length, length), pl.ds(3 * length, 8)
    head[...] = faces[low, :] + other_faces[low, :]
    tail[...] = faces[high, :] + other_faces[high, :]
    new_message[pl.ds(2 * rows, length), :] = head[...]
    new_message[pl.ds(2 * rows + length, length), :] = faces[late, :] + other_faces[late, :]
    energy = faces[number, :] + other_faces[number, :] + energy
    new_message[pl.ds(2 * rows + 2 * length, 8), :] = energy


def late_solve(length, message, other, wrap, ratio, edge, late, sweep):
    rows, depth = wrap.shape
    own = pl.ds(2 * rows + length, length)
    late[pl.ds(0, length), :] = message[own, :] + other[own, :]

    def down(index, previous):
        current = edge[0] * late[pl.ds(index, 1), :] + ratio[index] * previous
        if isinstance(index, int):
            current = current + wrap if index == 0 else current
        else:
            current = current + jnp.where(index == 0, wrap, 0.0)
        sweep[index] = current
        return current

    zero = jnp.zeros((rows, depth), F32)
    loop(0, length, down, zero)

    def up(back, following):
        index = length - 1 - back
        value = ratio[index + 1] * (sweep[index] + following)
        sweep[index] = value
        late[pl.ds(length + index, 1), :] = jnp.sum(value * edge[0], axis=0, keepdims=True)
        return value

    loop(0, length, up, zero)
    sweep[length] = zero


def wrap_kernel(group, alone, side, *refs):
    wraps, wrap = refs[:-1], refs[-1]
    here = position(group) == group - 1
    value = jnp.where(here, side[...], 0.0) if alone else jnp.zeros(side.shape, F32)
    for part in wraps:
        value = value + part[...]
    wrap[...] = value


def close_kernel(
    turn, group, length, message, other, sums, weight, ratio, edge, wrap, ends, late, sweep
):
    forward, backward, _, _, _ = joined(turn, group, message, other, sums, weight)
    late_solve(length, message, other, wrap[...], ratio, edge, late, sweep)
    ends[0] = ratio[length] * forward + sweep[length - 1]
    ends[1] = ratio[length] * backward + sweep[0]


def coarse_kernel(
    turn, group, length, source, message, other, sums, faces_in, weight, ratio, edge, thermal,
    wrap, *refs
):
    layers, rows, depth = source.shape[0] - 1, *source.shape[1:]
    outer, (precond, image, report, faces, after_heat, late, sweep, ends) = refs[:-8], refs[-8:]
    after_heat[...] = thermal[:2]
    first = position(group) * layers
    wrap = wrap[...]
    below, below_far, above, above_far = faces_in
    forward, backward, before, after, energy = joined(turn, group, message, other, sums, weight)
    late_solve(length, message, other, wrap, ratio, edge, late, sweep)
    ends[0] = ratio[length] * forward + sweep[length - 1]
    ends[1] = ratio[length] * backward + sweep[0]
    beyond = outer[0] if outer else ends
    own = pl.ds(2 * rows, length)
    faces[pl.ds(0, length), :] = message[own, :] + other[own, :]
    faces[pl.ds(length, length), :] = below[...] + below_far[...]
    faces[pl.ds(2 * length, length), :] = above[...] + above_far[...]
    number = pl.ds(2 * rows + 2 * length, 8)
    energy = message[number, :] + other[number, :] + energy
    late_rows = late[pl.ds(0, length), :]
    energy = energy + total(
        late_rows * (2.0 * faces[pl.ds(0, length), :] - late[pl.ds(length, length), :])
    )
    energy = energy + total(wrap * (2.0 * ratio[length] * backward + sweep[0]))
    forward = before
    for index in range(layers):
        forward = source[index] + ratio[first + index] * forward
        precond[index] = forward
    lone = weight[weight.shape[0] - 1]
    value = lone * (after + source[layers] + ratio[first + layers] * forward)
    is_last = first + layers == length
    precond[layers] = jnp.where(is_last, beyond[1], value + sweep[first + layers])
    for index in range(layers - 1, -1, -1):
        value = ratio[first + index + 1] * (precond[index] + value)
        precond[index] = value + sweep[first + index]
    lead, trail = edge[0], edge[1]

    def pull(index):
        below = faces[pl.ds(length + index, 1), :]
        above = faces[pl.ds(2 * length + index, 1), :]
        return below, above

    def down(index, previous):
        below, above = pull(index)
        current = lead * below + trail * above + ratio[index] * previous
        if isinstance(index, int):
            if index == 0:
                current = current + beyond[0]
            if index == length - 1:
                current = current + beyond[1]
        else:
            current = current + jnp.where(index == 0, beyond[0], 0.0)
            current = current + jnp.where(index == length - 1, beyond[1], 0.0)
        sweep[index] = current
        return current

    zero = jnp.zeros((rows, depth), F32)
    loop(0, length, down, zero)
    line = jnp.zeros((1, depth), F32)

    def up(back, carry):
        following, linked, squared = carry
        index = length - 1 - back
        value = ratio[index + 1] * (sweep[index] + following)
        sweep[index] = value
        low, high = face_rows(value, edge)
        report[pl.ds(index, 1), :] = low
        report[pl.ds(length + index, 1), :] = high
        below, above = pull(index)
        linked = linked + faces[pl.ds(index, 1), :] * below
        squared = squared + low * below + high * above
        return value, linked, squared

    _, linked, squared = loop(0, length, up, (zero, line, line))
    sweep[length] = sweep[0]
    for index in range(layers + 1):
        image[index] = sweep[first + index]
    head, tail = sweep[0], sweep[length - 1]
    linked = 2.0 * total(linked) + total(ends[1] * beyond[0] + ends[0] * beyond[1])
    squared = total(squared) + total(head * beyond[0] + tail * beyond[1])
    crossing = 2.0 * total(head * tail)
    where = 2 * length
    report[pl.ds(where, 1), :] = energy[0:1]
    report[pl.ds(where + 1, 1), :] = jnp.broadcast_to(linked, (1, depth))
    report[pl.ds(where + 2, 1), :] = jnp.broadcast_to(squared, (1, depth))
    report[pl.ds(where + 3, 1), :] = jnp.broadcast_to(crossing, (1, depth))
    report[pl.ds(where + 4, 4), :] = jnp.zeros((4, depth), F32)


def physical_kernel(precond, image, table_y, table_z, precond_out, image_out):
    for index in range(precond.shape[0]):
        precond_out[index] = dot(dot(table_y[...], precond[index]), table_z[...])
        image_out[index] = dot(dot(table_y[...], image[index]), table_z[...])


def project_kernel(
    group, length, paired, star, precond, image, faces, table_z, warm_low, warm_high, *refs
):
    reports, (flow, pressure, warmed, field, rows_) = refs[:-5], refs[-5:]
    warmed[:2] = warm_low[...]
    warmed[2:] = warm_high[...]
    _, layers, rows, depth = star.shape
    first = position(group) * layers
    where = 2 * length
    sums = reports[0][pl.ds(where, 8), :]
    for other in reports[1:]:
        sums = sums + other[pl.ds(where, 8), :]
    pairs = jnp.zeros((1, depth), F32)
    for index in range(len(reports)):
        upper, lower = reports[index], reports[(index + 1) % len(reports)]
        pairs = pairs + jnp.sum(
            upper[pl.ds(0, length), :] * lower[pl.ds(length, length), :], axis=0, keepdims=True
        )
    energy, linked, squared, crossing = (sums[k : k + 1, 0:1] for k in range(4))
    if not paired:
        crossing = crossing + 2.0 * total(pairs)
    first_image = energy - linked
    step = energy / first_image
    beta = (energy * squared - linked * linked) / (first_image * first_image)
    rest = -linked / first_image
    second_image = (
        rest * rest * first_image
        + 2.0 * rest * step * (linked - squared)
        + step * step * (squared - crossing)
        - beta * beta * first_image
    )
    second_step = beta * energy / second_image
    alpha = step + second_step * (rest + beta)
    gamma = second_step * step
    for index in range(layers + 1):
        field[index] = alpha * precond[index] + gamma * image[index]
    own = pl.ds(2 * length + first, layers)
    following = alpha * faces[own, :] + gamma * reports[-1][pl.ds(first, layers), :]
    following = dot(following, table_z[...])
    for index in range(layers):
        value = field[index]
        pressure[index] = value
        rows_[pl.ds(0, rows), :] = value
        rows_[pl.ds(rows, 1), :] = following[index : index + 1]
        flow[0, index] = star[0, index] - (field[index + 1] - value)
        flow[1, index] = star[1, index] - (rows_[pl.ds(1, rows), :] - value)
        flow[2, index] = star[2, index] - (lane_shift(value, 1) - value)


def along(array, axis, by):
    length = lax.axis_size(axis)
    return lax.ppermute(array, axis, [(i, (i + by) % length) for i in range(length)])


def swapped(array, bit, by=0):
    count_x, count_y = lax.axis_size("gx"), lax.axis_size("gy")
    pairs = [
        (x * count_y + y, (x ^ bit) * count_y + (y + by) % count_y)
        for x in range(count_x)
        for y in range(count_y)
    ]
    return lax.ppermute(array, ("gx", "gy"), pairs)


def pack(melt_flow, thermal_state):
    parts, layers, rows, depth = melt_flow.shape
    shape = jax.ShapeDtypeStruct((2 * parts * rows + 8, max(rows, depth)), F32)
    return pl.pallas_call(
        pack_kernel,
        out_shape=[shape, shape],
        in_specs=[pl.BlockSpec(memory_space=pltpu.HBM)] * 2,
        out_specs=[VMEM, VMEM],
        scratch_shapes=[
            pltpu.VMEM((2, rows, depth), F32),
            pltpu.SemaphoreType.DMA((4 * parts + 2,)),
        ],
        compiler_params=pltpu.CompilerParams(vmem_limit_bytes=4 << 20),
    )(melt_flow, thermal_state)


def per_device(melt_flow, thermal_state, powder_flag, spot_lateral_a_cell, spot_lateral_b_cell):
    layers, rows, depth = thermal_state.shape
    count_x, count_y = lax.axis_size("gx"), lax.axis_size("gy")
    group = min(count_x, BLOCK // layers)
    blocks = count_x // group
    length = group * layers
    rounds = group.bit_length() - 1
    sine_y, values_y = sines(rows)
    sine_z, values_z = sines(depth)
    table_y = jnp.asarray(sine_y, F32)
    table_z = jnp.asarray(sine_z, F32)
    edge = jnp.asarray(
        np.broadcast_to(sine_y[[0, rows - 1]][:, :, None], (2, rows, depth)), F32
    )
    diagonal = jnp.asarray(2.0 + values_y[:, None] + values_z[None, :], F32)
    plane = (rows, depth)
    line = (length, depth)

    ahead, behind = pack(melt_flow, thermal_state)
    low_x = along(ahead, "gx", 1)
    high_x = along(behind, "gx", -1)
    states = jnp.concatenate([melt_flow, thermal_state[None]], 0)
    low_y = along(states[:, :, -2:], "gy", 1)
    high_y = along(states[:, :, :2], "gy", -1)
    ratio, weight = call(
        functools.partial(tables_kernel, group, layers),
        [diagonal],
        [(length + 1,) + plane, (4 * rounds + 1,) + plane],
    )
    star, side_y = call(
        march_kernel,
        [melt_flow, low_x, high_x, thermal_state, powder_flag, low_y, high_y, weight],
        [(3, layers) + plane, (layers, depth)],
        [pltpu.VMEM((4, rows + 16, depth), F32)],
    )
    before_y = along(side_y, "gy", 1)
    early = along(thermal_state[-2:], "gx", 1)
    source, message, side = call(
        functools.partial(transform_kernel, group, length),
        [star, table_y, table_z, ratio],
        [(layers + 1,) + plane, (2 * rows, depth), plane],
        [pltpu.VMEM((rows + 16, depth), F32)],
    )
    alone = blocks == 1
    (faces,) = call(
        functools.partial(faces_kernel, group, length, alone),
        [
            source, side if alone else along(side, "gx", 1), before_y, table_z, ratio, weight,
            edge, early,
        ],
        [(3 * length + 8, depth)],
        [pltpu.VMEM((max(length, layers + 1),) + plane, F32)],
    )
    wraps = []
    for target in range(group - 1 if alone else group):
        pairs = [
            (block * group + group - 1, (block + 1) % blocks * group + target)
            for block in range(blocks)
        ]
        wraps.append(lax.ppermute(side, "gx", pairs))
    (wrap,) = call(
        functools.partial(wrap_kernel, group, alone), [side] + wraps, [plane], flops=1 << 30
    )
    sums = jnp.zeros((2,) + plane, F32)
    for turn in range(rounds - 1):
        message, sums, head, tail = call(
            functools.partial(merge_kernel, turn, group, length),
            [
                message, swapped(message, 1 << turn), faces, swapped(faces, 1 << turn),
                sums, weight,
            ],
            [(2 * rows + 2 * length + 8, depth), (2,) + plane, line, line],
        )
        if turn + 2 < rounds:
            rest = message[2 * rows + length :]
            message, faces = message[: 2 * rows], jnp.concatenate([head, tail, rest], 0)
    bit = group >> 1
    other = swapped(message, bit)
    rim = [
        swapped(tail, 0, 1), swapped(tail, bit, 1), swapped(head, 0, -1), swapped(head, bit, -1)
    ]
    outer = []
    scratch = [pltpu.VMEM((2 * length, depth), F32), pltpu.VMEM((length + 1,) + plane, F32)]
    if not alone:
        (ends,) = call(
            functools.partial(close_kernel, rounds - 1, group, length),
            [message, other, sums, weight, ratio, edge, wrap],
            [(2,) + plane],
            scratch,
        )
        outer = [jnp.stack([along(ends[0], "gx", group), along(ends[1], "gx", -group)])]
    operands = [source, message, other, sums] + rim
    operands += [weight, ratio, edge, thermal_state, wrap] + outer

    def coarse(*refs):
        coarse_kernel(rounds - 1, group, length, *refs[:4], refs[4:8], *refs[8:])

    precond, image, report, faces, late = call(
        coarse,
        operands,
        [
            (layers + 1,) + plane, (layers + 1,) + plane, (2 * length + 8, depth),
            (3 * length, depth), (2,) + plane,
        ],
        scratch + [pltpu.VMEM((2,) + plane, F32)],
    )
    if blocks > 1:
        onward = along(image[0], "gx", -1)
        at_end = position(group) == group - 1
        image = image.at[layers].set(jnp.where(at_end, onward, image[layers]))
        upper = along(report[:length], "gy", -1)
        crossing = jnp.sum(onward * image[layers - 1])
        crossing = crossing + jnp.sum(upper * report[length : 2 * length])
        numbers = report[2 * length :].at[3].set(2.0 * crossing)
        numbers = lax.psum(jnp.where(at_end, numbers, 0.0), "gx")
        report = report.at[2 * length :].set(numbers)
    reports = [report] + [along(report, "gy", by) for by in range(1, count_y)]
    precond, image = call(
        physical_kernel,
        [precond, image, table_y, table_z],
        [(layers + 1,) + plane, (layers + 1,) + plane],
    )
    late = along(late, "gx", -1)
    warmed = []
    for halo, span in ((early, range(0, 2)), (late, range(2, layers))):
        warmed += call(
            functools.partial(heat_kernel, span),
            [spot_lateral_a_cell, spot_lateral_b_cell, thermal_state, halo, low_y, high_y, melt_flow],
            [(len(span),) + plane],
            [pltpu.VMEM((1, rows + 16, depth), F32)],
            )
    flow, pressure, warmed = call(
        functools.partial(project_kernel, group, length, blocks > 1),
        [star, precond, image, faces, table_z] + warmed + reports,
        [(3, layers) + plane, (layers,) + plane, (layers,) + plane],
        [pltpu.VMEM((layers + 1,) + plane, F32), pltpu.VMEM((rows + 16, depth), F32)],
    )
    return (flow, warmed, pressure)


def solution(mesh):
    placed = (
        P(None, ("runs", "gx"), "gy", None),
        P(("runs", "gx"), "gy", None),
        P(("runs", "gx"), "gy", None),
        P("runs"),
        P("runs"),
    )
    return jax.shard_map(
        per_device,
        mesh=mesh,
        in_specs=placed,
        out_specs=(
            P(None, ("runs", "gx"), "gy", None),
            P(("runs", "gx"), "gy", None),
            P(("runs", "gx"), "gy", None),
        ),
        check_vma=False,
    )
```

```python
import functools
import math

import jax
import jax.numpy as jnp
import numpy as np
from jax import lax
from jax.experimental import pallas as pl
from jax.experimental.pallas import tpu as pltpu
from jax.sharding import PartitionSpec as P

BLOCK = 128

TIME_INCREMENT = 0.2
MARANGONI = 1.5
DRAG_RATE = 4.0
LASER_POWER = 3.0
SPOT_RADIUS = 5.0

F32 = jnp.float32
VMEM = pl.BlockSpec(memory_space=pltpu.VMEM)
SMEM = pl.BlockSpec(memory_space=pltpu.SMEM)


def call(body, operands, shapes, scratch=(), scalars=0, loose=0, flops=1 << 20):
    out_shape = [jax.ShapeDtypeStruct(shape, F32) for shape in shapes]
    moved = 4 * sum(math.prod(shape) for shape in shapes)
    held = moved + 4 * sum(operand.size for operand in operands)
    held += 4 * sum(math.prod(space.shape) for space in scratch)
    return pl.pallas_call(
        body,
        out_shape=out_shape,
        in_specs=[SMEM] * scalars
        + [VMEM] * (len(operands) - scalars - loose)
        + [pl.BlockSpec(memory_space=pl.ANY)] * loose,
        out_specs=[VMEM] * len(shapes),
        scratch_shapes=list(scratch),
        compiler_params=pltpu.CompilerParams(vmem_limit_bytes=held + (4 << 20)),
        cost_estimate=pl.CostEstimate(flops=flops, bytes_accessed=2 * moved, transcendentals=0),
    )(*operands)


def dot(left, right):
    return jnp.dot(left, right, precision=lax.Precision.HIGHEST, preferred_element_type=F32)


def total(cells):
    return jnp.sum(jnp.sum(cells, axis=0, keepdims=True), axis=1, keepdims=True)


def loop(low, high, body, start):
    if isinstance(high, int) and isinstance(low, int) and high - low <= 24:
        carry = start
        for index in range(low, high):
            carry = body(index, carry)
        return carry
    return lax.fori_loop(low, high, body, start)


def position(group):
    return lax.rem(lax.axis_index("gx"), group)


def sines(length):
    positions = np.arange(length) + 1.0
    step = math.pi / (length + 1)
    table = np.sqrt(2.0 / (length + 1)) * np.sin(step * positions[:, None] * positions[None, :])
    return table, 2.0 - 2.0 * np.cos(step * positions)


def lane_shift(cells, offset):
    width = cells.shape[1]
    lane = lax.broadcasted_iota(jnp.int32, cells.shape, 1)
    moved = pltpu.roll(cells, (-offset) % width, 1)
    keep = lane < width - offset if offset > 0 else lane >= -offset
    return jnp.where(keep, moved, 0.0)


def column(row):
    length = row.shape[1]
    shape = (length, length)
    same = lax.broadcasted_iota(jnp.int32, shape, 0) == lax.broadcasted_iota(jnp.int32, shape, 1)
    return jnp.sum(jnp.where(same, row, 0.0), axis=1, keepdims=True)


def advance(layers, padded, index, speed, start=0):
    middle = layers[2]
    rows = middle.shape[0]
    speed_x, speed_y, speed_z = speed
    ahead = speed_x >= 0.0
    near = jnp.where(ahead, layers[1], layers[3])
    far = jnp.where(ahead, layers[0], layers[4])
    rate = jnp.abs(speed_x) * (1.5 * middle - 2.0 * near + 0.5 * far)
    ahead = speed_y >= 0.0
    near = jnp.where(ahead, padded[index, pl.ds(7 + start, rows), :], padded[index, pl.ds(9 + start, rows), :])
    far = jnp.where(ahead, padded[index, pl.ds(6 + start, rows), :], padded[index, pl.ds(10 + start, rows), :])
    rate = rate + jnp.abs(speed_y) * (1.5 * middle - 2.0 * near + 0.5 * far)
    ahead = speed_z >= 0.0
    near = jnp.where(ahead, lane_shift(middle, -1), lane_shift(middle, 1))
    far = jnp.where(ahead, lane_shift(middle, -2), lane_shift(middle, 2))
    rate = rate + jnp.abs(speed_z) * (1.5 * middle - 2.0 * near + 0.5 * far)
    return middle - TIME_INCREMENT * rate


def pad_rows(padded, index, before, middle, after):
    rows = middle.shape[0]
    padded[index, pl.ds(8, rows), :] = middle
    padded[index, pl.ds(6, 2), :] = before
    padded[index, pl.ds(8 + rows, 2), :] = after


def march_layer(refs, padded, index, parts, start, count):
    flow, low_x, high_x, thermal, flag = refs
    _, layers, rows, depth = flow.shape
    span = pl.ds(start, count)
    speed = [flow[part, index, span, :] for part in range(3)]
    drag = 1.0 / (1.0 + TIME_INCREMENT * DRAG_RATE * flag[index, span, :].astype(F32))
    top = lax.broadcasted_iota(jnp.int32, (count, depth), 1) == depth - 1
    pull = -MARANGONI * 0.5 * TIME_INCREMENT
    out = []
    for part in parts:
        around = []
        for other in range(index - 2, index + 3):
            if other < 0:
                first = (2 * part + other + 2) * rows + start
                around.append(low_x[pl.ds(first, count), :])
            elif other >= layers:
                first = (2 * part + other - layers) * rows + start
                around.append(high_x[pl.ds(first, count), :])
            else:
                around.append(flow[part, other, span, :])
        moved = advance(around, padded, part, speed, start)
        if part == 0:
            edge = lambda halo: column(halo[pl.ds(halo.shape[0] - 8, 1), pl.ds(0, rows)])
            behind = thermal[index - 1] if index > 0 else edge(low_x)
            before = thermal[index + 1] if index + 1 < layers else edge(high_x)
            moved = moved + jnp.where(top, pull * (before - behind), 0.0)
        if part == 1:
            slope = padded[3, pl.ds(9 + start, count), :] - padded[3, pl.ds(7 + start, count), :]
            moved = moved + jnp.where(top, pull * slope, 0.0)
        out.append(moved * drag)
    return out


def pad_layer(refs, low_y, high_y, padded, index):
    flow, _, _, thermal, _ = refs
    for part in range(3):
        pad_rows(
            padded, part, low_y[part, index, 6:], flow[part, index], high_y[part, index, :2]
        )
    pad_rows(padded, 3, low_y[3, index, 6:], thermal[index], high_y[3, index, :2])


def march_kernel(
    flow, low_x, high_x, thermal, flag, low_y, high_y, extra, weight,
    star, side_x, side_y, padded,
):
    refs = (flow, low_x, high_x, thermal, flag)
    _, layers, rows, depth = flow.shape
    for index in range(layers):
        pad_layer(refs, low_y, high_y, padded, index)
        value = march_layer(refs, padded, index, range(3), 0, rows)
        for part in range(3):
            star[part, index] = value[part]
        side_y[pl.ds(index, 1), :] = value[1][rows - 1 :, :]
    plane = lambda index: low_x[pl.ds(index * rows, rows), pl.ds(0, depth)]
    beside = extra[pl.ds(2 * rows, 8), pl.ds(0, depth)]
    pad_rows(padded, 0, beside[2:4], plane(1), beside[4:6])
    around = [extra[pl.ds(0, rows), pl.ds(0, depth)], plane(0), plane(1), flow[0, 0], flow[0, 1]]
    moved = advance(around, padded, 0, [plane(1), plane(3), plane(5)])
    top = lax.broadcasted_iota(jnp.int32, (rows, depth), 1) == depth - 1
    pull = -MARANGONI * 0.5 * TIME_INCREMENT
    behind = column(extra[pl.ds(2 * rows, 1), pl.ds(0, rows)])
    moved = moved + jnp.where(top, pull * (thermal[0] - behind), 0.0)
    drag = 1.0 + TIME_INCREMENT * DRAG_RATE * extra[pl.ds(rows, rows), pl.ds(0, depth)]
    side_x[...] = moved / drag


def transform_kernel(
    group, length, star, side_x, table_y, table_z, ratio, source, message, rows_
):
    _, layers, rows, depth = star.shape
    first = position(group) * layers
    rows_[pl.ds(0, 8), :] = jnp.zeros((8, depth), F32)
    for index in range(layers):
        rows_[pl.ds(8, rows), :] = star[1, index]
        behind = star[0, index - 1] if index > 0 else side_x[...]
        sink = star[0, index] - behind
        sink = sink + (star[1, index] - rows_[pl.ds(7, rows), :])
        sink = sink + (star[2, index] - lane_shift(star[2, index], -1))
        source[index] = dot(dot(table_y[...], -sink), table_z[...])
    forward = source[0]
    for index in range(1, layers):
        forward = source[index] + ratio[first + index] * forward
    message[pl.ds(0, rows), :] = forward
    backward = source[layers - 1]
    for index in range(layers - 2, -1, -1):
        backward = source[index] + ratio[length - 1 - first - index] * backward
    message[pl.ds(rows, rows), :] = backward


def started(copies):
    for copy in copies:
        copy.start()
    return copies


def surface(plane):
    rows, depth = plane.shape
    shape = (rows, rows)
    same = lax.broadcasted_iota(jnp.int32, shape, 0) == lax.broadcasted_iota(jnp.int32, shape, 1)
    return jnp.sum(jnp.where(same, plane[:, depth - 1 :], 0.0), axis=0, keepdims=True)


def halo_kernel(flow, thermal, ahead, behind, last_rows, first_rows, tops, sems):
    parts, layers, rows, depth = flow.shape
    pairs = [(thermal.at[layers - 1], tops.at[0]), (thermal.at[0], tops.at[1])]
    for part in range(parts + 1):
        for layer in range(layers):
            source = thermal.at[layer] if part == parts else flow.at[part, layer]
            pairs.append((source.at[pl.ds(rows - 8, 8), :], last_rows.at[part, layer]))
            pairs.append((source.at[pl.ds(0, 8), :], first_rows.at[part, layer]))
    for part in range(parts):
        for layer in range(2):
            span = pl.ds((2 * part + layer) * rows, rows)
            pairs.append((flow.at[part, layers - 2 + layer], ahead.at[span, :]))
            pairs.append((flow.at[part, layer], behind.at[span, :]))
    copies = started(
        [pltpu.make_async_copy(*pair, sems.at[index]) for index, pair in enumerate(pairs)]
    )
    for side, message in enumerate((ahead, behind)):
        copies[side].wait()
        row = jnp.broadcast_to(surface(tops[side]), (8, rows))
        message[pl.ds(2 * parts * rows, 8), pl.ds(0, rows)] = row
    for copy in copies[2:]:
        copy.wait()


def extra_kernel(flow, thermal, flag, low_y, high_y, extra, last, first, flags, sems):
    _, layers, rows, depth = flow.shape
    pairs = [(flag.at[layers - 1], flags), (thermal.at[pl.ds(layers - 2, 2)], last)]
    pairs.append((thermal.at[pl.ds(0, 2)], first))
    pairs.append((flow.at[0, layers - 3], extra.at[pl.ds(0, rows), :]))
    copies = started(
        [pltpu.make_async_copy(*pair, sems.at[index]) for index, pair in enumerate(pairs)]
    )
    base = 2 * rows
    extra[pl.ds(base, 8), :] = jnp.zeros((8, extra.shape[1]), F32)
    extra[pl.ds(base + 2, 2), pl.ds(0, depth)] = low_y[0, layers - 1, 6:, :]
    extra[pl.ds(base + 4, 2), pl.ds(0, depth)] = high_y[0, layers - 1, :2, :]
    for copy in copies[:2]:
        copy.wait()
    extra[pl.ds(rows, rows), :] = flags[...].astype(F32)
    extra[pl.ds(base, 1), pl.ds(0, rows)] = surface(last[0])
    for copy in copies[2:]:
        copy.wait()


def wrapped(distance, span):
    moved = distance + span // 2
    moved = jnp.where(moved < 0, moved + span, moved)
    moved = jnp.where(moved >= span, moved - span, moved)
    return (moved - span // 2).astype(F32)


def laser_row(index, layers, rows, spots_a, spots_b):
    total_x = layers * lax.axis_size("gx")
    total_y = rows * lax.axis_size("gy")
    cell_x = lax.axis_index("gx") * layers + index
    cells_y = lax.broadcasted_iota(jnp.int32, (1, rows), 1) + lax.axis_index("gy") * rows
    heat = jnp.zeros((1, rows), F32)
    for spot in range(spots_a.shape[0]):
        dist_x = wrapped(jnp.full((1, rows), cell_x - spots_a[spot], jnp.int32), total_x)
        dist_y = wrapped(cells_y - spots_b[spot], total_y)
        square = dist_x * dist_x + dist_y * dist_y
        heat = heat + jnp.exp(square * (-1.0 / (SPOT_RADIUS * SPOT_RADIUS)))
    return LASER_POWER * heat


def heat_kernel(
    spots_a, spots_b, thermal, low_x, high_x, low_y, high_y, flow, warmed, padded
):
    layers, rows, depth = thermal.shape
    top = lax.broadcasted_iota(jnp.int32, (rows, depth), 1) == depth - 1
    for index in range(layers):
        pad_rows(padded, 0, low_y[3, index, 6:], thermal[index], high_y[3, index, :2])
        around = []
        for other in range(index - 2, index + 3):
            if other < 0:
                around.append(low_x[other + 2])
            elif other >= layers:
                around.append(high_x[other - layers])
            else:
                around.append(thermal[other])
        speed = [flow[part, index] for part in range(3)]
        gain = TIME_INCREMENT * column(laser_row(index, layers, rows, spots_a, spots_b))
        warmed[index] = advance(around, padded, 0, speed) + jnp.where(top, gain, 0.0)


def tables_kernel(group, layers, diagonal, ratio, weight):
    length = group * layers
    mine = position(group)
    first = mine * layers
    diag = diagonal[...]
    ratio[0] = jnp.zeros_like(diag)

    def step(index, previous):
        current = 1.0 / (diag - previous)
        ratio[index] = current
        return current

    loop(1, length + 1, step, jnp.zeros_like(diag))

    def decay(low, high):
        return lax.fori_loop(
            low + 1, high + 1, lambda index, value: value * ratio[index], jnp.ones_like(diag)
        )

    def green(index):
        return 1.0 / (diag - ratio[index] - ratio[jnp.maximum(length - 1 - index, 0)])

    rounds = group.bit_length() - 1
    for turn in range(rounds):
        half = 1 << turn
        right = ((mine >> turn) & 1) == 1
        start = (mine >> (turn + 1)) << (turn + 1)
        cut = (start + half) * layers
        end = (start + 2 * half) * layers
        weight[4 * turn] = decay(cut - 1, end - 1)
        weight[4 * turn + 1] = decay(length - 1 - cut, length - 1 - start * layers)
        low = jnp.where(right, cut - 1, length - 1 - cut)
        high = jnp.where(right, first - 1, length - 1 - first - layers)
        weight[4 * turn + 2] = decay(low, high)
        weight[4 * turn + 3] = green(cut) * ratio[cut]
    inner = jnp.where(mine == group - 1, 0.0, 1.0)
    weight[4 * rounds] = inner * green(first + layers)


def face_rows(plane, edge):
    return (
        jnp.sum(plane * edge[0], axis=0, keepdims=True),
        jnp.sum(plane * edge[1], axis=0, keepdims=True),
    )


def faces_kernel(
    group, length, source, before_y, table_z, ratio, weight, edge, *refs
):
    faces, sweep = refs[-2:]
    layers, rows, depth = source.shape
    first = position(group) * layers
    zero = jnp.zeros((rows, depth), F32)
    extra = dot(before_y[...], table_z[...])
    faces[...] = jnp.zeros(faces.shape, F32)
    for index in range(layers):
        faces[pl.ds(2 * length + first + index, 1), :] = extra[index : index + 1]
    forward = zero
    for index in range(layers):
        forward = source[index] + ratio[first + index] * forward
        sweep[index] = forward
    value = weight[weight.shape[0] - 1] * (ratio[first + layers] * forward)
    energy = zero
    for index in range(layers - 1, -1, -1):
        value = ratio[first + index + 1] * (sweep[index] + value)
        energy = energy + source[index] * value
    faces[pl.ds(3 * length, 8), :] = jnp.broadcast_to(total(energy), (8, depth))

    def down(index, previous):
        inside = (index >= first) & (index < first + layers)
        own = jnp.where(inside, source[jnp.clip(index - first, 0, layers - 1)], 0.0)
        current = own + edge[0] * faces[pl.ds(2 * length + index, 1), :] + ratio[index] * previous
        sweep[index] = current
        return current

    loop(0, length, down, zero)

    def up(back, following):
        index = length - 1 - back
        value = ratio[index + 1] * (sweep[index] + following)
        low, high = face_rows(value, edge)
        faces[pl.ds(index, 1), :] = low
        faces[pl.ds(length + index, 1), :] = high
        return value

    loop(0, length, up, zero)


def joined(turn, group, message, other, sums, weight):
    rows, depth = weight.shape[1:]
    right = ((position(group) >> turn) & 1) == 1
    upper, lower = pl.ds(0, rows), pl.ds(rows, rows)
    left_s = jnp.where(right, other[upper, :], message[upper, :])
    right_s = jnp.where(right, message[upper, :], other[upper, :])
    left_t = jnp.where(right, other[lower, :], message[lower, :])
    right_t = jnp.where(right, message[lower, :], other[lower, :])
    own = weight[4 * turn + 2]
    before = sums[0] + jnp.where(right, left_s * own, 0.0)
    after = sums[1] + jnp.where(right, 0.0, right_t * own)
    forward = right_s + left_s * weight[4 * turn]
    backward = left_t + right_t * weight[4 * turn + 1]
    energy = 2.0 * total(left_s * right_t * weight[4 * turn + 3])
    return forward, backward, before, after, energy


def merge_kernel(
    turn, group, length, message, other, faces, other_faces, sums, weight, _,
    new_message, new_sums, head, tail,
):
    rows, depth = weight.shape[1:]
    forward, backward, before, after, energy = joined(turn, group, message, other, sums, weight)
    new_sums[0] = before
    new_sums[1] = after
    new_message[pl.ds(0, rows), :] = forward
    new_message[pl.ds(rows, rows), :] = backward
    low, high = pl.ds(0, length), pl.ds(length, length)
    late, number = pl.ds(2 * length, length), pl.ds(3 * length, 8)
    head[...] = faces[low, :] + other_faces[low, :]
    tail[...] = faces[high, :] + other_faces[high, :]
    new_message[pl.ds(2 * rows, length), :] = head[...]
    new_message[pl.ds(2 * rows + length, length), :] = faces[late, :] + other_faces[late, :]
    energy = faces[number, :] + other_faces[number, :] + energy
    new_message[pl.ds(2 * rows + 2 * length, 8), :] = energy


def late_solve(length, message, other, ratio, edge, late, sweep):
    rows, depth = edge.shape[1:]
    own = pl.ds(2 * rows + length, length)
    late[pl.ds(0, length), :] = message[own, :] + other[own, :]

    def down(index, previous):
        current = edge[0] * late[pl.ds(index, 1), :] + ratio[index] * previous
        sweep[index] = current
        return current

    zero = jnp.zeros((rows, depth), F32)
    loop(0, length, down, zero)

    def up(back, following):
        index = length - 1 - back
        value = ratio[index + 1] * (sweep[index] + following)
        sweep[index] = value
        late[pl.ds(length + index, 1), :] = jnp.sum(value * edge[0], axis=0, keepdims=True)
        return value

    loop(0, length, up, zero)
    sweep[length] = zero


def close_kernel(
    turn, group, length, message, other, sums, weight, ratio, edge, ends, late, sweep
):
    forward, backward, _, _, _ = joined(turn, group, message, other, sums, weight)
    late_solve(length, message, other, ratio, edge, late, sweep)
    ends[0] = ratio[length] * forward + sweep[length - 1]
    ends[1] = ratio[length] * backward + sweep[0]


def coarse_kernel(
    turn, group, length, alone, source, message, other, sums, faces_in, weight, ratio, edge, *refs
):
    precond, image, report, faces, late, sweep, ends = refs[-7:]
    layers, rows, depth = source.shape
    first = position(group) * layers
    below, below_far, above, above_far = faces_in
    forward, backward, before, after, energy = joined(turn, group, message, other, sums, weight)
    late_solve(length, message, other, ratio, edge, late, sweep)
    ends[0] = ratio[length] * forward + sweep[length - 1]
    ends[1] = ratio[length] * backward + sweep[0]
    beyond = ends if alone else refs[0]
    own = pl.ds(2 * rows, length)
    faces[pl.ds(0, length), :] = message[own, :] + other[own, :]
    faces[pl.ds(length, length), :] = below[...] + below_far[...]
    faces[pl.ds(2 * length, length), :] = above[...] + above_far[...]
    number = pl.ds(2 * rows + 2 * length, 8)
    energy = message[number, :] + other[number, :] + energy
    late_rows = late[pl.ds(0, length), :]
    energy = energy + total(
        late_rows * (2.0 * faces[pl.ds(0, length), :] - late[pl.ds(length, length), :])
    )
    forward = before
    for index in range(layers):
        forward = source[index] + ratio[first + index] * forward
        precond[index] = forward
    value = weight[weight.shape[0] - 1] * (after + ratio[first + layers] * forward)
    is_last = first + layers == length
    precond[layers] = jnp.where(is_last, beyond[1], value + sweep[first + layers])
    for index in range(layers - 1, -1, -1):
        value = ratio[first + index + 1] * (precond[index] + value)
        precond[index] = value + sweep[first + index]
    lead, trail = edge[0], edge[1]

    def pull(index):
        below = faces[pl.ds(length + index, 1), :]
        above = faces[pl.ds(2 * length + index, 1), :]
        return below, above

    def down(index, previous):
        below, above = pull(index)
        current = lead * below + trail * above + ratio[index] * previous
        if isinstance(index, int):
            if index == 0:
                current = current + beyond[0]
            if index == length - 1:
                current = current + beyond[1]
        else:
            current = current + jnp.where(index == 0, beyond[0], 0.0)
            current = current + jnp.where(index == length - 1, beyond[1], 0.0)
        sweep[index] = current
        return current

    zero = jnp.zeros((rows, depth), F32)
    loop(0, length, down, zero)
    line = jnp.zeros((1, depth), F32)

    def up(back, carry):
        following, linked, squared = carry
        index = length - 1 - back
        value = ratio[index + 1] * (sweep[index] + following)
        sweep[index] = value
        low, high = face_rows(value, edge)
        report[pl.ds(index, 1), :] = low
        report[pl.ds(length + index, 1), :] = high
        below, above = pull(index)
        linked = linked + faces[pl.ds(index, 1), :] * below
        squared = squared + low * below + high * above
        return value, linked, squared

    _, linked, squared = loop(0, length, up, (zero, line, line))
    sweep[length] = sweep[0]
    for index in range(layers + 1):
        image[index] = sweep[first + index]
    head, tail = sweep[0], sweep[length - 1]
    linked = 2.0 * total(linked) + total(ends[1] * beyond[0] + ends[0] * beyond[1])
    squared = total(squared) + total(head * beyond[0] + tail * beyond[1])
    crossing = 2.0 * total(head * tail)
    where = 2 * length
    report[pl.ds(where, 1), :] = energy[0:1]
    report[pl.ds(where + 1, 1), :] = jnp.broadcast_to(linked, (1, depth))
    report[pl.ds(where + 2, 1), :] = jnp.broadcast_to(squared, (1, depth))
    report[pl.ds(where + 3, 1), :] = jnp.broadcast_to(crossing, (1, depth))
    report[pl.ds(where + 4, 4), :] = jnp.zeros((4, depth), F32)


def physical_kernel(precond, image, table_y, table_z, precond_out, image_out):
    for index in range(precond.shape[0]):
        precond_out[index] = dot(dot(table_y[...], precond[index]), table_z[...])
        image_out[index] = dot(dot(table_y[...], image[index]), table_z[...])


def project_kernel(
    group, length, paired, star, precond, image, faces, table_z, *refs
):
    reports, (flow, pressure, field, rows_) = refs[:-4], refs[-4:]
    _, layers, rows, depth = star.shape
    first = position(group) * layers
    where = 2 * length
    sums = reports[0][pl.ds(where, 8), :]
    for other in reports[1:]:
        sums = sums + other[pl.ds(where, 8), :]
    pairs = jnp.zeros((1, depth), F32)
    for index in range(len(reports)):
        upper, lower = reports[index], reports[(index + 1) % len(reports)]
        pairs = pairs + jnp.sum(
            upper[pl.ds(0, length), :] * lower[pl.ds(length, length), :], axis=0, keepdims=True
        )
    energy, linked, squared, crossing = (sums[k : k + 1, 0:1] for k in range(4))
    if not paired:
        crossing = crossing + 2.0 * total(pairs)
    first_image = energy - linked
    step = energy / first_image
    beta = (energy * squared - linked * linked) / (first_image * first_image)
    rest = -linked / first_image
    second_image = (
        rest * rest * first_image
        + 2.0 * rest * step * (linked - squared)
        + step * step * (squared - crossing)
        - beta * beta * first_image
    )
    second_step = beta * energy / second_image
    alpha = step + second_step * (rest + beta)
    gamma = second_step * step
    for index in range(layers + 1):
        field[index] = alpha * precond[index] + gamma * image[index]
    own = pl.ds(2 * length + first, layers)
    following = alpha * faces[own, :] + gamma * reports[-1][pl.ds(first, layers), :]
    following = dot(following, table_z[...])
    for index in range(layers):
        value = field[index]
        pressure[index] = value
        rows_[pl.ds(0, rows), :] = value
        rows_[pl.ds(rows, 1), :] = following[index : index + 1]
        flow[0, index] = star[0, index] - (field[index + 1] - value)
        flow[1, index] = star[1, index] - (rows_[pl.ds(1, rows), :] - value)
        flow[2, index] = star[2, index] - (lane_shift(value, 1) - value)


def along(array, axis, by):
    length = lax.axis_size(axis)
    return lax.ppermute(array, axis, [(i, (i + by) % length) for i in range(length)])


def swapped(array, bit, by=0):
    count_x, count_y = lax.axis_size("gx"), lax.axis_size("gy")
    pairs = [
        (x * count_y + y, (x ^ bit) * count_y + (y + by) % count_y)
        for x in range(count_x)
        for y in range(count_y)
    ]
    return lax.ppermute(array, ("gx", "gy"), pairs)


def pack(body, inputs, received, shapes, scratch, count):
    inputs = [pltpu.with_memory_space_constraint(each, pltpu.HBM) for each in inputs]
    return pl.pallas_call(
        body,
        out_shape=[jax.ShapeDtypeStruct(shape, F32) for shape in shapes],
        in_specs=[pl.BlockSpec(memory_space=pltpu.HBM)] * len(inputs) + [VMEM] * len(received),
        out_specs=[VMEM] * len(shapes),
        scratch_shapes=[scratch, pltpu.SemaphoreType.DMA((count,))],
        compiler_params=pltpu.CompilerParams(vmem_limit_bytes=4 << 20),
    )(*inputs, *received)


def per_device(melt_flow, thermal_state, powder_flag, spot_lateral_a_cell, spot_lateral_b_cell):
    layers, rows, depth = thermal_state.shape
    count_x, count_y = lax.axis_size("gx"), lax.axis_size("gy")
    group = min(count_x, BLOCK // layers)
    blocks = count_x // group
    length = group * layers
    rounds = group.bit_length() - 1
    sine_y, values_y = sines(rows)
    sine_z, values_z = sines(depth)
    table_y = jnp.asarray(sine_y, F32)
    table_z = jnp.asarray(sine_z, F32)
    edge = jnp.asarray(
        np.broadcast_to(sine_y[[0, rows - 1]][:, :, None], (2, rows, depth)), F32
    )
    diagonal = jnp.asarray(2.0 + values_y[:, None] + values_z[None, :], F32)
    plane = (rows, depth)
    line = (length, depth)

    parts = melt_flow.shape[0]
    width = max(rows, depth)
    outer_planes = (2 * parts * rows + 8, width)
    ahead, behind, last_rows, first_rows = pack(
        halo_kernel,
        [melt_flow, thermal_state],
        [],
        [outer_planes, outer_planes] + [(parts + 1, layers, 8, depth)] * 2,
        pltpu.VMEM((2,) + plane, F32),
        2 + 2 * layers * (parts + 1) + 4 * parts,
    )
    low_x = along(ahead, "gx", 1)
    high_x = along(behind, "gx", -1)
    low_y = along(last_rows, "gy", 1)
    high_y = along(first_rows, "gy", -1)
    extra, last, first = pack(
        extra_kernel,
        [melt_flow, thermal_state, powder_flag],
        [low_y, high_y],
        [(2 * rows + 8, width), (2,) + plane, (2,) + plane],
        pltpu.VMEM(plane, jnp.int32),
        4,
    )
    extra = along(extra, "gx", 1)
    ratio, weight = call(
        functools.partial(tables_kernel, group, layers),
        [diagonal],
        [(length + 1,) + plane, (4 * rounds + 1,) + plane],
    )
    early_low = along(last, "gx", 1)
    early_high = along(first, "gx", -1)
    star, side_x, side_y = call(
        march_kernel,
        [
            melt_flow, low_x, high_x, thermal_state, powder_flag, low_y, high_y, extra, weight,
        ],
        [(3, layers) + plane, plane, (layers, depth)],
        [pltpu.VMEM((4, rows + 16, depth), F32)],
    )
    before_y = along(side_y, "gy", 1)
    source, message = call(
        functools.partial(transform_kernel, group, length),
        [star, side_x, table_y, table_z, ratio],
        [(layers,) + plane, (2 * rows, depth)],
        [pltpu.VMEM((rows + 16, depth), F32)],
    )
    (faces,) = call(
        functools.partial(faces_kernel, group, length),
        [source, before_y, table_z, ratio, weight, edge, early_low],
        [(3 * length + 8, depth)],
        [pltpu.VMEM((max(length, layers + 1),) + plane, F32)],
        loose=1,
    )
    alone = blocks == 1
    (warmed,) = call(
        heat_kernel,
        [
            spot_lateral_a_cell, spot_lateral_b_cell, thermal_state, early_low, early_high,
            low_y, high_y, melt_flow,
        ],
        [(layers,) + plane],
        [pltpu.VMEM((1, rows + 16, depth), F32)],
        scalars=2,
    )
    sums = jnp.zeros((2,) + plane, F32)
    for turn in range(rounds - 1):
        message, sums, head, tail = call(
            functools.partial(merge_kernel, turn, group, length),
            [
                message, swapped(message, 1 << turn), faces, swapped(faces, 1 << turn),
                sums, weight, early_high,
            ],
            [(2 * rows + 2 * length + 8, depth), (2,) + plane, line, line],
            loose=1,
        )
        if turn + 2 < rounds:
            rest = message[2 * rows + length :]
            message, faces = message[: 2 * rows], jnp.concatenate([head, tail, rest], 0)
    bit = group >> 1
    other = swapped(message, bit)
    rim = [
        swapped(tail, 0, 1), swapped(tail, bit, 1), swapped(head, 0, -1), swapped(head, bit, -1)
    ]
    outer = []
    scratch = [pltpu.VMEM((2 * length, depth), F32), pltpu.VMEM((length + 1,) + plane, F32)]
    if not alone:
        (ends,) = call(
            functools.partial(close_kernel, rounds - 1, group, length),
            [message, other, sums, weight, ratio, edge],
            [(2,) + plane],
            scratch,
        )
        outer = [jnp.stack([along(ends[0], "gx", group), along(ends[1], "gx", -group)])]
    operands = [source, message, other, sums] + rim
    operands += [weight, ratio, edge] + outer + [warmed]

    def coarse(*refs):
        coarse_kernel(rounds - 1, group, length, alone, *refs[:4], refs[4:8], *refs[8:])

    precond, image, report, faces = call(
        coarse,
        operands,
        [
            (layers + 1,) + plane, (layers + 1,) + plane, (2 * length + 8, depth),
            (3 * length, depth),
        ],
        scratch + [pltpu.VMEM((2,) + plane, F32)],
        loose=1,
    )
    if blocks > 1:
        onward = along(image[0], "gx", -1)
        at_end = position(group) == group - 1
        image = image.at[layers].set(jnp.where(at_end, onward, image[layers]))
        upper = along(report[:length], "gy", -1)
        crossing = jnp.sum(onward * image[layers - 1])
        crossing = crossing + jnp.sum(upper * report[length : 2 * length])
        numbers = report[2 * length :].at[3].set(2.0 * crossing)
        numbers = lax.psum(jnp.where(at_end, numbers, 0.0), "gx")
        report = report.at[2 * length :].set(numbers)
    reports = [report] + [along(report, "gy", by) for by in range(1, count_y)]
    precond, image = call(
        physical_kernel,
        [precond, image, table_y, table_z],
        [(layers + 1,) + plane, (layers + 1,) + plane],
    )
    flow, pressure = call(
        functools.partial(project_kernel, group, length, blocks > 1),
        [star, precond, image, faces, table_z] + reports,
        [(3, layers) + plane, (layers,) + plane],
        [pltpu.VMEM((layers + 1,) + plane, F32), pltpu.VMEM((rows + 16, depth), F32)],
    )
    return (flow, warmed, pressure)


def solution(mesh):
    placed = (
        P(None, ("runs", "gx"), "gy", None),
        P(("runs", "gx"), "gy", None),
        P(("runs", "gx"), "gy", None),
        P("runs"),
        P("runs"),
    )
    return jax.shard_map(
        per_device,
        mesh=mesh,
        in_specs=placed,
        out_specs=(
            P(None, ("runs", "gx"), "gy", None),
            P(("runs", "gx"), "gy", None),
            P(("runs", "gx"), "gy", None),
        ),
        check_vma=False,
    )
```

```python
import functools
import math

import jax
import jax.numpy as jnp
import numpy as np
from jax import lax
from jax.experimental import pallas as pl
from jax.experimental.pallas import tpu as pltpu
from jax.sharding import PartitionSpec as P

BLOCK = 128

TIME_INCREMENT = 0.2
MARANGONI = 1.5
DRAG_RATE = 4.0
LASER_POWER = 3.0
SPOT_RADIUS = 5.0

F32 = jnp.float32
VMEM = pl.BlockSpec(memory_space=pltpu.VMEM)
SMEM = pl.BlockSpec(memory_space=pltpu.SMEM)


def call(body, operands, shapes, scratch=(), scalars=0, loose=0, flops=1 << 20):
    out_shape = [jax.ShapeDtypeStruct(shape, F32) for shape in shapes]
    moved = 4 * sum(math.prod(shape) for shape in shapes)
    held = moved + 4 * sum(operand.size for operand in operands)
    held += 4 * sum(math.prod(space.shape) for space in scratch)
    return pl.pallas_call(
        body,
        out_shape=out_shape,
        in_specs=[SMEM] * scalars
        + [VMEM] * (len(operands) - scalars - loose)
        + [pl.BlockSpec(memory_space=pl.ANY)] * loose,
        out_specs=[VMEM] * len(shapes),
        scratch_shapes=list(scratch),
        compiler_params=pltpu.CompilerParams(vmem_limit_bytes=held + (4 << 20)),
        cost_estimate=pl.CostEstimate(flops=flops, bytes_accessed=2 * moved, transcendentals=0),
    )(*operands)


def dot(left, right):
    return jnp.dot(left, right, precision=lax.Precision.HIGHEST, preferred_element_type=F32)


def total(cells):
    return jnp.sum(jnp.sum(cells, axis=0, keepdims=True), axis=1, keepdims=True)


def loop(low, high, body, start):
    if isinstance(high, int) and isinstance(low, int) and high - low <= 24:
        carry = start
        for index in range(low, high):
            carry = body(index, carry)
        return carry
    return lax.fori_loop(low, high, body, start)


def position(group):
    return lax.rem(lax.axis_index("gx"), group)


def sines(length):
    positions = np.arange(length) + 1.0
    step = math.pi / (length + 1)
    table = np.sqrt(2.0 / (length + 1)) * np.sin(step * positions[:, None] * positions[None, :])
    return table, 2.0 - 2.0 * np.cos(step * positions)


def lane_shift(cells, offset):
    width = cells.shape[1]
    lane = lax.broadcasted_iota(jnp.int32, cells.shape, 1)
    moved = pltpu.roll(cells, (-offset) % width, 1)
    keep = lane < width - offset if offset > 0 else lane >= -offset
    return jnp.where(keep, moved, 0.0)


def column(row):
    length = row.shape[1]
    shape = (length, length)
    same = lax.broadcasted_iota(jnp.int32, shape, 0) == lax.broadcasted_iota(jnp.int32, shape, 1)
    return jnp.sum(jnp.where(same, row, 0.0), axis=1, keepdims=True)


def advance(layers, padded, index, speed, start=0):
    middle = layers[2]
    rows = middle.shape[0]
    speed_x, speed_y, speed_z = speed
    ahead = speed_x >= 0.0
    near = jnp.where(ahead, layers[1], layers[3])
    far = jnp.where(ahead, layers[0], layers[4])
    rate = jnp.abs(speed_x) * (1.5 * middle - 2.0 * near + 0.5 * far)
    ahead = speed_y >= 0.0
    near = jnp.where(ahead, padded[index, pl.ds(7 + start, rows), :], padded[index, pl.ds(9 + start, rows), :])
    far = jnp.where(ahead, padded[index, pl.ds(6 + start, rows), :], padded[index, pl.ds(10 + start, rows), :])
    rate = rate + jnp.abs(speed_y) * (1.5 * middle - 2.0 * near + 0.5 * far)
    ahead = speed_z >= 0.0
    near = jnp.where(ahead, lane_shift(middle, -1), lane_shift(middle, 1))
    far = jnp.where(ahead, lane_shift(middle, -2), lane_shift(middle, 2))
    rate = rate + jnp.abs(speed_z) * (1.5 * middle - 2.0 * near + 0.5 * far)
    return middle - TIME_INCREMENT * rate


def pad_rows(padded, index, before, middle, after):
    rows = middle.shape[0]
    padded[index, pl.ds(8, rows), :] = middle
    padded[index, pl.ds(6, 2), :] = before
    padded[index, pl.ds(8 + rows, 2), :] = after


def march_layer(refs, padded, index, parts, start, count):
    flow, low_x, high_x, thermal, flag = refs
    _, layers, rows, depth = flow.shape
    span = pl.ds(start, count)
    speed = [flow[part, index, span, :] for part in range(3)]
    drag = 1.0 / (1.0 + TIME_INCREMENT * DRAG_RATE * flag[index, span, :].astype(F32))
    top = lax.broadcasted_iota(jnp.int32, (count, depth), 1) == depth - 1
    pull = -MARANGONI * 0.5 * TIME_INCREMENT
    out = []
    for part in parts:
        around = []
        for other in range(index - 2, index + 3):
            if other < 0:
                first = (2 * part + other + 2) * rows + start
                around.append(low_x[pl.ds(first, count), :])
            elif other >= layers:
                first = (2 * part + other - layers) * rows + start
                around.append(high_x[pl.ds(first, count), :])
            else:
                around.append(flow[part, other, span, :])
        moved = advance(around, padded, part, speed, start)
        if part == 0:
            edge = lambda halo: column(halo[pl.ds(halo.shape[0] - 8, 1), pl.ds(0, rows)])
            behind = thermal[index - 1] if index > 0 else edge(low_x)
            before = thermal[index + 1] if index + 1 < layers else edge(high_x)
            moved = moved + jnp.where(top, pull * (before - behind), 0.0)
        if part == 1:
            slope = padded[3, pl.ds(9 + start, count), :] - padded[3, pl.ds(7 + start, count), :]
            moved = moved + jnp.where(top, pull * slope, 0.0)
        out.append(moved * drag)
    return out


def pad_layer(refs, low_y, high_y, padded, index):
    flow, _, _, thermal, _ = refs
    for part in range(3):
        pad_rows(
            padded, part, low_y[part, index, 6:], flow[part, index], high_y[part, index, :2]
        )
    pad_rows(padded, 3, low_y[3, index, 6:], thermal[index], high_y[3, index, :2])


def row_kernel(flow, low_x, high_x, thermal, flag, low_y, high_y, _, side_y, padded):
    refs = (flow, low_x, high_x, thermal, flag)
    _, layers, rows, depth = flow.shape
    for index in range(layers):
        for part, cells in ((1, flow.at[1, index]), (3, thermal.at[index])):
            padded[part, pl.ds(rows - 8, 16), :] = cells[pl.ds(rows - 16, 16), :]
            padded[part, pl.ds(8 + rows, 2), :] = high_y[part, index, :2]
        (value,) = march_layer(refs, padded, index, [1], rows - 8, 8)
        side_y[pl.ds(index, 1), :] = value[7:, :]


def march_kernel(
    flow, low_x, high_x, thermal, flag, low_y, high_y, extra, _,
    star, side_x, padded,
):
    refs = (flow, low_x, high_x, thermal, flag)
    _, layers, rows, depth = flow.shape
    for index in range(layers):
        pad_layer(refs, low_y, high_y, padded, index)
        value = march_layer(refs, padded, index, range(3), 0, rows)
        for part in range(3):
            star[part, index] = value[part]
    plane = lambda index: low_x[pl.ds(index * rows, rows), pl.ds(0, depth)]
    beside = extra[pl.ds(2 * rows, 8), pl.ds(0, depth)]
    pad_rows(padded, 0, beside[2:4], plane(1), beside[4:6])
    around = [extra[pl.ds(0, rows), pl.ds(0, depth)], plane(0), plane(1), flow[0, 0], flow[0, 1]]
    moved = advance(around, padded, 0, [plane(1), plane(3), plane(5)])
    top = lax.broadcasted_iota(jnp.int32, (rows, depth), 1) == depth - 1
    pull = -MARANGONI * 0.5 * TIME_INCREMENT
    behind = column(extra[pl.ds(2 * rows, 1), pl.ds(0, rows)])
    moved = moved + jnp.where(top, pull * (thermal[0] - behind), 0.0)
    drag = 1.0 + TIME_INCREMENT * DRAG_RATE * extra[pl.ds(rows, rows), pl.ds(0, depth)]
    side_x[...] = moved / drag


def transform_kernel(
    group, length, star, side_x, table_y, table_z, ratio, _, source, message, rows_
):
    _, layers, rows, depth = star.shape
    first = position(group) * layers
    rows_[pl.ds(0, 8), :] = jnp.zeros((8, depth), F32)
    for index in range(layers):
        rows_[pl.ds(8, rows), :] = star[1, index]
        behind = star[0, index - 1] if index > 0 else side_x[...]
        sink = star[0, index] - behind
        sink = sink + (star[1, index] - rows_[pl.ds(7, rows), :])
        sink = sink + (star[2, index] - lane_shift(star[2, index], -1))
        source[index] = dot(dot(table_y[...], -sink), table_z[...])
    forward = source[0]
    for index in range(1, layers):
        forward = source[index] + ratio[first + index] * forward
    message[pl.ds(0, rows), :] = forward
    backward = source[layers - 1]
    for index in range(layers - 2, -1, -1):
        backward = source[index] + ratio[length - 1 - first - index] * backward
    message[pl.ds(rows, rows), :] = backward


def started(copies):
    for copy in copies:
        copy.start()
    return copies


def surface(plane):
    rows, depth = plane.shape
    shape = (rows, rows)
    same = lax.broadcasted_iota(jnp.int32, shape, 0) == lax.broadcasted_iota(jnp.int32, shape, 1)
    return jnp.sum(jnp.where(same, plane[:, depth - 1 :], 0.0), axis=0, keepdims=True)


def halo_kernel(flow, thermal, ahead, behind, last_rows, first_rows, tops, sems):
    parts, layers, rows, depth = flow.shape
    pairs = [(thermal.at[layers - 1], tops.at[0]), (thermal.at[0], tops.at[1])]
    for part in range(parts):
        for layer in range(2):
            span = pl.ds((2 * part + layer) * rows, rows)
            pairs.append((flow.at[part, layers - 2 + layer], ahead.at[span, :]))
            pairs.append((flow.at[part, layer], behind.at[span, :]))
    for target, start in ((last_rows, rows - 8), (first_rows, 0)):
        span = pl.ds(start, 8)
        pairs.append((flow.at[:, :, span, :], target.at[pl.ds(0, parts)]))
        pairs.append((thermal.at[:, span, :], target.at[parts]))
    copies = started(
        [pltpu.make_async_copy(*pair, sems.at[index]) for index, pair in enumerate(pairs)]
    )
    for side, message in enumerate((ahead, behind)):
        copies[side].wait()
        row = jnp.broadcast_to(surface(tops[side]), (8, rows))
        message[pl.ds(2 * parts * rows, 8), pl.ds(0, rows)] = row
    for copy in copies[2:]:
        copy.wait()


def extra_kernel(flow, thermal, flag, low_y, high_y, extra, last, flags, sems):
    _, layers, rows, depth = flow.shape
    pairs = [(flag.at[layers - 1], flags), (thermal.at[pl.ds(layers - 2, 2)], last)]
    pairs.append((flow.at[0, layers - 3], extra.at[pl.ds(0, rows), :]))
    copies = started(
        [pltpu.make_async_copy(*pair, sems.at[index]) for index, pair in enumerate(pairs)]
    )
    base = 2 * rows
    extra[pl.ds(base, 8), :] = jnp.zeros((8, extra.shape[1]), F32)
    extra[pl.ds(base + 2, 2), pl.ds(0, depth)] = low_y[0, layers - 1, 6:, :]
    extra[pl.ds(base + 4, 2), pl.ds(0, depth)] = high_y[0, layers - 1, :2, :]
    for copy in copies[:2]:
        copy.wait()
    extra[pl.ds(rows, rows), :] = flags[...].astype(F32)
    extra[pl.ds(base, 1), pl.ds(0, rows)] = surface(last[0])
    for copy in copies[2:]:
        copy.wait()


def wrapped(distance, span):
    moved = distance + span // 2
    moved = jnp.where(moved < 0, moved + span, moved)
    moved = jnp.where(moved >= span, moved - span, moved)
    return (moved - span // 2).astype(F32)


def laser_row(index, layers, rows, spots_a, spots_b):
    total_x = layers * lax.axis_size("gx")
    total_y = rows * lax.axis_size("gy")
    cell_x = lax.axis_index("gx") * layers + index
    cells_y = lax.broadcasted_iota(jnp.int32, (1, rows), 1) + lax.axis_index("gy") * rows
    heat = jnp.zeros((1, rows), F32)
    for spot in range(spots_a.shape[0]):
        dist_x = wrapped(jnp.full((1, rows), cell_x - spots_a[spot], jnp.int32), total_x)
        dist_y = wrapped(cells_y - spots_b[spot], total_y)
        square = dist_x * dist_x + dist_y * dist_y
        heat = heat + jnp.exp(square * (-1.0 / (SPOT_RADIUS * SPOT_RADIUS)))
    return LASER_POWER * heat


def heat_kernel(
    spots_a, spots_b, thermal, low_x, high_x, low_y, high_y, flow,
    warmed, token, padded,
):
    layers, rows, depth = thermal.shape
    token[...] = jnp.zeros(token.shape, F32)
    top = lax.broadcasted_iota(jnp.int32, (rows, depth), 1) == depth - 1
    for index in range(layers):
        pad_rows(padded, 0, low_y[3, index, 6:], thermal[index], high_y[3, index, :2])
        around = []
        for other in range(index - 2, index + 3):
            if other < 0:
                around.append(low_x[other + 2])
            elif other >= layers:
                around.append(high_x[other - layers])
            else:
                around.append(thermal[other])
        speed = [flow[part, index] for part in range(3)]
        gain = TIME_INCREMENT * column(laser_row(index, layers, rows, spots_a, spots_b))
        warmed[index] = advance(around, padded, 0, speed) + jnp.where(top, gain, 0.0)


def tables_kernel(group, layers, diagonal, ratio, weight):
    length = group * layers
    mine = position(group)
    first = mine * layers
    diag = diagonal[...]
    ratio[0] = jnp.zeros_like(diag)

    def step(index, previous):
        current = 1.0 / (diag - previous)
        ratio[index] = current
        return current

    loop(1, length + 1, step, jnp.zeros_like(diag))

    def decay(low, high):
        return lax.fori_loop(
            low + 1, high + 1, lambda index, value: value * ratio[index], jnp.ones_like(diag)
        )

    def green(index):
        return 1.0 / (diag - ratio[index] - ratio[jnp.maximum(length - 1 - index, 0)])

    rounds = group.bit_length() - 1
    for turn in range(rounds):
        half = 1 << turn
        right = ((mine >> turn) & 1) == 1
        start = (mine >> (turn + 1)) << (turn + 1)
        cut = (start + half) * layers
        end = (start + 2 * half) * layers
        weight[4 * turn] = decay(cut - 1, end - 1)
        weight[4 * turn + 1] = decay(length - 1 - cut, length - 1 - start * layers)
        low = jnp.where(right, cut - 1, length - 1 - cut)
        high = jnp.where(right, first - 1, length - 1 - first - layers)
        weight[4 * turn + 2] = decay(low, high)
        weight[4 * turn + 3] = green(cut) * ratio[cut]
    inner = jnp.where(mine == group - 1, 0.0, 1.0)
    weight[4 * rounds] = inner * green(first + layers)


def face_rows(plane, edge):
    return (
        jnp.sum(plane * edge[0], axis=0, keepdims=True),
        jnp.sum(plane * edge[1], axis=0, keepdims=True),
    )


def faces_kernel(
    group, length, source, before_y, table_z, ratio, weight, edge, thermal, _, faces, late, sweep
):
    layers, rows, depth = source.shape
    late[...] = thermal[:2]
    first = position(group) * layers
    zero = jnp.zeros((rows, depth), F32)
    extra = dot(before_y[...], table_z[...])
    faces[...] = jnp.zeros(faces.shape, F32)
    for index in range(layers):
        faces[pl.ds(2 * length + first + index, 1), :] = extra[index : index + 1]
    forward = zero
    for index in range(layers):
        forward = source[index] + ratio[first + index] * forward
        sweep[index] = forward
    value = weight[weight.shape[0] - 1] * (ratio[first + layers] * forward)
    energy = zero
    for index in range(layers - 1, -1, -1):
        value = ratio[first + index + 1] * (sweep[index] + value)
        energy = energy + source[index] * value
    faces[pl.ds(3 * length, 8), :] = jnp.broadcast_to(total(energy), (8, depth))

    def down(index, previous):
        inside = (index >= first) & (index < first + layers)
        own = jnp.where(inside, source[jnp.clip(index - first, 0, layers - 1)], 0.0)
        current = own + edge[0] * faces[pl.ds(2 * length + index, 1), :] + ratio[index] * previous
        sweep[index] = current
        return current

    loop(0, length, down, zero)

    def up(back, following):
        index = length - 1 - back
        value = ratio[index + 1] * (sweep[index] + following)
        low, high = face_rows(value, edge)
        faces[pl.ds(index, 1), :] = low
        faces[pl.ds(length + index, 1), :] = high
        return value

    loop(0, length, up, zero)


def joined(turn, group, message, other, sums, weight):
    rows, depth = weight.shape[1:]
    right = ((position(group) >> turn) & 1) == 1
    upper, lower = pl.ds(0, rows), pl.ds(rows, rows)
    left_s = jnp.where(right, other[upper, :], message[upper, :])
    right_s = jnp.where(right, message[upper, :], other[upper, :])
    left_t = jnp.where(right, other[lower, :], message[lower, :])
    right_t = jnp.where(right, message[lower, :], other[lower, :])
    own = weight[4 * turn + 2]
    before = sums[0] + jnp.where(right, left_s * own, 0.0)
    after = sums[1] + jnp.where(right, 0.0, right_t * own)
    forward = right_s + left_s * weight[4 * turn]
    backward = left_t + right_t * weight[4 * turn + 1]
    energy = 2.0 * total(left_s * right_t * weight[4 * turn + 3])
    return forward, backward, before, after, energy


def merge_kernel(
    turn, group, length, message, other, faces, other_faces, sums, weight,
    new_message, new_sums, head, tail,
):
    rows, depth = weight.shape[1:]
    forward, backward, before, after, energy = joined(turn, group, message, other, sums, weight)
    new_sums[0] = before
    new_sums[1] = after
    new_message[pl.ds(0, rows), :] = forward
    new_message[pl.ds(rows, rows), :] = backward
    low, high = pl.ds(0, length), pl.ds(length, length)
    late, number = pl.ds(2 * length, length), pl.ds(3 * length, 8)
    head[...] = faces[low, :] + other_faces[low, :]
    tail[...] = faces[high, :] + other_faces[high, :]
    new_message[pl.ds(2 * rows, length), :] = head[...]
    new_message[pl.ds(2 * rows + length, length), :] = faces[late, :] + other_faces[late, :]
    energy = faces[number, :] + other_faces[number, :] + energy
    new_message[pl.ds(2 * rows + 2 * length, 8), :] = energy


def late_solve(length, message, other, ratio, edge, late, sweep):
    rows, depth = edge.shape[1:]
    own = pl.ds(2 * rows + length, length)
    late[pl.ds(0, length), :] = message[own, :] + other[own, :]

    def down(index, previous):
        current = edge[0] * late[pl.ds(index, 1), :] + ratio[index] * previous
        sweep[index] = current
        return current

    zero = jnp.zeros((rows, depth), F32)
    loop(0, length, down, zero)

    def up(back, following):
        index = length - 1 - back
        value = ratio[index + 1] * (sweep[index] + following)
        sweep[index] = value
        late[pl.ds(length + index, 1), :] = jnp.sum(value * edge[0], axis=0, keepdims=True)
        return value

    loop(0, length, up, zero)
    sweep[length] = zero


def close_kernel(
    turn, group, length, message, other, sums, weight, ratio, edge, ends, late, sweep
):
    forward, backward, _, _, _ = joined(turn, group, message, other, sums, weight)
    late_solve(length, message, other, ratio, edge, late, sweep)
    ends[0] = ratio[length] * forward + sweep[length - 1]
    ends[1] = ratio[length] * backward + sweep[0]


def coarse_kernel(
    turn, group, length, alone, source, message, other, sums, faces_in, weight, ratio, edge, *refs
):
    precond, image, report, faces, late, sweep, ends = refs[-7:]
    layers, rows, depth = source.shape
    first = position(group) * layers
    below, below_far, above, above_far = faces_in
    forward, backward, before, after, energy = joined(turn, group, message, other, sums, weight)
    late_solve(length, message, other, ratio, edge, late, sweep)
    ends[0] = ratio[length] * forward + sweep[length - 1]
    ends[1] = ratio[length] * backward + sweep[0]
    beyond = ends if alone else refs[0]
    own = pl.ds(2 * rows, length)
    faces[pl.ds(0, length), :] = message[own, :] + other[own, :]
    faces[pl.ds(length, length), :] = below[...] + below_far[...]
    faces[pl.ds(2 * length, length), :] = above[...] + above_far[...]
    number = pl.ds(2 * rows + 2 * length, 8)
    energy = message[number, :] + other[number, :] + energy
    late_rows = late[pl.ds(0, length), :]
    energy = energy + total(
        late_rows * (2.0 * faces[pl.ds(0, length), :] - late[pl.ds(length, length), :])
    )
    forward = before
    for index in range(layers):
        forward = source[index] + ratio[first + index] * forward
        precond[index] = forward
    value = weight[weight.shape[0] - 1] * (after + ratio[first + layers] * forward)
    is_last = first + layers == length
    precond[layers] = jnp.where(is_last, beyond[1], value + sweep[first + layers])
    for index in range(layers - 1, -1, -1):
        value = ratio[first + index + 1] * (precond[index] + value)
        precond[index] = value + sweep[first + index]
    lead, trail = edge[0], edge[1]

    def pull(index):
        below = faces[pl.ds(length + index, 1), :]
        above = faces[pl.ds(2 * length + index, 1), :]
        return below, above

    def down(index, previous):
        below, above = pull(index)
        current = lead * below + trail * above + ratio[index] * previous
        if isinstance(index, int):
            if index == 0:
                current = current + beyond[0]
            if index == length - 1:
                current = current + beyond[1]
        else:
            current = current + jnp.where(index == 0, beyond[0], 0.0)
            current = current + jnp.where(index == length - 1, beyond[1], 0.0)
        sweep[index] = current
        return current

    zero = jnp.zeros((rows, depth), F32)
    loop(0, length, down, zero)
    line = jnp.zeros((1, depth), F32)

    def up(back, carry):
        following, linked, squared = carry
        index = length - 1 - back
        value = ratio[index + 1] * (sweep[index] + following)
        sweep[index] = value
        low, high = face_rows(value, edge)
        report[pl.ds(index, 1), :] = low
        report[pl.ds(length + index, 1), :] = high
        below, above = pull(index)
        linked = linked + faces[pl.ds(index, 1), :] * below
        squared = squared + low * below + high * above
        return value, linked, squared

    _, linked, squared = loop(0, length, up, (zero, line, line))
    sweep[length] = sweep[0]
    for index in range(layers + 1):
        image[index] = sweep[first + index]
    head, tail = sweep[0], sweep[length - 1]
    linked = 2.0 * total(linked) + total(ends[1] * beyond[0] + ends[0] * beyond[1])
    squared = total(squared) + total(head * beyond[0] + tail * beyond[1])
    crossing = 2.0 * total(head * tail)
    where = 2 * length
    report[pl.ds(where, 1), :] = energy[0:1]
    report[pl.ds(where + 1, 1), :] = jnp.broadcast_to(linked, (1, depth))
    report[pl.ds(where + 2, 1), :] = jnp.broadcast_to(squared, (1, depth))
    report[pl.ds(where + 3, 1), :] = jnp.broadcast_to(crossing, (1, depth))
    report[pl.ds(where + 4, 4), :] = jnp.zeros((4, depth), F32)


def physical_kernel(precond, image, table_y, table_z, precond_out, image_out):
    for index in range(precond.shape[0]):
        precond_out[index] = dot(dot(table_y[...], precond[index]), table_z[...])
        image_out[index] = dot(dot(table_y[...], image[index]), table_z[...])


def project_kernel(
    group, length, paired, star, precond, image, faces, table_z, *refs
):
    reports, (flow, pressure, field, rows_) = refs[:-4], refs[-4:]
    _, layers, rows, depth = star.shape
    first = position(group) * layers
    where = 2 * length
    sums = reports[0][pl.ds(where, 8), :]
    for other in reports[1:]:
        sums = sums + other[pl.ds(where, 8), :]
    pairs = jnp.zeros((1, depth), F32)
    for index in range(len(reports)):
        upper, lower = reports[index], reports[(index + 1) % len(reports)]
        pairs = pairs + jnp.sum(
            upper[pl.ds(0, length), :] * lower[pl.ds(length, length), :], axis=0, keepdims=True
        )
    energy, linked, squared, crossing = (sums[k : k + 1, 0:1] for k in range(4))
    if not paired:
        crossing = crossing + 2.0 * total(pairs)
    first_image = energy - linked
    step = energy / first_image
    beta = (energy * squared - linked * linked) / (first_image * first_image)
    rest = -linked / first_image
    second_image = (
        rest * rest * first_image
        + 2.0 * rest * step * (linked - squared)
        + step * step * (squared - crossing)
        - beta * beta * first_image
    )
    second_step = beta * energy / second_image
    alpha = step + second_step * (rest + beta)
    gamma = second_step * step
    for index in range(layers + 1):
        field[index] = alpha * precond[index] + gamma * image[index]
    own = pl.ds(2 * length + first, layers)
    following = alpha * faces[own, :] + gamma * reports[-1][pl.ds(first, layers), :]
    following = dot(following, table_z[...])
    for index in range(layers):
        value = field[index]
        pressure[index] = value
        rows_[pl.ds(0, rows), :] = value
        rows_[pl.ds(rows, 1), :] = following[index : index + 1]
        flow[0, index] = star[0, index] - (field[index + 1] - value)
        flow[1, index] = star[1, index] - (rows_[pl.ds(1, rows), :] - value)
        flow[2, index] = star[2, index] - (lane_shift(value, 1) - value)


def along(array, axis, by):
    length = lax.axis_size(axis)
    return lax.ppermute(array, axis, [(i, (i + by) % length) for i in range(length)])


def swapped(array, bit, by=0):
    count_x, count_y = lax.axis_size("gx"), lax.axis_size("gy")
    pairs = [
        (x * count_y + y, (x ^ bit) * count_y + (y + by) % count_y)
        for x in range(count_x)
        for y in range(count_y)
    ]
    return lax.ppermute(array, ("gx", "gy"), pairs)


def pack(body, inputs, received, shapes, scratch, count):
    inputs = [pltpu.with_memory_space_constraint(each, pltpu.HBM) for each in inputs]
    return pl.pallas_call(
        body,
        out_shape=[jax.ShapeDtypeStruct(shape, F32) for shape in shapes],
        in_specs=[pl.BlockSpec(memory_space=pltpu.HBM)] * len(inputs) + [VMEM] * len(received),
        out_specs=[VMEM] * len(shapes),
        scratch_shapes=[scratch, pltpu.SemaphoreType.DMA((count,))],
        compiler_params=pltpu.CompilerParams(vmem_limit_bytes=4 << 20),
    )(*inputs, *received)


def per_device(melt_flow, thermal_state, powder_flag, spot_lateral_a_cell, spot_lateral_b_cell):
    layers, rows, depth = thermal_state.shape
    count_x, count_y = lax.axis_size("gx"), lax.axis_size("gy")
    group = min(count_x, BLOCK // layers)
    blocks = count_x // group
    length = group * layers
    rounds = group.bit_length() - 1
    sine_y, values_y = sines(rows)
    sine_z, values_z = sines(depth)
    table_y = jnp.asarray(sine_y, F32)
    table_z = jnp.asarray(sine_z, F32)
    edge = jnp.asarray(
        np.broadcast_to(sine_y[[0, rows - 1]][:, :, None], (2, rows, depth)), F32
    )
    diagonal = jnp.asarray(2.0 + values_y[:, None] + values_z[None, :], F32)
    plane = (rows, depth)
    line = (length, depth)

    parts = melt_flow.shape[0]
    width = max(rows, depth)
    outer_planes = (2 * parts * rows + 8, width)
    ahead, behind, last_rows, first_rows = pack(
        halo_kernel,
        [melt_flow, thermal_state],
        [],
        [outer_planes, outer_planes] + [(parts + 1, layers, 8, depth)] * 2,
        pltpu.VMEM((2,) + plane, F32),
        6 + 4 * parts,
    )
    low_x = along(ahead, "gx", 1)
    high_x = along(behind, "gx", -1)
    low_y = along(last_rows, "gy", 1)
    high_y = along(first_rows, "gy", -1)
    extra, last = pack(
        extra_kernel,
        [melt_flow, thermal_state, powder_flag],
        [low_y, high_y],
        [(2 * rows + 8, width), (2,) + plane],
        pltpu.VMEM(plane, jnp.int32),
        3,
    )
    extra = along(extra, "gx", 1)
    ratio, weight = call(
        functools.partial(tables_kernel, group, layers),
        [diagonal],
        [(length + 1,) + plane, (4 * rounds + 1,) + plane],
    )
    early_low = along(last, "gx", 1)
    marched = [melt_flow, low_x, high_x, thermal_state, powder_flag, low_y, high_y]
    padded = pltpu.VMEM((4, rows + 16, depth), F32)
    (side_y,) = call(row_kernel, marched + [weight], [(layers, depth)], [padded], loose=1)
    before_y = along(side_y, "gy", 1)
    star, side_x = call(
        march_kernel,
        marched + [extra, side_y],
        [(3, layers) + plane, plane],
        [padded],
        loose=1,
        flops=3 << 29,
    )
    source, message = call(
        functools.partial(transform_kernel, group, length),
        [star, side_x, table_y, table_z, ratio, before_y],
        [(layers,) + plane, (2 * rows, depth)],
        [pltpu.VMEM((rows + 16, depth), F32)],
        loose=1,
        flops=1 << 30,
    )
    faces, late = call(
        functools.partial(faces_kernel, group, length),
        [source, before_y, table_z, ratio, weight, edge, thermal_state, early_low],
        [(3 * length + 8, depth), (2,) + plane],
        [pltpu.VMEM((max(length, layers + 1),) + plane, F32)],
        loose=1,
    )
    early_high = along(late, "gx", -1)
    alone = blocks == 1
    warmed, token = call(
        heat_kernel,
        [
            spot_lateral_a_cell, spot_lateral_b_cell, thermal_state, early_low, early_high,
            low_y, high_y, melt_flow,
        ],
        [(layers,) + plane, (8, depth)],
        [pltpu.VMEM((1, rows + 16, depth), F32)],
        scalars=2,
        flops=1 << 28,
    )
    sums = jnp.zeros((2,) + plane, F32)
    for turn in range(rounds - 1):
        message, sums, head, tail = call(
            functools.partial(merge_kernel, turn, group, length),
            [
                message, swapped(message, 1 << turn), faces, swapped(faces, 1 << turn),
                sums, weight,
            ],
            [(2 * rows + 2 * length + 8, depth), (2,) + plane, line, line],
        )
        if turn + 2 < rounds:
            rest = message[2 * rows + length :]
            message, faces = message[: 2 * rows], jnp.concatenate([head, tail, rest], 0)
    bit = group >> 1
    other = swapped(message, bit)
    rim = [
        swapped(tail, 0, 1), swapped(tail, bit, 1), swapped(head, 0, -1), swapped(head, bit, -1)
    ]
    outer = []
    scratch = [pltpu.VMEM((2 * length, depth), F32), pltpu.VMEM((length + 1,) + plane, F32)]
    if not alone:
        (ends,) = call(
            functools.partial(close_kernel, rounds - 1, group, length),
            [message, other, sums, weight, ratio, edge],
            [(2,) + plane],
            scratch,
        )
        outer = [jnp.stack([along(ends[0], "gx", group), along(ends[1], "gx", -group)])]
    operands = [source, message, other, sums] + rim
    operands += [weight, ratio, edge] + outer + [token]

    def coarse(*refs):
        coarse_kernel(rounds - 1, group, length, alone, *refs[:4], refs[4:8], *refs[8:])

    precond, image, report, faces = call(
        coarse,
        operands,
        [
            (layers + 1,) + plane, (layers + 1,) + plane, (2 * length + 8, depth),
            (3 * length, depth),
        ],
        scratch + [pltpu.VMEM((2,) + plane, F32)],
        loose=1,
    )
    if blocks > 1:
        onward = along(image[0], "gx", -1)
        at_end = position(group) == group - 1
        image = image.at[layers].set(jnp.where(at_end, onward, image[layers]))
        upper = along(report[:length], "gy", -1)
        crossing = jnp.sum(onward * image[layers - 1])
        crossing = crossing + jnp.sum(upper * report[length : 2 * length])
        numbers = report[2 * length :].at[3].set(2.0 * crossing)
        numbers = lax.psum(jnp.where(at_end, numbers, 0.0), "gx")
        report = report.at[2 * length :].set(numbers)
    reports = [report] + [along(report, "gy", by) for by in range(1, count_y)]
    precond, image = call(
        physical_kernel,
        [precond, image, table_y, table_z],
        [(layers + 1,) + plane, (layers + 1,) + plane],
    )
    flow, pressure = call(
        functools.partial(project_kernel, group, length, blocks > 1),
        [star, precond, image, faces, table_z] + reports,
        [(3, layers) + plane, (layers,) + plane],
        [pltpu.VMEM((layers + 1,) + plane, F32), pltpu.VMEM((rows + 16, depth), F32)],
    )
    return (flow, warmed, pressure)


def solution(mesh):
    placed = (
        P(None, ("runs", "gx"), "gy", None),
        P(("runs", "gx"), "gy", None),
        P(("runs", "gx"), "gy", None),
        P("runs"),
        P("runs"),
    )
    return jax.shard_map(
        per_device,
        mesh=mesh,
        in_specs=placed,
        out_specs=(
            P(None, ("runs", "gx"), "gy", None),
            P(("runs", "gx"), "gy", None),
            P(("runs", "gx"), "gy", None),
        ),
        check_vma=False,
    )
```

```python
import functools
import math

import jax
import jax.numpy as jnp
import numpy as np
from jax import lax
from jax.experimental import pallas as pl
from jax.experimental.pallas import tpu as pltpu
from jax.sharding import PartitionSpec as P

BLOCK = 128

TIME_INCREMENT = 0.2
MARANGONI = 1.5
DRAG_RATE = 4.0
LASER_POWER = 3.0
SPOT_RADIUS = 5.0

F32 = jnp.float32
VMEM = pl.BlockSpec(memory_space=pltpu.VMEM)
SMEM = pl.BlockSpec(memory_space=pltpu.SMEM)


def call(body, operands, shapes, scratch=(), scalars=0, loose=0, semaphores=0, flops=1 << 20):
    out_shape = [jax.ShapeDtypeStruct(shape, F32) for shape in shapes]
    moved = 4 * sum(math.prod(shape) for shape in shapes)
    held = moved + 4 * sum(operand.size for operand in operands)
    held += 4 * sum(math.prod(space.shape) for space in scratch)
    where = pl.BlockSpec(memory_space=pl.ANY) if semaphores else VMEM
    waits = [pltpu.SemaphoreType.DMA((semaphores,))] if semaphores else []
    return pl.pallas_call(
        body,
        out_shape=out_shape,
        in_specs=[SMEM] * scalars
        + [VMEM] * (len(operands) - scalars - loose)
        + [pl.BlockSpec(memory_space=pl.ANY)] * loose,
        out_specs=[where] * len(shapes),
        scratch_shapes=list(scratch) + waits,
        compiler_params=pltpu.CompilerParams(vmem_limit_bytes=held + (4 << 20)),
        cost_estimate=pl.CostEstimate(flops=flops, bytes_accessed=2 * moved, transcendentals=0),
    )(*operands)


def dot(left, right):
    return jnp.dot(left, right, precision=lax.Precision.HIGHEST, preferred_element_type=F32)


def split(cells):
    high = cells.astype(jnp.bfloat16)
    return high, (cells - high.astype(F32)).astype(jnp.bfloat16)


def folded(product):
    half = product.shape[1] // 2
    return product[:, :half] + product[:, half:]


def packed_tables(left, right):
    left_high, left_low = split(np.asarray(left, np.float32))
    right_high, right_low = split(np.asarray(right, np.float32))
    zero = np.zeros_like(right_low)
    return (
        jnp.asarray(np.concatenate([left_high, left_low], 1)),
        jnp.asarray(np.block([[right_high, right_low], [right_high, zero]])),
    )


def transformed(planes, left, right):
    rows = planes[0].shape[0]
    high, low = split(jnp.concatenate(planes, 0))
    cells = jnp.concatenate([high, low], 1)
    cells = folded(jnp.dot(cells, right[...], preferred_element_type=F32))
    out = []
    for index in range(len(planes)):
        high, low = split(cells[index * rows : (index + 1) * rows])
        upper = jnp.concatenate([high, low], 1)
        lower = jnp.concatenate([high, jnp.zeros_like(low)], 1)
        cells_ = jnp.concatenate([upper, lower], 0)
        out.append(folded(jnp.dot(left[...], cells_, preferred_element_type=F32)))
    return out


def total(cells):
    return jnp.sum(jnp.sum(cells, axis=0, keepdims=True), axis=1, keepdims=True)


def loop(low, high, body, start):
    if isinstance(high, int) and isinstance(low, int) and high - low <= 24:
        carry = start
        for index in range(low, high):
            carry = body(index, carry)
        return carry
    return lax.fori_loop(low, high, body, start)


def position(group):
    return lax.rem(lax.axis_index("gx"), group)


def sines(length):
    positions = np.arange(length) + 1.0
    step = math.pi / (length + 1)
    table = np.sqrt(2.0 / (length + 1)) * np.sin(step * positions[:, None] * positions[None, :])
    return table, 2.0 - 2.0 * np.cos(step * positions)


def lane_shift(cells, offset):
    width = cells.shape[1]
    lane = lax.broadcasted_iota(jnp.int32, cells.shape, 1)
    moved = pltpu.roll(cells, (-offset) % width, 1)
    keep = lane < width - offset if offset > 0 else lane >= -offset
    return jnp.where(keep, moved, 0.0)


def column(row):
    length = row.shape[1]
    shape = (length, length)
    same = lax.broadcasted_iota(jnp.int32, shape, 0) == lax.broadcasted_iota(jnp.int32, shape, 1)
    return jnp.sum(jnp.where(same, row, 0.0), axis=1, keepdims=True)


def coefficients(speed, scale):
    factors = [0.5 * TIME_INCREMENT * jnp.abs(each) for each in speed]
    if scale is not None:
        factors = [each * scale for each in factors]
    centre = (1.0 if scale is None else scale) - 3.0 * (factors[0] + factors[1] + factors[2])
    near, far = 4.0 * factors[2], -factors[2]
    ahead = speed[2] >= 0.0
    lane = lax.broadcasted_iota(jnp.int32, near.shape, 1)
    width = near.shape[1]
    depth = (
        jnp.where(ahead & (lane >= 1), near, 0.0),
        jnp.where(ahead & (lane >= 2), far, 0.0),
        jnp.where(ahead | (lane >= width - 1), 0.0, near),
        jnp.where(ahead | (lane >= width - 2), 0.0, far),
    )
    return centre, speed[0] >= 0.0, factors[0], speed[1] >= 0.0, factors[1], depth


def advance(layers, padded, index, weights, start=0):
    middle = layers[2]
    rows, width = middle.shape
    centre, ahead_x, factor_x, ahead_y, factor_y, depth = weights
    near = jnp.where(ahead_x, layers[1], layers[3])
    far = jnp.where(ahead_x, layers[0], layers[4])
    moved = centre * middle + factor_x * (4.0 * near - far)
    beside = lambda offset: padded[index, pl.ds(8 + offset + start, rows), :]
    near = jnp.where(ahead_y, beside(-1), beside(1))
    far = jnp.where(ahead_y, beside(-2), beside(2))
    moved = moved + factor_y * (4.0 * near - far)
    for factor, offset in zip(depth, (1, 2, width - 1, width - 2)):
        moved = moved + factor * pltpu.roll(middle, offset, 1)
    return moved


def pad_rows(padded, index, before, middle, after):
    rows = middle.shape[0]
    padded[index, pl.ds(8, rows), :] = middle
    padded[index, pl.ds(6, 2), :] = before
    padded[index, pl.ds(8 + rows, 2), :] = after


def march_layer(refs, padded, index, parts, start, count):
    flow, low_x, high_x, thermal, flag = refs
    _, layers, rows, depth = flow.shape
    span = pl.ds(start, count)
    speed = [flow[part, index, span, :] for part in range(3)]
    drag = 1.0 / (1.0 + TIME_INCREMENT * DRAG_RATE * flag[index, span, :].astype(F32))
    top = lax.broadcasted_iota(jnp.int32, (count, depth), 1) == depth - 1
    pull = jnp.where(top, (-MARANGONI * 0.5 * TIME_INCREMENT) * drag, 0.0)
    weights = coefficients(speed, drag)
    out = []
    for part in parts:
        around = []
        for other in range(index - 2, index + 3):
            if other < 0:
                first = (2 * part + other + 2) * rows + start
                around.append(low_x[pl.ds(first, count), :])
            elif other >= layers:
                first = (2 * part + other - layers) * rows + start
                around.append(high_x[pl.ds(first, count), :])
            else:
                around.append(flow[part, other, span, :])
        moved = advance(around, padded, part, weights, start)
        if part == 0:
            edge = lambda halo: column(halo[pl.ds(halo.shape[0] - 8, 1), pl.ds(0, rows)])
            behind = thermal[index - 1] if index > 0 else edge(low_x)
            before = thermal[index + 1] if index + 1 < layers else edge(high_x)
            moved = moved + pull * (before - behind)
        if part == 1:
            slope = padded[3, pl.ds(9 + start, count), :] - padded[3, pl.ds(7 + start, count), :]
            moved = moved + pull * slope
        out.append(moved)
    return out


def pad_layer(refs, low_y, high_y, padded, index):
    flow, _, _, thermal, _ = refs
    for part in range(3):
        pad_rows(
            padded, part, low_y[part, index, 6:], flow[part, index], high_y[part, index, :2]
        )
    pad_rows(padded, 3, low_y[3, index, 6:], thermal[index], high_y[3, index, :2])


def row_kernel(flow, low_x, high_x, thermal, flag, low_y, high_y, _, side_y, padded):
    refs = (flow, low_x, high_x, thermal, flag)
    _, layers, rows, depth = flow.shape
    for index in range(layers):
        for part, cells in ((1, flow.at[1, index]), (3, thermal.at[index])):
            padded[part, pl.ds(rows - 8, 16), :] = cells[pl.ds(rows - 16, 16), :]
            padded[part, pl.ds(8 + rows, 2), :] = high_y[part, index, :2]
        (value,) = march_layer(refs, padded, index, [1], rows - 8, 8)
        side_y[pl.ds(index, 1), :] = value[7:, :]


def march_kernel(
    flow, low_x, high_x, thermal, flag, low_y, high_y, extra, _,
    star, side_x, padded,
):
    refs = (flow, low_x, high_x, thermal, flag)
    _, layers, rows, depth = flow.shape
    for index in range(layers):
        pad_layer(refs, low_y, high_y, padded, index)
        value = march_layer(refs, padded, index, range(3), 0, rows)
        for part in range(3):
            star[part, index] = value[part]
    plane = lambda index: low_x[pl.ds(index * rows, rows), pl.ds(0, depth)]
    beside = extra[pl.ds(2 * rows, 8), pl.ds(0, depth)]
    pad_rows(padded, 0, beside[2:4], plane(1), beside[4:6])
    around = [extra[pl.ds(0, rows), pl.ds(0, depth)], plane(0), plane(1), flow[0, 0], flow[0, 1]]
    top = lax.broadcasted_iota(jnp.int32, (rows, depth), 1) == depth - 1
    drag = 1.0 / (1.0 + TIME_INCREMENT * DRAG_RATE * extra[pl.ds(rows, rows), pl.ds(0, depth)])
    pull = jnp.where(top, (-MARANGONI * 0.5 * TIME_INCREMENT) * drag, 0.0)
    behind = column(extra[pl.ds(2 * rows, 1), pl.ds(0, rows)])
    weights = coefficients([plane(1), plane(3), plane(5)], drag)
    side_x[...] = advance(around, padded, 0, weights) + pull * (thermal[0] - behind)


def transform_kernel(
    group, length, star, side_x, left, right, ratio, _, source, message, rows_
):
    _, layers, rows, depth = star.shape
    first = position(group) * layers
    rows_[pl.ds(0, 8), :] = jnp.zeros((8, depth), F32)
    planes = []
    for index in range(layers):
        rows_[pl.ds(8, rows), :] = star[1, index]
        behind = star[0, index - 1] if index > 0 else side_x[...]
        sink = star[0, index] - behind
        sink = sink + (star[1, index] - rows_[pl.ds(7, rows), :])
        sink = sink + (star[2, index] - lane_shift(star[2, index], -1))
        planes.append(-sink)
    for index, plane in enumerate(transformed(planes, left, right)):
        source[index] = plane
    forward = source[0]
    for index in range(1, layers):
        forward = source[index] + ratio[first + index] * forward
    message[pl.ds(0, rows), :] = forward
    backward = source[layers - 1]
    for index in range(layers - 2, -1, -1):
        backward = source[index] + ratio[length - 1 - first - index] * backward
    message[pl.ds(rows, rows), :] = backward


def started(copies):
    for copy in copies:
        copy.start()
    return copies


def surface(plane):
    rows, depth = plane.shape
    shape = (rows, rows)
    same = lax.broadcasted_iota(jnp.int32, shape, 0) == lax.broadcasted_iota(jnp.int32, shape, 1)
    return jnp.sum(jnp.where(same, plane[:, depth - 1 :], 0.0), axis=0, keepdims=True)


def halo_kernel(flow, thermal, ahead, behind, last_rows, first_rows, tops, sems):
    parts, layers, rows, depth = flow.shape
    pairs = [(thermal.at[layers - 1], tops.at[0]), (thermal.at[0], tops.at[1])]
    for part in range(parts):
        for layer in range(2):
            span = pl.ds((2 * part + layer) * rows, rows)
            pairs.append((flow.at[part, layers - 2 + layer], ahead.at[span, :]))
            pairs.append((flow.at[part, layer], behind.at[span, :]))
    for target, start in ((last_rows, rows - 8), (first_rows, 0)):
        span = pl.ds(start, 8)
        pairs.append((flow.at[:, :, span, :], target.at[pl.ds(0, parts)]))
        pairs.append((thermal.at[:, span, :], target.at[parts]))
    copies = started(
        [pltpu.make_async_copy(*pair, sems.at[index]) for index, pair in enumerate(pairs)]
    )
    for side, message in enumerate((ahead, behind)):
        copies[side].wait()
        row = jnp.broadcast_to(surface(tops[side]), (8, rows))
        message[pl.ds(2 * parts * rows, 8), pl.ds(0, rows)] = row
    for copy in copies[2:]:
        copy.wait()


def extra_kernel(flow, thermal, flag, low_y, high_y, extra, last, flags, sems):
    _, layers, rows, depth = flow.shape
    pairs = [(flag.at[layers - 1], flags), (thermal.at[pl.ds(layers - 2, 2)], last)]
    pairs.append((flow.at[0, layers - 3], extra.at[pl.ds(0, rows), :]))
    copies = started(
        [pltpu.make_async_copy(*pair, sems.at[index]) for index, pair in enumerate(pairs)]
    )
    base = 2 * rows
    extra[pl.ds(base, 8), :] = jnp.zeros((8, extra.shape[1]), F32)
    extra[pl.ds(base + 2, 2), pl.ds(0, depth)] = low_y[0, layers - 1, 6:, :]
    extra[pl.ds(base + 4, 2), pl.ds(0, depth)] = high_y[0, layers - 1, :2, :]
    for copy in copies[:2]:
        copy.wait()
    extra[pl.ds(rows, rows), :] = flags[...].astype(F32)
    extra[pl.ds(base, 1), pl.ds(0, rows)] = surface(last[0])
    for copy in copies[2:]:
        copy.wait()


def wrapped(distance, span):
    moved = distance + span // 2
    moved = jnp.where(moved < 0, moved + span, moved)
    moved = jnp.where(moved >= span, moved - span, moved)
    return (moved - span // 2).astype(F32)


def laser_row(index, layers, rows, spots_a, spots_b):
    total_x = layers * lax.axis_size("gx")
    total_y = rows * lax.axis_size("gy")
    cell_x = lax.axis_index("gx") * layers + index
    cells_y = lax.broadcasted_iota(jnp.int32, (1, rows), 1) + lax.axis_index("gy") * rows
    heat = jnp.zeros((1, rows), F32)
    for spot in range(spots_a.shape[0]):
        dist_x = wrapped(jnp.full((1, rows), cell_x - spots_a[spot], jnp.int32), total_x)
        dist_y = wrapped(cells_y - spots_b[spot], total_y)
        square = dist_x * dist_x + dist_y * dist_y
        heat = heat + jnp.exp(square * (-1.0 / (SPOT_RADIUS * SPOT_RADIUS)))
    return LASER_POWER * heat


def heat_kernel(
    spots_a, spots_b, thermal, low_x, high_x, low_y, high_y, flow,
    warmed, token, padded,
):
    layers, rows, depth = thermal.shape
    token[...] = jnp.zeros(token.shape, F32)
    top = lax.broadcasted_iota(jnp.int32, (rows, depth), 1) == depth - 1
    for index in range(layers):
        pad_rows(padded, 0, low_y[3, index, 6:], thermal[index], high_y[3, index, :2])
        around = []
        for other in range(index - 2, index + 3):
            if other < 0:
                around.append(low_x[other + 2])
            elif other >= layers:
                around.append(high_x[other - layers])
            else:
                around.append(thermal[other])
        speed = [flow[part, index] for part in range(3)]
        gain = TIME_INCREMENT * column(laser_row(index, layers, rows, spots_a, spots_b))
        moved = advance(around, padded, 0, coefficients(speed, None))
        warmed[index] = moved + jnp.where(top, gain, 0.0)


def tables_kernel(group, layers, diagonal, ratio, weight):
    length = group * layers
    mine = position(group)
    first = mine * layers
    diag = diagonal[...]
    ratio[0] = jnp.zeros_like(diag)

    def step(index, previous):
        current = 1.0 / (diag - previous)
        ratio[index] = current
        return current

    loop(1, length + 1, step, jnp.zeros_like(diag))

    def decay(low, high):
        return lax.fori_loop(
            low + 1, high + 1, lambda index, value: value * ratio[index], jnp.ones_like(diag)
        )

    def green(index):
        return 1.0 / (diag - ratio[index] - ratio[jnp.maximum(length - 1 - index, 0)])

    rounds = group.bit_length() - 1
    for turn in range(rounds):
        half = 1 << turn
        right = ((mine >> turn) & 1) == 1
        start = (mine >> (turn + 1)) << (turn + 1)
        cut = (start + half) * layers
        end = (start + 2 * half) * layers
        weight[4 * turn] = decay(cut - 1, end - 1)
        weight[4 * turn + 1] = decay(length - 1 - cut, length - 1 - start * layers)
        low = jnp.where(right, cut - 1, length - 1 - cut)
        high = jnp.where(right, first - 1, length - 1 - first - layers)
        weight[4 * turn + 2] = decay(low, high)
        weight[4 * turn + 3] = green(cut) * ratio[cut]
    inner = jnp.where(mine == group - 1, 0.0, 1.0)
    weight[4 * rounds] = inner * green(first + layers)


def grouped(plane):
    return plane.reshape(plane.shape[0] // 8, 8, plane.shape[1])


def signs(depth):
    row = lax.broadcasted_iota(jnp.int32, (8, depth), 0)
    return jnp.where(row % 2 == 0, 1.0, -1.0)


def face_rows(plane, lead):
    sums = jnp.sum(plane * lead, axis=0)
    return (
        jnp.sum(sums, axis=0, keepdims=True),
        jnp.sum(sums * signs(sums.shape[1]), axis=0, keepdims=True),
    )


def faces_kernel(
    group, length, source, before_y, table_z, ratio, weight, edge, thermal, _, faces, late, sweep
):
    layers, rows, depth = source.shape
    late[...] = thermal[:2]
    first = position(group) * layers
    zero = jnp.zeros((rows, depth), F32)
    extra = dot(before_y[...], table_z[...])
    faces[...] = jnp.zeros(faces.shape, F32)
    for index in range(layers):
        faces[pl.ds(2 * length + first + index, 1), :] = extra[index : index + 1]
    forward = zero
    for index in range(layers):
        forward = source[index] + ratio[first + index] * forward
        sweep[index] = forward
    value = weight[weight.shape[0] - 1] * (ratio[first + layers] * forward)
    energy = zero
    for index in range(layers - 1, -1, -1):
        value = ratio[first + index + 1] * (sweep[index] + value)
        energy = energy + source[index] * value
    faces[pl.ds(3 * length, 8), :] = jnp.broadcast_to(total(energy), (8, depth))

    lead = grouped(edge[...])
    zero = grouped(zero)

    def down(index, previous):
        inside = (index >= first) & (index < first + layers)
        own = jnp.where(inside, source[jnp.clip(index - first, 0, layers - 1)], 0.0)
        row = faces[pl.ds(2 * length + index, 1), :]
        current = grouped(own) + lead * row + grouped(ratio[index]) * previous
        sweep[index] = current.reshape(rows, depth)
        return current

    loop(0, length, down, zero)

    def up(back, following):
        index = length - 1 - back
        value = grouped(ratio[index + 1]) * (grouped(sweep[index]) + following)
        low, high = face_rows(value, lead)
        faces[pl.ds(index, 1), :] = low
        faces[pl.ds(length + index, 1), :] = high
        return value

    loop(0, length, up, zero)


def joined(turn, group, message, other, sums, weight):
    rows, depth = weight.shape[1:]
    right = ((position(group) >> turn) & 1) == 1
    upper, lower = pl.ds(0, rows), pl.ds(rows, rows)
    left_s = jnp.where(right, other[upper, :], message[upper, :])
    right_s = jnp.where(right, message[upper, :], other[upper, :])
    left_t = jnp.where(right, other[lower, :], message[lower, :])
    right_t = jnp.where(right, message[lower, :], other[lower, :])
    own = weight[4 * turn + 2]
    before = sums[0] + jnp.where(right, left_s * own, 0.0)
    after = sums[1] + jnp.where(right, 0.0, right_t * own)
    forward = right_s + left_s * weight[4 * turn]
    backward = left_t + right_t * weight[4 * turn + 1]
    energy = 2.0 * total(left_s * right_t * weight[4 * turn + 3])
    return forward, backward, before, after, energy


def merge_kernel(
    turn, group, length, message, other, faces, other_faces, sums, weight,
    new_message, new_sums, head, tail,
):
    rows, depth = weight.shape[1:]
    forward, backward, before, after, energy = joined(turn, group, message, other, sums, weight)
    new_sums[0] = before
    new_sums[1] = after
    new_message[pl.ds(0, rows), :] = forward
    new_message[pl.ds(rows, rows), :] = backward
    low, high = pl.ds(0, length), pl.ds(length, length)
    late, number = pl.ds(2 * length, length), pl.ds(3 * length, 8)
    head[...] = faces[low, :] + other_faces[low, :]
    tail[...] = faces[high, :] + other_faces[high, :]
    new_message[pl.ds(2 * rows, length), :] = head[...]
    new_message[pl.ds(2 * rows + length, length), :] = faces[late, :] + other_faces[late, :]
    energy = faces[number, :] + other_faces[number, :] + energy
    new_message[pl.ds(2 * rows + 2 * length, 8), :] = energy


def late_solve(length, message, other, ratio, edge, late, sweep):
    rows, depth = edge.shape
    lead = grouped(edge[...])
    own = pl.ds(2 * rows + length, length)
    late[pl.ds(0, length), :] = message[own, :] + other[own, :]

    def down(index, previous):
        current = lead * late[pl.ds(index, 1), :] + grouped(ratio[index]) * previous
        sweep[index] = current.reshape(rows, depth)
        return current

    zero = jnp.zeros(lead.shape, F32)
    loop(0, length, down, zero)

    def up(back, following):
        index = length - 1 - back
        value = grouped(ratio[index + 1]) * (grouped(sweep[index]) + following)
        sweep[index] = value.reshape(rows, depth)
        late[pl.ds(length + index, 1), :] = face_rows(value, lead)[0]
        return value

    loop(0, length, up, zero)
    sweep[length] = jnp.zeros((rows, depth), F32)


def close_kernel(
    turn, group, length, message, other, sums, weight, ratio, edge, ends, late, sweep
):
    forward, backward, _, _, _ = joined(turn, group, message, other, sums, weight)
    late_solve(length, message, other, ratio, edge, late, sweep)
    ends[0] = ratio[length] * forward + sweep[length - 1]
    ends[1] = ratio[length] * backward + sweep[0]


def coarse_kernel(
    turn, group, length, alone, source, message, other, sums, faces_in, weight, ratio, edge, *refs
):
    precond, image, report, faces, late, sweep, ends = refs[-7:]
    layers, rows, depth = source.shape
    first = position(group) * layers
    below, below_far, above, above_far = faces_in
    forward, backward, before, after, energy = joined(turn, group, message, other, sums, weight)
    late_solve(length, message, other, ratio, edge, late, sweep)
    ends[0] = ratio[length] * forward + sweep[length - 1]
    ends[1] = ratio[length] * backward + sweep[0]
    beyond = ends if alone else refs[0]
    own = pl.ds(2 * rows, length)
    faces[pl.ds(0, length), :] = message[own, :] + other[own, :]
    faces[pl.ds(length, length), :] = below[...] + below_far[...]
    faces[pl.ds(2 * length, length), :] = above[...] + above_far[...]
    number = pl.ds(2 * rows + 2 * length, 8)
    energy = message[number, :] + other[number, :] + energy
    late_rows = late[pl.ds(0, length), :]
    energy = energy + total(
        late_rows * (2.0 * faces[pl.ds(0, length), :] - late[pl.ds(length, length), :])
    )
    forward = before
    for index in range(layers):
        forward = source[index] + ratio[first + index] * forward
        precond[index] = forward
    value = weight[weight.shape[0] - 1] * (after + ratio[first + layers] * forward)
    is_last = first + layers == length
    precond[layers] = jnp.where(is_last, beyond[1], value + sweep[first + layers])
    for index in range(layers - 1, -1, -1):
        value = ratio[first + index + 1] * (precond[index] + value)
        precond[index] = value + sweep[first + index]
    lead = grouped(edge[...])
    sign = signs(depth)

    def pull(index):
        below = faces[pl.ds(length + index, 1), :]
        above = faces[pl.ds(2 * length + index, 1), :]
        return below, above

    def down(index, previous):
        below, above = pull(index)
        current = lead * (below + sign * above) + grouped(ratio[index]) * previous
        if isinstance(index, int):
            if index == 0:
                current = current + grouped(beyond[0])
            if index == length - 1:
                current = current + grouped(beyond[1])
        else:
            current = current + jnp.where(index == 0, grouped(beyond[0]), 0.0)
            current = current + jnp.where(index == length - 1, grouped(beyond[1]), 0.0)
        sweep[index] = current.reshape(rows, depth)
        return current

    zero = jnp.zeros(lead.shape, F32)
    loop(0, length, down, zero)
    line = jnp.zeros((1, depth), F32)

    def up(back, carry):
        following, linked, squared = carry
        index = length - 1 - back
        value = grouped(ratio[index + 1]) * (grouped(sweep[index]) + following)
        sweep[index] = value.reshape(rows, depth)
        low, high = face_rows(value, lead)
        report[pl.ds(index, 1), :] = low
        report[pl.ds(length + index, 1), :] = high
        below, above = pull(index)
        linked = linked + faces[pl.ds(index, 1), :] * below
        squared = squared + low * below + high * above
        return value, linked, squared

    _, linked, squared = loop(0, length, up, (zero, line, line))
    sweep[length] = sweep[0]
    for index in range(layers + 1):
        image[index] = sweep[first + index]
    head, tail = sweep[0], sweep[length - 1]
    linked = 2.0 * total(linked) + total(ends[1] * beyond[0] + ends[0] * beyond[1])
    squared = total(squared) + total(head * beyond[0] + tail * beyond[1])
    crossing = 2.0 * total(head * tail)
    where = 2 * length
    report[pl.ds(where, 1), :] = energy[0:1]
    report[pl.ds(where + 1, 1), :] = jnp.broadcast_to(linked, (1, depth))
    report[pl.ds(where + 2, 1), :] = jnp.broadcast_to(squared, (1, depth))
    report[pl.ds(where + 3, 1), :] = jnp.broadcast_to(crossing, (1, depth))
    report[pl.ds(where + 4, 4), :] = jnp.zeros((4, depth), F32)


def physical_kernel(precond, image, left, right, precond_out, image_out):
    count = precond.shape[0]
    planes = [precond[index] for index in range(count)] + [image[index] for index in range(count)]
    planes = transformed(planes, left, right)
    for index in range(count):
        precond_out[index] = planes[index]
        image_out[index] = planes[count + index]


def project_kernel(
    group, length, paired, star, precond, image, faces, table_z, *refs
):
    given, (flow, pressure, flows, field, rows_, sems) = refs[:-6], refs[-6:]
    _, layers, rows, depth = star.shape
    first = position(group) * layers
    where = 2 * length
    reports = ring([each[...] for each in given])
    sums = reports[0][where:]
    for other in reports[1:]:
        sums = sums + other[where:]
    pairs = jnp.zeros((1, depth), F32)
    for index in range(len(reports)):
        upper, lower = reports[index], reports[(index + 1) % len(reports)]
        pairs = pairs + jnp.sum(
            upper[:length] * lower[length:where], axis=0, keepdims=True
        )
    energy, linked, squared, crossing = (sums[k : k + 1, 0:1] for k in range(4))
    if not paired:
        crossing = crossing + 2.0 * total(pairs)
    first_image = energy - linked
    step = energy / first_image
    beta = (energy * squared - linked * linked) / (first_image * first_image)
    rest = -linked / first_image
    second_image = (
        rest * rest * first_image
        + 2.0 * rest * step * (linked - squared)
        + step * step * (squared - crossing)
        - beta * beta * first_image
    )
    second_step = beta * energy / second_image
    alpha = step + second_step * (rest + beta)
    gamma = second_step * step
    for index in range(layers + 1):
        field[index] = alpha * precond[index] + gamma * image[index]
    after = rows_.at[pl.ds(rows + 8, length), :]
    after[...] = alpha * faces[pl.ds(2 * length, length), :] + gamma * reports[-1][:length]
    following = dot(after[pl.ds(first, layers), :], table_z[...])
    copies = []
    for index in range(layers):
        value = field[index]
        rows_[pl.ds(0, rows), :] = value
        rows_[pl.ds(rows, 1), :] = following[index : index + 1]
        flows[0, index] = star[0, index] - (field[index + 1] - value)
        flows[1, index] = star[1, index] - (rows_[pl.ds(1, rows), :] - value)
        flows[2, index] = star[2, index] - (lane_shift(value, 1) - value)
        pairs = ((flows.at[:, index], flow.at[:, index]), (field.at[index], pressure.at[index]))
        copies += started(
            [
                pltpu.make_async_copy(*pair, sems.at[2 * index + side])
                for side, pair in enumerate(pairs)
            ]
        )
    for copy in copies:
        copy.wait()


def ring(reports):
    if len(reports) != 4:
        return reports
    own, near, across, far = reports
    even = lax.rem(lax.axis_index("gy"), 2) == 0
    return [own, jnp.where(even, far, near), across, jnp.where(even, near, far)]


def along(array, axis, by):
    length = lax.axis_size(axis)
    return lax.ppermute(array, axis, [(i, (i + by) % length) for i in range(length)])


def swapped(array, bit, by=0):
    count_x, count_y = lax.axis_size("gx"), lax.axis_size("gy")
    pairs = [
        (x * count_y + y, (x ^ bit) * count_y + (y + by) % count_y)
        for x in range(count_x)
        for y in range(count_y)
    ]
    return lax.ppermute(array, ("gx", "gy"), pairs)


def pack(body, inputs, received, shapes, scratch, count):
    inputs = [pltpu.with_memory_space_constraint(each, pltpu.HBM) for each in inputs]
    return pl.pallas_call(
        body,
        out_shape=[jax.ShapeDtypeStruct(shape, F32) for shape in shapes],
        in_specs=[pl.BlockSpec(memory_space=pltpu.HBM)] * len(inputs) + [VMEM] * len(received),
        out_specs=[VMEM] * len(shapes),
        scratch_shapes=[scratch, pltpu.SemaphoreType.DMA((count,))],
        compiler_params=pltpu.CompilerParams(vmem_limit_bytes=4 << 20),
    )(*inputs, *received)


def per_device(melt_flow, thermal_state, powder_flag, spot_lateral_a_cell, spot_lateral_b_cell):
    layers, rows, depth = thermal_state.shape
    count_x, count_y = lax.axis_size("gx"), lax.axis_size("gy")
    group = min(count_x, BLOCK // layers)
    blocks = count_x // group
    length = group * layers
    rounds = group.bit_length() - 1
    plane = (rows, depth)
    sine_y, values_y = sines(rows)
    sine_z, values_z = sines(depth)
    left, right = packed_tables(sine_y, sine_z)
    table_z = jnp.asarray(sine_z, F32)
    edge = jnp.asarray(np.broadcast_to(sine_y[0][:, None], plane), F32)
    diagonal = jnp.asarray(2.0 + values_y[:, None] + values_z[None, :], F32)
    line = (length, depth)

    parts = melt_flow.shape[0]
    width = max(rows, depth)
    outer_planes = (2 * parts * rows + 8, width)
    ahead, behind, last_rows, first_rows = pack(
        halo_kernel,
        [melt_flow, thermal_state],
        [],
        [outer_planes, outer_planes] + [(parts + 1, layers, 8, depth)] * 2,
        pltpu.VMEM((2,) + plane, F32),
        6 + 4 * parts,
    )
    low_x = along(ahead, "gx", 1)
    high_x = along(behind, "gx", -1)
    low_y = along(last_rows, "gy", 1)
    high_y = along(first_rows, "gy", -1)
    extra, last = pack(
        extra_kernel,
        [melt_flow, thermal_state, powder_flag],
        [low_y, high_y],
        [(2 * rows + 8, width), (2,) + plane],
        pltpu.VMEM(plane, jnp.int32),
        3,
    )
    extra = along(extra, "gx", 1)
    ratio, weight = call(
        functools.partial(tables_kernel, group, layers),
        [diagonal],
        [(length + 1,) + plane, (4 * rounds + 1,) + plane],
    )
    early_low = along(last, "gx", 1)
    marched = [melt_flow, low_x, high_x, thermal_state, powder_flag, low_y, high_y]
    padded = pltpu.VMEM((4, rows + 16, depth), F32)
    (side_y,) = call(row_kernel, marched + [weight], [(layers, depth)], [padded], loose=1)
    before_y = along(side_y, "gy", 1)
    star, side_x = call(
        march_kernel,
        marched + [extra, side_y],
        [(3, layers) + plane, plane],
        [padded],
        loose=1,
        flops=3 << 29,
    )
    source, message = call(
        functools.partial(transform_kernel, group, length),
        [star, side_x, left, right, ratio, before_y],
        [(layers,) + plane, (2 * rows, depth)],
        [pltpu.VMEM((rows + 16, depth), F32)],
        loose=1,
        flops=1 << 30,
    )
    faces, late = call(
        functools.partial(faces_kernel, group, length),
        [source, before_y, table_z, ratio, weight, edge, thermal_state, early_low],
        [(3 * length + 8, depth), (2,) + plane],
        [pltpu.VMEM((max(length, layers + 1),) + plane, F32)],
        loose=1,
    )
    early_high = along(late, "gx", -1)
    alone = blocks == 1
    warmed, token = call(
        heat_kernel,
        [
            spot_lateral_a_cell, spot_lateral_b_cell, thermal_state, early_low, early_high,
            low_y, high_y, melt_flow,
        ],
        [(layers,) + plane, (8, depth)],
        [pltpu.VMEM((1, rows + 16, depth), F32)],
        scalars=2,
        flops=1 << 28,
    )
    sums = jnp.zeros((2,) + plane, F32)
    for turn in range(rounds - 1):
        message, sums, head, tail = call(
            functools.partial(merge_kernel, turn, group, length),
            [
                message, swapped(message, 1 << turn), faces, swapped(faces, 1 << turn),
                sums, weight,
            ],
            [(2 * rows + 2 * length + 8, depth), (2,) + plane, line, line],
        )
        if turn + 2 < rounds:
            rest = message[2 * rows + length :]
            message, faces = message[: 2 * rows], jnp.concatenate([head, tail, rest], 0)
    bit = group >> 1
    other = swapped(message, bit)
    rim = [
        swapped(tail, 0, 1), swapped(tail, bit, 1), swapped(head, 0, -1), swapped(head, bit, -1)
    ]
    outer = []
    scratch = [pltpu.VMEM((2 * length, depth), F32), pltpu.VMEM((length + 1,) + plane, F32)]
    if not alone:
        (ends,) = call(
            functools.partial(close_kernel, rounds - 1, group, length),
            [message, other, sums, weight, ratio, edge],
            [(2,) + plane],
            scratch,
        )
        outer = [jnp.stack([along(ends[0], "gx", group), along(ends[1], "gx", -group)])]
    operands = [source, message, other, sums] + rim
    operands += [weight, ratio, edge] + outer + [token]

    def coarse(*refs):
        coarse_kernel(rounds - 1, group, length, alone, *refs[:4], refs[4:8], *refs[8:])

    precond, image, report, faces = call(
        coarse,
        operands,
        [
            (layers + 1,) + plane, (layers + 1,) + plane, (2 * length + 8, depth),
            (3 * length, depth),
        ],
        scratch + [pltpu.VMEM((2,) + plane, F32)],
        loose=1,
    )
    if blocks > 1:
        onward = along(image[0], "gx", -1)
        at_end = position(group) == group - 1
        image = image.at[layers].set(jnp.where(at_end, onward, image[layers]))
        upper = along(report[:length], "gy", -1)
        crossing = jnp.sum(onward * image[layers - 1])
        crossing = crossing + jnp.sum(upper * report[length : 2 * length])
        numbers = report[2 * length :].at[3].set(2.0 * crossing)
        numbers = lax.psum(jnp.where(at_end, numbers, 0.0), "gx")
        report = report.at[2 * length :].set(numbers)
    reports = [report]
    for by in range(1, count_y):
        pairs = [(i, i ^ by if count_y == 4 else (i + by) % count_y) for i in range(count_y)]
        reports.append(lax.ppermute(report, "gy", pairs))
    precond, image = call(
        physical_kernel,
        [precond, image, left, right],
        [(layers + 1,) + plane, (layers + 1,) + plane],
    )
    flow, pressure = call(
        functools.partial(project_kernel, group, length, blocks > 1),
        [star, precond, image, faces, table_z] + reports,
        [(3, layers) + plane, (layers,) + plane],
        [
            pltpu.VMEM((3, layers) + plane, F32),
            pltpu.VMEM((layers + 1,) + plane, F32),
            pltpu.VMEM((rows + 8 + length, depth), F32),
        ],
        semaphores=2 * layers,
    )
    return (flow, warmed, pressure)


def solution(mesh):
    placed = (
        P(None, ("runs", "gx"), "gy", None),
        P(("runs", "gx"), "gy", None),
        P(("runs", "gx"), "gy", None),
        P("runs"),
        P("runs"),
    )
    return jax.shard_map(
        per_device,
        mesh=mesh,
        in_specs=placed,
        out_specs=(
            P(None, ("runs", "gx"), "gy", None),
            P(("runs", "gx"), "gy", None),
            P(("runs", "gx"), "gy", None),
        ),
        check_vma=False,
    )
```

```python
import functools
import math

import jax
import jax.numpy as jnp
import numpy as np
from jax import lax
from jax.experimental import pallas as pl
from jax.experimental.pallas import tpu as pltpu
from jax.sharding import PartitionSpec as P

BLOCK = 128

TIME_INCREMENT = 0.2
MARANGONI = 1.5
DRAG_RATE = 4.0
LASER_POWER = 3.0
SPOT_RADIUS = 5.0

F32 = jnp.float32
VMEM = pl.BlockSpec(memory_space=pltpu.VMEM)
SMEM = pl.BlockSpec(memory_space=pltpu.SMEM)


def call(body, operands, shapes, scratch=(), scalars=0, loose=0, flops=1 << 20):
    out_shape = [jax.ShapeDtypeStruct(shape, F32) for shape in shapes]
    moved = 4 * sum(math.prod(shape) for shape in shapes)
    held = moved + 4 * sum(operand.size for operand in operands)
    held += 4 * sum(math.prod(space.shape) for space in scratch)
    return pl.pallas_call(
        body,
        out_shape=out_shape,
        in_specs=[SMEM] * scalars
        + [VMEM] * (len(operands) - scalars - loose)
        + [pl.BlockSpec(memory_space=pl.ANY)] * loose,
        out_specs=[VMEM] * len(shapes),
        scratch_shapes=list(scratch),
        compiler_params=pltpu.CompilerParams(vmem_limit_bytes=held + (4 << 20)),
        cost_estimate=pl.CostEstimate(flops=flops, bytes_accessed=2 * moved, transcendentals=0),
    )(*operands)


def dot(left, right):
    return jnp.dot(left, right, precision=lax.Precision.HIGHEST, preferred_element_type=F32)


def split(cells):
    high = cells.astype(jnp.bfloat16)
    return high, (cells - high.astype(F32)).astype(jnp.bfloat16)


def folded(product):
    half = product.shape[1] // 2
    return product[:, :half] + product[:, half:]


def packed_tables(left, right):
    left_high, left_low = split(np.asarray(left, np.float32))
    right_high, right_low = split(np.asarray(right, np.float32))
    zero = np.zeros_like(right_low)
    return (
        jnp.asarray(np.concatenate([left_high, left_low], 1)),
        jnp.asarray(np.block([[right_high, right_low], [right_high, zero]])),
    )


def transformed(planes, left, right):
    rows = planes[0].shape[0]
    high, low = split(jnp.concatenate(planes, 0))
    cells = jnp.concatenate([high, low], 1)
    cells = folded(jnp.dot(cells, right[...], preferred_element_type=F32))
    out = []
    for index in range(len(planes)):
        high, low = split(cells[index * rows : (index + 1) * rows])
        upper = jnp.concatenate([high, low], 1)
        lower = jnp.concatenate([high, jnp.zeros_like(low)], 1)
        cells_ = jnp.concatenate([upper, lower], 0)
        out.append(folded(jnp.dot(left[...], cells_, preferred_element_type=F32)))
    return out


def total(cells):
    return jnp.sum(jnp.sum(cells, axis=0, keepdims=True), axis=1, keepdims=True)


def loop(low, high, body, start):
    if isinstance(high, int) and isinstance(low, int) and high - low <= 24:
        carry = start
        for index in range(low, high):
            carry = body(index, carry)
        return carry
    return lax.fori_loop(low, high, body, start)


def position(group):
    return lax.rem(lax.axis_index("gx"), group)


def sines(length):
    positions = np.arange(length) + 1.0
    step = math.pi / (length + 1)
    table = np.sqrt(2.0 / (length + 1)) * np.sin(step * positions[:, None] * positions[None, :])
    return table, 2.0 - 2.0 * np.cos(step * positions)


def lane_shift(cells, offset):
    width = cells.shape[1]
    lane = lax.broadcasted_iota(jnp.int32, cells.shape, 1)
    moved = pltpu.roll(cells, (-offset) % width, 1)
    keep = lane < width - offset if offset > 0 else lane >= -offset
    return jnp.where(keep, moved, 0.0)


def column(row):
    length = row.shape[1]
    shape = (length, length)
    same = lax.broadcasted_iota(jnp.int32, shape, 0) == lax.broadcasted_iota(jnp.int32, shape, 1)
    return jnp.sum(jnp.where(same, row, 0.0), axis=1, keepdims=True)


def coefficients(speed, scale):
    factors = [0.5 * TIME_INCREMENT * jnp.abs(each) for each in speed]
    if scale is not None:
        factors = [each * scale for each in factors]
    centre = (1.0 if scale is None else scale) - 3.0 * (factors[0] + factors[1] + factors[2])
    near, far = 4.0 * factors[2], -factors[2]
    ahead = speed[2] >= 0.0
    lane = lax.broadcasted_iota(jnp.int32, near.shape, 1)
    width = near.shape[1]
    depth = (
        jnp.where(ahead & (lane >= 1), near, 0.0),
        jnp.where(ahead & (lane >= 2), far, 0.0),
        jnp.where(ahead | (lane >= width - 1), 0.0, near),
        jnp.where(ahead | (lane >= width - 2), 0.0, far),
    )
    return centre, speed[0] >= 0.0, factors[0], speed[1] >= 0.0, factors[1], depth


def advance(layers, padded, index, weights, start=0):
    middle = layers[2]
    rows, width = middle.shape
    centre, ahead_x, factor_x, ahead_y, factor_y, depth = weights
    near = jnp.where(ahead_x, layers[1], layers[3])
    far = jnp.where(ahead_x, layers[0], layers[4])
    moved = centre * middle + factor_x * (4.0 * near - far)
    beside = lambda offset: padded[index, pl.ds(8 + offset + start, rows), :]
    near = jnp.where(ahead_y, beside(-1), beside(1))
    far = jnp.where(ahead_y, beside(-2), beside(2))
    moved = moved + factor_y * (4.0 * near - far)
    for factor, offset in zip(depth, (1, 2, width - 1, width - 2)):
        moved = moved + factor * pltpu.roll(middle, offset, 1)
    return moved


def pad_rows(padded, index, before, middle, after):
    rows = middle.shape[0]
    padded[index, pl.ds(8, rows), :] = middle
    padded[index, pl.ds(6, 2), :] = before
    padded[index, pl.ds(8 + rows, 2), :] = after


def march_layer(refs, padded, index, parts, start, count, edges=None):
    flow, low_x, high_x, thermal, flag = refs
    _, layers, rows, depth = flow.shape
    span = pl.ds(start, count)
    speed = [flow[part, index, span, :] for part in range(3)]
    drag = 1.0 / (1.0 + TIME_INCREMENT * DRAG_RATE * flag[index, span, :].astype(F32))
    top = lax.broadcasted_iota(jnp.int32, (count, depth), 1) == depth - 1
    pull = jnp.where(top, (-MARANGONI * 0.5 * TIME_INCREMENT) * drag, 0.0)
    weights = coefficients(speed, drag)
    out = []
    for part in parts:
        around = []
        for other in range(index - 2, index + 3):
            if other < 0:
                first = (2 * part + other + 2) * rows + start
                around.append(low_x[pl.ds(first, count), :])
            elif other >= layers:
                first = (2 * part + other - layers) * rows + start
                around.append(high_x[pl.ds(first, count), :])
            else:
                around.append(flow[part, other, span, :])
        moved = advance(around, padded, part, weights, start)
        if part == 0:
            behind = edges[0][start : start + count]
            before = edges[1][start : start + count]
            behind = thermal[index - 1, span, :] if index > 0 else behind
            before = thermal[index + 1, span, :] if index + 1 < layers else before
            moved = moved + pull * (before - behind)
        if part == 1:
            slope = padded[3, pl.ds(9 + start, count), :] - padded[3, pl.ds(7 + start, count), :]
            moved = moved + pull * slope
        out.append(moved)
    return out


def pad_layer(refs, low_y, high_y, padded, index):
    flow, _, _, thermal, _ = refs
    for part in range(3):
        pad_rows(
            padded, part, low_y[part, index, 6:], flow[part, index], high_y[part, index, :2]
        )
    pad_rows(padded, 3, low_y[3, index, 6:], thermal[index], high_y[3, index, :2])


def row_kernel(flow, low_x, high_x, thermal, flag, low_y, high_y, _, side_y, padded):
    refs = (flow, low_x, high_x, thermal, flag)
    _, layers, rows, depth = flow.shape
    for index in range(layers):
        for part, cells in ((1, flow.at[1, index]), (3, thermal.at[index])):
            padded[part, pl.ds(rows - 8, 16), :] = cells[pl.ds(rows - 16, 16), :]
            padded[part, pl.ds(8 + rows, 2), :] = high_y[part, index, :2]
        (value,) = march_layer(refs, padded, index, [1], rows - 8, 8)
        side_y[pl.ds(index, 1), :] = value[7:, :]


def march_kernel(
    flow, low_x, high_x, thermal, flag, low_y, high_y, _, star, padded
):
    refs = (flow, low_x, high_x, thermal, flag)
    _, layers, rows, depth = flow.shape
    edges = [column(halo[pl.ds(halo.shape[0] - 8, 1), pl.ds(0, rows)]) for halo in (low_x, high_x)]
    count = math.gcd(rows, 16)
    for index in range(layers):
        pad_layer(refs, low_y, high_y, padded, index)
        for start in range(0, rows, count):
            value = march_layer(refs, padded, index, range(3), start, count, edges)
            for part in range(3):
                star[part, index, pl.ds(start, count), :] = value[part]


def side_plane(flow, low_x, thermal, extra, padded):
    rows, depth = flow.shape[2:]
    plane = lambda index: low_x[pl.ds(index * rows, rows), pl.ds(0, depth)]
    beside = extra[pl.ds(2 * rows, 8), pl.ds(0, depth)]
    pad_rows(padded, 0, beside[2:4], plane(1), beside[4:6])
    around = [extra[pl.ds(0, rows), pl.ds(0, depth)], plane(0), plane(1), flow[0, 0], flow[0, 1]]
    top = lax.broadcasted_iota(jnp.int32, (rows, depth), 1) == depth - 1
    drag = 1.0 / (1.0 + TIME_INCREMENT * DRAG_RATE * extra[pl.ds(rows, rows), pl.ds(0, depth)])
    pull = jnp.where(top, (-MARANGONI * 0.5 * TIME_INCREMENT) * drag, 0.0)
    behind = column(extra[pl.ds(2 * rows, 1), pl.ds(0, rows)])
    weights = coefficients([plane(1), plane(3), plane(5)], drag)
    return advance(around, padded, 0, weights) + pull * (thermal[0] - behind)


def transform_kernel(star, left, right, partial, rows_):
    _, layers, rows, depth = star.shape
    rows_[pl.ds(0, 8), :] = jnp.zeros((8, depth), F32)
    planes = []
    for index in range(layers):
        rows_[pl.ds(8, rows), :] = star[1, index]
        sink = star[0, index]
        if index > 0:
            sink = sink - star[0, index - 1]
        sink = sink + (star[1, index] - rows_[pl.ds(7, rows), :])
        sink = sink + (star[2, index] - lane_shift(star[2, index], -1))
        planes.append(-sink)
    for index, plane in enumerate(transformed(planes, left, right)):
        partial[index] = plane


def source_kernel(
    group, length, flow, low_x, thermal, extra, partial, left, right, ratio, _,
    source, message, padded,
):
    layers, rows, depth = partial.shape
    first = position(group) * layers
    (onward,) = transformed([side_plane(flow, low_x, thermal, extra, padded)], left, right)
    source[0] = partial[0] + onward
    for index in range(1, layers):
        source[index] = partial[index]
    backward = partial[layers - 1]
    for index in range(layers - 2, 0, -1):
        backward = partial[index] + ratio[length - 1 - first - index] * backward
    forward = source[0]
    message[pl.ds(rows, rows), :] = forward + ratio[length - 1 - first] * backward
    for index in range(1, layers):
        forward = partial[index] + ratio[first + index] * forward
    message[pl.ds(0, rows), :] = forward


def started(copies):
    for copy in copies:
        copy.start()
    return copies


def surface(plane):
    rows, depth = plane.shape
    shape = (rows, rows)
    same = lax.broadcasted_iota(jnp.int32, shape, 0) == lax.broadcasted_iota(jnp.int32, shape, 1)
    return jnp.sum(jnp.where(same, plane[:, depth - 1 :], 0.0), axis=0, keepdims=True)


def halo_kernel(flow, thermal, ahead, behind, last_rows, first_rows, tops, sems):
    parts, layers, rows, depth = flow.shape
    pairs = [(thermal.at[layers - 1], tops.at[0]), (thermal.at[0], tops.at[1])]
    for part in range(parts):
        for layer in range(2):
            span = pl.ds((2 * part + layer) * rows, rows)
            pairs.append((flow.at[part, layers - 2 + layer], ahead.at[span, :]))
            pairs.append((flow.at[part, layer], behind.at[span, :]))
    for target, start in ((last_rows, rows - 8), (first_rows, 0)):
        span = pl.ds(start, 8)
        pairs.append((flow.at[:, :, span, :], target.at[pl.ds(0, parts)]))
        pairs.append((thermal.at[:, span, :], target.at[parts]))
    copies = started(
        [pltpu.make_async_copy(*pair, sems.at[index]) for index, pair in enumerate(pairs)]
    )
    for side, message in enumerate((ahead, behind)):
        copies[side].wait()
        row = jnp.broadcast_to(surface(tops[side]), (8, rows))
        message[pl.ds(2 * parts * rows, 8), pl.ds(0, rows)] = row
    for copy in copies[2:]:
        copy.wait()


def extra_kernel(flow, thermal, flag, low_y, high_y, extra, flags, top, sems):
    _, layers, rows, depth = flow.shape
    pairs = [(flag.at[layers - 1], flags), (thermal.at[layers - 2], top)]
    pairs.append((flow.at[0, layers - 3], extra.at[pl.ds(0, rows), :]))
    copies = started(
        [pltpu.make_async_copy(*pair, sems.at[index]) for index, pair in enumerate(pairs)]
    )
    base = 2 * rows
    extra[pl.ds(base, 8), :] = jnp.zeros((8, extra.shape[1]), F32)
    extra[pl.ds(base + 2, 2), pl.ds(0, depth)] = low_y[0, layers - 1, 6:, :]
    extra[pl.ds(base + 4, 2), pl.ds(0, depth)] = high_y[0, layers - 1, :2, :]
    for copy in copies[:2]:
        copy.wait()
    extra[pl.ds(rows, rows), :] = flags[...].astype(F32)
    extra[pl.ds(base, 1), pl.ds(0, rows)] = surface(top[...])
    for copy in copies[2:]:
        copy.wait()


def wrapped(distance, span):
    moved = distance + span // 2
    moved = jnp.where(moved < 0, moved + span, moved)
    moved = jnp.where(moved >= span, moved - span, moved)
    return (moved - span // 2).astype(F32)


def laser_row(index, layers, rows, spots_a, spots_b):
    total_x = layers * lax.axis_size("gx")
    total_y = rows * lax.axis_size("gy")
    cell_x = lax.axis_index("gx") * layers + index
    cells_y = lax.broadcasted_iota(jnp.int32, (1, rows), 1) + lax.axis_index("gy") * rows
    heat = jnp.zeros((1, rows), F32)
    for spot in range(spots_a.shape[0]):
        dist_x = wrapped(jnp.full((1, rows), cell_x - spots_a[spot], jnp.int32), total_x)
        dist_y = wrapped(cells_y - spots_b[spot], total_y)
        square = dist_x * dist_x + dist_y * dist_y
        heat = heat + jnp.exp(square * (-1.0 / (SPOT_RADIUS * SPOT_RADIUS)))
    return LASER_POWER * heat


def heat_kernel(
    spots_a, spots_b, thermal, halo, low_y, high_y, flow, warmed, token, padded
):
    layers, rows, depth = thermal.shape
    token[...] = jnp.zeros(token.shape, F32)
    top = lax.broadcasted_iota(jnp.int32, (rows, depth), 1) == depth - 1
    none = jnp.zeros((rows, depth), F32)
    for index in range(layers):
        pad_rows(padded, 0, low_y[3, index, 6:], thermal[index], high_y[3, index, :2])
        around = []
        for other in range(index - 2, index + 3):
            if other < 0:
                around.append(halo[other + 2])
            elif other >= layers:
                around.append(none)
            else:
                around.append(thermal[other])
        speed = [flow[part, index] for part in range(3)]
        gain = TIME_INCREMENT * column(laser_row(index, layers, rows, spots_a, spots_b))
        moved = advance(around, padded, 0, coefficients(speed, None))
        warmed[index] = moved + jnp.where(top, gain, 0.0)


def heat_last_kernel(flow, halo, warm, warmed):
    layers = warm.shape[0]
    warmed[: layers - 2] = warm[: layers - 2]
    for index, added in ((layers - 2, -halo[0]), (layers - 1, 4.0 * halo[0] - halo[1])):
        speed = flow[0, index]
        factor = jnp.where(speed >= 0.0, 0.0, 0.5 * TIME_INCREMENT * jnp.abs(speed))
        warmed[index] = warm[index] + factor * added


def tables_kernel(group, layers, diagonal, ratio, weight):
    length = group * layers
    mine = position(group)
    first = mine * layers
    diag = diagonal[...]
    ratio[0] = jnp.zeros_like(diag)

    def step(index, previous):
        current = 1.0 / (diag - previous)
        ratio[index] = current
        return current

    loop(1, length + 1, step, jnp.zeros_like(diag))

    def decay(low, high):
        return lax.fori_loop(
            low + 1, high + 1, lambda index, value: value * ratio[index], jnp.ones_like(diag)
        )

    def green(index):
        return 1.0 / (diag - ratio[index] - ratio[jnp.maximum(length - 1 - index, 0)])

    rounds = group.bit_length() - 1
    for turn in range(rounds):
        half = 1 << turn
        right = ((mine >> turn) & 1) == 1
        start = (mine >> (turn + 1)) << (turn + 1)
        cut = (start + half) * layers
        end = (start + 2 * half) * layers
        weight[4 * turn] = decay(cut - 1, end - 1)
        weight[4 * turn + 1] = decay(length - 1 - cut, length - 1 - start * layers)
        low = jnp.where(right, cut - 1, length - 1 - cut)
        high = jnp.where(right, first - 1, length - 1 - first - layers)
        weight[4 * turn + 2] = decay(low, high)
        weight[4 * turn + 3] = green(cut) * ratio[cut]
    inner = jnp.where(mine == group - 1, 0.0, 1.0)
    weight[4 * rounds] = inner * green(first + layers)


def grouped(plane):
    return plane.reshape(plane.shape[0] // 8, 8, plane.shape[1])


def signs(depth):
    row = lax.broadcasted_iota(jnp.int32, (8, depth), 0)
    return jnp.where(row % 2 == 0, 1.0, -1.0)


def face_rows(plane, lead):
    sums = jnp.sum(plane * lead, axis=0)
    return (
        jnp.sum(sums, axis=0, keepdims=True),
        jnp.sum(sums * signs(sums.shape[1]), axis=0, keepdims=True),
    )


def faces_kernel(
    group, length, source, before_y, table_z, ratio, weight, edge, thermal, faces, late, sweep
):
    layers, rows, depth = source.shape
    late[...] = thermal[layers - 2 :]
    first = position(group) * layers
    zero = jnp.zeros((rows, depth), F32)
    extra = dot(before_y[...], table_z[...])
    faces[...] = jnp.zeros(faces.shape, F32)
    for index in range(layers):
        faces[pl.ds(2 * length + first + index, 1), :] = extra[index : index + 1]
    forward = zero
    for index in range(layers):
        forward = source[index] + ratio[first + index] * forward
        sweep[index] = forward
    value = weight[weight.shape[0] - 1] * (ratio[first + layers] * forward)
    energy = zero
    for index in range(layers - 1, -1, -1):
        value = ratio[first + index + 1] * (sweep[index] + value)
        energy = energy + source[index] * value
    faces[pl.ds(3 * length, 8), :] = jnp.broadcast_to(total(energy), (8, depth))

    lead = grouped(edge[...])
    zero = grouped(zero)

    def down(index, previous):
        inside = (index >= first) & (index < first + layers)
        own = jnp.where(inside, source[jnp.clip(index - first, 0, layers - 1)], 0.0)
        row = faces[pl.ds(2 * length + index, 1), :]
        current = grouped(own) + lead * row + grouped(ratio[index]) * previous
        sweep[index] = current.reshape(rows, depth)
        return current

    loop(0, length, down, zero)

    def up(back, following):
        index = length - 1 - back
        value = grouped(ratio[index + 1]) * (grouped(sweep[index]) + following)
        low, high = face_rows(value, lead)
        faces[pl.ds(index, 1), :] = low
        faces[pl.ds(length + index, 1), :] = high
        return value

    loop(0, length, up, zero)


def joined(turn, group, message, other, sums, weight):
    rows, depth = weight.shape[1:]
    right = ((position(group) >> turn) & 1) == 1
    upper, lower = pl.ds(0, rows), pl.ds(rows, rows)
    left_s = jnp.where(right, other[upper, :], message[upper, :])
    right_s = jnp.where(right, message[upper, :], other[upper, :])
    left_t = jnp.where(right, other[lower, :], message[lower, :])
    right_t = jnp.where(right, message[lower, :], other[lower, :])
    own = weight[4 * turn + 2]
    before = sums[0] + jnp.where(right, left_s * own, 0.0)
    after = sums[1] + jnp.where(right, 0.0, right_t * own)
    forward = right_s + left_s * weight[4 * turn]
    backward = left_t + right_t * weight[4 * turn + 1]
    energy = 2.0 * total(left_s * right_t * weight[4 * turn + 3])
    return forward, backward, before, after, energy


def merge_kernel(
    turn, group, length, message, other, faces, other_faces, sums, weight,
    new_message, new_sums, head, tail,
):
    rows, depth = weight.shape[1:]
    forward, backward, before, after, energy = joined(turn, group, message, other, sums, weight)
    new_sums[0] = before
    new_sums[1] = after
    new_message[pl.ds(0, rows), :] = forward
    new_message[pl.ds(rows, rows), :] = backward
    low, high = pl.ds(0, length), pl.ds(length, length)
    late, number = pl.ds(2 * length, length), pl.ds(3 * length, 8)
    head[...] = faces[low, :] + other_faces[low, :]
    tail[...] = faces[high, :] + other_faces[high, :]
    new_message[pl.ds(2 * rows, length), :] = head[...]
    new_message[pl.ds(2 * rows + length, length), :] = faces[late, :] + other_faces[late, :]
    energy = faces[number, :] + other_faces[number, :] + energy
    new_message[pl.ds(2 * rows + 2 * length, 8), :] = energy


def late_solve(length, message, other, ratio, edge, late, sweep):
    rows, depth = edge.shape
    lead = grouped(edge[...])
    own = pl.ds(2 * rows + length, length)
    late[pl.ds(0, length), :] = message[own, :] + other[own, :]

    def down(index, previous):
        current = lead * late[pl.ds(index, 1), :] + grouped(ratio[index]) * previous
        sweep[index] = current.reshape(rows, depth)
        return current

    zero = jnp.zeros(lead.shape, F32)
    loop(0, length, down, zero)

    def up(back, following):
        index = length - 1 - back
        value = grouped(ratio[index + 1]) * (grouped(sweep[index]) + following)
        sweep[index] = value.reshape(rows, depth)
        late[pl.ds(length + index, 1), :] = face_rows(value, lead)[0]
        return value

    loop(0, length, up, zero)
    sweep[length] = jnp.zeros((rows, depth), F32)


def close_kernel(
    turn, group, length, message, other, sums, weight, ratio, edge, ends, late, sweep
):
    forward, backward, _, _, _ = joined(turn, group, message, other, sums, weight)
    late_solve(length, message, other, ratio, edge, late, sweep)
    ends[0] = ratio[length] * forward + sweep[length - 1]
    ends[1] = ratio[length] * backward + sweep[0]


def coarse_kernel(
    turn, group, length, alone, source, message, other, sums, faces_in, weight, ratio, edge,
    thermal, *refs
):
    precond, image, report, faces, onward, late, sweep, ends = refs[-8:]
    layers, rows, depth = source.shape
    onward[...] = thermal[:2]
    first = position(group) * layers
    below, below_far, above, above_far = faces_in
    forward, backward, before, after, energy = joined(turn, group, message, other, sums, weight)
    late_solve(length, message, other, ratio, edge, late, sweep)
    ends[0] = ratio[length] * forward + sweep[length - 1]
    ends[1] = ratio[length] * backward + sweep[0]
    beyond = ends if alone else refs[0]
    own = pl.ds(2 * rows, length)
    faces[pl.ds(0, length), :] = message[own, :] + other[own, :]
    faces[pl.ds(length, length), :] = below[...] + below_far[...]
    faces[pl.ds(2 * length, length), :] = above[...] + above_far[...]
    number = pl.ds(2 * rows + 2 * length, 8)
    energy = message[number, :] + other[number, :] + energy
    late_rows = late[pl.ds(0, length), :]
    energy = energy + total(
        late_rows * (2.0 * faces[pl.ds(0, length), :] - late[pl.ds(length, length), :])
    )
    forward = before
    for index in range(layers):
        forward = source[index] + ratio[first + index] * forward
        precond[index] = forward
    value = weight[weight.shape[0] - 1] * (after + ratio[first + layers] * forward)
    is_last = first + layers == length
    precond[layers] = jnp.where(is_last, beyond[1], value + sweep[first + layers])
    for index in range(layers - 1, -1, -1):
        value = ratio[first + index + 1] * (precond[index] + value)
        precond[index] = value + sweep[first + index]
    lead = grouped(edge[...])
    sign = signs(depth)

    def pull(index):
        below = faces[pl.ds(length + index, 1), :]
        above = faces[pl.ds(2 * length + index, 1), :]
        return below, above

    def down(index, previous):
        below, above = pull(index)
        current = lead * (below + sign * above) + grouped(ratio[index]) * previous
        if isinstance(index, int):
            if index == 0:
                current = current + grouped(beyond[0])
            if index == length - 1:
                current = current + grouped(beyond[1])
        else:
            current = current + jnp.where(index == 0, grouped(beyond[0]), 0.0)
            current = current + jnp.where(index == length - 1, grouped(beyond[1]), 0.0)
        sweep[index] = current.reshape(rows, depth)
        return current

    zero = jnp.zeros(lead.shape, F32)
    loop(0, length, down, zero)
    line = jnp.zeros((1, depth), F32)

    def up(back, carry):
        following, linked, squared = carry
        index = length - 1 - back
        value = grouped(ratio[index + 1]) * (grouped(sweep[index]) + following)
        sweep[index] = value.reshape(rows, depth)
        low, high = face_rows(value, lead)
        report[pl.ds(index, 1), :] = low
        report[pl.ds(length + index, 1), :] = high
        below, above = pull(index)
        linked = linked + faces[pl.ds(index, 1), :] * below
        squared = squared + low * below + high * above
        return value, linked, squared

    _, linked, squared = loop(0, length, up, (zero, line, line))
    sweep[length] = sweep[0]
    for index in range(layers + 1):
        image[index] = sweep[first + index]
    head, tail = sweep[0], sweep[length - 1]
    linked = 2.0 * total(linked) + total(ends[1] * beyond[0] + ends[0] * beyond[1])
    squared = total(squared) + total(head * beyond[0] + tail * beyond[1])
    crossing = 2.0 * total(head * tail)
    where = 2 * length
    report[pl.ds(where, 1), :] = energy[0:1]
    report[pl.ds(where + 1, 1), :] = jnp.broadcast_to(linked, (1, depth))
    report[pl.ds(where + 2, 1), :] = jnp.broadcast_to(squared, (1, depth))
    report[pl.ds(where + 3, 1), :] = jnp.broadcast_to(crossing, (1, depth))
    report[pl.ds(where + 4, 4), :] = jnp.zeros((4, depth), F32)


def physical_kernel(precond, image, left, right, precond_out, image_out):
    count = precond.shape[0]
    planes = [precond[index] for index in range(count)] + [image[index] for index in range(count)]
    planes = transformed(planes, left, right)
    for index in range(count):
        precond_out[index] = planes[index]
        image_out[index] = planes[count + index]


def project_kernel(
    group, length, paired, star, precond, image, faces, table_z, *refs
):
    given, (flow, pressure, field, rows_) = refs[:-4], refs[-4:]
    _, layers, rows, depth = star.shape
    first = position(group) * layers
    where = 2 * length
    reports = ring([each[...] for each in given])
    sums = reports[0][where:]
    for other in reports[1:]:
        sums = sums + other[where:]
    pairs = jnp.zeros((1, depth), F32)
    for index in range(len(reports)):
        upper, lower = reports[index], reports[(index + 1) % len(reports)]
        pairs = pairs + jnp.sum(
            upper[:length] * lower[length:where], axis=0, keepdims=True
        )
    energy, linked, squared, crossing = (sums[k : k + 1, 0:1] for k in range(4))
    if not paired:
        crossing = crossing + 2.0 * total(pairs)
    first_image = energy - linked
    step = energy / first_image
    beta = (energy * squared - linked * linked) / (first_image * first_image)
    rest = -linked / first_image
    second_image = (
        rest * rest * first_image
        + 2.0 * rest * step * (linked - squared)
        + step * step * (squared - crossing)
        - beta * beta * first_image
    )
    second_step = beta * energy / second_image
    alpha = step + second_step * (rest + beta)
    gamma = second_step * step
    for index in range(layers + 1):
        field[index] = alpha * precond[index] + gamma * image[index]
    after = rows_.at[pl.ds(rows + 8, length), :]
    after[...] = alpha * faces[pl.ds(2 * length, length), :] + gamma * reports[-1][:length]
    following = dot(after[pl.ds(first, layers), :], table_z[...])
    for index in range(layers):
        value = field[index]
        pressure[index] = value
        rows_[pl.ds(0, rows), :] = value
        rows_[pl.ds(rows, 1), :] = following[index : index + 1]
        flow[0, index] = star[0, index] - (field[index + 1] - value)
        flow[1, index] = star[1, index] - (rows_[pl.ds(1, rows), :] - value)
        flow[2, index] = star[2, index] - (lane_shift(value, 1) - value)


def ring(reports):
    if len(reports) != 4:
        return reports
    own, near, across, far = reports
    even = lax.rem(lax.axis_index("gy"), 2) == 0
    return [own, jnp.where(even, far, near), across, jnp.where(even, near, far)]


def along(array, axis, by):
    length = lax.axis_size(axis)
    return lax.ppermute(array, axis, [(i, (i + by) % length) for i in range(length)])


def swapped(array, bit, by=0):
    count_x, count_y = lax.axis_size("gx"), lax.axis_size("gy")
    pairs = [
        (x * count_y + y, (x ^ bit) * count_y + (y + by) % count_y)
        for x in range(count_x)
        for y in range(count_y)
    ]
    return lax.ppermute(array, ("gx", "gy"), pairs)


def pack(body, inputs, received, shapes, scratch, count):
    inputs = [pltpu.with_memory_space_constraint(each, pltpu.HBM) for each in inputs]
    return pl.pallas_call(
        body,
        out_shape=[jax.ShapeDtypeStruct(shape, F32) for shape in shapes],
        in_specs=[pl.BlockSpec(memory_space=pltpu.HBM)] * len(inputs) + [VMEM] * len(received),
        out_specs=[VMEM] * len(shapes),
        scratch_shapes=scratch + [pltpu.SemaphoreType.DMA((count,))],
        compiler_params=pltpu.CompilerParams(vmem_limit_bytes=4 << 20),
    )(*inputs, *received)


def per_device(melt_flow, thermal_state, powder_flag, spot_lateral_a_cell, spot_lateral_b_cell):
    layers, rows, depth = thermal_state.shape
    count_x, count_y = lax.axis_size("gx"), lax.axis_size("gy")
    group = min(count_x, BLOCK // layers)
    blocks = count_x // group
    length = group * layers
    rounds = group.bit_length() - 1
    plane = (rows, depth)
    sine_y, values_y = sines(rows)
    sine_z, values_z = sines(depth)
    left, right = packed_tables(sine_y, sine_z)
    table_z = jnp.asarray(sine_z, F32)
    edge = jnp.asarray(np.broadcast_to(sine_y[0][:, None], plane), F32)
    diagonal = jnp.asarray(2.0 + values_y[:, None] + values_z[None, :], F32)
    line = (length, depth)

    parts = melt_flow.shape[0]
    width = max(rows, depth)
    outer_planes = (2 * parts * rows + 8, width)
    ahead, behind, last_rows, first_rows = pack(
        halo_kernel,
        [melt_flow, thermal_state],
        [],
        [outer_planes, outer_planes] + [(parts + 1, layers, 8, depth)] * 2,
        [pltpu.VMEM((2,) + plane, F32)],
        6 + 4 * parts,
    )
    low_x = along(ahead, "gx", 1)
    high_x = along(behind, "gx", -1)
    low_y = along(last_rows, "gy", 1)
    high_y = along(first_rows, "gy", -1)
    (extra,) = pack(
        extra_kernel,
        [melt_flow, thermal_state, powder_flag],
        [low_y, high_y],
        [(2 * rows + 8, width)],
        [pltpu.VMEM(plane, jnp.int32), pltpu.VMEM(plane, F32)],
        3,
    )
    extra = along(extra, "gx", 1)
    ratio, weight = call(
        functools.partial(tables_kernel, group, layers),
        [diagonal],
        [(length + 1,) + plane, (4 * rounds + 1,) + plane],
    )
    marched = [melt_flow, low_x, high_x, thermal_state, powder_flag, low_y, high_y]
    padded = pltpu.VMEM((4, rows + 16, depth), F32)
    one_padded = pltpu.VMEM((1, rows + 16, depth), F32)
    (side_y,) = call(row_kernel, marched + [weight], [(layers, depth)], [padded], loose=1)
    before_y = along(side_y, "gy", 1)
    (star,) = call(
        march_kernel, marched + [side_y], [(3, layers) + plane], [padded], loose=1, flops=3 << 29
    )
    (partial,) = call(
        transform_kernel,
        [star, left, right],
        [(layers,) + plane],
        [pltpu.VMEM((rows + 16, depth), F32)],
        flops=1 << 29,
    )
    source, message = call(
        functools.partial(source_kernel, group, length),
        [melt_flow, low_x, thermal_state, extra, partial, left, right, ratio, before_y],
        [(layers,) + plane, (2 * rows, depth)],
        [one_padded],
        loose=1,
    )
    faces, late = call(
        functools.partial(faces_kernel, group, length),
        [source, before_y, table_z, ratio, weight, edge, thermal_state],
        [(3 * length + 8, depth), (2,) + plane],
        [pltpu.VMEM((max(length, layers + 1),) + plane, F32)],
    )
    alone = blocks == 1
    warm, token = call(
        heat_kernel,
        [
            spot_lateral_a_cell, spot_lateral_b_cell, thermal_state, along(late, "gx", 1),
            low_y, high_y, melt_flow,
        ],
        [(layers,) + plane, (8, depth)],
        [one_padded],
        scalars=2,
        flops=1 << 28,
    )
    sums = jnp.zeros((2,) + plane, F32)
    for turn in range(rounds - 1):
        message, sums, head, tail = call(
            functools.partial(merge_kernel, turn, group, length),
            [
                message, swapped(message, 1 << turn), faces, swapped(faces, 1 << turn),
                sums, weight,
            ],
            [(2 * rows + 2 * length + 8, depth), (2,) + plane, line, line],
        )
        if turn + 2 < rounds:
            rest = message[2 * rows + length :]
            message, faces = message[: 2 * rows], jnp.concatenate([head, tail, rest], 0)
    bit = group >> 1
    other = swapped(message, bit)
    rim = [
        swapped(tail, 0, 1), swapped(tail, bit, 1), swapped(head, 0, -1), swapped(head, bit, -1)
    ]
    outer = []
    scratch = [pltpu.VMEM((2 * length, depth), F32), pltpu.VMEM((length + 1,) + plane, F32)]
    if not alone:
        (ends,) = call(
            functools.partial(close_kernel, rounds - 1, group, length),
            [message, other, sums, weight, ratio, edge],
            [(2,) + plane],
            scratch,
        )
        outer = [jnp.stack([along(ends[0], "gx", group), along(ends[1], "gx", -group)])]
    operands = [source, message, other, sums] + rim
    operands += [weight, ratio, edge, thermal_state] + outer + [token]

    def coarse(*refs):
        coarse_kernel(rounds - 1, group, length, alone, *refs[:4], refs[4:8], *refs[8:])

    precond, image, report, faces, late = call(
        coarse,
        operands,
        [
            (layers + 1,) + plane, (layers + 1,) + plane, (2 * length + 8, depth),
            (3 * length, depth), (2,) + plane,
        ],
        scratch + [pltpu.VMEM((2,) + plane, F32)],
        loose=1,
    )
    if blocks > 1:
        onward = along(image[0], "gx", -1)
        at_end = position(group) == group - 1
        image = image.at[layers].set(jnp.where(at_end, onward, image[layers]))
        upper = along(report[:length], "gy", -1)
        crossing = jnp.sum(onward * image[layers - 1])
        crossing = crossing + jnp.sum(upper * report[length : 2 * length])
        numbers = report[2 * length :].at[3].set(2.0 * crossing)
        numbers = lax.psum(jnp.where(at_end, numbers, 0.0), "gx")
        report = report.at[2 * length :].set(numbers)
    reports = [report]
    for by in range(1, count_y):
        pairs = [(i, i ^ by if count_y == 4 else (i + by) % count_y) for i in range(count_y)]
        reports.append(lax.ppermute(report, "gy", pairs))
    precond, image = call(
        physical_kernel,
        [precond, image, left, right],
        [(layers + 1,) + plane, (layers + 1,) + plane],
    )
    late = along(late, "gx", -1)
    (warmed,) = call(heat_last_kernel, [melt_flow, late, warm], [(layers,) + plane])
    flow, pressure = call(
        functools.partial(project_kernel, group, length, blocks > 1),
        [star, precond, image, faces, table_z] + reports,
        [(3, layers) + plane, (layers,) + plane],
        [
            pltpu.VMEM((layers + 1,) + plane, F32),
            pltpu.VMEM((rows + 8 + length, depth), F32),
        ],
    )
    return (flow, warmed, pressure)


def solution(mesh):
    placed = (
        P(None, ("runs", "gx"), "gy", None),
        P(("runs", "gx"), "gy", None),
        P(("runs", "gx"), "gy", None),
        P("runs"),
        P("runs"),
    )
    return jax.shard_map(
        per_device,
        mesh=mesh,
        in_specs=placed,
        out_specs=(
            P(None, ("runs", "gx"), "gy", None),
            P(("runs", "gx"), "gy", None),
            P(("runs", "gx"), "gy", None),
        ),
        check_vma=False,
    )
```

```python
import functools
import math

import jax
import jax.numpy as jnp
import numpy as np
from jax import lax
from jax.experimental import pallas as pl
from jax.experimental.pallas import tpu as pltpu
from jax.sharding import PartitionSpec as P

BLOCK = 128

TIME_INCREMENT = 0.2
MARANGONI = 1.5
DRAG_RATE = 4.0
LASER_POWER = 3.0
SPOT_RADIUS = 5.0

F32 = jnp.float32
VMEM = pl.BlockSpec(memory_space=pltpu.VMEM)
SMEM = pl.BlockSpec(memory_space=pltpu.SMEM)


def call(body, operands, shapes, scratch=(), scalars=0, loose=0, flops=1 << 20):
    out_shape = [jax.ShapeDtypeStruct(shape, F32) for shape in shapes]
    moved = 4 * sum(math.prod(shape) for shape in shapes)
    held = moved + 4 * sum(operand.size for operand in operands)
    held += 4 * sum(math.prod(space.shape) for space in scratch)
    return pl.pallas_call(
        body,
        out_shape=out_shape,
        in_specs=[SMEM] * scalars
        + [VMEM] * (len(operands) - scalars - loose)
        + [pl.BlockSpec(memory_space=pl.ANY)] * loose,
        out_specs=[VMEM] * len(shapes),
        scratch_shapes=list(scratch),
        compiler_params=pltpu.CompilerParams(vmem_limit_bytes=held + (4 << 20)),
        cost_estimate=pl.CostEstimate(flops=flops, bytes_accessed=2 * moved, transcendentals=0),
    )(*operands)


def dot(left, right):
    return jnp.dot(left, right, precision=lax.Precision.HIGHEST, preferred_element_type=F32)


def split(cells):
    high = cells.astype(jnp.bfloat16)
    return high, (cells - high.astype(F32)).astype(jnp.bfloat16)


def folded(product):
    half = product.shape[1] // 2
    return product[:, :half] + product[:, half:]


def packed_tables(left, right):
    left_high, left_low = split(np.asarray(left, np.float32))
    right_high, right_low = split(np.asarray(right, np.float32))
    zero = np.zeros_like(right_low)
    return (
        jnp.asarray(np.concatenate([left_high, left_low], 1)),
        jnp.asarray(np.block([[right_high, right_low], [right_high, zero]])),
    )


def transformed(planes, left, right):
    rows = planes[0].shape[0]
    high, low = split(jnp.concatenate(planes, 0))
    cells = jnp.concatenate([high, low], 1)
    cells = folded(jnp.dot(cells, right[...], preferred_element_type=F32))
    out = []
    for index in range(len(planes)):
        high, low = split(cells[index * rows : (index + 1) * rows])
        upper = jnp.concatenate([high, low], 1)
        lower = jnp.concatenate([high, jnp.zeros_like(low)], 1)
        cells_ = jnp.concatenate([upper, lower], 0)
        out.append(folded(jnp.dot(left[...], cells_, preferred_element_type=F32)))
    return out


def total(cells):
    return jnp.sum(jnp.sum(cells, axis=0, keepdims=True), axis=1, keepdims=True)


def loop(low, high, body, start):
    if isinstance(high, int) and isinstance(low, int) and high - low <= 24:
        carry = start
        for index in range(low, high):
            carry = body(index, carry)
        return carry
    return lax.fori_loop(low, high, body, start)


def position(group):
    return lax.rem(lax.axis_index("gx"), group)


def sines(length):
    positions = np.arange(length) + 1.0
    step = math.pi / (length + 1)
    table = np.sqrt(2.0 / (length + 1)) * np.sin(step * positions[:, None] * positions[None, :])
    return table, 2.0 - 2.0 * np.cos(step * positions)


def lane_shift(cells, offset):
    width = cells.shape[1]
    lane = lax.broadcasted_iota(jnp.int32, cells.shape, 1)
    moved = pltpu.roll(cells, (-offset) % width, 1)
    keep = lane < width - offset if offset > 0 else lane >= -offset
    return jnp.where(keep, moved, 0.0)


def column(row):
    length = row.shape[1]
    shape = (length, length)
    same = lax.broadcasted_iota(jnp.int32, shape, 0) == lax.broadcasted_iota(jnp.int32, shape, 1)
    return jnp.sum(jnp.where(same, row, 0.0), axis=1, keepdims=True)


def coefficients(speed, scale):
    factors = [0.5 * TIME_INCREMENT * jnp.abs(each) for each in speed]
    if scale is not None:
        factors = [each * scale for each in factors]
    centre = (1.0 if scale is None else scale) - 3.0 * (factors[0] + factors[1] + factors[2])
    near, far = 4.0 * factors[2], -factors[2]
    ahead = speed[2] >= 0.0
    lane = lax.broadcasted_iota(jnp.int32, near.shape, 1)
    width = near.shape[1]
    depth = (
        jnp.where(ahead & (lane >= 1), near, 0.0),
        jnp.where(ahead & (lane >= 2), far, 0.0),
        jnp.where(ahead | (lane >= width - 1), 0.0, near),
        jnp.where(ahead | (lane >= width - 2), 0.0, far),
    )
    return centre, speed[0] >= 0.0, factors[0], speed[1] >= 0.0, factors[1], depth


def advance(layers, padded, index, weights, start=0):
    middle = layers[2]
    rows, width = middle.shape
    centre, ahead_x, factor_x, ahead_y, factor_y, depth = weights
    near = jnp.where(ahead_x, layers[1], layers[3])
    far = jnp.where(ahead_x, layers[0], layers[4])
    moved = centre * middle + factor_x * (4.0 * near - far)
    beside = lambda offset: padded[index, pl.ds(8 + offset + start, rows), :]
    near = jnp.where(ahead_y, beside(-1), beside(1))
    far = jnp.where(ahead_y, beside(-2), beside(2))
    moved = moved + factor_y * (4.0 * near - far)
    for factor, offset in zip(depth, (1, 2, width - 1, width - 2)):
        moved = moved + factor * pltpu.roll(middle, offset, 1)
    return moved


def pad_rows(padded, index, before, middle, after):
    rows = middle.shape[0]
    padded[index, pl.ds(8, rows), :] = middle
    padded[index, pl.ds(6, 2), :] = before
    padded[index, pl.ds(8 + rows, 2), :] = after


def march_layer(refs, padded, index, parts, start, count, edges=None):
    flow, low_x, high_x, thermal, flag = refs
    _, layers, rows, depth = flow.shape
    span = pl.ds(start, count)
    speed = [flow[part, index, span, :] for part in range(3)]
    drag = 1.0 / (1.0 + TIME_INCREMENT * DRAG_RATE * flag[index, span, :].astype(F32))
    top = lax.broadcasted_iota(jnp.int32, (count, depth), 1) == depth - 1
    pull = jnp.where(top, (-MARANGONI * 0.5 * TIME_INCREMENT) * drag, 0.0)
    weights = coefficients(speed, drag)
    out = []
    for part in parts:
        around = []
        for other in range(index - 2, index + 3):
            if other < 0:
                first = (2 * part + other + 2) * rows + start
                around.append(low_x[pl.ds(first, count), :])
            elif other >= layers:
                first = (2 * part + other - layers) * rows + start
                around.append(high_x[pl.ds(first, count), :])
            else:
                around.append(flow[part, other, span, :])
        moved = advance(around, padded, part, weights, start)
        if part == 0:
            behind = edges[0][start : start + count]
            before = edges[1][start : start + count]
            behind = thermal[index - 1, span, :] if index > 0 else behind
            before = thermal[index + 1, span, :] if index + 1 < layers else before
            moved = moved + pull * (before - behind)
        if part == 1:
            slope = padded[3, pl.ds(9 + start, count), :] - padded[3, pl.ds(7 + start, count), :]
            moved = moved + pull * slope
        out.append(moved)
    return out


def pad_layer(refs, low_y, high_y, padded, index):
    flow, _, _, thermal, _ = refs
    for part in range(3):
        pad_rows(
            padded, part, low_y[part, index, 6:], flow[part, index], high_y[part, index, :2]
        )
    pad_rows(padded, 3, low_y[3, index, 6:], thermal[index], high_y[3, index, :2])


def row_kernel(flow, low_x, high_x, thermal, flag, low_y, high_y, _, side_y, padded):
    refs = (flow, low_x, high_x, thermal, flag)
    _, layers, rows, depth = flow.shape
    for index in range(layers):
        for part, cells in ((1, flow.at[1, index]), (3, thermal.at[index])):
            padded[part, pl.ds(rows - 8, 16), :] = cells[pl.ds(rows - 16, 16), :]
            padded[part, pl.ds(8 + rows, 2), :] = high_y[part, index, :2]
        (value,) = march_layer(refs, padded, index, [1], rows - 8, 8)
        side_y[pl.ds(index, 1), :] = value[7:, :]


def march_kernel(
    flow, low_x, high_x, thermal, flag, low_y, high_y, _, star, padded
):
    refs = (flow, low_x, high_x, thermal, flag)
    _, layers, rows, depth = flow.shape
    edges = [column(halo[pl.ds(halo.shape[0] - 8, 1), pl.ds(0, rows)]) for halo in (low_x, high_x)]
    count = math.gcd(rows, 16)
    for index in range(layers):
        pad_layer(refs, low_y, high_y, padded, index)
        for start in range(0, rows, count):
            value = march_layer(refs, padded, index, range(3), start, count, edges)
            for part in range(3):
                star[part, index, pl.ds(start, count), :] = value[part]


def side_plane(flow, low_x, thermal, extra, padded):
    rows, depth = flow.shape[2:]
    plane = lambda index: low_x[pl.ds(index * rows, rows), pl.ds(0, depth)]
    beside = extra[pl.ds(2 * rows, 8), pl.ds(0, depth)]
    pad_rows(padded, 0, beside[2:4], plane(1), beside[4:6])
    around = [extra[pl.ds(0, rows), pl.ds(0, depth)], plane(0), plane(1), flow[0, 0], flow[0, 1]]
    top = lax.broadcasted_iota(jnp.int32, (rows, depth), 1) == depth - 1
    drag = 1.0 / (1.0 + TIME_INCREMENT * DRAG_RATE * extra[pl.ds(rows, rows), pl.ds(0, depth)])
    pull = jnp.where(top, (-MARANGONI * 0.5 * TIME_INCREMENT) * drag, 0.0)
    behind = column(extra[pl.ds(2 * rows, 1), pl.ds(0, rows)])
    weights = coefficients([plane(1), plane(3), plane(5)], drag)
    return advance(around, padded, 0, weights) + pull * (thermal[0] - behind)


def transform_kernel(star, left, right, partial, rows_):
    _, layers, rows, depth = star.shape
    rows_[pl.ds(0, 8), :] = jnp.zeros((8, depth), F32)
    planes = []
    for index in range(layers):
        rows_[pl.ds(8, rows), :] = star[1, index]
        sink = star[0, index]
        if index > 0:
            sink = sink - star[0, index - 1]
        sink = sink + (star[1, index] - rows_[pl.ds(7, rows), :])
        sink = sink + (star[2, index] - lane_shift(star[2, index], -1))
        planes.append(-sink)
    for index, plane in enumerate(transformed(planes, left, right)):
        partial[index] = plane


def source_kernel(
    group, length, flow, low_x, thermal, extra, partial, left, right, ratio, _,
    source, message, padded,
):
    layers, rows, depth = partial.shape
    first = position(group) * layers
    (onward,) = transformed([side_plane(flow, low_x, thermal, extra, padded)], left, right)
    source[0] = partial[0] + onward
    for index in range(1, layers):
        source[index] = partial[index]
    backward = partial[layers - 1]
    for index in range(layers - 2, 0, -1):
        backward = partial[index] + ratio[length - 1 - first - index] * backward
    forward = source[0]
    message[pl.ds(rows, rows), :] = forward + ratio[length - 1 - first] * backward
    for index in range(1, layers):
        forward = partial[index] + ratio[first + index] * forward
    message[pl.ds(0, rows), :] = forward


def started(copies):
    for copy in copies:
        copy.start()
    return copies


def surface(plane):
    rows, depth = plane.shape
    shape = (rows, rows)
    same = lax.broadcasted_iota(jnp.int32, shape, 0) == lax.broadcasted_iota(jnp.int32, shape, 1)
    return jnp.sum(jnp.where(same, plane[:, depth - 1 :], 0.0), axis=0, keepdims=True)


def halo_kernel(flow, thermal, ahead, behind, last_rows, first_rows, tops, sems):
    parts, layers, rows, depth = flow.shape
    pairs = [(thermal.at[layers - 1], tops.at[0]), (thermal.at[0], tops.at[1])]
    for part in range(parts):
        for layer in range(2):
            span = pl.ds((2 * part + layer) * rows, rows)
            pairs.append((flow.at[part, layers - 2 + layer], ahead.at[span, :]))
            pairs.append((flow.at[part, layer], behind.at[span, :]))
    for target, start in ((last_rows, rows - 8), (first_rows, 0)):
        span = pl.ds(start, 8)
        pairs.append((flow.at[:, :, span, :], target.at[pl.ds(0, parts)]))
        pairs.append((thermal.at[:, span, :], target.at[parts]))
    copies = started(
        [pltpu.make_async_copy(*pair, sems.at[index]) for index, pair in enumerate(pairs)]
    )
    for side, message in enumerate((ahead, behind)):
        copies[side].wait()
        row = jnp.broadcast_to(surface(tops[side]), (8, rows))
        message[pl.ds(2 * parts * rows, 8), pl.ds(0, rows)] = row
    for copy in copies[2:]:
        copy.wait()


def extra_kernel(flow, thermal, flag, low_y, high_y, extra, last, flags, sems):
    _, layers, rows, depth = flow.shape
    pairs = [(flag.at[layers - 1], flags), (thermal.at[pl.ds(layers - 2, 2)], last)]
    pairs.append((flow.at[0, layers - 3], extra.at[pl.ds(0, rows), :]))
    copies = started(
        [pltpu.make_async_copy(*pair, sems.at[index]) for index, pair in enumerate(pairs)]
    )
    base = 2 * rows
    extra[pl.ds(base, 8), :] = jnp.zeros((8, extra.shape[1]), F32)
    extra[pl.ds(base + 2, 2), pl.ds(0, depth)] = low_y[0, layers - 1, 6:, :]
    extra[pl.ds(base + 4, 2), pl.ds(0, depth)] = high_y[0, layers - 1, :2, :]
    for copy in copies[:2]:
        copy.wait()
    extra[pl.ds(rows, rows), :] = flags[...].astype(F32)
    extra[pl.ds(base, 1), pl.ds(0, rows)] = surface(last[0])
    for copy in copies[2:]:
        copy.wait()


def wrapped(distance, span):
    moved = distance + span // 2
    moved = jnp.where(moved < 0, moved + span, moved)
    moved = jnp.where(moved >= span, moved - span, moved)
    return (moved - span // 2).astype(F32)


def laser_row(index, layers, rows, spots_a, spots_b):
    total_x = layers * lax.axis_size("gx")
    total_y = rows * lax.axis_size("gy")
    cell_x = lax.axis_index("gx") * layers + index
    cells_y = lax.broadcasted_iota(jnp.int32, (1, rows), 1) + lax.axis_index("gy") * rows
    heat = jnp.zeros((1, rows), F32)
    for spot in range(spots_a.shape[0]):
        dist_x = wrapped(jnp.full((1, rows), cell_x - spots_a[spot], jnp.int32), total_x)
        dist_y = wrapped(cells_y - spots_b[spot], total_y)
        square = dist_x * dist_x + dist_y * dist_y
        heat = heat + jnp.exp(square * (-1.0 / (SPOT_RADIUS * SPOT_RADIUS)))
    return LASER_POWER * heat


def heat_kernel(
    spots_a, spots_b, thermal, low_x, high_x, low_y, high_y, flow, warmed, token, padded
):
    layers, rows, depth = thermal.shape
    token[...] = jnp.zeros(token.shape, F32)
    top = lax.broadcasted_iota(jnp.int32, (rows, depth), 1) == depth - 1
    for index in range(layers):
        pad_rows(padded, 0, low_y[3, index, 6:], thermal[index], high_y[3, index, :2])
        around = []
        for other in range(index - 2, index + 3):
            if other < 0:
                around.append(low_x[other + 2])
            elif other >= layers:
                around.append(high_x[other - layers])
            else:
                around.append(thermal[other])
        speed = [flow[part, index] for part in range(3)]
        gain = TIME_INCREMENT * column(laser_row(index, layers, rows, spots_a, spots_b))
        moved = advance(around, padded, 0, coefficients(speed, None))
        warmed[index] = moved + jnp.where(top, gain, 0.0)


def tables_kernel(group, layers, diagonal, ratio, weight):
    length = group * layers
    mine = position(group)
    first = mine * layers
    diag = diagonal[...]
    ratio[0] = jnp.zeros_like(diag)

    def step(index, previous):
        current = 1.0 / (diag - previous)
        ratio[index] = current
        return current

    loop(1, length + 1, step, jnp.zeros_like(diag))

    def decay(low, high):
        return lax.fori_loop(
            low + 1, high + 1, lambda index, value: value * ratio[index], jnp.ones_like(diag)
        )

    def green(index):
        return 1.0 / (diag - ratio[index] - ratio[jnp.maximum(length - 1 - index, 0)])

    rounds = group.bit_length() - 1
    for turn in range(rounds):
        half = 1 << turn
        right = ((mine >> turn) & 1) == 1
        start = (mine >> (turn + 1)) << (turn + 1)
        cut = (start + half) * layers
        end = (start + 2 * half) * layers
        weight[4 * turn] = decay(cut - 1, end - 1)
        weight[4 * turn + 1] = decay(length - 1 - cut, length - 1 - start * layers)
        low = jnp.where(right, cut - 1, length - 1 - cut)
        high = jnp.where(right, first - 1, length - 1 - first - layers)
        weight[4 * turn + 2] = decay(low, high)
        weight[4 * turn + 3] = green(cut) * ratio[cut]
    inner = jnp.where(mine == group - 1, 0.0, 1.0)
    weight[4 * rounds] = inner * green(first + layers)


def grouped(plane):
    return plane.reshape(plane.shape[0] // 8, 8, plane.shape[1])


def signs(depth):
    row = lax.broadcasted_iota(jnp.int32, (8, depth), 0)
    return jnp.where(row % 2 == 0, 1.0, -1.0)


def face_rows(plane, lead):
    sums = jnp.sum(plane * lead, axis=0)
    return (
        jnp.sum(sums, axis=0, keepdims=True),
        jnp.sum(sums * signs(sums.shape[1]), axis=0, keepdims=True),
    )


def faces_kernel(
    group, length, source, before_y, table_z, ratio, weight, edge, thermal, _, faces, late, sweep
):
    layers, rows, depth = source.shape
    late[...] = thermal[:2]
    first = position(group) * layers
    zero = jnp.zeros((rows, depth), F32)
    extra = dot(before_y[...], table_z[...])
    faces[...] = jnp.zeros(faces.shape, F32)
    for index in range(layers):
        faces[pl.ds(2 * length + first + index, 1), :] = extra[index : index + 1]
    forward = zero
    for index in range(layers):
        forward = source[index] + ratio[first + index] * forward
        sweep[index] = forward
    value = weight[weight.shape[0] - 1] * (ratio[first + layers] * forward)
    energy = zero
    for index in range(layers - 1, -1, -1):
        value = ratio[first + index + 1] * (sweep[index] + value)
        energy = energy + source[index] * value
    faces[pl.ds(3 * length, 8), :] = jnp.broadcast_to(total(energy), (8, depth))

    lead = grouped(edge[...])
    zero = grouped(zero)

    def down(index, previous):
        inside = (index >= first) & (index < first + layers)
        own = jnp.where(inside, source[jnp.clip(index - first, 0, layers - 1)], 0.0)
        row = faces[pl.ds(2 * length + index, 1), :]
        current = grouped(own) + lead * row + grouped(ratio[index]) * previous
        sweep[index] = current.reshape(rows, depth)
        return current

    loop(0, length, down, zero)

    def up(back, following):
        index = length - 1 - back
        value = grouped(ratio[index + 1]) * (grouped(sweep[index]) + following)
        low, high = face_rows(value, lead)
        faces[pl.ds(index, 1), :] = low
        faces[pl.ds(length + index, 1), :] = high
        return value

    loop(0, length, up, zero)


def joined(turn, group, message, other, sums, weight):
    rows, depth = weight.shape[1:]
    right = ((position(group) >> turn) & 1) == 1
    upper, lower = pl.ds(0, rows), pl.ds(rows, rows)
    left_s = jnp.where(right, other[upper, :], message[upper, :])
    right_s = jnp.where(right, message[upper, :], other[upper, :])
    left_t = jnp.where(right, other[lower, :], message[lower, :])
    right_t = jnp.where(right, message[lower, :], other[lower, :])
    own = weight[4 * turn + 2]
    before = sums[0] + jnp.where(right, left_s * own, 0.0)
    after = sums[1] + jnp.where(right, 0.0, right_t * own)
    forward = right_s + left_s * weight[4 * turn]
    backward = left_t + right_t * weight[4 * turn + 1]
    energy = 2.0 * total(left_s * right_t * weight[4 * turn + 3])
    return forward, backward, before, after, energy


def merge_kernel(
    turn, group, length, message, other, faces, other_faces, sums, weight,
    new_message, new_sums, head, tail,
):
    rows, depth = weight.shape[1:]
    forward, backward, before, after, energy = joined(turn, group, message, other, sums, weight)
    new_sums[0] = before
    new_sums[1] = after
    new_message[pl.ds(0, rows), :] = forward
    new_message[pl.ds(rows, rows), :] = backward
    low, high = pl.ds(0, length), pl.ds(length, length)
    late, number = pl.ds(2 * length, length), pl.ds(3 * length, 8)
    head[...] = faces[low, :] + other_faces[low, :]
    tail[...] = faces[high, :] + other_faces[high, :]
    new_message[pl.ds(2 * rows, length), :] = head[...]
    new_message[pl.ds(2 * rows + length, length), :] = faces[late, :] + other_faces[late, :]
    energy = faces[number, :] + other_faces[number, :] + energy
    new_message[pl.ds(2 * rows + 2 * length, 8), :] = energy


def late_solve(length, message, other, ratio, edge, late, sweep):
    rows, depth = edge.shape
    lead = grouped(edge[...])
    own = pl.ds(2 * rows + length, length)
    late[pl.ds(0, length), :] = message[own, :] + other[own, :]

    def down(index, previous):
        current = lead * late[pl.ds(index, 1), :] + grouped(ratio[index]) * previous
        sweep[index] = current.reshape(rows, depth)
        return current

    zero = jnp.zeros(lead.shape, F32)
    loop(0, length, down, zero)

    def up(back, following):
        index = length - 1 - back
        value = grouped(ratio[index + 1]) * (grouped(sweep[index]) + following)
        sweep[index] = value.reshape(rows, depth)
        late[pl.ds(length + index, 1), :] = face_rows(value, lead)[0]
        return value

    loop(0, length, up, zero)
    sweep[length] = jnp.zeros((rows, depth), F32)


def close_kernel(
    turn, group, length, message, other, sums, weight, ratio, edge, ends, late, sweep
):
    forward, backward, _, _, _ = joined(turn, group, message, other, sums, weight)
    late_solve(length, message, other, ratio, edge, late, sweep)
    ends[0] = ratio[length] * forward + sweep[length - 1]
    ends[1] = ratio[length] * backward + sweep[0]


def coarse_kernel(
    turn, group, length, alone, source, message, other, sums, faces_in, weight, ratio, edge, *refs
):
    precond, image, report, faces, late, sweep, ends = refs[-7:]
    layers, rows, depth = source.shape
    first = position(group) * layers
    below, below_far, above, above_far = faces_in
    forward, backward, before, after, energy = joined(turn, group, message, other, sums, weight)
    late_solve(length, message, other, ratio, edge, late, sweep)
    ends[0] = ratio[length] * forward + sweep[length - 1]
    ends[1] = ratio[length] * backward + sweep[0]
    beyond = ends if alone else refs[0]
    own = pl.ds(2 * rows, length)
    faces[pl.ds(0, length), :] = message[own, :] + other[own, :]
    faces[pl.ds(length, length), :] = below[...] + below_far[...]
    faces[pl.ds(2 * length, length), :] = above[...] + above_far[...]
    number = pl.ds(2 * rows + 2 * length, 8)
    energy = message[number, :] + other[number, :] + energy
    late_rows = late[pl.ds(0, length), :]
    energy = energy + total(
        late_rows * (2.0 * faces[pl.ds(0, length), :] - late[pl.ds(length, length), :])
    )
    forward = before
    for index in range(layers):
        forward = source[index] + ratio[first + index] * forward
        precond[index] = forward
    value = weight[weight.shape[0] - 1] * (after + ratio[first + layers] * forward)
    is_last = first + layers == length
    precond[layers] = jnp.where(is_last, beyond[1], value + sweep[first + layers])
    for index in range(layers - 1, -1, -1):
        value = ratio[first + index + 1] * (precond[index] + value)
        precond[index] = value + sweep[first + index]
    lead = grouped(edge[...])
    sign = signs(depth)

    def pull(index):
        below = faces[pl.ds(length + index, 1), :]
        above = faces[pl.ds(2 * length + index, 1), :]
        return below, above

    def down(index, previous):
        below, above = pull(index)
        current = lead * (below + sign * above) + grouped(ratio[index]) * previous
        if isinstance(index, int):
            if index == 0:
                current = current + grouped(beyond[0])
            if index == length - 1:
                current = current + grouped(beyond[1])
        else:
            current = current + jnp.where(index == 0, grouped(beyond[0]), 0.0)
            current = current + jnp.where(index == length - 1, grouped(beyond[1]), 0.0)
        sweep[index] = current.reshape(rows, depth)
        return current

    zero = jnp.zeros(lead.shape, F32)
    loop(0, length, down, zero)
    line = jnp.zeros((1, depth), F32)

    def up(back, carry):
        following, linked, squared = carry
        index = length - 1 - back
        value = grouped(ratio[index + 1]) * (grouped(sweep[index]) + following)
        sweep[index] = value.reshape(rows, depth)
        low, high = face_rows(value, lead)
        report[pl.ds(index, 1), :] = low
        report[pl.ds(length + index, 1), :] = high
        below, above = pull(index)
        linked = linked + faces[pl.ds(index, 1), :] * below
        squared = squared + low * below + high * above
        return value, linked, squared

    _, linked, squared = loop(0, length, up, (zero, line, line))
    sweep[length] = sweep[0]
    for index in range(layers + 1):
        image[index] = sweep[first + index]
    head, tail = sweep[0], sweep[length - 1]
    linked = 2.0 * total(linked) + total(ends[1] * beyond[0] + ends[0] * beyond[1])
    squared = total(squared) + total(head * beyond[0] + tail * beyond[1])
    crossing = 2.0 * total(head * tail)
    where = 2 * length
    report[pl.ds(where, 1), :] = energy[0:1]
    report[pl.ds(where + 1, 1), :] = jnp.broadcast_to(linked, (1, depth))
    report[pl.ds(where + 2, 1), :] = jnp.broadcast_to(squared, (1, depth))
    report[pl.ds(where + 3, 1), :] = jnp.broadcast_to(crossing, (1, depth))
    report[pl.ds(where + 4, 4), :] = jnp.zeros((4, depth), F32)


def physical_kernel(precond, image, left, right, precond_out, image_out):
    count = precond.shape[0]
    planes = [precond[index] for index in range(count)] + [image[index] for index in range(count)]
    planes = transformed(planes, left, right)
    for index in range(count):
        precond_out[index] = planes[index]
        image_out[index] = planes[count + index]


def project_kernel(
    group, length, paired, star, precond, image, faces, table_z, *refs
):
    given, (flow, pressure, field, rows_) = refs[:-4], refs[-4:]
    _, layers, rows, depth = star.shape
    first = position(group) * layers
    where = 2 * length
    reports = ring([each[...] for each in given])
    sums = reports[0][where:]
    for other in reports[1:]:
        sums = sums + other[where:]
    pairs = jnp.zeros((1, depth), F32)
    for index in range(len(reports)):
        upper, lower = reports[index], reports[(index + 1) % len(reports)]
        pairs = pairs + jnp.sum(
            upper[:length] * lower[length:where], axis=0, keepdims=True
        )
    energy, linked, squared, crossing = (sums[k : k + 1, 0:1] for k in range(4))
    if not paired:
        crossing = crossing + 2.0 * total(pairs)
    first_image = energy - linked
    step = energy / first_image
    beta = (energy * squared - linked * linked) / (first_image * first_image)
    rest = -linked / first_image
    second_image = (
        rest * rest * first_image
        + 2.0 * rest * step * (linked - squared)
        + step * step * (squared - crossing)
        - beta * beta * first_image
    )
    second_step = beta * energy / second_image
    alpha = step + second_step * (rest + beta)
    gamma = second_step * step
    for index in range(layers + 1):
        field[index] = alpha * precond[index] + gamma * image[index]
    after = rows_.at[pl.ds(rows + 8, length), :]
    after[...] = alpha * faces[pl.ds(2 * length, length), :] + gamma * reports[-1][:length]
    following = dot(after[pl.ds(first, layers), :], table_z[...])
    for index in range(layers):
        value = field[index]
        pressure[index] = value
        rows_[pl.ds(0, rows), :] = value
        rows_[pl.ds(rows, 1), :] = following[index : index + 1]
        flow[0, index] = star[0, index] - (field[index + 1] - value)
        flow[1, index] = star[1, index] - (rows_[pl.ds(1, rows), :] - value)
        flow[2, index] = star[2, index] - (lane_shift(value, 1) - value)


def ring(reports):
    if len(reports) != 4:
        return reports
    own, near, across, far = reports
    even = lax.rem(lax.axis_index("gy"), 2) == 0
    return [own, jnp.where(even, far, near), across, jnp.where(even, near, far)]


def along(array, axis, by):
    length = lax.axis_size(axis)
    return lax.ppermute(array, axis, [(i, (i + by) % length) for i in range(length)])


def swapped(array, bit, by=0):
    count_x, count_y = lax.axis_size("gx"), lax.axis_size("gy")
    pairs = [
        (x * count_y + y, (x ^ bit) * count_y + (y + by) % count_y)
        for x in range(count_x)
        for y in range(count_y)
    ]
    return lax.ppermute(array, ("gx", "gy"), pairs)


def pack(body, inputs, received, shapes, scratch, count):
    inputs = [pltpu.with_memory_space_constraint(each, pltpu.HBM) for each in inputs]
    return pl.pallas_call(
        body,
        out_shape=[jax.ShapeDtypeStruct(shape, F32) for shape in shapes],
        in_specs=[pl.BlockSpec(memory_space=pltpu.HBM)] * len(inputs) + [VMEM] * len(received),
        out_specs=[VMEM] * len(shapes),
        scratch_shapes=scratch + [pltpu.SemaphoreType.DMA((count,))],
        compiler_params=pltpu.CompilerParams(vmem_limit_bytes=4 << 20),
    )(*inputs, *received)


def per_device(melt_flow, thermal_state, powder_flag, spot_lateral_a_cell, spot_lateral_b_cell):
    layers, rows, depth = thermal_state.shape
    count_x, count_y = lax.axis_size("gx"), lax.axis_size("gy")
    group = min(count_x, BLOCK // layers)
    blocks = count_x // group
    length = group * layers
    rounds = group.bit_length() - 1
    plane = (rows, depth)
    sine_y, values_y = sines(rows)
    sine_z, values_z = sines(depth)
    left, right = packed_tables(sine_y, sine_z)
    table_z = jnp.asarray(sine_z, F32)
    edge = jnp.asarray(np.broadcast_to(sine_y[0][:, None], plane), F32)
    diagonal = jnp.asarray(2.0 + values_y[:, None] + values_z[None, :], F32)
    line = (length, depth)

    parts = melt_flow.shape[0]
    width = max(rows, depth)
    outer_planes = (2 * parts * rows + 8, width)
    ahead, behind, last_rows, first_rows = pack(
        halo_kernel,
        [melt_flow, thermal_state],
        [],
        [outer_planes, outer_planes] + [(parts + 1, layers, 8, depth)] * 2,
        [pltpu.VMEM((2,) + plane, F32)],
        6 + 4 * parts,
    )
    low_x = along(ahead, "gx", 1)
    high_x = along(behind, "gx", -1)
    low_y = along(last_rows, "gy", 1)
    high_y = along(first_rows, "gy", -1)
    extra, last = pack(
        extra_kernel,
        [melt_flow, thermal_state, powder_flag],
        [low_y, high_y],
        [(2 * rows + 8, width), (2,) + plane],
        [pltpu.VMEM(plane, jnp.int32)],
        3,
    )
    extra = along(extra, "gx", 1)
    early_low = along(last, "gx", 1)
    ratio, weight = call(
        functools.partial(tables_kernel, group, layers),
        [diagonal],
        [(length + 1,) + plane, (4 * rounds + 1,) + plane],
    )
    marched = [melt_flow, low_x, high_x, thermal_state, powder_flag, low_y, high_y]
    padded = pltpu.VMEM((4, rows + 16, depth), F32)
    one_padded = pltpu.VMEM((1, rows + 16, depth), F32)
    (side_y,) = call(row_kernel, marched + [weight], [(layers, depth)], [padded], loose=1)
    before_y = along(side_y, "gy", 1)
    (star,) = call(
        march_kernel, marched + [side_y], [(3, layers) + plane], [padded], loose=1, flops=3 << 27
    )
    (partial,) = call(
        transform_kernel,
        [star, left, right],
        [(layers,) + plane],
        [pltpu.VMEM((rows + 16, depth), F32)],
        flops=1 << 27,
    )
    source, message = call(
        functools.partial(source_kernel, group, length),
        [melt_flow, low_x, thermal_state, extra, partial, left, right, ratio, before_y],
        [(layers,) + plane, (2 * rows, depth)],
        [one_padded],
        loose=1,
    )
    faces, late = call(
        functools.partial(faces_kernel, group, length),
        [source, before_y, table_z, ratio, weight, edge, thermal_state, early_low],
        [(3 * length + 8, depth), (2,) + plane],
        [pltpu.VMEM((max(length, layers + 1),) + plane, F32)],
        loose=1,
    )
    alone = blocks == 1
    early_high = along(late, "gx", -1)
    warmed, token = call(
        heat_kernel,
        [
            spot_lateral_a_cell, spot_lateral_b_cell, thermal_state, early_low, early_high,
            low_y, high_y, melt_flow,
        ],
        [(layers,) + plane, (8, depth)],
        [one_padded],
        scalars=2,
        flops=1 << 28,
    )
    sums = jnp.zeros((2,) + plane, F32)
    for turn in range(rounds - 1):
        message, sums, head, tail = call(
            functools.partial(merge_kernel, turn, group, length),
            [
                message, swapped(message, 1 << turn), faces, swapped(faces, 1 << turn),
                sums, weight,
            ],
            [(2 * rows + 2 * length + 8, depth), (2,) + plane, line, line],
        )
        if turn + 2 < rounds:
            rest = message[2 * rows + length :]
            message, faces = message[: 2 * rows], jnp.concatenate([head, tail, rest], 0)
    bit = group >> 1
    other = swapped(message, bit)
    rim = [
        swapped(tail, 0, 1), swapped(tail, bit, 1), swapped(head, 0, -1), swapped(head, bit, -1)
    ]
    outer = []
    scratch = [pltpu.VMEM((2 * length, depth), F32), pltpu.VMEM((length + 1,) + plane, F32)]
    if not alone:
        (ends,) = call(
            functools.partial(close_kernel, rounds - 1, group, length),
            [message, other, sums, weight, ratio, edge],
            [(2,) + plane],
            scratch,
        )
        outer = [jnp.stack([along(ends[0], "gx", group), along(ends[1], "gx", -group)])]
    operands = [source, message, other, sums] + rim
    operands += [weight, ratio, edge] + outer + [token]

    def coarse(*refs):
        coarse_kernel(rounds - 1, group, length, alone, *refs[:4], refs[4:8], *refs[8:])

    precond, image, report, faces = call(
        coarse,
        operands,
        [
            (layers + 1,) + plane, (layers + 1,) + plane, (2 * length + 8, depth),
            (3 * length, depth),
        ],
        scratch + [pltpu.VMEM((2,) + plane, F32)],
        loose=1,
    )
    if blocks > 1:
        onward = along(image[0], "gx", -1)
        at_end = position(group) == group - 1
        image = image.at[layers].set(jnp.where(at_end, onward, image[layers]))
        upper = along(report[:length], "gy", -1)
        crossing = jnp.sum(onward * image[layers - 1])
        crossing = crossing + jnp.sum(upper * report[length : 2 * length])
        numbers = report[2 * length :].at[3].set(2.0 * crossing)
        numbers = lax.psum(jnp.where(at_end, numbers, 0.0), "gx")
        report = report.at[2 * length :].set(numbers)
    reports = [report]
    for by in range(1, count_y):
        pairs = [(i, i ^ by if count_y == 4 else (i + by) % count_y) for i in range(count_y)]
        reports.append(lax.ppermute(report, "gy", pairs))
    precond, image = call(
        physical_kernel,
        [precond, image, left, right],
        [(layers + 1,) + plane, (layers + 1,) + plane],
    )
    flow, pressure = call(
        functools.partial(project_kernel, group, length, blocks > 1),
        [star, precond, image, faces, table_z] + reports,
        [(3, layers) + plane, (layers,) + plane],
        [
            pltpu.VMEM((layers + 1,) + plane, F32),
            pltpu.VMEM((rows + 8 + length, depth), F32),
        ],
    )
    return (flow, warmed, pressure)


def solution(mesh):
    placed = (
        P(None, ("runs", "gx"), "gy", None),
        P(("runs", "gx"), "gy", None),
        P(("runs", "gx"), "gy", None),
        P("runs"),
        P("runs"),
    )
    return jax.shard_map(
        per_device,
        mesh=mesh,
        in_specs=placed,
        out_specs=(
            P(None, ("runs", "gx"), "gy", None),
            P(("runs", "gx"), "gy", None),
            P(("runs", "gx"), "gy", None),
        ),
        check_vma=False,
    )
```

```python
import functools
import math

import jax
import jax.numpy as jnp
import numpy as np
from jax import lax
from jax.experimental import pallas as pl
from jax.experimental.pallas import tpu as pltpu
from jax.sharding import PartitionSpec as P

BLOCK = 128

TIME_INCREMENT = 0.2
MARANGONI = 1.5
DRAG_RATE = 4.0
LASER_POWER = 3.0
SPOT_RADIUS = 5.0

F32 = jnp.float32
VMEM = pl.BlockSpec(memory_space=pltpu.VMEM)
SMEM = pl.BlockSpec(memory_space=pltpu.SMEM)


def call(body, operands, shapes, scratch=(), scalars=0, loose=0, flops=1 << 20):
    out_shape = [jax.ShapeDtypeStruct(shape, F32) for shape in shapes]
    moved = 4 * sum(math.prod(shape) for shape in shapes)
    held = moved + 4 * sum(operand.size for operand in operands)
    held += 4 * sum(math.prod(space.shape) for space in scratch)
    return pl.pallas_call(
        body,
        out_shape=out_shape,
        in_specs=[SMEM] * scalars
        + [VMEM] * (len(operands) - scalars - loose)
        + [pl.BlockSpec(memory_space=pl.ANY)] * loose,
        out_specs=[VMEM] * len(shapes),
        scratch_shapes=list(scratch),
        compiler_params=pltpu.CompilerParams(vmem_limit_bytes=held + (4 << 20)),
        cost_estimate=pl.CostEstimate(flops=flops, bytes_accessed=2 * moved, transcendentals=0),
    )(*operands)


def dot(left, right):
    return jnp.dot(left, right, precision=lax.Precision.HIGHEST, preferred_element_type=F32)


def split(cells):
    high = cells.astype(jnp.bfloat16)
    return high, (cells - high.astype(F32)).astype(jnp.bfloat16)


def folded(product):
    half = product.shape[1] // 2
    return product[:, :half] + product[:, half:]


def packed_tables(left, right):
    left_high, left_low = split(np.asarray(left, np.float32))
    right_high, right_low = split(np.asarray(right, np.float32))
    zero = np.zeros_like(right_low)
    return (
        jnp.asarray(np.concatenate([left_high, left_low], 1)),
        jnp.asarray(np.block([[right_high, right_low], [right_high, zero]])),
    )


def transformed(planes, left, right):
    rows = planes[0].shape[0]
    high, low = split(jnp.concatenate(planes, 0))
    cells = jnp.concatenate([high, low], 1)
    cells = folded(jnp.dot(cells, right[...], preferred_element_type=F32))
    out = []
    for index in range(len(planes)):
        high, low = split(cells[index * rows : (index + 1) * rows])
        upper = jnp.concatenate([high, low], 1)
        lower = jnp.concatenate([high, jnp.zeros_like(low)], 1)
        cells_ = jnp.concatenate([upper, lower], 0)
        out.append(folded(jnp.dot(left[...], cells_, preferred_element_type=F32)))
    return out


def total(cells):
    return jnp.sum(jnp.sum(cells, axis=0, keepdims=True), axis=1, keepdims=True)


def loop(low, high, body, start):
    if isinstance(high, int) and isinstance(low, int) and high - low <= 24:
        carry = start
        for index in range(low, high):
            carry = body(index, carry)
        return carry
    return lax.fori_loop(low, high, body, start)


def position(group):
    return lax.rem(lax.axis_index("gx"), group)


def sines(length):
    positions = np.arange(length) + 1.0
    step = math.pi / (length + 1)
    table = np.sqrt(2.0 / (length + 1)) * np.sin(step * positions[:, None] * positions[None, :])
    return table, 2.0 - 2.0 * np.cos(step * positions)


def lane_shift(cells, offset):
    width = cells.shape[1]
    lane = lax.broadcasted_iota(jnp.int32, cells.shape, 1)
    moved = pltpu.roll(cells, (-offset) % width, 1)
    keep = lane < width - offset if offset > 0 else lane >= -offset
    return jnp.where(keep, moved, 0.0)


def column(row):
    length = row.shape[1]
    shape = (length, length)
    same = lax.broadcasted_iota(jnp.int32, shape, 0) == lax.broadcasted_iota(jnp.int32, shape, 1)
    return jnp.sum(jnp.where(same, row, 0.0), axis=1, keepdims=True)


def coefficients(speed, scale):
    factors = [0.5 * TIME_INCREMENT * jnp.abs(each) for each in speed]
    if scale is not None:
        factors = [each * scale for each in factors]
    centre = (1.0 if scale is None else scale) - 3.0 * (factors[0] + factors[1] + factors[2])
    near, far = 4.0 * factors[2], -factors[2]
    ahead = speed[2] >= 0.0
    lane = lax.broadcasted_iota(jnp.int32, near.shape, 1)
    width = near.shape[1]
    depth = (
        jnp.where(ahead & (lane >= 1), near, 0.0),
        jnp.where(ahead & (lane >= 2), far, 0.0),
        jnp.where(ahead | (lane >= width - 1), 0.0, near),
        jnp.where(ahead | (lane >= width - 2), 0.0, far),
    )
    return centre, speed[0] >= 0.0, factors[0], speed[1] >= 0.0, factors[1], depth


def advance(layers, padded, index, weights, start=0):
    middle = layers[2]
    rows, width = middle.shape
    centre, ahead_x, factor_x, ahead_y, factor_y, depth = weights
    near = jnp.where(ahead_x, layers[1], layers[3])
    far = jnp.where(ahead_x, layers[0], layers[4])
    moved = centre * middle + factor_x * (4.0 * near - far)
    beside = lambda offset: padded[index, pl.ds(8 + offset + start, rows), :]
    near = jnp.where(ahead_y, beside(-1), beside(1))
    far = jnp.where(ahead_y, beside(-2), beside(2))
    moved = moved + factor_y * (4.0 * near - far)
    for factor, offset in zip(depth, (1, 2, width - 1, width - 2)):
        moved = moved + factor * pltpu.roll(middle, offset, 1)
    return moved


def pad_rows(padded, index, before, middle, after):
    rows = middle.shape[0]
    padded[index, pl.ds(8, rows), :] = middle
    padded[index, pl.ds(6, 2), :] = before
    padded[index, pl.ds(8 + rows, 2), :] = after


def march_layer(refs, padded, index, parts, start, count, edges=None):
    flow, low_x, high_x, thermal, flag = refs
    _, layers, rows, depth = flow.shape
    span = pl.ds(start, count)
    speed = [flow[part, index, span, :] for part in range(3)]
    drag = 1.0 / (1.0 + TIME_INCREMENT * DRAG_RATE * flag[index, span, :].astype(F32))
    top = lax.broadcasted_iota(jnp.int32, (count, depth), 1) == depth - 1
    pull = jnp.where(top, (-MARANGONI * 0.5 * TIME_INCREMENT) * drag, 0.0)
    weights = coefficients(speed, drag)
    out = []
    for part in parts:
        around = []
        for other in range(index - 2, index + 3):
            if other < 0:
                first = (2 * part + other + 2) * rows + start
                around.append(low_x[pl.ds(first, count), :])
            elif other >= layers:
                first = (2 * part + other - layers) * rows + start
                around.append(high_x[pl.ds(first, count), :])
            else:
                around.append(flow[part, other, span, :])
        moved = advance(around, padded, part, weights, start)
        if part == 0:
            behind = edges[0][start : start + count]
            before = edges[1][start : start + count]
            behind = thermal[index - 1, span, :] if index > 0 else behind
            before = thermal[index + 1, span, :] if index + 1 < layers else before
            moved = moved + pull * (before - behind)
        if part == 1:
            slope = padded[3, pl.ds(9 + start, count), :] - padded[3, pl.ds(7 + start, count), :]
            moved = moved + pull * slope
        out.append(moved)
    return out


def pad_layer(refs, low_y, high_y, padded, index):
    flow, _, _, thermal, _ = refs
    for part in range(3):
        pad_rows(
            padded, part, low_y[part, index, 6:], flow[part, index], high_y[part, index, :2]
        )
    pad_rows(padded, 3, low_y[3, index, 6:], thermal[index], high_y[3, index, :2])


def row_kernel(flow, low_x, high_x, thermal, flag, low_y, high_y, _, side_y, padded):
    refs = (flow, low_x, high_x, thermal, flag)
    _, layers, rows, depth = flow.shape
    for index in range(layers):
        for part, cells in ((1, flow.at[1, index]), (3, thermal.at[index])):
            padded[part, pl.ds(rows - 8, 16), :] = cells[pl.ds(rows - 16, 16), :]
            padded[part, pl.ds(8 + rows, 2), :] = high_y[part, index, :2]
        (value,) = march_layer(refs, padded, index, [1], rows - 8, 8)
        side_y[pl.ds(index, 1), :] = value[7:, :]


def march_kernel(
    flow, low_x, high_x, thermal, flag, low_y, high_y, _, star, padded
):
    refs = (flow, low_x, high_x, thermal, flag)
    _, layers, rows, depth = flow.shape
    edges = [column(halo[pl.ds(halo.shape[0] - 8, 1), pl.ds(0, rows)]) for halo in (low_x, high_x)]
    count = math.gcd(rows, 16)
    for index in range(layers):
        pad_layer(refs, low_y, high_y, padded, index)
        for start in range(0, rows, count):
            value = march_layer(refs, padded, index, range(3), start, count, edges)
            for part in range(3):
                star[part, index, pl.ds(start, count), :] = value[part]


def side_plane(flow, low_x, thermal, extra, padded):
    rows, depth = flow.shape[2:]
    plane = lambda index: low_x[pl.ds(index * rows, rows), pl.ds(0, depth)]
    beside = extra[pl.ds(rows, 8), pl.ds(0, depth)]
    given = extra[pl.ds(0, rows), pl.ds(0, depth)]
    pad_rows(padded, 0, beside[2:4], plane(1), beside[4:6])
    none = jnp.zeros((rows, depth), F32)
    around = [none, plane(0), plane(1), flow[0, 0], flow[0, 1]]
    moved = advance(around, padded, 0, coefficients([plane(1), plane(3), plane(5)], given))
    moved = jnp.where(plane(1) >= 0.0, given, moved)
    top = lax.broadcasted_iota(jnp.int32, (rows, depth), 1) == depth - 1
    behind = column(extra[pl.ds(rows, 1), pl.ds(0, rows)])
    drag = column(extra[pl.ds(rows + 6, 1), pl.ds(0, rows)])
    pull = (-MARANGONI * 0.5 * TIME_INCREMENT) * drag
    return moved + jnp.where(top, pull * (thermal[0] - behind), 0.0)


def transform_kernel(star, left, right, partial, rows_):
    _, layers, rows, depth = star.shape
    rows_[pl.ds(0, 8), :] = jnp.zeros((8, depth), F32)
    planes = []
    for index in range(layers):
        rows_[pl.ds(8, rows), :] = star[1, index]
        sink = star[0, index]
        if index > 0:
            sink = sink - star[0, index - 1]
        sink = sink + (star[1, index] - rows_[pl.ds(7, rows), :])
        sink = sink + (star[2, index] - lane_shift(star[2, index], -1))
        planes.append(-sink)
    for index, plane in enumerate(transformed(planes, left, right)):
        partial[index] = plane


def source_kernel(
    group, length, flow, low_x, thermal, extra, partial, left, right, ratio, _,
    source, message, padded,
):
    layers, rows, depth = partial.shape
    first = position(group) * layers
    (onward,) = transformed([side_plane(flow, low_x, thermal, extra, padded)], left, right)
    source[0] = partial[0] + onward
    for index in range(1, layers):
        source[index] = partial[index]
    backward = partial[layers - 1]
    for index in range(layers - 2, 0, -1):
        backward = partial[index] + ratio[length - 1 - first - index] * backward
    forward = source[0]
    message[pl.ds(rows, rows), :] = forward + ratio[length - 1 - first] * backward
    for index in range(1, layers):
        forward = partial[index] + ratio[first + index] * forward
    message[pl.ds(0, rows), :] = forward


def started(copies):
    for copy in copies:
        copy.start()
    return copies


def surface(plane):
    rows, depth = plane.shape
    shape = (rows, rows)
    same = lax.broadcasted_iota(jnp.int32, shape, 0) == lax.broadcasted_iota(jnp.int32, shape, 1)
    return jnp.sum(jnp.where(same, plane[:, depth - 1 :], 0.0), axis=0, keepdims=True)


def halo_kernel(flow, thermal, ahead, behind, last_rows, first_rows, tops, sems):
    parts, layers, rows, depth = flow.shape
    pairs = [(thermal.at[layers - 1], tops.at[0]), (thermal.at[0], tops.at[1])]
    for part in range(parts):
        for layer in range(2):
            span = pl.ds((2 * part + layer) * rows, rows)
            pairs.append((flow.at[part, layers - 2 + layer], ahead.at[span, :]))
            pairs.append((flow.at[part, layer], behind.at[span, :]))
    for target, start in ((last_rows, rows - 8), (first_rows, 0)):
        span = pl.ds(start, 8)
        pairs.append((flow.at[:, :, span, :], target.at[pl.ds(0, parts)]))
        pairs.append((thermal.at[:, span, :], target.at[parts]))
    copies = started(
        [pltpu.make_async_copy(*pair, sems.at[index]) for index, pair in enumerate(pairs)]
    )
    for side, message in enumerate((ahead, behind)):
        copies[side].wait()
        row = jnp.broadcast_to(surface(tops[side]), (8, rows))
        message[pl.ds(2 * parts * rows, 8), pl.ds(0, rows)] = row
    for copy in copies[2:]:
        copy.wait()


def extra_kernel(
    flow, thermal, flag, low_y, high_y, extra, last, planes, flags, padded, sems
):
    _, layers, rows, depth = flow.shape
    pairs = [(flag.at[layers - 1], flags), (thermal.at[pl.ds(layers - 2, 2)], last)]
    sources = [(0, layers - 3), (0, layers - 2), (0, layers - 1), (1, layers - 1), (2, layers - 1)]
    for index, (part, layer) in enumerate(sources):
        pairs.append((flow.at[part, layer], planes.at[index]))
    copies = started(
        [pltpu.make_async_copy(*pair, sems.at[index]) for index, pair in enumerate(pairs)]
    )
    extra[pl.ds(rows, 8), :] = jnp.zeros((8, extra.shape[1]), F32)
    extra[pl.ds(rows + 2, 2), pl.ds(0, depth)] = low_y[0, layers - 1, 6:, :]
    extra[pl.ds(rows + 4, 2), pl.ds(0, depth)] = high_y[0, layers - 1, :2, :]
    for copy in copies:
        copy.wait()
    speed = [planes[index] for index in (2, 3, 4)]
    drag = 1.0 / (1.0 + TIME_INCREMENT * DRAG_RATE * flags[...].astype(F32))
    pad_rows(padded, 0, low_y[0, layers - 1, 6:], speed[0], high_y[0, layers - 1, :2])
    none = jnp.zeros((rows, depth), F32)
    around = [planes[0], planes[1], speed[0], none, none]
    moved = advance(around, padded, 0, coefficients(speed, drag))
    extra[pl.ds(0, rows), pl.ds(0, depth)] = jnp.where(speed[0] >= 0.0, moved, drag)
    extra[pl.ds(rows, 1), pl.ds(0, rows)] = surface(last[0])
    extra[pl.ds(rows + 6, 1), pl.ds(0, rows)] = surface(drag)


def wrapped(distance, span):
    moved = distance + span // 2
    moved = jnp.where(moved < 0, moved + span, moved)
    moved = jnp.where(moved >= span, moved - span, moved)
    return (moved - span // 2).astype(F32)


def laser_row(index, layers, rows, spots_a, spots_b):
    total_x = layers * lax.axis_size("gx")
    total_y = rows * lax.axis_size("gy")
    cell_x = lax.axis_index("gx") * layers + index
    cells_y = lax.broadcasted_iota(jnp.int32, (1, rows), 1) + lax.axis_index("gy") * rows
    heat = jnp.zeros((1, rows), F32)
    for spot in range(spots_a.shape[0]):
        dist_x = wrapped(jnp.full((1, rows), cell_x - spots_a[spot], jnp.int32), total_x)
        dist_y = wrapped(cells_y - spots_b[spot], total_y)
        square = dist_x * dist_x + dist_y * dist_y
        heat = heat + jnp.exp(square * (-1.0 / (SPOT_RADIUS * SPOT_RADIUS)))
    return LASER_POWER * heat


def heat_kernel(
    spots_a, spots_b, thermal, low_x, high_x, low_y, high_y, flow, warmed, token, padded
):
    layers, rows, depth = thermal.shape
    token[...] = jnp.zeros(token.shape, F32)
    top = lax.broadcasted_iota(jnp.int32, (rows, depth), 1) == depth - 1
    for index in range(layers):
        pad_rows(padded, 0, low_y[3, index, 6:], thermal[index], high_y[3, index, :2])
        around = []
        for other in range(index - 2, index + 3):
            if other < 0:
                around.append(low_x[other + 2])
            elif other >= layers:
                around.append(high_x[other - layers])
            else:
                around.append(thermal[other])
        speed = [flow[part, index] for part in range(3)]
        gain = TIME_INCREMENT * column(laser_row(index, layers, rows, spots_a, spots_b))
        moved = advance(around, padded, 0, coefficients(speed, None))
        warmed[index] = moved + jnp.where(top, gain, 0.0)


def tables_kernel(group, layers, diagonal, ratio, weight):
    length = group * layers
    mine = position(group)
    first = mine * layers
    diag = diagonal[...]
    ratio[0] = jnp.zeros_like(diag)

    def step(index, previous):
        current = 1.0 / (diag - previous)
        ratio[index] = current
        return current

    loop(1, length + 1, step, jnp.zeros_like(diag))

    def decay(low, high):
        return lax.fori_loop(
            low + 1, high + 1, lambda index, value: value * ratio[index], jnp.ones_like(diag)
        )

    def green(index):
        return 1.0 / (diag - ratio[index] - ratio[jnp.maximum(length - 1 - index, 0)])

    rounds = group.bit_length() - 1
    for turn in range(rounds):
        half = 1 << turn
        right = ((mine >> turn) & 1) == 1
        start = (mine >> (turn + 1)) << (turn + 1)
        cut = (start + half) * layers
        end = (start + 2 * half) * layers
        weight[4 * turn] = decay(cut - 1, end - 1)
        weight[4 * turn + 1] = decay(length - 1 - cut, length - 1 - start * layers)
        low = jnp.where(right, cut - 1, length - 1 - cut)
        high = jnp.where(right, first - 1, length - 1 - first - layers)
        weight[4 * turn + 2] = decay(low, high)
        weight[4 * turn + 3] = green(cut) * ratio[cut]
    inner = jnp.where(mine == group - 1, 0.0, 1.0)
    weight[4 * rounds] = inner * green(first + layers)


def grouped(plane):
    return plane.reshape(plane.shape[0] // 8, 8, plane.shape[1])


def signs(depth):
    row = lax.broadcasted_iota(jnp.int32, (8, depth), 0)
    return jnp.where(row % 2 == 0, 1.0, -1.0)


def face_rows(plane, lead):
    sums = jnp.sum(plane * lead, axis=0)
    return (
        jnp.sum(sums, axis=0, keepdims=True),
        jnp.sum(sums * signs(sums.shape[1]), axis=0, keepdims=True),
    )


def faces_kernel(
    group, length, source, before_y, table_z, ratio, weight, edge, thermal, _, faces, late, sweep
):
    layers, rows, depth = source.shape
    late[...] = thermal[:2]
    first = position(group) * layers
    zero = jnp.zeros((rows, depth), F32)
    extra = dot(before_y[...], table_z[...])
    faces[...] = jnp.zeros(faces.shape, F32)
    for index in range(layers):
        faces[pl.ds(2 * length + first + index, 1), :] = extra[index : index + 1]
    forward = zero
    for index in range(layers):
        forward = source[index] + ratio[first + index] * forward
        sweep[index] = forward
    value = weight[weight.shape[0] - 1] * (ratio[first + layers] * forward)
    energy = zero
    for index in range(layers - 1, -1, -1):
        value = ratio[first + index + 1] * (sweep[index] + value)
        energy = energy + source[index] * value
    faces[pl.ds(3 * length, 8), :] = jnp.broadcast_to(total(energy), (8, depth))

    lead = grouped(edge[...])
    zero = grouped(zero)

    def down(index, previous):
        inside = (index >= first) & (index < first + layers)
        own = jnp.where(inside, source[jnp.clip(index - first, 0, layers - 1)], 0.0)
        row = faces[pl.ds(2 * length + index, 1), :]
        current = grouped(own) + lead * row + grouped(ratio[index]) * previous
        sweep[index] = current.reshape(rows, depth)
        return current

    loop(0, length, down, zero)

    def up(back, following):
        index = length - 1 - back
        value = grouped(ratio[index + 1]) * (grouped(sweep[index]) + following)
        low, high = face_rows(value, lead)
        faces[pl.ds(index, 1), :] = low
        faces[pl.ds(length + index, 1), :] = high
        return value

    loop(0, length, up, zero)


def joined(turn, group, message, other, sums, weight):
    rows, depth = weight.shape[1:]
    right = ((position(group) >> turn) & 1) == 1
    upper, lower = pl.ds(0, rows), pl.ds(rows, rows)
    left_s = jnp.where(right, other[upper, :], message[upper, :])
    right_s = jnp.where(right, message[upper, :], other[upper, :])
    left_t = jnp.where(right, other[lower, :], message[lower, :])
    right_t = jnp.where(right, message[lower, :], other[lower, :])
    own = weight[4 * turn + 2]
    before = sums[0] + jnp.where(right, left_s * own, 0.0)
    after = sums[1] + jnp.where(right, 0.0, right_t * own)
    forward = right_s + left_s * weight[4 * turn]
    backward = left_t + right_t * weight[4 * turn + 1]
    energy = 2.0 * total(left_s * right_t * weight[4 * turn + 3])
    return forward, backward, before, after, energy


def merge_kernel(
    turn, group, length, message, other, faces, other_faces, sums, weight,
    new_message, new_sums, head, tail,
):
    rows, depth = weight.shape[1:]
    forward, backward, before, after, energy = joined(turn, group, message, other, sums, weight)
    new_sums[0] = before
    new_sums[1] = after
    new_message[pl.ds(0, rows), :] = forward
    new_message[pl.ds(rows, rows), :] = backward
    low, high = pl.ds(0, length), pl.ds(length, length)
    late, number = pl.ds(2 * length, length), pl.ds(3 * length, 8)
    head[...] = faces[low, :] + other_faces[low, :]
    tail[...] = faces[high, :] + other_faces[high, :]
    new_message[pl.ds(2 * rows, length), :] = head[...]
    new_message[pl.ds(2 * rows + length, length), :] = faces[late, :] + other_faces[late, :]
    energy = faces[number, :] + other_faces[number, :] + energy
    new_message[pl.ds(2 * rows + 2 * length, 8), :] = energy


def late_solve(length, message, other, ratio, edge, late, sweep):
    rows, depth = edge.shape
    lead = grouped(edge[...])
    own = pl.ds(2 * rows + length, length)
    late[pl.ds(0, length), :] = message[own, :] + other[own, :]

    def down(index, previous):
        current = lead * late[pl.ds(index, 1), :] + grouped(ratio[index]) * previous
        sweep[index] = current.reshape(rows, depth)
        return current

    zero = jnp.zeros(lead.shape, F32)
    loop(0, length, down, zero)

    def up(back, following):
        index = length - 1 - back
        value = grouped(ratio[index + 1]) * (grouped(sweep[index]) + following)
        sweep[index] = value.reshape(rows, depth)
        late[pl.ds(length + index, 1), :] = face_rows(value, lead)[0]
        return value

    loop(0, length, up, zero)
    sweep[length] = jnp.zeros((rows, depth), F32)


def close_kernel(
    turn, group, length, message, other, sums, weight, ratio, edge, ends, late, sweep
):
    forward, backward, _, _, _ = joined(turn, group, message, other, sums, weight)
    late_solve(length, message, other, ratio, edge, late, sweep)
    ends[0] = ratio[length] * forward + sweep[length - 1]
    ends[1] = ratio[length] * backward + sweep[0]


def coarse_kernel(
    turn, group, length, alone, source, message, other, sums, faces_in, weight, ratio, edge, *refs
):
    precond, image, report, faces, late, sweep, ends = refs[-7:]
    layers, rows, depth = source.shape
    first = position(group) * layers
    below, below_far, above, above_far = faces_in
    forward, backward, before, after, energy = joined(turn, group, message, other, sums, weight)
    late_solve(length, message, other, ratio, edge, late, sweep)
    ends[0] = ratio[length] * forward + sweep[length - 1]
    ends[1] = ratio[length] * backward + sweep[0]
    beyond = ends if alone else refs[0]
    own = pl.ds(2 * rows, length)
    faces[pl.ds(0, length), :] = message[own, :] + other[own, :]
    faces[pl.ds(length, length), :] = below[...] + below_far[...]
    faces[pl.ds(2 * length, length), :] = above[...] + above_far[...]
    number = pl.ds(2 * rows + 2 * length, 8)
    energy = message[number, :] + other[number, :] + energy
    late_rows = late[pl.ds(0, length), :]
    energy = energy + total(
        late_rows * (2.0 * faces[pl.ds(0, length), :] - late[pl.ds(length, length), :])
    )
    forward = before
    for index in range(layers):
        forward = source[index] + ratio[first + index] * forward
        precond[index] = forward
    value = weight[weight.shape[0] - 1] * (after + ratio[first + layers] * forward)
    is_last = first + layers == length
    precond[layers] = jnp.where(is_last, beyond[1], value + sweep[first + layers])
    for index in range(layers - 1, -1, -1):
        value = ratio[first + index + 1] * (precond[index] + value)
        precond[index] = value + sweep[first + index]
    lead = grouped(edge[...])
    sign = signs(depth)

    def pull(index):
        below = faces[pl.ds(length + index, 1), :]
        above = faces[pl.ds(2 * length + index, 1), :]
        return below, above

    def down(index, previous):
        below, above = pull(index)
        current = lead * (below + sign * above) + grouped(ratio[index]) * previous
        if isinstance(index, int):
            if index == 0:
                current = current + grouped(beyond[0])
            if index == length - 1:
                current = current + grouped(beyond[1])
        else:
            current = current + jnp.where(index == 0, grouped(beyond[0]), 0.0)
            current = current + jnp.where(index == length - 1, grouped(beyond[1]), 0.0)
        sweep[index] = current.reshape(rows, depth)
        return current

    zero = jnp.zeros(lead.shape, F32)
    loop(0, length, down, zero)
    line = jnp.zeros((1, depth), F32)

    def up(back, carry):
        following, linked, squared = carry
        index = length - 1 - back
        value = grouped(ratio[index + 1]) * (grouped(sweep[index]) + following)
        sweep[index] = value.reshape(rows, depth)
        low, high = face_rows(value, lead)
        report[pl.ds(index, 1), :] = low
        report[pl.ds(length + index, 1), :] = high
        below, above = pull(index)
        linked = linked + faces[pl.ds(index, 1), :] * below
        squared = squared + low * below + high * above
        return value, linked, squared

    _, linked, squared = loop(0, length, up, (zero, line, line))
    sweep[length] = sweep[0]
    for index in range(layers + 1):
        image[index] = sweep[first + index]
    head, tail = sweep[0], sweep[length - 1]
    linked = 2.0 * total(linked) + total(ends[1] * beyond[0] + ends[0] * beyond[1])
    squared = total(squared) + total(head * beyond[0] + tail * beyond[1])
    crossing = 2.0 * total(head * tail)
    where = 2 * length
    report[pl.ds(where, 1), :] = energy[0:1]
    report[pl.ds(where + 1, 1), :] = jnp.broadcast_to(linked, (1, depth))
    report[pl.ds(where + 2, 1), :] = jnp.broadcast_to(squared, (1, depth))
    report[pl.ds(where + 3, 1), :] = jnp.broadcast_to(crossing, (1, depth))
    report[pl.ds(where + 4, 4), :] = jnp.zeros((4, depth), F32)


def physical_kernel(precond, image, left, right, precond_out, image_out):
    count = precond.shape[0]
    planes = [precond[index] for index in range(count)] + [image[index] for index in range(count)]
    planes = transformed(planes, left, right)
    for index in range(count):
        precond_out[index] = planes[index]
        image_out[index] = planes[count + index]


def project_kernel(
    group, length, paired, star, precond, image, faces, table_z, *refs
):
    given, (flow, pressure, field, rows_) = refs[:-4], refs[-4:]
    _, layers, rows, depth = star.shape
    first = position(group) * layers
    where = 2 * length
    reports = ring([each[...] for each in given])
    sums = reports[0][where:]
    for other in reports[1:]:
        sums = sums + other[where:]
    pairs = jnp.zeros((1, depth), F32)
    for index in range(len(reports)):
        upper, lower = reports[index], reports[(index + 1) % len(reports)]
        pairs = pairs + jnp.sum(
            upper[:length] * lower[length:where], axis=0, keepdims=True
        )
    energy, linked, squared, crossing = (sums[k : k + 1, 0:1] for k in range(4))
    if not paired:
        crossing = crossing + 2.0 * total(pairs)
    first_image = energy - linked
    step = energy / first_image
    beta = (energy * squared - linked * linked) / (first_image * first_image)
    rest = -linked / first_image
    second_image = (
        rest * rest * first_image
        + 2.0 * rest * step * (linked - squared)
        + step * step * (squared - crossing)
        - beta * beta * first_image
    )
    second_step = beta * energy / second_image
    alpha = step + second_step * (rest + beta)
    gamma = second_step * step
    for index in range(layers + 1):
        field[index] = alpha * precond[index] + gamma * image[index]
    after = rows_.at[pl.ds(rows + 8, length), :]
    after[...] = alpha * faces[pl.ds(2 * length, length), :] + gamma * reports[-1][:length]
    following = dot(after[pl.ds(first, layers), :], table_z[...])
    for index in range(layers):
        value = field[index]
        pressure[index] = value
        rows_[pl.ds(0, rows), :] = value
        rows_[pl.ds(rows, 1), :] = following[index : index + 1]
        flow[0, index] = star[0, index] - (field[index + 1] - value)
        flow[1, index] = star[1, index] - (rows_[pl.ds(1, rows), :] - value)
        flow[2, index] = star[2, index] - (lane_shift(value, 1) - value)


def ring(reports):
    if len(reports) != 4:
        return reports
    own, near, across, far = reports
    even = lax.rem(lax.axis_index("gy"), 2) == 0
    return [own, jnp.where(even, far, near), across, jnp.where(even, near, far)]


def along(array, axis, by):
    length = lax.axis_size(axis)
    return lax.ppermute(array, axis, [(i, (i + by) % length) for i in range(length)])


def swapped(array, bit, by=0):
    count_x, count_y = lax.axis_size("gx"), lax.axis_size("gy")
    pairs = [
        (x * count_y + y, (x ^ bit) * count_y + (y + by) % count_y)
        for x in range(count_x)
        for y in range(count_y)
    ]
    return lax.ppermute(array, ("gx", "gy"), pairs)


def pack(body, inputs, received, shapes, scratch, count):
    inputs = [pltpu.with_memory_space_constraint(each, pltpu.HBM) for each in inputs]
    return pl.pallas_call(
        body,
        out_shape=[jax.ShapeDtypeStruct(shape, F32) for shape in shapes],
        in_specs=[pl.BlockSpec(memory_space=pltpu.HBM)] * len(inputs) + [VMEM] * len(received),
        out_specs=[VMEM] * len(shapes),
        scratch_shapes=scratch + [pltpu.SemaphoreType.DMA((count,))],
        compiler_params=pltpu.CompilerParams(vmem_limit_bytes=4 << 20),
    )(*inputs, *received)


def per_device(melt_flow, thermal_state, powder_flag, spot_lateral_a_cell, spot_lateral_b_cell):
    layers, rows, depth = thermal_state.shape
    count_x, count_y = lax.axis_size("gx"), lax.axis_size("gy")
    group = min(count_x, BLOCK // layers)
    blocks = count_x // group
    length = group * layers
    rounds = group.bit_length() - 1
    plane = (rows, depth)
    sine_y, values_y = sines(rows)
    sine_z, values_z = sines(depth)
    left, right = packed_tables(sine_y, sine_z)
    table_z = jnp.asarray(sine_z, F32)
    edge = jnp.asarray(np.broadcast_to(sine_y[0][:, None], plane), F32)
    diagonal = jnp.asarray(2.0 + values_y[:, None] + values_z[None, :], F32)
    line = (length, depth)

    parts = melt_flow.shape[0]
    width = max(rows, depth)
    outer_planes = (2 * parts * rows + 8, width)
    ahead, behind, last_rows, first_rows = pack(
        halo_kernel,
        [melt_flow, thermal_state],
        [],
        [outer_planes, outer_planes] + [(parts + 1, layers, 8, depth)] * 2,
        [pltpu.VMEM((2,) + plane, F32)],
        6 + 4 * parts,
    )
    low_x = along(ahead, "gx", 1)
    high_x = along(behind, "gx", -1)
    low_y = along(last_rows, "gy", 1)
    high_y = along(first_rows, "gy", -1)
    extra, last = pack(
        extra_kernel,
        [melt_flow, thermal_state, powder_flag],
        [low_y, high_y],
        [(rows + 8, width), (2,) + plane],
        [
            pltpu.VMEM((5,) + plane, F32),
            pltpu.VMEM(plane, jnp.int32),
            pltpu.VMEM((1, rows + 16, depth), F32),
        ],
        7,
    )
    extra = along(extra, "gx", 1)
    early_low = along(last, "gx", 1)
    ratio, weight = call(
        functools.partial(tables_kernel, group, layers),
        [diagonal],
        [(length + 1,) + plane, (4 * rounds + 1,) + plane],
    )
    marched = [melt_flow, low_x, high_x, thermal_state, powder_flag, low_y, high_y]
    padded = pltpu.VMEM((4, rows + 16, depth), F32)
    one_padded = pltpu.VMEM((1, rows + 16, depth), F32)
    (side_y,) = call(row_kernel, marched + [weight], [(layers, depth)], [padded], loose=1)
    before_y = along(side_y, "gy", 1)
    (star,) = call(
        march_kernel, marched + [side_y], [(3, layers) + plane], [padded], loose=1, flops=3 << 27
    )
    (partial,) = call(
        transform_kernel,
        [star, left, right],
        [(layers,) + plane],
        [pltpu.VMEM((rows + 16, depth), F32)],
        flops=1 << 27,
    )
    source, message = call(
        functools.partial(source_kernel, group, length),
        [melt_flow, low_x, thermal_state, extra, partial, left, right, ratio, before_y],
        [(layers,) + plane, (2 * rows, depth)],
        [one_padded],
        loose=1,
    )
    faces, late = call(
        functools.partial(faces_kernel, group, length),
        [source, before_y, table_z, ratio, weight, edge, thermal_state, early_low],
        [(3 * length + 8, depth), (2,) + plane],
        [pltpu.VMEM((max(length, layers + 1),) + plane, F32)],
        loose=1,
    )
    alone = blocks == 1
    early_high = along(late, "gx", -1)
    warmed, token = call(
        heat_kernel,
        [
            spot_lateral_a_cell, spot_lateral_b_cell, thermal_state, early_low, early_high,
            low_y, high_y, melt_flow,
        ],
        [(layers,) + plane, (8, depth)],
        [one_padded],
        scalars=2,
        flops=1 << 28,
    )
    sums = jnp.zeros((2,) + plane, F32)
    for turn in range(rounds - 1):
        message, sums, head, tail = call(
            functools.partial(merge_kernel, turn, group, length),
            [
                message, swapped(message, 1 << turn), faces, swapped(faces, 1 << turn),
                sums, weight,
            ],
            [(2 * rows + 2 * length + 8, depth), (2,) + plane, line, line],
        )
        if turn + 2 < rounds:
            rest = message[2 * rows + length :]
            message, faces = message[: 2 * rows], jnp.concatenate([head, tail, rest], 0)
    bit = group >> 1
    other = swapped(message, bit)
    rim = [
        swapped(tail, 0, 1), swapped(tail, bit, 1), swapped(head, 0, -1), swapped(head, bit, -1)
    ]
    outer = []
    scratch = [pltpu.VMEM((2 * length, depth), F32), pltpu.VMEM((length + 1,) + plane, F32)]
    if not alone:
        (ends,) = call(
            functools.partial(close_kernel, rounds - 1, group, length),
            [message, other, sums, weight, ratio, edge],
            [(2,) + plane],
            scratch,
        )
        outer = [jnp.stack([along(ends[0], "gx", group), along(ends[1], "gx", -group)])]
    operands = [source, message, other, sums] + rim
    operands += [weight, ratio, edge] + outer + [token]

    def coarse(*refs):
        coarse_kernel(rounds - 1, group, length, alone, *refs[:4], refs[4:8], *refs[8:])

    precond, image, report, faces = call(
        coarse,
        operands,
        [
            (layers + 1,) + plane, (layers + 1,) + plane, (2 * length + 8, depth),
            (3 * length, depth),
        ],
        scratch + [pltpu.VMEM((2,) + plane, F32)],
        loose=1,
    )
    if blocks > 1:
        onward = along(image[0], "gx", -1)
        at_end = position(group) == group - 1
        image = image.at[layers].set(jnp.where(at_end, onward, image[layers]))
        upper = along(report[:length], "gy", -1)
        crossing = jnp.sum(onward * image[layers - 1])
        crossing = crossing + jnp.sum(upper * report[length : 2 * length])
        numbers = report[2 * length :].at[3].set(2.0 * crossing)
        numbers = lax.psum(jnp.where(at_end, numbers, 0.0), "gx")
        report = report.at[2 * length :].set(numbers)
    reports = [report]
    for by in range(1, count_y):
        pairs = [(i, i ^ by if count_y == 4 else (i + by) % count_y) for i in range(count_y)]
        reports.append(lax.ppermute(report, "gy", pairs))
    precond, image = call(
        physical_kernel,
        [precond, image, left, right],
        [(layers + 1,) + plane, (layers + 1,) + plane],
    )
    flow, pressure = call(
        functools.partial(project_kernel, group, length, blocks > 1),
        [star, precond, image, faces, table_z] + reports,
        [(3, layers) + plane, (layers,) + plane],
        [
            pltpu.VMEM((layers + 1,) + plane, F32),
            pltpu.VMEM((rows + 8 + length, depth), F32),
        ],
    )
    return (flow, warmed, pressure)


def solution(mesh):
    placed = (
        P(None, ("runs", "gx"), "gy", None),
        P(("runs", "gx"), "gy", None),
        P(("runs", "gx"), "gy", None),
        P("runs"),
        P("runs"),
    )
    return jax.shard_map(
        per_device,
        mesh=mesh,
        in_specs=placed,
        out_specs=(
            P(None, ("runs", "gx"), "gy", None),
            P(("runs", "gx"), "gy", None),
            P(("runs", "gx"), "gy", None),
        ),
        check_vma=False,
    )
```

```python
import functools
import math

import jax
import jax.numpy as jnp
import numpy as np
from jax import lax
from jax.experimental import pallas as pl
from jax.experimental.pallas import tpu as pltpu
from jax.sharding import PartitionSpec as P

BLOCK = 128

TIME_INCREMENT = 0.2
MARANGONI = 1.5
DRAG_RATE = 4.0
LASER_POWER = 3.0
SPOT_RADIUS = 5.0

F32 = jnp.float32
VMEM = pl.BlockSpec(memory_space=pltpu.VMEM)
SMEM = pl.BlockSpec(memory_space=pltpu.SMEM)


def call(body, operands, shapes, scratch=(), scalars=0, loose=0, flops=1 << 20):
    out_shape = [jax.ShapeDtypeStruct(shape, F32) for shape in shapes]
    moved = 4 * sum(math.prod(shape) for shape in shapes)
    held = moved + 4 * sum(operand.size for operand in operands)
    held += 4 * sum(math.prod(space.shape) for space in scratch)
    return pl.pallas_call(
        body,
        out_shape=out_shape,
        in_specs=[SMEM] * scalars
        + [VMEM] * (len(operands) - scalars - loose)
        + [pl.BlockSpec(memory_space=pl.ANY)] * loose,
        out_specs=[VMEM] * len(shapes),
        scratch_shapes=list(scratch),
        compiler_params=pltpu.CompilerParams(vmem_limit_bytes=held + (4 << 20)),
        cost_estimate=pl.CostEstimate(flops=flops, bytes_accessed=2 * moved, transcendentals=0),
    )(*operands)


def dot(left, right):
    return jnp.dot(left, right, precision=lax.Precision.HIGHEST, preferred_element_type=F32)


def split(cells):
    high = cells.astype(jnp.bfloat16)
    return high, (cells - high.astype(F32)).astype(jnp.bfloat16)


def folded(product):
    half = product.shape[1] // 2
    return product[:, :half] + product[:, half:]


def packed_tables(left, right):
    left_high, left_low = split(np.asarray(left, np.float32))
    right_high, right_low = split(np.asarray(right, np.float32))
    zero = np.zeros_like(right_low)
    return (
        jnp.asarray(np.concatenate([left_high, left_low], 1)),
        jnp.asarray(np.block([[right_high, right_low], [right_high, zero]])),
    )


def transformed(planes, left, right):
    rows = planes[0].shape[0]
    high, low = split(jnp.concatenate(planes, 0))
    cells = jnp.concatenate([high, low], 1)
    cells = folded(jnp.dot(cells, right[...], preferred_element_type=F32))
    out = []
    for index in range(len(planes)):
        high, low = split(cells[index * rows : (index + 1) * rows])
        upper = jnp.concatenate([high, low], 1)
        lower = jnp.concatenate([high, jnp.zeros_like(low)], 1)
        cells_ = jnp.concatenate([upper, lower], 0)
        out.append(folded(jnp.dot(left[...], cells_, preferred_element_type=F32)))
    return out


def total(cells):
    return jnp.sum(jnp.sum(cells, axis=0, keepdims=True), axis=1, keepdims=True)


def loop(low, high, body, start):
    if isinstance(high, int) and isinstance(low, int) and high - low <= 24:
        carry = start
        for index in range(low, high):
            carry = body(index, carry)
        return carry
    return lax.fori_loop(low, high, body, start)


def position(group):
    return lax.rem(lax.axis_index("gx"), group)


def sines(length):
    positions = np.arange(length) + 1.0
    step = math.pi / (length + 1)
    table = np.sqrt(2.0 / (length + 1)) * np.sin(step * positions[:, None] * positions[None, :])
    return table, 2.0 - 2.0 * np.cos(step * positions)


def lane_shift(cells, offset):
    width = cells.shape[1]
    lane = lax.broadcasted_iota(jnp.int32, cells.shape, 1)
    moved = pltpu.roll(cells, (-offset) % width, 1)
    keep = lane < width - offset if offset > 0 else lane >= -offset
    return jnp.where(keep, moved, 0.0)


def column(row):
    length = row.shape[1]
    shape = (length, length)
    same = lax.broadcasted_iota(jnp.int32, shape, 0) == lax.broadcasted_iota(jnp.int32, shape, 1)
    return jnp.sum(jnp.where(same, row, 0.0), axis=1, keepdims=True)


def coefficients(speed, scale):
    factors = [0.5 * TIME_INCREMENT * jnp.abs(each) for each in speed]
    if scale is not None:
        factors = [each * scale for each in factors]
    centre = (1.0 if scale is None else scale) - 3.0 * (factors[0] + factors[1] + factors[2])
    near, far = 4.0 * factors[2], -factors[2]
    ahead = speed[2] >= 0.0
    lane = lax.broadcasted_iota(jnp.int32, near.shape, 1)
    width = near.shape[1]
    depth = (
        jnp.where(ahead & (lane >= 1), near, 0.0),
        jnp.where(ahead & (lane >= 2), far, 0.0),
        jnp.where(ahead | (lane >= width - 1), 0.0, near),
        jnp.where(ahead | (lane >= width - 2), 0.0, far),
    )
    return centre, speed[0] >= 0.0, factors[0], speed[1] >= 0.0, factors[1], depth


def advance(layers, padded, index, weights, start=0):
    middle = layers[2]
    rows, width = middle.shape
    centre, ahead_x, factor_x, ahead_y, factor_y, depth = weights
    near = jnp.where(ahead_x, layers[1], layers[3])
    far = jnp.where(ahead_x, layers[0], layers[4])
    moved = centre * middle + factor_x * (4.0 * near - far)
    beside = lambda offset: padded[index, pl.ds(8 + offset + start, rows), :]
    near = jnp.where(ahead_y, beside(-1), beside(1))
    far = jnp.where(ahead_y, beside(-2), beside(2))
    moved = moved + factor_y * (4.0 * near - far)
    for factor, offset in zip(depth, (1, 2, width - 1, width - 2)):
        moved = moved + factor * pltpu.roll(middle, offset, 1)
    return moved


def pad_rows(padded, index, before, middle, after):
    rows = middle.shape[0]
    padded[index, pl.ds(8, rows), :] = middle
    padded[index, pl.ds(6, 2), :] = before
    padded[index, pl.ds(8 + rows, 2), :] = after


def march_layer(refs, padded, index, parts, start, count, edges=None):
    flow, low_x, high_x, thermal, flag = refs
    _, layers, rows, depth = flow.shape
    span = pl.ds(start, count)
    speed = [flow[part, index, span, :] for part in range(3)]
    drag = 1.0 / (1.0 + TIME_INCREMENT * DRAG_RATE * flag[index, span, :].astype(F32))
    top = lax.broadcasted_iota(jnp.int32, (count, depth), 1) == depth - 1
    pull = jnp.where(top, (-MARANGONI * 0.5 * TIME_INCREMENT) * drag, 0.0)
    weights = coefficients(speed, drag)
    out = []
    for part in parts:
        around = []
        for other in range(index - 2, index + 3):
            if other < 0:
                first = (2 * part + other + 2) * rows + start
                around.append(low_x[pl.ds(first, count), :])
            elif other >= layers:
                first = (2 * part + other - layers) * rows + start
                around.append(high_x[pl.ds(first, count), :])
            else:
                around.append(flow[part, other, span, :])
        moved = advance(around, padded, part, weights, start)
        if part == 0:
            behind = edges[0][start : start + count]
            before = edges[1][start : start + count]
            behind = thermal[index - 1, span, :] if index > 0 else behind
            before = thermal[index + 1, span, :] if index + 1 < layers else before
            moved = moved + pull * (before - behind)
        if part == 1:
            slope = padded[3, pl.ds(9 + start, count), :] - padded[3, pl.ds(7 + start, count), :]
            moved = moved + pull * slope
        out.append(moved)
    return out


def pad_layer(refs, low_y, high_y, padded, index):
    flow, _, _, thermal, _ = refs
    for part in range(3):
        pad_rows(
            padded, part, low_y[part, index, 6:], flow[part, index], high_y[part, index, :2]
        )
    pad_rows(padded, 3, low_y[3, index, 6:], thermal[index], high_y[3, index, :2])


def march_kernel(
    flow, low_x, high_x, thermal, flag, low_y, high_y, _, star, padded
):
    refs = (flow, low_x, high_x, thermal, flag)
    _, layers, rows, depth = flow.shape
    edges = [column(halo[pl.ds(halo.shape[0] - 8, 1), pl.ds(0, rows)]) for halo in (low_x, high_x)]
    count = math.gcd(rows, 16)
    for index in range(layers):
        pad_layer(refs, low_y, high_y, padded, index)
        for start in range(0, rows, count):
            value = march_layer(refs, padded, index, range(3), start, count, edges)
            for part in range(3):
                star[part, index, pl.ds(start, count), :] = value[part]


def side_plane(flow, low_x, thermal, extra, padded):
    rows, depth = flow.shape[2:]
    plane = lambda index: low_x[pl.ds(index * rows, rows), pl.ds(0, depth)]
    beside = extra[pl.ds(rows, 8), pl.ds(0, depth)]
    given = extra[pl.ds(0, rows), pl.ds(0, depth)]
    pad_rows(padded, 0, beside[2:4], plane(1), beside[4:6])
    none = jnp.zeros((rows, depth), F32)
    around = [none, plane(0), plane(1), flow[0, 0], flow[0, 1]]
    moved = advance(around, padded, 0, coefficients([plane(1), plane(3), plane(5)], given))
    moved = jnp.where(plane(1) >= 0.0, given, moved)
    top = lax.broadcasted_iota(jnp.int32, (rows, depth), 1) == depth - 1
    behind = column(extra[pl.ds(rows, 1), pl.ds(0, rows)])
    drag = column(extra[pl.ds(rows + 6, 1), pl.ds(0, rows)])
    pull = (-MARANGONI * 0.5 * TIME_INCREMENT) * drag
    return moved + jnp.where(top, pull * (thermal[0] - behind), 0.0)


def transform_kernel(star, left, right, partial, rows_):
    _, layers, rows, depth = star.shape
    rows_[pl.ds(0, 8), :] = jnp.zeros((8, depth), F32)
    planes = []
    for index in range(layers):
        rows_[pl.ds(8, rows), :] = star[1, index]
        sink = star[0, index]
        if index > 0:
            sink = sink - star[0, index - 1]
        sink = sink + (star[1, index] - rows_[pl.ds(7, rows), :])
        sink = sink + (star[2, index] - lane_shift(star[2, index], -1))
        planes.append(-sink)
    for index, plane in enumerate(transformed(planes, left, right)):
        partial[index] = plane


def side_rows(flow, thermal, low_y, extra, back, padded):
    _, layers, rows, depth = flow.shape
    row = lambda ref, index: jnp.broadcast_to(ref[pl.ds(index, 1), pl.ds(0, depth)], (8, depth))
    top = lax.broadcasted_iota(jnp.int32, (8, depth), 1) == depth - 1
    padded[0, pl.ds(0, 8), :] = jnp.zeros((8, depth), F32)
    out = []
    for index in range(layers):
        around = []
        for other in range(index - 2, index + 3):
            if other < 0:
                around.append(row(extra, rows + 1 if other == -2 else rows + 7))
            elif other >= layers:
                around.append(row(back, other - layers))
            else:
                around.append(low_y[1, other])
        drag = 1.0 / (1.0 + TIME_INCREMENT * DRAG_RATE * low_y[4, index])
        pull = jnp.where(top, (-MARANGONI * 0.5 * TIME_INCREMENT) * drag, 0.0)
        padded[0, pl.ds(8, 8), :] = low_y[3, index]
        padded[0, pl.ds(16, 8), :] = thermal[index, :8, :]
        slope = padded[0, pl.ds(9, 8), :] - padded[0, pl.ds(7, 8), :]
        padded[0, pl.ds(8, 8), :] = low_y[1, index]
        padded[0, pl.ds(16, 8), :] = flow[1, index, :8, :]
        weights = coefficients([low_y[part, index] for part in range(3)], drag)
        moved = advance(around, padded, 0, weights) + pull * slope
        out.append(moved[7:])
    return out


def source_kernel(
    group, length, flow, low_x, thermal, extra, back, low_y, partial, left, right, table_z, edge,
    ratio, source, message, padded, rows_,
):
    layers, rows, depth = partial.shape
    first = position(group) * layers
    for index, row in enumerate(side_rows(flow, thermal, low_y, extra, back, padded)):
        rows_[pl.ds(index, 1), :] = row
    beside = dot(rows_[...], table_z[...])
    (onward,) = transformed([side_plane(flow, low_x, thermal, extra, padded)], left, right)
    for index in range(layers):
        value = partial[index] + edge[...] * beside[index : index + 1]
        source[index] = value + onward if index == 0 else value
    backward = source[layers - 1]
    for index in range(layers - 2, -1, -1):
        backward = source[index] + ratio[length - 1 - first - index] * backward
    message[pl.ds(rows, rows), :] = backward
    forward = source[0]
    for index in range(1, layers):
        forward = source[index] + ratio[first + index] * forward
    message[pl.ds(0, rows), :] = forward


def started(copies):
    for copy in copies:
        copy.start()
    return copies


def surface(plane):
    rows, depth = plane.shape
    shape = (rows, rows)
    same = lax.broadcasted_iota(jnp.int32, shape, 0) == lax.broadcasted_iota(jnp.int32, shape, 1)
    return jnp.sum(jnp.where(same, plane[:, depth - 1 :], 0.0), axis=0, keepdims=True)


def halo_kernel(
    flow, thermal, flag, ahead, behind, last_rows, first_rows, tops, flags, sems
):
    parts, layers, rows, depth = flow.shape
    pairs = [(thermal.at[layers - 1], tops.at[0]), (thermal.at[0], tops.at[1])]
    for part in range(parts):
        for layer in range(2):
            span = pl.ds((2 * part + layer) * rows, rows)
            pairs.append((flow.at[part, layers - 2 + layer], ahead.at[span, :]))
            pairs.append((flow.at[part, layer], behind.at[span, :]))
    for target, start in ((last_rows, rows - 8), (first_rows, 0)):
        span = pl.ds(start, 8)
        pairs.append((flow.at[:, :, span, :], target.at[pl.ds(0, parts)]))
        pairs.append((thermal.at[:, span, :], target.at[parts]))
    pairs.append((flag.at[:, pl.ds(rows - 8, 8), :], flags))
    copies = started(
        [pltpu.make_async_copy(*pair, sems.at[index]) for index, pair in enumerate(pairs)]
    )
    for side, message in enumerate((ahead, behind)):
        copies[side].wait()
        row = jnp.broadcast_to(surface(tops[side]), (8, rows))
        message[pl.ds(2 * parts * rows, 8), pl.ds(0, rows)] = row
    for copy in copies[2:]:
        copy.wait()
    last_rows[parts + 1] = flags[...].astype(F32)


def extra_kernel(
    flow, thermal, flag, low_y, high_y, extra, back, last, planes, flags, padded, sems
):
    _, layers, rows, depth = flow.shape
    pairs = [(flag.at[layers - 1], flags), (thermal.at[pl.ds(layers - 2, 2)], last)]
    sources = [(0, layers - 3), (0, layers - 2), (0, layers - 1), (1, layers - 1), (2, layers - 1)]
    for index, (part, layer) in enumerate(sources):
        pairs.append((flow.at[part, layer], planes.at[index]))
    copies = started(
        [pltpu.make_async_copy(*pair, sems.at[index]) for index, pair in enumerate(pairs)]
    )
    extra[pl.ds(rows, 8), :] = jnp.zeros((8, extra.shape[1]), F32)
    extra[pl.ds(rows + 2, 2), pl.ds(0, depth)] = low_y[0, layers - 1, 6:, :]
    extra[pl.ds(rows + 4, 2), pl.ds(0, depth)] = high_y[0, layers - 1, :2, :]
    extra[pl.ds(rows + 1, 1), pl.ds(0, depth)] = low_y[1, layers - 2, 7:, :]
    extra[pl.ds(rows + 7, 1), pl.ds(0, depth)] = low_y[1, layers - 1, 7:, :]
    back[...] = jnp.zeros(back.shape, F32)
    for index in range(2):
        back[pl.ds(index, 1), :] = low_y[1, index, 7:, :]
    for copy in copies:
        copy.wait()
    speed = [planes[index] for index in (2, 3, 4)]
    drag = 1.0 / (1.0 + TIME_INCREMENT * DRAG_RATE * flags[...].astype(F32))
    pad_rows(padded, 0, low_y[0, layers - 1, 6:], speed[0], high_y[0, layers - 1, :2])
    none = jnp.zeros((rows, depth), F32)
    around = [planes[0], planes[1], speed[0], none, none]
    moved = advance(around, padded, 0, coefficients(speed, drag))
    extra[pl.ds(0, rows), pl.ds(0, depth)] = jnp.where(speed[0] >= 0.0, moved, drag)
    extra[pl.ds(rows, 1), pl.ds(0, rows)] = surface(last[0])
    extra[pl.ds(rows + 6, 1), pl.ds(0, rows)] = surface(drag)


def wrapped(distance, span):
    moved = distance + span // 2
    moved = jnp.where(moved < 0, moved + span, moved)
    moved = jnp.where(moved >= span, moved - span, moved)
    return (moved - span // 2).astype(F32)


def laser_row(index, layers, rows, spots_a, spots_b):
    total_x = layers * lax.axis_size("gx")
    total_y = rows * lax.axis_size("gy")
    cell_x = lax.axis_index("gx") * layers + index
    cells_y = lax.broadcasted_iota(jnp.int32, (1, rows), 1) + lax.axis_index("gy") * rows
    heat = jnp.zeros((1, rows), F32)
    for spot in range(spots_a.shape[0]):
        dist_x = wrapped(jnp.full((1, rows), cell_x - spots_a[spot], jnp.int32), total_x)
        dist_y = wrapped(cells_y - spots_b[spot], total_y)
        square = dist_x * dist_x + dist_y * dist_y
        heat = heat + jnp.exp(square * (-1.0 / (SPOT_RADIUS * SPOT_RADIUS)))
    return LASER_POWER * heat


def heat_kernel(
    spots_a, spots_b, thermal, low_x, high_x, low_y, high_y, flow, warmed, token, padded
):
    layers, rows, depth = thermal.shape
    token[...] = jnp.zeros(token.shape, F32)
    top = lax.broadcasted_iota(jnp.int32, (rows, depth), 1) == depth - 1
    for index in range(layers):
        pad_rows(padded, 0, low_y[3, index, 6:], thermal[index], high_y[3, index, :2])
        around = []
        for other in range(index - 2, index + 3):
            if other < 0:
                around.append(low_x[other + 2])
            elif other >= layers:
                around.append(high_x[other - layers])
            else:
                around.append(thermal[other])
        speed = [flow[part, index] for part in range(3)]
        gain = TIME_INCREMENT * column(laser_row(index, layers, rows, spots_a, spots_b))
        moved = advance(around, padded, 0, coefficients(speed, None))
        warmed[index] = moved + jnp.where(top, gain, 0.0)


def tables_kernel(group, layers, diagonal, ratio, weight):
    length = group * layers
    mine = position(group)
    first = mine * layers
    diag = diagonal[...]
    ratio[0] = jnp.zeros_like(diag)

    def step(index, previous):
        current = 1.0 / (diag - previous)
        ratio[index] = current
        return current

    loop(1, length + 1, step, jnp.zeros_like(diag))

    def decay(low, high):
        return lax.fori_loop(
            low + 1, high + 1, lambda index, value: value * ratio[index], jnp.ones_like(diag)
        )

    def green(index):
        return 1.0 / (diag - ratio[index] - ratio[jnp.maximum(length - 1 - index, 0)])

    rounds = group.bit_length() - 1
    for turn in range(rounds):
        half = 1 << turn
        right = ((mine >> turn) & 1) == 1
        start = (mine >> (turn + 1)) << (turn + 1)
        cut = (start + half) * layers
        end = (start + 2 * half) * layers
        weight[4 * turn] = decay(cut - 1, end - 1)
        weight[4 * turn + 1] = decay(length - 1 - cut, length - 1 - start * layers)
        low = jnp.where(right, cut - 1, length - 1 - cut)
        high = jnp.where(right, first - 1, length - 1 - first - layers)
        weight[4 * turn + 2] = decay(low, high)
        weight[4 * turn + 3] = green(cut) * ratio[cut]
    inner = jnp.where(mine == group - 1, 0.0, 1.0)
    weight[4 * rounds] = inner * green(first + layers)


def grouped(plane):
    return plane.reshape(plane.shape[0] // 8, 8, plane.shape[1])


def signs(depth):
    row = lax.broadcasted_iota(jnp.int32, (8, depth), 0)
    return jnp.where(row % 2 == 0, 1.0, -1.0)


def face_rows(plane, lead):
    sums = jnp.sum(plane * lead, axis=0)
    return (
        jnp.sum(sums, axis=0, keepdims=True),
        jnp.sum(sums * signs(sums.shape[1]), axis=0, keepdims=True),
    )


def faces_kernel(
    group, length, source, ratio, weight, edge, thermal, _, faces, late, sweep
):
    layers, rows, depth = source.shape
    late[...] = thermal[:2]
    first = position(group) * layers
    zero = jnp.zeros((rows, depth), F32)
    forward = zero
    for index in range(layers):
        forward = source[index] + ratio[first + index] * forward
        sweep[index] = forward
    value = weight[weight.shape[0] - 1] * (ratio[first + layers] * forward)
    energy = zero
    for index in range(layers - 1, -1, -1):
        value = ratio[first + index + 1] * (sweep[index] + value)
        energy = energy + source[index] * value
    faces[pl.ds(2 * length, 8), :] = jnp.broadcast_to(total(energy), (8, depth))

    lead = grouped(edge[...])
    zero = grouped(zero)

    def down(index, previous):
        inside = (index >= first) & (index < first + layers)
        own = jnp.where(inside, source[jnp.clip(index - first, 0, layers - 1)], 0.0)
        current = grouped(own) + grouped(ratio[index]) * previous
        sweep[index] = current.reshape(rows, depth)
        return current

    loop(0, length, down, zero)

    def up(back, following):
        index = length - 1 - back
        value = grouped(ratio[index + 1]) * (grouped(sweep[index]) + following)
        low, high = face_rows(value, lead)
        faces[pl.ds(index, 1), :] = low
        faces[pl.ds(length + index, 1), :] = high
        return value

    loop(0, length, up, zero)


def joined(turn, group, message, other, sums, weight):
    rows, depth = weight.shape[1:]
    right = ((position(group) >> turn) & 1) == 1
    upper, lower = pl.ds(0, rows), pl.ds(rows, rows)
    left_s = jnp.where(right, other[upper, :], message[upper, :])
    right_s = jnp.where(right, message[upper, :], other[upper, :])
    left_t = jnp.where(right, other[lower, :], message[lower, :])
    right_t = jnp.where(right, message[lower, :], other[lower, :])
    own = weight[4 * turn + 2]
    before = sums[0] + jnp.where(right, left_s * own, 0.0)
    after = sums[1] + jnp.where(right, 0.0, right_t * own)
    forward = right_s + left_s * weight[4 * turn]
    backward = left_t + right_t * weight[4 * turn + 1]
    energy = 2.0 * total(left_s * right_t * weight[4 * turn + 3])
    return forward, backward, before, after, energy


def merge_kernel(
    turn, group, length, message, other, faces, other_faces, sums, weight,
    new_message, new_sums, head, tail,
):
    rows, depth = weight.shape[1:]
    forward, backward, before, after, energy = joined(turn, group, message, other, sums, weight)
    new_sums[0] = before
    new_sums[1] = after
    new_message[pl.ds(0, rows), :] = forward
    new_message[pl.ds(rows, rows), :] = backward
    low, high = pl.ds(0, length), pl.ds(length, length)
    number = pl.ds(2 * length, 8)
    head[...] = faces[low, :] + other_faces[low, :]
    tail[...] = faces[high, :] + other_faces[high, :]
    new_message[pl.ds(2 * rows, length), :] = head[...]
    energy = faces[number, :] + other_faces[number, :] + energy
    new_message[pl.ds(2 * rows + length, 8), :] = energy


def close_kernel(turn, group, length, message, other, sums, weight, ratio, ends):
    forward, backward, _, _, _ = joined(turn, group, message, other, sums, weight)
    ends[0] = ratio[length] * forward
    ends[1] = ratio[length] * backward


def coarse_kernel(
    turn, group, length, alone, source, message, other, sums, faces_in, weight, ratio, edge, *refs
):
    precond, image, report, faces, sweep, ends = refs[-6:]
    layers, rows, depth = source.shape
    first = position(group) * layers
    below, below_far, above, above_far = faces_in
    forward, backward, before, after, energy = joined(turn, group, message, other, sums, weight)
    ends[0] = ratio[length] * forward
    ends[1] = ratio[length] * backward
    beyond = ends if alone else refs[0]
    own = pl.ds(2 * rows, length)
    faces[pl.ds(0, length), :] = message[own, :] + other[own, :]
    faces[pl.ds(length, length), :] = below[...] + below_far[...]
    faces[pl.ds(2 * length, length), :] = above[...] + above_far[...]
    number = pl.ds(2 * rows + length, 8)
    energy = message[number, :] + other[number, :] + energy
    forward = before
    for index in range(layers):
        forward = source[index] + ratio[first + index] * forward
        precond[index] = forward
    value = weight[weight.shape[0] - 1] * (after + ratio[first + layers] * forward)
    is_last = first + layers == length
    precond[layers] = jnp.where(is_last, beyond[1], value)
    for index in range(layers - 1, -1, -1):
        value = ratio[first + index + 1] * (precond[index] + value)
        precond[index] = value
    lead = grouped(edge[...])
    sign = signs(depth)

    def pull(index):
        below = faces[pl.ds(length + index, 1), :]
        above = faces[pl.ds(2 * length + index, 1), :]
        return below, above

    def down(index, previous):
        below, above = pull(index)
        current = lead * (below + sign * above) + grouped(ratio[index]) * previous
        if isinstance(index, int):
            if index == 0:
                current = current + grouped(beyond[0])
            if index == length - 1:
                current = current + grouped(beyond[1])
        else:
            current = current + jnp.where(index == 0, grouped(beyond[0]), 0.0)
            current = current + jnp.where(index == length - 1, grouped(beyond[1]), 0.0)
        sweep[index] = current.reshape(rows, depth)
        return current

    zero = jnp.zeros(lead.shape, F32)
    loop(0, length, down, zero)
    line = jnp.zeros((1, depth), F32)

    def up(back, carry):
        following, linked, squared = carry
        index = length - 1 - back
        value = grouped(ratio[index + 1]) * (grouped(sweep[index]) + following)
        sweep[index] = value.reshape(rows, depth)
        low, high = face_rows(value, lead)
        report[pl.ds(index, 1), :] = low
        report[pl.ds(length + index, 1), :] = high
        below, above = pull(index)
        linked = linked + faces[pl.ds(index, 1), :] * below
        squared = squared + low * below + high * above
        return value, linked, squared

    _, linked, squared = loop(0, length, up, (zero, line, line))
    sweep[length] = sweep[0]
    for index in range(layers + 1):
        image[index] = sweep[first + index]
    head, tail = sweep[0], sweep[length - 1]
    linked = 2.0 * total(linked) + total(ends[1] * beyond[0] + ends[0] * beyond[1])
    squared = total(squared) + total(head * beyond[0] + tail * beyond[1])
    crossing = 2.0 * total(head * tail)
    where = 2 * length
    report[pl.ds(where, 1), :] = energy[0:1]
    report[pl.ds(where + 1, 1), :] = jnp.broadcast_to(linked, (1, depth))
    report[pl.ds(where + 2, 1), :] = jnp.broadcast_to(squared, (1, depth))
    report[pl.ds(where + 3, 1), :] = jnp.broadcast_to(crossing, (1, depth))
    report[pl.ds(where + 4, 4), :] = jnp.zeros((4, depth), F32)


def physical_kernel(precond, image, left, right, precond_out, image_out):
    count = precond.shape[0]
    planes = [precond[index] for index in range(count)] + [image[index] for index in range(count)]
    planes = transformed(planes, left, right)
    for index in range(count):
        precond_out[index] = planes[index]
        image_out[index] = planes[count + index]


def project_kernel(
    group, length, paired, star, precond, image, faces, table_z, *refs
):
    given, (flow, pressure, field, rows_) = refs[:-4], refs[-4:]
    _, layers, rows, depth = star.shape
    first = position(group) * layers
    where = 2 * length
    reports = ring([each[...] for each in given])
    sums = reports[0][where:]
    for other in reports[1:]:
        sums = sums + other[where:]
    pairs = jnp.zeros((1, depth), F32)
    for index in range(len(reports)):
        upper, lower = reports[index], reports[(index + 1) % len(reports)]
        pairs = pairs + jnp.sum(
            upper[:length] * lower[length:where], axis=0, keepdims=True
        )
    energy, linked, squared, crossing = (sums[k : k + 1, 0:1] for k in range(4))
    if not paired:
        crossing = crossing + 2.0 * total(pairs)
    first_image = energy - linked
    step = energy / first_image
    beta = (energy * squared - linked * linked) / (first_image * first_image)
    rest = -linked / first_image
    second_image = (
        rest * rest * first_image
        + 2.0 * rest * step * (linked - squared)
        + step * step * (squared - crossing)
        - beta * beta * first_image
    )
    second_step = beta * energy / second_image
    alpha = step + second_step * (rest + beta)
    gamma = second_step * step
    for index in range(layers + 1):
        field[index] = alpha * precond[index] + gamma * image[index]
    after = rows_.at[pl.ds(rows + 8, length), :]
    after[...] = alpha * faces[pl.ds(2 * length, length), :] + gamma * reports[-1][:length]
    following = dot(after[pl.ds(first, layers), :], table_z[...])
    for index in range(layers):
        value = field[index]
        pressure[index] = value
        rows_[pl.ds(0, rows), :] = value
        rows_[pl.ds(rows, 1), :] = following[index : index + 1]
        flow[0, index] = star[0, index] - (field[index + 1] - value)
        flow[1, index] = star[1, index] - (rows_[pl.ds(1, rows), :] - value)
        flow[2, index] = star[2, index] - (lane_shift(value, 1) - value)


def ring(reports):
    if len(reports) != 4:
        return reports
    own, near, across, far = reports
    even = lax.rem(lax.axis_index("gy"), 2) == 0
    return [own, jnp.where(even, far, near), across, jnp.where(even, near, far)]


def along(array, axis, by):
    length = lax.axis_size(axis)
    return lax.ppermute(array, axis, [(i, (i + by) % length) for i in range(length)])


def swapped(array, bit, by=0):
    count_x, count_y = lax.axis_size("gx"), lax.axis_size("gy")
    pairs = [
        (x * count_y + y, (x ^ bit) * count_y + (y + by) % count_y)
        for x in range(count_x)
        for y in range(count_y)
    ]
    return lax.ppermute(array, ("gx", "gy"), pairs)


def pack(body, inputs, received, shapes, scratch, count):
    inputs = [pltpu.with_memory_space_constraint(each, pltpu.HBM) for each in inputs]
    return pl.pallas_call(
        body,
        out_shape=[jax.ShapeDtypeStruct(shape, F32) for shape in shapes],
        in_specs=[pl.BlockSpec(memory_space=pltpu.HBM)] * len(inputs) + [VMEM] * len(received),
        out_specs=[VMEM] * len(shapes),
        scratch_shapes=scratch + [pltpu.SemaphoreType.DMA((count,))],
        compiler_params=pltpu.CompilerParams(vmem_limit_bytes=4 << 20),
    )(*inputs, *received)


def per_device(melt_flow, thermal_state, powder_flag, spot_lateral_a_cell, spot_lateral_b_cell):
    layers, rows, depth = thermal_state.shape
    count_x, count_y = lax.axis_size("gx"), lax.axis_size("gy")
    group = min(count_x, BLOCK // layers)
    blocks = count_x // group
    length = group * layers
    rounds = group.bit_length() - 1
    plane = (rows, depth)
    sine_y, values_y = sines(rows)
    sine_z, values_z = sines(depth)
    left, right = packed_tables(sine_y, sine_z)
    table_z = jnp.asarray(sine_z, F32)
    edge = jnp.asarray(np.broadcast_to(sine_y[0][:, None], plane), F32)
    diagonal = jnp.asarray(2.0 + values_y[:, None] + values_z[None, :], F32)
    line = (length, depth)

    parts = melt_flow.shape[0]
    width = max(rows, depth)
    outer_planes = (2 * parts * rows + 8, width)
    ahead, behind, last_rows, first_rows = pack(
        halo_kernel,
        [melt_flow, thermal_state, powder_flag],
        [],
        [outer_planes] * 2 + [(parts + extra, layers, 8, depth) for extra in (2, 1)],
        [pltpu.VMEM((2,) + plane, F32), pltpu.VMEM((layers, 8, depth), jnp.int32)],
        7 + 4 * parts,
    )
    low_x = along(ahead, "gx", 1)
    high_x = along(behind, "gx", -1)
    low_y = along(last_rows, "gy", 1)
    high_y = along(first_rows, "gy", -1)
    extra, back, last = pack(
        extra_kernel,
        [melt_flow, thermal_state, powder_flag],
        [low_y, high_y],
        [(rows + 8, width), (8, depth), (2,) + plane],
        [
            pltpu.VMEM((5,) + plane, F32),
            pltpu.VMEM(plane, jnp.int32),
            pltpu.VMEM((1, rows + 16, depth), F32),
        ],
        7,
    )
    extra = along(extra, "gx", 1)
    back = along(back, "gx", -1)
    early_low = along(last, "gx", 1)
    ratio, weight = call(
        functools.partial(tables_kernel, group, layers),
        [diagonal],
        [(length + 1,) + plane, (4 * rounds + 1,) + plane],
    )
    marched = [melt_flow, low_x, high_x, thermal_state, powder_flag, low_y, high_y]
    padded = pltpu.VMEM((4, rows + 16, depth), F32)
    one_padded = pltpu.VMEM((1, rows + 16, depth), F32)
    (star,) = call(
        march_kernel, marched + [weight], [(3, layers) + plane], [padded], loose=1, flops=3 << 27
    )
    (partial,) = call(
        transform_kernel,
        [star, left, right],
        [(layers,) + plane],
        [pltpu.VMEM((rows + 16, depth), F32)],
        flops=1 << 27,
    )
    source, message = call(
        functools.partial(source_kernel, group, length),
        [
            melt_flow, low_x, thermal_state, extra, back, low_y, partial, left, right, table_z,
            edge, ratio,
        ],
        [(layers,) + plane, (2 * rows, depth)],
        [one_padded, pltpu.VMEM((layers, depth), F32)],
    )
    faces, late = call(
        functools.partial(faces_kernel, group, length),
        [source, ratio, weight, edge, thermal_state, early_low],
        [(2 * length + 8, depth), (2,) + plane],
        [pltpu.VMEM((max(length, layers + 1),) + plane, F32)],
        loose=1,
    )
    alone = blocks == 1
    early_high = along(late, "gx", -1)
    warmed, token = call(
        heat_kernel,
        [
            spot_lateral_a_cell, spot_lateral_b_cell, thermal_state, early_low, early_high,
            low_y, high_y, melt_flow,
        ],
        [(layers,) + plane, (8, depth)],
        [one_padded],
        scalars=2,
        flops=1 << 28,
    )
    sums = jnp.zeros((2,) + plane, F32)
    for turn in range(rounds - 1):
        message, sums, head, tail = call(
            functools.partial(merge_kernel, turn, group, length),
            [
                message, swapped(message, 1 << turn), faces, swapped(faces, 1 << turn),
                sums, weight,
            ],
            [(2 * rows + length + 8, depth), (2,) + plane, line, line],
        )
        if turn + 2 < rounds:
            rest = message[2 * rows + length :]
            message, faces = message[: 2 * rows], jnp.concatenate([head, tail, rest], 0)
    bit = group >> 1
    other = swapped(message, bit)
    rim = [
        swapped(tail, 0, 1), swapped(tail, bit, 1), swapped(head, 0, -1), swapped(head, bit, -1)
    ]
    outer = []
    scratch = [pltpu.VMEM((length + 1,) + plane, F32)]
    if not alone:
        (ends,) = call(
            functools.partial(close_kernel, rounds - 1, group, length),
            [message, other, sums, weight, ratio],
            [(2,) + plane],
        )
        outer = [jnp.stack([along(ends[0], "gx", group), along(ends[1], "gx", -group)])]
    operands = [source, message, other, sums] + rim
    operands += [weight, ratio, edge] + outer + [token]

    def coarse(*refs):
        coarse_kernel(rounds - 1, group, length, alone, *refs[:4], refs[4:8], *refs[8:])

    precond, image, report, faces = call(
        coarse,
        operands,
        [
            (layers + 1,) + plane, (layers + 1,) + plane, (2 * length + 8, depth),
            (3 * length, depth),
        ],
        scratch + [pltpu.VMEM((2,) + plane, F32)],
        loose=1,
    )
    if blocks > 1:
        onward = along(image[0], "gx", -1)
        at_end = position(group) == group - 1
        image = image.at[layers].set(jnp.where(at_end, onward, image[layers]))
        upper = along(report[:length], "gy", -1)
        crossing = jnp.sum(onward * image[layers - 1])
        crossing = crossing + jnp.sum(upper * report[length : 2 * length])
        numbers = report[2 * length :].at[3].set(2.0 * crossing)
        numbers = lax.psum(jnp.where(at_end, numbers, 0.0), "gx")
        report = report.at[2 * length :].set(numbers)
    reports = [report]
    for by in range(1, count_y):
        pairs = [(i, i ^ by if count_y == 4 else (i + by) % count_y) for i in range(count_y)]
        reports.append(lax.ppermute(report, "gy", pairs))
    precond, image = call(
        physical_kernel,
        [precond, image, left, right],
        [(layers + 1,) + plane, (layers + 1,) + plane],
    )
    flow, pressure = call(
        functools.partial(project_kernel, group, length, blocks > 1),
        [star, precond, image, faces, table_z] + reports,
        [(3, layers) + plane, (layers,) + plane],
        [
            pltpu.VMEM((layers + 1,) + plane, F32),
            pltpu.VMEM((rows + 8 + length, depth), F32),
        ],
    )
    return (flow, warmed, pressure)


def solution(mesh):
    placed = (
        P(None, ("runs", "gx"), "gy", None),
        P(("runs", "gx"), "gy", None),
        P(("runs", "gx"), "gy", None),
        P("runs"),
        P("runs"),
    )
    return jax.shard_map(
        per_device,
        mesh=mesh,
        in_specs=placed,
        out_specs=(
            P(None, ("runs", "gx"), "gy", None),
            P(("runs", "gx"), "gy", None),
            P(("runs", "gx"), "gy", None),
        ),
        check_vma=False,
    )
```

```python
import functools
import math

import jax
import jax.numpy as jnp
import numpy as np
from jax import lax
from jax.experimental import pallas as pl
from jax.experimental.pallas import tpu as pltpu
from jax.sharding import PartitionSpec as P

BLOCK = 128

TIME_INCREMENT = 0.2
MARANGONI = 1.5
DRAG_RATE = 4.0
LASER_POWER = 3.0
SPOT_RADIUS = 5.0

F32 = jnp.float32
VMEM = pl.BlockSpec(memory_space=pltpu.VMEM)
SMEM = pl.BlockSpec(memory_space=pltpu.SMEM)


def call(body, operands, shapes, scratch=(), scalars=0, loose=0, flops=1 << 20):
    out_shape = [jax.ShapeDtypeStruct(shape, F32) for shape in shapes]
    moved = 4 * sum(math.prod(shape) for shape in shapes)
    held = moved + 4 * sum(operand.size for operand in operands)
    held += 4 * sum(math.prod(space.shape) for space in scratch)
    return pl.pallas_call(
        body,
        out_shape=out_shape,
        in_specs=[SMEM] * scalars
        + [VMEM] * (len(operands) - scalars - loose)
        + [pl.BlockSpec(memory_space=pl.ANY)] * loose,
        out_specs=[VMEM] * len(shapes),
        scratch_shapes=list(scratch),
        compiler_params=pltpu.CompilerParams(vmem_limit_bytes=held + (4 << 20)),
        cost_estimate=pl.CostEstimate(flops=flops, bytes_accessed=2 * moved, transcendentals=0),
    )(*operands)


def dot(left, right):
    return jnp.dot(left, right, precision=lax.Precision.HIGHEST, preferred_element_type=F32)


def split(cells):
    high = cells.astype(jnp.bfloat16)
    return high, (cells - high.astype(F32)).astype(jnp.bfloat16)


def folded(product):
    half = product.shape[1] // 2
    return product[:, :half] + product[:, half:]


def packed_tables(left, right):
    left_high, left_low = split(np.asarray(left, np.float32))
    right_high, right_low = split(np.asarray(right, np.float32))
    zero = np.zeros_like(right_low)
    return (
        jnp.asarray(np.concatenate([left_high, left_low], 1)),
        jnp.asarray(np.block([[right_high, right_low], [right_high, zero]])),
    )


def transformed(planes, left, right):
    rows = planes[0].shape[0]
    high, low = split(jnp.concatenate(planes, 0))
    cells = jnp.concatenate([high, low], 1)
    cells = folded(jnp.dot(cells, right[...], preferred_element_type=F32))
    out = []
    for index in range(len(planes)):
        high, low = split(cells[index * rows : (index + 1) * rows])
        upper = jnp.concatenate([high, low], 1)
        lower = jnp.concatenate([high, jnp.zeros_like(low)], 1)
        cells_ = jnp.concatenate([upper, lower], 0)
        out.append(folded(jnp.dot(left[...], cells_, preferred_element_type=F32)))
    return out


def total(cells):
    return jnp.sum(jnp.sum(cells, axis=0, keepdims=True), axis=1, keepdims=True)


def loop(low, high, body, start):
    if isinstance(high, int) and isinstance(low, int) and high - low <= 24:
        carry = start
        for index in range(low, high):
            carry = body(index, carry)
        return carry
    return lax.fori_loop(low, high, body, start)


def position(group):
    return lax.rem(lax.axis_index("gx"), group)


def sines(length):
    positions = np.arange(length) + 1.0
    step = math.pi / (length + 1)
    table = np.sqrt(2.0 / (length + 1)) * np.sin(step * positions[:, None] * positions[None, :])
    return table, 2.0 - 2.0 * np.cos(step * positions)


def lane_shift(cells, offset):
    width = cells.shape[1]
    lane = lax.broadcasted_iota(jnp.int32, cells.shape, 1)
    moved = pltpu.roll(cells, (-offset) % width, 1)
    keep = lane < width - offset if offset > 0 else lane >= -offset
    return jnp.where(keep, moved, 0.0)


def column(row):
    length = row.shape[1]
    shape = (length, length)
    same = lax.broadcasted_iota(jnp.int32, shape, 0) == lax.broadcasted_iota(jnp.int32, shape, 1)
    return jnp.sum(jnp.where(same, row, 0.0), axis=1, keepdims=True)


def coefficients(speed, scale):
    factors = [0.5 * TIME_INCREMENT * jnp.abs(each) for each in speed]
    if scale is not None:
        factors = [each * scale for each in factors]
    centre = (1.0 if scale is None else scale) - 3.0 * (factors[0] + factors[1] + factors[2])
    near, far = 4.0 * factors[2], -factors[2]
    ahead = speed[2] >= 0.0
    lane = lax.broadcasted_iota(jnp.int32, near.shape, 1)
    width = near.shape[1]
    depth = (
        jnp.where(ahead & (lane >= 1), near, 0.0),
        jnp.where(ahead & (lane >= 2), far, 0.0),
        jnp.where(ahead | (lane >= width - 1), 0.0, near),
        jnp.where(ahead | (lane >= width - 2), 0.0, far),
    )
    return centre, speed[0] >= 0.0, factors[0], speed[1] >= 0.0, factors[1], depth


def advance(layers, padded, index, weights, start=0):
    middle = layers[2]
    rows, width = middle.shape
    centre, ahead_x, factor_x, ahead_y, factor_y, depth = weights
    near = jnp.where(ahead_x, layers[1], layers[3])
    far = jnp.where(ahead_x, layers[0], layers[4])
    moved = centre * middle + factor_x * (4.0 * near - far)
    beside = lambda offset: padded[index, pl.ds(8 + offset + start, rows), :]
    near = jnp.where(ahead_y, beside(-1), beside(1))
    far = jnp.where(ahead_y, beside(-2), beside(2))
    moved = moved + factor_y * (4.0 * near - far)
    for factor, offset in zip(depth, (1, 2, width - 1, width - 2)):
        moved = moved + factor * pltpu.roll(middle, offset, 1)
    return moved


def pad_rows(padded, index, before, middle, after):
    rows = middle.shape[0]
    padded[index, pl.ds(8, rows), :] = middle
    padded[index, pl.ds(6, 2), :] = before
    padded[index, pl.ds(8 + rows, 2), :] = after


def march_layer(refs, padded, index, parts, start, count, edges=None):
    flow, low_x, high_x, thermal, flag = refs
    _, layers, rows, depth = flow.shape
    span = pl.ds(start, count)
    speed = [flow[part, index, span, :] for part in range(3)]
    drag = 1.0 / (1.0 + TIME_INCREMENT * DRAG_RATE * flag[index, span, :].astype(F32))
    top = lax.broadcasted_iota(jnp.int32, (count, depth), 1) == depth - 1
    pull = jnp.where(top, (-MARANGONI * 0.5 * TIME_INCREMENT) * drag, 0.0)
    weights = coefficients(speed, drag)
    out = []
    for part in parts:
        around = []
        for other in range(index - 2, index + 3):
            if other < 0:
                first = (2 * part + other + 2) * rows + start
                around.append(low_x[pl.ds(first, count), :])
            elif other >= layers:
                first = (2 * part + other - layers) * rows + start
                around.append(high_x[pl.ds(first, count), :])
            else:
                around.append(flow[part, other, span, :])
        moved = advance(around, padded, part, weights, start)
        if part == 0:
            behind = edges[0][start : start + count]
            before = edges[1][start : start + count]
            behind = thermal[index - 1, span, :] if index > 0 else behind
            before = thermal[index + 1, span, :] if index + 1 < layers else before
            moved = moved + pull * (before - behind)
        if part == 1:
            slope = padded[3, pl.ds(9 + start, count), :] - padded[3, pl.ds(7 + start, count), :]
            moved = moved + pull * slope
        out.append(moved)
    return out


def pad_layer(refs, low_y, high_y, padded, index):
    flow, _, _, thermal, _ = refs
    for part in range(3):
        pad_rows(
            padded, part, low_y[part, index, 6:], flow[part, index], high_y[part, index, :2]
        )
    pad_rows(padded, 3, low_y[3, index, 6:], thermal[index], high_y[3, index, :2])


def march_kernel(
    flow, low_x, high_x, thermal, flag, low_y, high_y, _, star, padded
):
    refs = (flow, low_x, high_x, thermal, flag)
    _, layers, rows, depth = flow.shape
    edges = [column(halo[pl.ds(halo.shape[0] - 8, 1), pl.ds(0, rows)]) for halo in (low_x, high_x)]
    count = math.gcd(rows, 16)
    for index in range(layers):
        pad_layer(refs, low_y, high_y, padded, index)
        for start in range(0, rows, count):
            value = march_layer(refs, padded, index, range(3), start, count, edges)
            for part in range(3):
                star[part, index, pl.ds(start, count), :] = value[part]


def side_plane(flow, low_x, thermal, extra, padded):
    rows, depth = flow.shape[2:]
    plane = lambda index: low_x[pl.ds(index * rows, rows), pl.ds(0, depth)]
    beside = extra[pl.ds(rows, 8), pl.ds(0, depth)]
    given = extra[pl.ds(0, rows), pl.ds(0, depth)]
    pad_rows(padded, 0, beside[2:4], plane(1), beside[4:6])
    none = jnp.zeros((rows, depth), F32)
    around = [none, plane(0), plane(1), flow[0, 0], flow[0, 1]]
    moved = advance(around, padded, 0, coefficients([plane(1), plane(3), plane(5)], given))
    moved = jnp.where(plane(1) >= 0.0, given, moved)
    top = lax.broadcasted_iota(jnp.int32, (rows, depth), 1) == depth - 1
    behind = column(extra[pl.ds(rows, 1), pl.ds(0, rows)])
    drag = column(extra[pl.ds(rows + 6, 1), pl.ds(0, rows)])
    pull = (-MARANGONI * 0.5 * TIME_INCREMENT) * drag
    return moved + jnp.where(top, pull * (thermal[0] - behind), 0.0)


def transform_kernel(star, left, right, partial, rows_):
    _, layers, rows, depth = star.shape
    rows_[pl.ds(0, 8), :] = jnp.zeros((8, depth), F32)
    planes = []
    for index in range(layers):
        rows_[pl.ds(8, rows), :] = star[1, index]
        sink = star[0, index]
        if index > 0:
            sink = sink - star[0, index - 1]
        sink = sink + (star[1, index] - rows_[pl.ds(7, rows), :])
        sink = sink + (star[2, index] - lane_shift(star[2, index], -1))
        planes.append(-sink)
    for index, plane in enumerate(transformed(planes, left, right)):
        partial[index] = plane


def side_rows(flow, thermal, low_y, extra, back, padded):
    _, layers, rows, depth = flow.shape
    row = lambda ref, index: jnp.broadcast_to(ref[pl.ds(index, 1), pl.ds(0, depth)], (8, depth))
    top = lax.broadcasted_iota(jnp.int32, (8, depth), 1) == depth - 1
    padded[0, pl.ds(0, 8), :] = jnp.zeros((8, depth), F32)
    out = []
    for index in range(layers):
        around = []
        for other in range(index - 2, index + 3):
            if other < 0:
                around.append(row(extra, rows + 1 if other == -2 else rows + 7))
            elif other >= layers:
                around.append(row(back, other - layers))
            else:
                around.append(low_y[1, other])
        drag = 1.0 / (1.0 + TIME_INCREMENT * DRAG_RATE * low_y[4, index])
        pull = jnp.where(top, (-MARANGONI * 0.5 * TIME_INCREMENT) * drag, 0.0)
        padded[0, pl.ds(8, 8), :] = low_y[3, index]
        padded[0, pl.ds(16, 8), :] = thermal[index, :8, :]
        slope = padded[0, pl.ds(9, 8), :] - padded[0, pl.ds(7, 8), :]
        padded[0, pl.ds(8, 8), :] = low_y[1, index]
        padded[0, pl.ds(16, 8), :] = flow[1, index, :8, :]
        weights = coefficients([low_y[part, index] for part in range(3)], drag)
        moved = advance(around, padded, 0, weights) + pull * slope
        out.append(moved[7:])
    return out


def source_kernel(
    group, length, flow, low_x, thermal, extra, back, low_y, partial, left, right, table_z, edge,
    ratio, source, message, padded, rows_,
):
    layers, rows, depth = partial.shape
    first = position(group) * layers
    for index, row in enumerate(side_rows(flow, thermal, low_y, extra, back, padded)):
        rows_[pl.ds(index, 1), :] = row
    beside = dot(rows_[...], table_z[...])
    (onward,) = transformed([side_plane(flow, low_x, thermal, extra, padded)], left, right)
    for index in range(layers):
        value = partial[index] + edge[...] * beside[index : index + 1]
        source[index] = value + onward if index == 0 else value
    backward = source[layers - 1]
    for index in range(layers - 2, -1, -1):
        backward = source[index] + ratio[length - 1 - first - index] * backward
    message[pl.ds(rows, rows), :] = backward
    forward = source[0]
    for index in range(1, layers):
        forward = source[index] + ratio[first + index] * forward
    message[pl.ds(0, rows), :] = forward


def started(copies):
    for copy in copies:
        copy.start()
    return copies


def surface(plane):
    rows, depth = plane.shape
    shape = (rows, rows)
    same = lax.broadcasted_iota(jnp.int32, shape, 0) == lax.broadcasted_iota(jnp.int32, shape, 1)
    return jnp.sum(jnp.where(same, plane[:, depth - 1 :], 0.0), axis=0, keepdims=True)


def outer_copies(flow, thermal, message, top, first):
    parts, layers, rows, depth = flow.shape
    pairs = [(thermal.at[0 if first == 0 else layers - 1], top)]
    for part in range(parts):
        for layer in range(2):
            span = pl.ds((2 * part + layer) * rows, rows)
            pairs.append((flow.at[part, first + layer], message.at[span, :]))
    return pairs


def finish(copies, message, top):
    rows = top.shape[0]
    copies[0].wait()
    row = jnp.broadcast_to(surface(top[...]), (8, rows))
    message[pl.ds(message.shape[0] - 8, 8), pl.ds(0, rows)] = row
    for copy in copies[1:]:
        copy.wait()


def ahead_kernel(flow, thermal, message, top, sems):
    pairs = outer_copies(flow, thermal, message, top, flow.shape[1] - 2)
    copies = started(
        [pltpu.make_async_copy(*pair, sems.at[index]) for index, pair in enumerate(pairs)]
    )
    finish(copies, message, top)


def behind_kernel(flow, thermal, flag, message, last_rows, first_rows, top, flags, sems):
    parts, layers, rows, depth = flow.shape
    pairs = outer_copies(flow, thermal, message, top, 0)
    for target, start in ((last_rows, rows - 8), (first_rows, 0)):
        span = pl.ds(start, 8)
        pairs.append((flow.at[:, :, span, :], target.at[pl.ds(0, parts)]))
        pairs.append((thermal.at[:, span, :], target.at[parts]))
    pairs.append((flag.at[:, pl.ds(rows - 8, 8), :], flags))
    copies = started(
        [pltpu.make_async_copy(*pair, sems.at[index]) for index, pair in enumerate(pairs)]
    )
    finish(copies, message, top)
    last_rows[parts + 1] = flags[...].astype(F32)


def extra_kernel(
    flow, thermal, flag, low_y, high_y, extra, back, last, planes, flags, padded, sems
):
    _, layers, rows, depth = flow.shape
    pairs = [(flag.at[layers - 1], flags), (thermal.at[pl.ds(layers - 2, 2)], last)]
    sources = [(0, layers - 3), (0, layers - 2), (0, layers - 1), (1, layers - 1), (2, layers - 1)]
    for index, (part, layer) in enumerate(sources):
        pairs.append((flow.at[part, layer], planes.at[index]))
    copies = started(
        [pltpu.make_async_copy(*pair, sems.at[index]) for index, pair in enumerate(pairs)]
    )
    extra[pl.ds(rows, 8), :] = jnp.zeros((8, extra.shape[1]), F32)
    extra[pl.ds(rows + 2, 2), pl.ds(0, depth)] = low_y[0, layers - 1, 6:, :]
    extra[pl.ds(rows + 4, 2), pl.ds(0, depth)] = high_y[0, layers - 1, :2, :]
    extra[pl.ds(rows + 1, 1), pl.ds(0, depth)] = low_y[1, layers - 2, 7:, :]
    extra[pl.ds(rows + 7, 1), pl.ds(0, depth)] = low_y[1, layers - 1, 7:, :]
    back[...] = jnp.zeros(back.shape, F32)
    for index in range(2):
        back[pl.ds(index, 1), :] = low_y[1, index, 7:, :]
    for copy in copies:
        copy.wait()
    speed = [planes[index] for index in (2, 3, 4)]
    drag = 1.0 / (1.0 + TIME_INCREMENT * DRAG_RATE * flags[...].astype(F32))
    pad_rows(padded, 0, low_y[0, layers - 1, 6:], speed[0], high_y[0, layers - 1, :2])
    none = jnp.zeros((rows, depth), F32)
    around = [planes[0], planes[1], speed[0], none, none]
    moved = advance(around, padded, 0, coefficients(speed, drag))
    extra[pl.ds(0, rows), pl.ds(0, depth)] = jnp.where(speed[0] >= 0.0, moved, drag)
    extra[pl.ds(rows, 1), pl.ds(0, rows)] = surface(last[0])
    extra[pl.ds(rows + 6, 1), pl.ds(0, rows)] = surface(drag)


def wrapped(distance, span):
    moved = distance + span // 2
    moved = jnp.where(moved < 0, moved + span, moved)
    moved = jnp.where(moved >= span, moved - span, moved)
    return (moved - span // 2).astype(F32)


def laser_row(index, layers, rows, spots_a, spots_b):
    total_x = layers * lax.axis_size("gx")
    total_y = rows * lax.axis_size("gy")
    cell_x = lax.axis_index("gx") * layers + index
    cells_y = lax.broadcasted_iota(jnp.int32, (1, rows), 1) + lax.axis_index("gy") * rows
    heat = jnp.zeros((1, rows), F32)
    for spot in range(spots_a.shape[0]):
        dist_x = wrapped(jnp.full((1, rows), cell_x - spots_a[spot], jnp.int32), total_x)
        dist_y = wrapped(cells_y - spots_b[spot], total_y)
        square = dist_x * dist_x + dist_y * dist_y
        heat = heat + jnp.exp(square * (-1.0 / (SPOT_RADIUS * SPOT_RADIUS)))
    return LASER_POWER * heat


def heat_kernel(
    spots_a, spots_b, thermal, low_x, high_x, low_y, high_y, flow, warmed, token, padded
):
    layers, rows, depth = thermal.shape
    token[...] = jnp.zeros(token.shape, F32)
    top = lax.broadcasted_iota(jnp.int32, (rows, depth), 1) == depth - 1
    for index in range(layers):
        pad_rows(padded, 0, low_y[3, index, 6:], thermal[index], high_y[3, index, :2])
        around = []
        for other in range(index - 2, index + 3):
            if other < 0:
                around.append(low_x[other + 2])
            elif other >= layers:
                around.append(high_x[other - layers])
            else:
                around.append(thermal[other])
        speed = [flow[part, index] for part in range(3)]
        gain = TIME_INCREMENT * column(laser_row(index, layers, rows, spots_a, spots_b))
        moved = advance(around, padded, 0, coefficients(speed, None))
        warmed[index] = moved + jnp.where(top, gain, 0.0)


def tables_kernel(group, layers, diagonal, ratio, weight):
    length = group * layers
    mine = position(group)
    first = mine * layers
    diag = diagonal[...]
    ratio[0] = jnp.zeros_like(diag)

    def step(index, previous):
        current = 1.0 / (diag - previous)
        ratio[index] = current
        return current

    loop(1, length + 1, step, jnp.zeros_like(diag))

    def decay(low, high):
        return lax.fori_loop(
            low + 1, high + 1, lambda index, value: value * ratio[index], jnp.ones_like(diag)
        )

    def green(index):
        return 1.0 / (diag - ratio[index] - ratio[jnp.maximum(length - 1 - index, 0)])

    rounds = group.bit_length() - 1
    for turn in range(rounds):
        half = 1 << turn
        right = ((mine >> turn) & 1) == 1
        start = (mine >> (turn + 1)) << (turn + 1)
        cut = (start + half) * layers
        end = (start + 2 * half) * layers
        weight[4 * turn] = decay(cut - 1, end - 1)
        weight[4 * turn + 1] = decay(length - 1 - cut, length - 1 - start * layers)
        low = jnp.where(right, cut - 1, length - 1 - cut)
        high = jnp.where(right, first - 1, length - 1 - first - layers)
        weight[4 * turn + 2] = decay(low, high)
        weight[4 * turn + 3] = green(cut) * ratio[cut]
    inner = jnp.where(mine == group - 1, 0.0, 1.0)
    weight[4 * rounds] = inner * green(first + layers)


def grouped(plane):
    return plane.reshape(plane.shape[0] // 8, 8, plane.shape[1])


def signs(depth):
    row = lax.broadcasted_iota(jnp.int32, (8, depth), 0)
    return jnp.where(row % 2 == 0, 1.0, -1.0)


def face_rows(plane, lead):
    sums = jnp.sum(plane * lead, axis=0)
    return (
        jnp.sum(sums, axis=0, keepdims=True),
        jnp.sum(sums * signs(sums.shape[1]), axis=0, keepdims=True),
    )


def faces_kernel(
    group, length, source, ratio, weight, edge, thermal, _, faces, late, sweep
):
    layers, rows, depth = source.shape
    late[...] = thermal[:2]
    first = position(group) * layers
    zero = jnp.zeros((rows, depth), F32)
    forward = zero
    for index in range(layers):
        forward = source[index] + ratio[first + index] * forward
        sweep[index] = forward
    value = weight[weight.shape[0] - 1] * (ratio[first + layers] * forward)
    energy = zero
    for index in range(layers - 1, -1, -1):
        value = ratio[first + index + 1] * (sweep[index] + value)
        energy = energy + source[index] * value
    faces[pl.ds(2 * length, 8), :] = jnp.broadcast_to(total(energy), (8, depth))

    lead = grouped(edge[...])
    zero = grouped(zero)

    def down(index, previous):
        inside = (index >= first) & (index < first + layers)
        own = jnp.where(inside, source[jnp.clip(index - first, 0, layers - 1)], 0.0)
        current = grouped(own) + grouped(ratio[index]) * previous
        sweep[index] = current.reshape(rows, depth)
        return current

    loop(0, length, down, zero)

    def up(back, following):
        index = length - 1 - back
        value = grouped(ratio[index + 1]) * (grouped(sweep[index]) + following)
        low, high = face_rows(value, lead)
        faces[pl.ds(index, 1), :] = low
        faces[pl.ds(length + index, 1), :] = high
        return value

    loop(0, length, up, zero)


def joined(turn, group, message, other, sums, weight):
    rows, depth = weight.shape[1:]
    right = ((position(group) >> turn) & 1) == 1
    upper, lower = pl.ds(0, rows), pl.ds(rows, rows)
    left_s = jnp.where(right, other[upper, :], message[upper, :])
    right_s = jnp.where(right, message[upper, :], other[upper, :])
    left_t = jnp.where(right, other[lower, :], message[lower, :])
    right_t = jnp.where(right, message[lower, :], other[lower, :])
    own = weight[4 * turn + 2]
    before = sums[0] + jnp.where(right, left_s * own, 0.0)
    after = sums[1] + jnp.where(right, 0.0, right_t * own)
    forward = right_s + left_s * weight[4 * turn]
    backward = left_t + right_t * weight[4 * turn + 1]
    energy = 2.0 * total(left_s * right_t * weight[4 * turn + 3])
    return forward, backward, before, after, energy


def merge_kernel(
    turn, group, length, message, other, faces, other_faces, sums, weight,
    new_message, new_sums, head, tail,
):
    rows, depth = weight.shape[1:]
    forward, backward, before, after, energy = joined(turn, group, message, other, sums, weight)
    new_sums[0] = before
    new_sums[1] = after
    new_message[pl.ds(0, rows), :] = forward
    new_message[pl.ds(rows, rows), :] = backward
    low, high = pl.ds(0, length), pl.ds(length, length)
    number = pl.ds(2 * length, 8)
    head[...] = faces[low, :] + other_faces[low, :]
    tail[...] = faces[high, :] + other_faces[high, :]
    new_message[pl.ds(2 * rows, length), :] = head[...]
    energy = faces[number, :] + other_faces[number, :] + energy
    new_message[pl.ds(2 * rows + length, 8), :] = energy


def close_kernel(turn, group, length, message, other, sums, weight, ratio, ends):
    forward, backward, _, _, _ = joined(turn, group, message, other, sums, weight)
    ends[0] = ratio[length] * forward
    ends[1] = ratio[length] * backward


def coarse_kernel(
    turn, group, length, alone, source, message, other, sums, faces_in, weight, ratio, edge, *refs
):
    precond, image, report, faces, sweep, ends = refs[-6:]
    layers, rows, depth = source.shape
    first = position(group) * layers
    below, below_far, above, above_far = faces_in
    forward, backward, before, after, energy = joined(turn, group, message, other, sums, weight)
    ends[0] = ratio[length] * forward
    ends[1] = ratio[length] * backward
    beyond = ends if alone else refs[0]
    own = pl.ds(2 * rows, length)
    faces[pl.ds(0, length), :] = message[own, :] + other[own, :]
    faces[pl.ds(length, length), :] = below[...] + below_far[...]
    faces[pl.ds(2 * length, length), :] = above[...] + above_far[...]
    number = pl.ds(2 * rows + length, 8)
    energy = message[number, :] + other[number, :] + energy
    forward = before
    for index in range(layers):
        forward = source[index] + ratio[first + index] * forward
        precond[index] = forward
    value = weight[weight.shape[0] - 1] * (after + ratio[first + layers] * forward)
    is_last = first + layers == length
    precond[layers] = jnp.where(is_last, beyond[1], value)
    for index in range(layers - 1, -1, -1):
        value = ratio[first + index + 1] * (precond[index] + value)
        precond[index] = value
    lead = grouped(edge[...])
    sign = signs(depth)

    def pull(index):
        below = faces[pl.ds(length + index, 1), :]
        above = faces[pl.ds(2 * length + index, 1), :]
        return below, above

    def down(index, previous):
        below, above = pull(index)
        current = lead * (below + sign * above) + grouped(ratio[index]) * previous
        if isinstance(index, int):
            if index == 0:
                current = current + grouped(beyond[0])
            if index == length - 1:
                current = current + grouped(beyond[1])
        else:
            current = current + jnp.where(index == 0, grouped(beyond[0]), 0.0)
            current = current + jnp.where(index == length - 1, grouped(beyond[1]), 0.0)
        sweep[index] = current.reshape(rows, depth)
        return current

    zero = jnp.zeros(lead.shape, F32)
    loop(0, length, down, zero)
    line = jnp.zeros((1, depth), F32)

    def up(back, carry):
        following, linked, squared = carry
        index = length - 1 - back
        value = grouped(ratio[index + 1]) * (grouped(sweep[index]) + following)
        sweep[index] = value.reshape(rows, depth)
        low, high = face_rows(value, lead)
        report[pl.ds(index, 1), :] = low
        report[pl.ds(length + index, 1), :] = high
        below, above = pull(index)
        linked = linked + faces[pl.ds(index, 1), :] * below
        squared = squared + low * below + high * above
        return value, linked, squared

    _, linked, squared = loop(0, length, up, (zero, line, line))
    sweep[length] = sweep[0]
    for index in range(layers + 1):
        image[index] = sweep[first + index]
    head, tail = sweep[0], sweep[length - 1]
    linked = 2.0 * total(linked) + total(ends[1] * beyond[0] + ends[0] * beyond[1])
    squared = total(squared) + total(head * beyond[0] + tail * beyond[1])
    crossing = 2.0 * total(head * tail)
    where = 2 * length
    report[pl.ds(where, 1), :] = energy[0:1]
    report[pl.ds(where + 1, 1), :] = jnp.broadcast_to(linked, (1, depth))
    report[pl.ds(where + 2, 1), :] = jnp.broadcast_to(squared, (1, depth))
    report[pl.ds(where + 3, 1), :] = jnp.broadcast_to(crossing, (1, depth))
    report[pl.ds(where + 4, 4), :] = jnp.zeros((4, depth), F32)


def physical_kernel(precond, image, left, right, precond_out, image_out):
    count = precond.shape[0]
    planes = [precond[index] for index in range(count)] + [image[index] for index in range(count)]
    planes = transformed(planes, left, right)
    for index in range(count):
        precond_out[index] = planes[index]
        image_out[index] = planes[count + index]


def project_kernel(
    group, length, paired, star, precond, image, faces, table_z, *refs
):
    given, (flow, pressure, field, rows_) = refs[:-4], refs[-4:]
    _, layers, rows, depth = star.shape
    first = position(group) * layers
    where = 2 * length
    reports = ring([each[...] for each in given])
    sums = reports[0][where:]
    for other in reports[1:]:
        sums = sums + other[where:]
    pairs = jnp.zeros((1, depth), F32)
    for index in range(len(reports)):
        upper, lower = reports[index], reports[(index + 1) % len(reports)]
        pairs = pairs + jnp.sum(
            upper[:length] * lower[length:where], axis=0, keepdims=True
        )
    energy, linked, squared, crossing = (sums[k : k + 1, 0:1] for k in range(4))
    if not paired:
        crossing = crossing + 2.0 * total(pairs)
    first_image = energy - linked
    step = energy / first_image
    beta = (energy * squared - linked * linked) / (first_image * first_image)
    rest = -linked / first_image
    second_image = (
        rest * rest * first_image
        + 2.0 * rest * step * (linked - squared)
        + step * step * (squared - crossing)
        - beta * beta * first_image
    )
    second_step = beta * energy / second_image
    alpha = step + second_step * (rest + beta)
    gamma = second_step * step
    for index in range(layers + 1):
        field[index] = alpha * precond[index] + gamma * image[index]
    after = rows_.at[pl.ds(rows + 8, length), :]
    after[...] = alpha * faces[pl.ds(2 * length, length), :] + gamma * reports[-1][:length]
    following = dot(after[pl.ds(first, layers), :], table_z[...])
    for index in range(layers):
        value = field[index]
        pressure[index] = value
        rows_[pl.ds(0, rows), :] = value
        rows_[pl.ds(rows, 1), :] = following[index : index + 1]
        flow[0, index] = star[0, index] - (field[index + 1] - value)
        flow[1, index] = star[1, index] - (rows_[pl.ds(1, rows), :] - value)
        flow[2, index] = star[2, index] - (lane_shift(value, 1) - value)


def ring(reports):
    if len(reports) != 4:
        return reports
    own, near, across, far = reports
    even = lax.rem(lax.axis_index("gy"), 2) == 0
    return [own, jnp.where(even, far, near), across, jnp.where(even, near, far)]


def along(array, axis, by):
    length = lax.axis_size(axis)
    return lax.ppermute(array, axis, [(i, (i + by) % length) for i in range(length)])


def swapped(array, bit, by=0):
    count_x, count_y = lax.axis_size("gx"), lax.axis_size("gy")
    pairs = [
        (x * count_y + y, (x ^ bit) * count_y + (y + by) % count_y)
        for x in range(count_x)
        for y in range(count_y)
    ]
    return lax.ppermute(array, ("gx", "gy"), pairs)


def pack(body, inputs, received, shapes, scratch, count):
    inputs = [pltpu.with_memory_space_constraint(each, pltpu.HBM) for each in inputs]
    return pl.pallas_call(
        body,
        out_shape=[jax.ShapeDtypeStruct(shape, F32) for shape in shapes],
        in_specs=[pl.BlockSpec(memory_space=pltpu.HBM)] * len(inputs) + [VMEM] * len(received),
        out_specs=[VMEM] * len(shapes),
        scratch_shapes=scratch + [pltpu.SemaphoreType.DMA((count,))],
        compiler_params=pltpu.CompilerParams(vmem_limit_bytes=4 << 20),
    )(*inputs, *received)


def per_device(melt_flow, thermal_state, powder_flag, spot_lateral_a_cell, spot_lateral_b_cell):
    layers, rows, depth = thermal_state.shape
    count_x, count_y = lax.axis_size("gx"), lax.axis_size("gy")
    group = min(count_x, BLOCK // layers)
    blocks = count_x // group
    length = group * layers
    rounds = group.bit_length() - 1
    plane = (rows, depth)
    sine_y, values_y = sines(rows)
    sine_z, values_z = sines(depth)
    left, right = packed_tables(sine_y, sine_z)
    table_z = jnp.asarray(sine_z, F32)
    edge = jnp.asarray(np.broadcast_to(sine_y[0][:, None], plane), F32)
    diagonal = jnp.asarray(2.0 + values_y[:, None] + values_z[None, :], F32)
    line = (length, depth)

    parts = melt_flow.shape[0]
    width = max(rows, depth)
    outer_planes = (2 * parts * rows + 8, width)
    (ahead,) = pack(
        ahead_kernel,
        [melt_flow, thermal_state],
        [],
        [outer_planes],
        [pltpu.VMEM(plane, F32)],
        1 + 2 * parts,
    )
    behind, last_rows, first_rows = pack(
        behind_kernel,
        [melt_flow, thermal_state, powder_flag],
        [],
        [outer_planes] + [(parts + extra, layers, 8, depth) for extra in (2, 1)],
        [pltpu.VMEM(plane, F32), pltpu.VMEM((layers, 8, depth), jnp.int32)],
        6 + 2 * parts,
    )
    low_x = along(ahead, "gx", 1)
    high_x = along(behind, "gx", -1)
    low_y = along(last_rows, "gy", 1)
    high_y = along(first_rows, "gy", -1)
    extra, back, last = pack(
        extra_kernel,
        [melt_flow, thermal_state, powder_flag],
        [low_y, high_y],
        [(rows + 8, width), (8, depth), (2,) + plane],
        [
            pltpu.VMEM((5,) + plane, F32),
            pltpu.VMEM(plane, jnp.int32),
            pltpu.VMEM((1, rows + 16, depth), F32),
        ],
        7,
    )
    extra = along(extra, "gx", 1)
    back = along(back, "gx", -1)
    early_low = along(last, "gx", 1)
    ratio, weight = call(
        functools.partial(tables_kernel, group, layers),
        [diagonal],
        [(length + 1,) + plane, (4 * rounds + 1,) + plane],
    )
    marched = [melt_flow, low_x, high_x, thermal_state, powder_flag, low_y, high_y]
    padded = pltpu.VMEM((4, rows + 16, depth), F32)
    one_padded = pltpu.VMEM((1, rows + 16, depth), F32)
    (star,) = call(
        march_kernel, marched + [weight], [(3, layers) + plane], [padded], loose=1, flops=3 << 27
    )
    (partial,) = call(
        transform_kernel,
        [star, left, right],
        [(layers,) + plane],
        [pltpu.VMEM((rows + 16, depth), F32)],
        flops=1 << 27,
    )
    source, message = call(
        functools.partial(source_kernel, group, length),
        [
            melt_flow, low_x, thermal_state, extra, back, low_y, partial, left, right, table_z,
            edge, ratio,
        ],
        [(layers,) + plane, (2 * rows, depth)],
        [one_padded, pltpu.VMEM((layers, depth), F32)],
    )
    faces, late = call(
        functools.partial(faces_kernel, group, length),
        [source, ratio, weight, edge, thermal_state, early_low],
        [(2 * length + 8, depth), (2,) + plane],
        [pltpu.VMEM((max(length, layers + 1),) + plane, F32)],
        loose=1,
    )
    alone = blocks == 1
    early_high = along(late, "gx", -1)
    warmed, token = call(
        heat_kernel,
        [
            spot_lateral_a_cell, spot_lateral_b_cell, thermal_state, early_low, early_high,
            low_y, high_y, melt_flow,
        ],
        [(layers,) + plane, (8, depth)],
        [one_padded],
        scalars=2,
        flops=1 << 28,
    )
    sums = jnp.zeros((2,) + plane, F32)
    for turn in range(rounds - 1):
        message, sums, head, tail = call(
            functools.partial(merge_kernel, turn, group, length),
            [
                message, swapped(message, 1 << turn), faces, swapped(faces, 1 << turn),
                sums, weight,
            ],
            [(2 * rows + length + 8, depth), (2,) + plane, line, line],
        )
        if turn + 2 < rounds:
            rest = message[2 * rows + length :]
            message, faces = message[: 2 * rows], jnp.concatenate([head, tail, rest], 0)
    bit = group >> 1
    other = swapped(message, bit)
    rim = [
        swapped(tail, 0, 1), swapped(tail, bit, 1), swapped(head, 0, -1), swapped(head, bit, -1)
    ]
    outer = []
    scratch = [pltpu.VMEM((length + 1,) + plane, F32)]
    if not alone:
        (ends,) = call(
            functools.partial(close_kernel, rounds - 1, group, length),
            [message, other, sums, weight, ratio],
            [(2,) + plane],
        )
        outer = [jnp.stack([along(ends[0], "gx", group), along(ends[1], "gx", -group)])]
    operands = [source, message, other, sums] + rim
    operands += [weight, ratio, edge] + outer + [token]

    def coarse(*refs):
        coarse_kernel(rounds - 1, group, length, alone, *refs[:4], refs[4:8], *refs[8:])

    precond, image, report, faces = call(
        coarse,
        operands,
        [
            (layers + 1,) + plane, (layers + 1,) + plane, (2 * length + 8, depth),
            (3 * length, depth),
        ],
        scratch + [pltpu.VMEM((2,) + plane, F32)],
        loose=1,
    )
    if blocks > 1:
        onward = along(image[0], "gx", -1)
        at_end = position(group) == group - 1
        image = image.at[layers].set(jnp.where(at_end, onward, image[layers]))
        upper = along(report[:length], "gy", -1)
        crossing = jnp.sum(onward * image[layers - 1])
        crossing = crossing + jnp.sum(upper * report[length : 2 * length])
        numbers = report[2 * length :].at[3].set(2.0 * crossing)
        numbers = lax.psum(jnp.where(at_end, numbers, 0.0), "gx")
        report = report.at[2 * length :].set(numbers)
    reports = [report]
    for by in range(1, count_y):
        pairs = [(i, i ^ by if count_y == 4 else (i + by) % count_y) for i in range(count_y)]
        reports.append(lax.ppermute(report, "gy", pairs))
    precond, image = call(
        physical_kernel,
        [precond, image, left, right],
        [(layers + 1,) + plane, (layers + 1,) + plane],
    )
    flow, pressure = call(
        functools.partial(project_kernel, group, length, blocks > 1),
        [star, precond, image, faces, table_z] + reports,
        [(3, layers) + plane, (layers,) + plane],
        [
            pltpu.VMEM((layers + 1,) + plane, F32),
            pltpu.VMEM((rows + 8 + length, depth), F32),
        ],
    )
    return (flow, warmed, pressure)


def solution(mesh):
    placed = (
        P(None, ("runs", "gx"), "gy", None),
        P(("runs", "gx"), "gy", None),
        P(("runs", "gx"), "gy", None),
        P("runs"),
        P("runs"),
    )
    return jax.shard_map(
        per_device,
        mesh=mesh,
        in_specs=placed,
        out_specs=(
            P(None, ("runs", "gx"), "gy", None),
            P(("runs", "gx"), "gy", None),
            P(("runs", "gx"), "gy", None),
        ),
        check_vma=False,
    )
```

```python
import functools
import math

import jax
import jax.numpy as jnp
import numpy as np
from jax import lax
from jax.experimental import pallas as pl
from jax.experimental.pallas import tpu as pltpu
from jax.sharding import PartitionSpec as P

BLOCK = 128

TIME_INCREMENT = 0.2
MARANGONI = 1.5
DRAG_RATE = 4.0
LASER_POWER = 3.0
SPOT_RADIUS = 5.0

F32 = jnp.float32
VMEM = pl.BlockSpec(memory_space=pltpu.VMEM)
SMEM = pl.BlockSpec(memory_space=pltpu.SMEM)


def call(body, operands, shapes, scratch=(), scalars=0, loose=0, flops=1 << 20):
    out_shape = [jax.ShapeDtypeStruct(shape, F32) for shape in shapes]
    moved = 4 * sum(math.prod(shape) for shape in shapes)
    held = moved + 4 * sum(operand.size for operand in operands)
    held += 4 * sum(math.prod(space.shape) for space in scratch)
    return pl.pallas_call(
        body,
        out_shape=out_shape,
        in_specs=[SMEM] * scalars
        + [VMEM] * (len(operands) - scalars - loose)
        + [pl.BlockSpec(memory_space=pl.ANY)] * loose,
        out_specs=[VMEM] * len(shapes),
        scratch_shapes=list(scratch),
        compiler_params=pltpu.CompilerParams(vmem_limit_bytes=held + (4 << 20)),
        cost_estimate=pl.CostEstimate(flops=flops, bytes_accessed=2 * moved, transcendentals=0),
    )(*operands)


def dot(left, right):
    return jnp.dot(left, right, precision=lax.Precision.HIGHEST, preferred_element_type=F32)


def split(cells):
    high = cells.astype(jnp.bfloat16)
    return high, (cells - high.astype(F32)).astype(jnp.bfloat16)


def folded(product):
    half = product.shape[1] // 2
    return product[:, :half] + product[:, half:]


def packed_tables(left, right):
    left_high, left_low = split(np.asarray(left, np.float32))
    right_high, right_low = split(np.asarray(right, np.float32))
    zero = np.zeros_like(right_low)
    return (
        jnp.asarray(np.concatenate([left_high, left_low], 1)),
        jnp.asarray(np.block([[right_high, right_low], [right_high, zero]])),
    )


def transformed(planes, left, right):
    rows = planes[0].shape[0]
    high, low = split(jnp.concatenate(planes, 0))
    cells = jnp.concatenate([high, low], 1)
    cells = folded(jnp.dot(cells, right[...], preferred_element_type=F32))
    out = []
    for index in range(len(planes)):
        high, low = split(cells[index * rows : (index + 1) * rows])
        upper = jnp.concatenate([high, low], 1)
        lower = jnp.concatenate([high, jnp.zeros_like(low)], 1)
        cells_ = jnp.concatenate([upper, lower], 0)
        out.append(folded(jnp.dot(left[...], cells_, preferred_element_type=F32)))
    return out


def total(cells):
    return jnp.sum(jnp.sum(cells, axis=0, keepdims=True), axis=1, keepdims=True)


def loop(low, high, body, start):
    if isinstance(high, int) and isinstance(low, int) and high - low <= 24:
        carry = start
        for index in range(low, high):
            carry = body(index, carry)
        return carry
    return lax.fori_loop(low, high, body, start)


def position(group):
    return lax.rem(lax.axis_index("gx"), group)


def sines(length):
    positions = np.arange(length) + 1.0
    step = math.pi / (length + 1)
    table = np.sqrt(2.0 / (length + 1)) * np.sin(step * positions[:, None] * positions[None, :])
    return table, 2.0 - 2.0 * np.cos(step * positions)


def lane_shift(cells, offset):
    width = cells.shape[1]
    lane = lax.broadcasted_iota(jnp.int32, cells.shape, 1)
    moved = pltpu.roll(cells, (-offset) % width, 1)
    keep = lane < width - offset if offset > 0 else lane >= -offset
    return jnp.where(keep, moved, 0.0)


def column(row):
    length = row.shape[1]
    shape = (length, length)
    same = lax.broadcasted_iota(jnp.int32, shape, 0) == lax.broadcasted_iota(jnp.int32, shape, 1)
    return jnp.sum(jnp.where(same, row, 0.0), axis=1, keepdims=True)


def coefficients(speed, scale):
    factors = [0.5 * TIME_INCREMENT * jnp.abs(each) for each in speed]
    if scale is not None:
        factors = [each * scale for each in factors]
    centre = (1.0 if scale is None else scale) - 3.0 * (factors[0] + factors[1] + factors[2])
    near, far = 4.0 * factors[2], -factors[2]
    ahead = speed[2] >= 0.0
    lane = lax.broadcasted_iota(jnp.int32, near.shape, 1)
    width = near.shape[1]
    depth = (
        jnp.where(ahead & (lane >= 1), near, 0.0),
        jnp.where(ahead & (lane >= 2), far, 0.0),
        jnp.where(ahead | (lane >= width - 1), 0.0, near),
        jnp.where(ahead | (lane >= width - 2), 0.0, far),
    )
    return centre, speed[0] >= 0.0, factors[0], speed[1] >= 0.0, factors[1], depth


def advance(layers, padded, index, weights, start=0):
    middle = layers[2]
    rows, width = middle.shape
    centre, ahead_x, factor_x, ahead_y, factor_y, depth = weights
    near = jnp.where(ahead_x, layers[1], layers[3])
    far = jnp.where(ahead_x, layers[0], layers[4])
    moved = centre * middle + factor_x * (4.0 * near - far)
    beside = lambda offset: padded[index, pl.ds(8 + offset + start, rows), :]
    near = jnp.where(ahead_y, beside(-1), beside(1))
    far = jnp.where(ahead_y, beside(-2), beside(2))
    moved = moved + factor_y * (4.0 * near - far)
    for factor, offset in zip(depth, (1, 2, width - 1, width - 2)):
        moved = moved + factor * pltpu.roll(middle, offset, 1)
    return moved


def pad_rows(padded, index, before, middle, after):
    rows = middle.shape[0]
    padded[index, pl.ds(8, rows), :] = middle
    padded[index, pl.ds(6, 2), :] = before
    padded[index, pl.ds(8 + rows, 2), :] = after


def march_layer(refs, padded, index, parts, start, count, edges=None):
    flow, low_x, high_x, thermal, flag = refs
    _, layers, rows, depth = flow.shape
    span = pl.ds(start, count)
    speed = [flow[part, index, span, :] for part in range(3)]
    drag = 1.0 / (1.0 + TIME_INCREMENT * DRAG_RATE * flag[index, span, :].astype(F32))
    top = lax.broadcasted_iota(jnp.int32, (count, depth), 1) == depth - 1
    pull = jnp.where(top, (-MARANGONI * 0.5 * TIME_INCREMENT) * drag, 0.0)
    weights = coefficients(speed, drag)
    out = []
    for part in parts:
        around = []
        for other in range(index - 2, index + 3):
            if other < 0:
                first = (2 * part + other + 2) * rows + start
                around.append(low_x[pl.ds(first, count), :])
            elif other >= layers:
                first = (2 * part + other - layers) * rows + start
                around.append(high_x[pl.ds(first, count), :])
            else:
                around.append(flow[part, other, span, :])
        moved = advance(around, padded, part, weights, start)
        if part == 0:
            behind = edges[0][start : start + count]
            before = edges[1][start : start + count]
            behind = thermal[index - 1, span, :] if index > 0 else behind
            before = thermal[index + 1, span, :] if index + 1 < layers else before
            moved = moved + pull * (before - behind)
        if part == 1:
            slope = padded[3, pl.ds(9 + start, count), :] - padded[3, pl.ds(7 + start, count), :]
            moved = moved + pull * slope
        out.append(moved)
    return out


def pad_layer(refs, low_y, high_y, padded, index):
    flow, _, _, thermal, _ = refs
    for part in range(3):
        pad_rows(
            padded, part, low_y[part, index, 6:], flow[part, index], high_y[part, index, :2]
        )
    pad_rows(padded, 3, low_y[3, index, 6:], thermal[index], high_y[3, index, :2])


def march_kernel(
    flow, low_x, high_x, thermal, flag, low_y, high_y, _, star, padded
):
    refs = (flow, low_x, high_x, thermal, flag)
    _, layers, rows, depth = flow.shape
    edges = [column(halo[pl.ds(halo.shape[0] - 8, 1), pl.ds(0, rows)]) for halo in (low_x, high_x)]
    count = math.gcd(rows, 16)
    for index in range(layers):
        pad_layer(refs, low_y, high_y, padded, index)
        for start in range(0, rows, count):
            value = march_layer(refs, padded, index, range(3), start, count, edges)
            for part in range(3):
                star[part, index, pl.ds(start, count), :] = value[part]


def side_plane(flow, low_x, thermal, extra, padded):
    rows, depth = flow.shape[2:]
    plane = lambda index: low_x[pl.ds(index * rows, rows), pl.ds(0, depth)]
    beside = extra[pl.ds(rows, 8), pl.ds(0, depth)]
    given = extra[pl.ds(0, rows), pl.ds(0, depth)]
    pad_rows(padded, 0, beside[2:4], plane(1), beside[4:6])
    none = jnp.zeros((rows, depth), F32)
    around = [none, plane(0), plane(1), flow[0, 0], flow[0, 1]]
    moved = advance(around, padded, 0, coefficients([plane(1), plane(3), plane(5)], given))
    moved = jnp.where(plane(1) >= 0.0, given, moved)
    top = lax.broadcasted_iota(jnp.int32, (rows, depth), 1) == depth - 1
    behind = column(extra[pl.ds(rows, 1), pl.ds(0, rows)])
    drag = column(extra[pl.ds(rows + 6, 1), pl.ds(0, rows)])
    pull = (-MARANGONI * 0.5 * TIME_INCREMENT) * drag
    return moved + jnp.where(top, pull * (thermal[0] - behind), 0.0)


def transform_kernel(star, left, right, partial, rows_):
    _, layers, rows, depth = star.shape
    rows_[pl.ds(0, 8), :] = jnp.zeros((8, depth), F32)
    planes = []
    for index in range(layers):
        rows_[pl.ds(8, rows), :] = star[1, index]
        sink = star[0, index]
        if index > 0:
            sink = sink - star[0, index - 1]
        sink = sink + (star[1, index] - rows_[pl.ds(7, rows), :])
        sink = sink + (star[2, index] - lane_shift(star[2, index], -1))
        planes.append(-sink)
    for index, plane in enumerate(transformed(planes, left, right)):
        partial[index] = plane


def side_rows(flow, thermal, low_y, extra, back, padded):
    _, layers, rows, depth = flow.shape
    row = lambda ref, index: jnp.broadcast_to(ref[pl.ds(index, 1), pl.ds(0, depth)], (8, depth))
    top = lax.broadcasted_iota(jnp.int32, (8, depth), 1) == depth - 1
    padded[0, pl.ds(0, 8), :] = jnp.zeros((8, depth), F32)
    out = []
    for index in range(layers):
        around = []
        for other in range(index - 2, index + 3):
            if other < 0:
                around.append(row(extra, rows + 1 if other == -2 else rows + 7))
            elif other >= layers:
                around.append(row(back, other - layers))
            else:
                around.append(low_y[1, other])
        drag = 1.0 / (1.0 + TIME_INCREMENT * DRAG_RATE * low_y[4, index])
        pull = jnp.where(top, (-MARANGONI * 0.5 * TIME_INCREMENT) * drag, 0.0)
        padded[0, pl.ds(8, 8), :] = low_y[3, index]
        padded[0, pl.ds(16, 8), :] = thermal[index, :8, :]
        slope = padded[0, pl.ds(9, 8), :] - padded[0, pl.ds(7, 8), :]
        padded[0, pl.ds(8, 8), :] = low_y[1, index]
        padded[0, pl.ds(16, 8), :] = flow[1, index, :8, :]
        weights = coefficients([low_y[part, index] for part in range(3)], drag)
        moved = advance(around, padded, 0, weights) + pull * slope
        out.append(moved[7:])
    return out


def source_kernel(
    group, length, flow, low_x, thermal, extra, back, low_y, partial, left, right, table_z, edge,
    ratio, source, message, padded, rows_,
):
    layers, rows, depth = partial.shape
    first = position(group) * layers
    for index, row in enumerate(side_rows(flow, thermal, low_y, extra, back, padded)):
        rows_[pl.ds(index, 1), :] = row
    beside = dot(rows_[...], table_z[...])
    (onward,) = transformed([side_plane(flow, low_x, thermal, extra, padded)], left, right)
    for index in range(layers):
        value = partial[index] + edge[...] * beside[index : index + 1]
        source[index] = value + onward if index == 0 else value
    backward = source[layers - 1]
    for index in range(layers - 2, -1, -1):
        backward = source[index] + ratio[length - 1 - first - index] * backward
    message[pl.ds(rows, rows), :] = backward
    forward = source[0]
    for index in range(1, layers):
        forward = source[index] + ratio[first + index] * forward
    message[pl.ds(0, rows), :] = forward


def started(copies):
    for copy in copies:
        copy.start()
    return copies


def surface(plane):
    rows, depth = plane.shape
    shape = (rows, rows)
    same = lax.broadcasted_iota(jnp.int32, shape, 0) == lax.broadcasted_iota(jnp.int32, shape, 1)
    return jnp.sum(jnp.where(same, plane[:, depth - 1 :], 0.0), axis=0, keepdims=True)


def halo_kernel(
    flow, thermal, flag, ahead, behind, last_rows, first_rows, tops, flags, sems
):
    parts, layers, rows, depth = flow.shape
    pairs = [(thermal.at[layers - 1], tops.at[0]), (thermal.at[0], tops.at[1])]
    for part in range(parts):
        for layer in range(2):
            span = pl.ds((2 * part + layer) * rows, rows)
            pairs.append((flow.at[part, layers - 2 + layer], ahead.at[span, :]))
            pairs.append((flow.at[part, layer], behind.at[span, :]))
    for target, start in ((last_rows, rows - 8), (first_rows, 0)):
        span = pl.ds(start, 8)
        pairs.append((flow.at[:, :, span, :], target.at[pl.ds(0, parts)]))
        pairs.append((thermal.at[:, span, :], target.at[parts]))
    pairs.append((flag.at[:, pl.ds(rows - 8, 8), :], flags))
    copies = started(
        [pltpu.make_async_copy(*pair, sems.at[index]) for index, pair in enumerate(pairs)]
    )
    for side, message in enumerate((ahead, behind)):
        copies[side].wait()
        row = jnp.broadcast_to(surface(tops[side]), (8, rows))
        message[pl.ds(2 * parts * rows, 8), pl.ds(0, rows)] = row
    for copy in copies[2:]:
        copy.wait()
    last_rows[parts + 1] = flags[...].astype(F32)


def extra_kernel(
    flow, thermal, flag, low_y, high_y, extra, back, last, planes, flags, padded, sems
):
    _, layers, rows, depth = flow.shape
    pairs = [(flag.at[layers - 1], flags), (thermal.at[pl.ds(layers - 2, 2)], last)]
    sources = [(0, layers - 3), (0, layers - 2), (0, layers - 1), (1, layers - 1), (2, layers - 1)]
    for index, (part, layer) in enumerate(sources):
        pairs.append((flow.at[part, layer], planes.at[index]))
    copies = started(
        [pltpu.make_async_copy(*pair, sems.at[index]) for index, pair in enumerate(pairs)]
    )
    extra[pl.ds(rows, 8), :] = jnp.zeros((8, extra.shape[1]), F32)
    extra[pl.ds(rows + 2, 2), pl.ds(0, depth)] = low_y[0, layers - 1, 6:, :]
    extra[pl.ds(rows + 4, 2), pl.ds(0, depth)] = high_y[0, layers - 1, :2, :]
    extra[pl.ds(rows + 1, 1), pl.ds(0, depth)] = low_y[1, layers - 2, 7:, :]
    extra[pl.ds(rows + 7, 1), pl.ds(0, depth)] = low_y[1, layers - 1, 7:, :]
    back[...] = jnp.zeros(back.shape, F32)
    for index in range(2):
        back[pl.ds(index, 1), :] = low_y[1, index, 7:, :]
    for copy in copies:
        copy.wait()
    speed = [planes[index] for index in (2, 3, 4)]
    drag = 1.0 / (1.0 + TIME_INCREMENT * DRAG_RATE * flags[...].astype(F32))
    pad_rows(padded, 0, low_y[0, layers - 1, 6:], speed[0], high_y[0, layers - 1, :2])
    none = jnp.zeros((rows, depth), F32)
    around = [planes[0], planes[1], speed[0], none, none]
    moved = advance(around, padded, 0, coefficients(speed, drag))
    extra[pl.ds(0, rows), pl.ds(0, depth)] = jnp.where(speed[0] >= 0.0, moved, drag)
    extra[pl.ds(rows, 1), pl.ds(0, rows)] = surface(last[0])
    extra[pl.ds(rows + 6, 1), pl.ds(0, rows)] = surface(drag)


def wrapped(distance, span):
    moved = distance + span // 2
    moved = jnp.where(moved < 0, moved + span, moved)
    moved = jnp.where(moved >= span, moved - span, moved)
    return (moved - span // 2).astype(F32)


def laser_row(index, layers, rows, spots_a, spots_b):
    total_x = layers * lax.axis_size("gx")
    total_y = rows * lax.axis_size("gy")
    cell_x = lax.axis_index("gx") * layers + index
    cells_y = lax.broadcasted_iota(jnp.int32, (1, rows), 1) + lax.axis_index("gy") * rows
    heat = jnp.zeros((1, rows), F32)
    for spot in range(spots_a.shape[0]):
        dist_x = wrapped(jnp.full((1, rows), cell_x - spots_a[spot], jnp.int32), total_x)
        dist_y = wrapped(cells_y - spots_b[spot], total_y)
        square = dist_x * dist_x + dist_y * dist_y
        heat = heat + jnp.exp(square * (-1.0 / (SPOT_RADIUS * SPOT_RADIUS)))
    return LASER_POWER * heat


def heat_kernel(
    spots_a, spots_b, thermal, low_x, high_x, low_y, high_y, flow, warmed, token, padded
):
    layers, rows, depth = thermal.shape
    token[...] = jnp.zeros(token.shape, F32)
    top = lax.broadcasted_iota(jnp.int32, (rows, depth), 1) == depth - 1
    for index in range(layers):
        pad_rows(padded, 0, low_y[3, index, 6:], thermal[index], high_y[3, index, :2])
        around = []
        for other in range(index - 2, index + 3):
            if other < 0:
                around.append(low_x[other + 2])
            elif other >= layers:
                around.append(high_x[other - layers])
            else:
                around.append(thermal[other])
        speed = [flow[part, index] for part in range(3)]
        gain = TIME_INCREMENT * column(laser_row(index, layers, rows, spots_a, spots_b))
        moved = advance(around, padded, 0, coefficients(speed, None))
        warmed[index] = moved + jnp.where(top, gain, 0.0)


def tables_kernel(group, layers, diagonal, ratio, weight):
    length = group * layers
    mine = position(group)
    first = mine * layers
    diag = diagonal[...]
    ratio[0] = jnp.zeros_like(diag)

    def step(index, previous):
        current = 1.0 / (diag - previous)
        ratio[index] = current
        return current

    loop(1, length + 1, step, jnp.zeros_like(diag))

    def decay(low, high):
        return lax.fori_loop(
            low + 1, high + 1, lambda index, value: value * ratio[index], jnp.ones_like(diag)
        )

    def green(index):
        return 1.0 / (diag - ratio[index] - ratio[jnp.maximum(length - 1 - index, 0)])

    rounds = group.bit_length() - 1
    for turn in range(rounds):
        half = 1 << turn
        right = ((mine >> turn) & 1) == 1
        start = (mine >> (turn + 1)) << (turn + 1)
        cut = (start + half) * layers
        end = (start + 2 * half) * layers
        weight[4 * turn] = decay(cut - 1, end - 1)
        weight[4 * turn + 1] = decay(length - 1 - cut, length - 1 - start * layers)
        low = jnp.where(right, cut - 1, length - 1 - cut)
        high = jnp.where(right, first - 1, length - 1 - first - layers)
        weight[4 * turn + 2] = decay(low, high)
        weight[4 * turn + 3] = green(cut) * ratio[cut]
    inner = jnp.where(mine == group - 1, 0.0, 1.0)
    weight[4 * rounds] = inner * green(first + layers)


def grouped(plane):
    return plane.reshape(plane.shape[0] // 8, 8, plane.shape[1])


def signs(depth):
    row = lax.broadcasted_iota(jnp.int32, (8, depth), 0)
    return jnp.where(row % 2 == 0, 1.0, -1.0)


def face_rows(plane, lead):
    sums = jnp.sum(plane * lead, axis=0)
    return (
        jnp.sum(sums, axis=0, keepdims=True),
        jnp.sum(sums * signs(sums.shape[1]), axis=0, keepdims=True),
    )


def faces_kernel(
    group, length, source, ratio, weight, edge, thermal, _, faces, late, sweep
):
    layers, rows, depth = source.shape
    late[...] = thermal[:2]
    first = position(group) * layers
    zero = jnp.zeros((rows, depth), F32)
    forward = zero
    for index in range(layers):
        forward = source[index] + ratio[first + index] * forward
        sweep[index] = forward
    value = weight[weight.shape[0] - 1] * (ratio[first + layers] * forward)
    energy = zero
    for index in range(layers - 1, -1, -1):
        value = ratio[first + index + 1] * (sweep[index] + value)
        energy = energy + source[index] * value
    faces[pl.ds(2 * length, 8), :] = jnp.broadcast_to(total(energy), (8, depth))

    lead = grouped(edge[...])
    zero = grouped(zero)

    def down(index, previous):
        inside = (index >= first) & (index < first + layers)
        own = jnp.where(inside, source[jnp.clip(index - first, 0, layers - 1)], 0.0)
        current = grouped(own) + grouped(ratio[index]) * previous
        sweep[index] = current.reshape(rows, depth)
        return current

    loop(0, length, down, zero)

    def up(back, following):
        index = length - 1 - back
        value = grouped(ratio[index + 1]) * (grouped(sweep[index]) + following)
        low, high = face_rows(value, lead)
        faces[pl.ds(index, 1), :] = low
        faces[pl.ds(length + index, 1), :] = high
        return value

    loop(0, length, up, zero)


def joined(turn, group, message, other, sums, weight):
    rows, depth = weight.shape[1:]
    right = ((position(group) >> turn) & 1) == 1
    upper, lower = pl.ds(0, rows), pl.ds(rows, rows)
    left_s = jnp.where(right, other[upper, :], message[upper, :])
    right_s = jnp.where(right, message[upper, :], other[upper, :])
    left_t = jnp.where(right, other[lower, :], message[lower, :])
    right_t = jnp.where(right, message[lower, :], other[lower, :])
    own = weight[4 * turn + 2]
    before = sums[0] + jnp.where(right, left_s * own, 0.0)
    after = sums[1] + jnp.where(right, 0.0, right_t * own)
    forward = right_s + left_s * weight[4 * turn]
    backward = left_t + right_t * weight[4 * turn + 1]
    energy = 2.0 * total(left_s * right_t * weight[4 * turn + 3])
    return forward, backward, before, after, energy


def merge_kernel(
    turn, group, length, message, other, faces, other_faces, sums, weight,
    new_message, new_sums, head, tail,
):
    rows, depth = weight.shape[1:]
    forward, backward, before, after, energy = joined(turn, group, message, other, sums, weight)
    new_sums[0] = before
    new_sums[1] = after
    new_message[pl.ds(0, rows), :] = forward
    new_message[pl.ds(rows, rows), :] = backward
    low, high = pl.ds(0, length), pl.ds(length, length)
    number = pl.ds(2 * length, 8)
    head[...] = faces[low, :] + other_faces[low, :]
    tail[...] = faces[high, :] + other_faces[high, :]
    new_message[pl.ds(2 * rows, length), :] = head[...]
    energy = faces[number, :] + other_faces[number, :] + energy
    new_message[pl.ds(2 * rows + length, 8), :] = energy


def close_kernel(turn, group, length, message, other, sums, weight, ratio, ends):
    forward, backward, _, _, _ = joined(turn, group, message, other, sums, weight)
    ends[0] = ratio[length] * forward
    ends[1] = ratio[length] * backward


def coarse_kernel(
    turn, group, length, alone, source, message, other, sums, faces_in, weight, ratio, edge, *refs
):
    precond, image, report, faces, sweep, ends = refs[-6:]
    layers, rows, depth = source.shape
    first = position(group) * layers
    below, below_far, above, above_far = faces_in
    forward, backward, before, after, energy = joined(turn, group, message, other, sums, weight)
    ends[0] = ratio[length] * forward
    ends[1] = ratio[length] * backward
    beyond = ends if alone else refs[0]
    own = pl.ds(2 * rows, length)
    faces[pl.ds(0, length), :] = message[own, :] + other[own, :]
    faces[pl.ds(length, length), :] = below[...] + below_far[...]
    faces[pl.ds(2 * length, length), :] = above[...] + above_far[...]
    number = pl.ds(2 * rows + length, 8)
    energy = message[number, :] + other[number, :] + energy
    forward = before
    for index in range(layers):
        forward = source[index] + ratio[first + index] * forward
        precond[index] = forward
    value = weight[weight.shape[0] - 1] * (after + ratio[first + layers] * forward)
    is_last = first + layers == length
    precond[layers] = jnp.where(is_last, beyond[1], value)
    for index in range(layers - 1, -1, -1):
        value = ratio[first + index + 1] * (precond[index] + value)
        precond[index] = value
    lead = grouped(edge[...])
    sign = signs(depth)

    def pull(index):
        below = faces[pl.ds(length + index, 1), :]
        above = faces[pl.ds(2 * length + index, 1), :]
        return below, above

    def down(index, previous):
        below, above = pull(index)
        current = lead * (below + sign * above) + grouped(ratio[index]) * previous
        if isinstance(index, int):
            if index == 0:
                current = current + grouped(beyond[0])
            if index == length - 1:
                current = current + grouped(beyond[1])
        else:
            current = current + jnp.where(index == 0, grouped(beyond[0]), 0.0)
            current = current + jnp.where(index == length - 1, grouped(beyond[1]), 0.0)
        sweep[index] = current.reshape(rows, depth)
        return current

    zero = jnp.zeros(lead.shape, F32)
    loop(0, length, down, zero)
    line = jnp.zeros((1, depth), F32)

    def up(back, carry):
        following, linked, squared = carry
        index = length - 1 - back
        value = grouped(ratio[index + 1]) * (grouped(sweep[index]) + following)
        sweep[index] = value.reshape(rows, depth)
        low, high = face_rows(value, lead)
        report[pl.ds(index, 1), :] = low
        report[pl.ds(length + index, 1), :] = high
        below, above = pull(index)
        linked = linked + faces[pl.ds(index, 1), :] * below
        squared = squared + low * below + high * above
        return value, linked, squared

    _, linked, squared = loop(0, length, up, (zero, line, line))
    sweep[length] = sweep[0]
    for index in range(layers + 1):
        image[index] = sweep[first + index]
    head, tail = sweep[0], sweep[length - 1]
    linked = 2.0 * total(linked) + total(ends[1] * beyond[0] + ends[0] * beyond[1])
    squared = total(squared) + total(head * beyond[0] + tail * beyond[1])
    crossing = 2.0 * total(head * tail)
    where = 2 * length
    report[pl.ds(where, 1), :] = energy[0:1]
    report[pl.ds(where + 1, 1), :] = jnp.broadcast_to(linked, (1, depth))
    report[pl.ds(where + 2, 1), :] = jnp.broadcast_to(squared, (1, depth))
    report[pl.ds(where + 3, 1), :] = jnp.broadcast_to(crossing, (1, depth))
    report[pl.ds(where + 4, 4), :] = jnp.zeros((4, depth), F32)


def physical_kernel(precond, image, left, right, precond_out, image_out):
    count = precond.shape[0]
    planes = [precond[index] for index in range(count)] + [image[index] for index in range(count)]
    planes = transformed(planes, left, right)
    for index in range(count):
        precond_out[index] = planes[index]
        image_out[index] = planes[count + index]


def project_kernel(
    group, length, paired, star, precond, image, faces, table_z, *refs
):
    given, (flow, pressure, field, rows_) = refs[:-4], refs[-4:]
    _, layers, rows, depth = star.shape
    first = position(group) * layers
    where = 2 * length
    reports = ring([each[...] for each in given])
    sums = reports[0][where:]
    for other in reports[1:]:
        sums = sums + other[where:]
    pairs = jnp.zeros((1, depth), F32)
    for index in range(len(reports)):
        upper, lower = reports[index], reports[(index + 1) % len(reports)]
        pairs = pairs + jnp.sum(
            upper[:length] * lower[length:where], axis=0, keepdims=True
        )
    energy, linked, squared, crossing = (sums[k : k + 1, 0:1] for k in range(4))
    if not paired:
        crossing = crossing + 2.0 * total(pairs)
    first_image = energy - linked
    step = energy / first_image
    beta = (energy * squared - linked * linked) / (first_image * first_image)
    rest = -linked / first_image
    second_image = (
        rest * rest * first_image
        + 2.0 * rest * step * (linked - squared)
        + step * step * (squared - crossing)
        - beta * beta * first_image
    )
    second_step = beta * energy / second_image
    alpha = step + second_step * (rest + beta)
    gamma = second_step * step
    for index in range(layers + 1):
        field[index] = alpha * precond[index] + gamma * image[index]
    after = rows_.at[pl.ds(rows + 8, length), :]
    after[...] = alpha * faces[pl.ds(2 * length, length), :] + gamma * reports[-1][:length]
    following = dot(after[pl.ds(first, layers), :], table_z[...])
    for index in range(layers):
        value = field[index]
        pressure[index] = value
        rows_[pl.ds(0, rows), :] = value
        rows_[pl.ds(rows, 1), :] = following[index : index + 1]
        flow[0, index] = star[0, index] - (field[index + 1] - value)
        flow[1, index] = star[1, index] - (rows_[pl.ds(1, rows), :] - value)
        flow[2, index] = star[2, index] - (lane_shift(value, 1) - value)


def ring(reports):
    if len(reports) != 4:
        return reports
    own, near, across, far = reports
    even = lax.rem(lax.axis_index("gy"), 2) == 0
    return [own, jnp.where(even, far, near), across, jnp.where(even, near, far)]


def along(array, axis, by):
    length = lax.axis_size(axis)
    return lax.ppermute(array, axis, [(i, (i + by) % length) for i in range(length)])


def swapped(array, bit, by=0):
    count_x, count_y = lax.axis_size("gx"), lax.axis_size("gy")
    pairs = [
        (x * count_y + y, (x ^ bit) * count_y + (y + by) % count_y)
        for x in range(count_x)
        for y in range(count_y)
    ]
    return lax.ppermute(array, ("gx", "gy"), pairs)


def pack(body, inputs, received, shapes, scratch, count):
    inputs = [pltpu.with_memory_space_constraint(each, pltpu.HBM) for each in inputs]
    return pl.pallas_call(
        body,
        out_shape=[jax.ShapeDtypeStruct(shape, F32) for shape in shapes],
        in_specs=[pl.BlockSpec(memory_space=pltpu.HBM)] * len(inputs) + [VMEM] * len(received),
        out_specs=[VMEM] * len(shapes),
        scratch_shapes=scratch + [pltpu.SemaphoreType.DMA((count,))],
        compiler_params=pltpu.CompilerParams(vmem_limit_bytes=4 << 20),
    )(*inputs, *received)


def per_device(melt_flow, thermal_state, powder_flag, spot_lateral_a_cell, spot_lateral_b_cell):
    layers, rows, depth = thermal_state.shape
    count_x, count_y = lax.axis_size("gx"), lax.axis_size("gy")
    group = min(count_x, BLOCK // layers)
    blocks = count_x // group
    length = group * layers
    rounds = group.bit_length() - 1
    plane = (rows, depth)
    sine_y, values_y = sines(rows)
    sine_z, values_z = sines(depth)
    left, right = packed_tables(sine_y, sine_z)
    table_z = jnp.asarray(sine_z, F32)
    edge = jnp.asarray(np.broadcast_to(sine_y[0][:, None], plane), F32)
    diagonal = jnp.asarray(2.0 + values_y[:, None] + values_z[None, :], F32)
    line = (length, depth)

    parts = melt_flow.shape[0]
    width = max(rows, depth)
    outer_planes = (2 * parts * rows + 8, width)
    ahead, behind, last_rows, first_rows = pack(
        halo_kernel,
        [melt_flow, thermal_state, powder_flag],
        [],
        [outer_planes] * 2 + [(parts + extra, layers, 8, depth) for extra in (2, 1)],
        [pltpu.VMEM((2,) + plane, F32), pltpu.VMEM((layers, 8, depth), jnp.int32)],
        7 + 4 * parts,
    )
    low_x = along(ahead, "gx", 1)
    high_x = along(behind, "gx", -1)
    low_y = along(last_rows, "gy", 1)
    high_y = along(first_rows, "gy", -1)
    extra, back, last = pack(
        extra_kernel,
        [melt_flow, thermal_state, powder_flag],
        [low_y, high_y],
        [(rows + 8, width), (8, depth), (2,) + plane],
        [
            pltpu.VMEM((5,) + plane, F32),
            pltpu.VMEM(plane, jnp.int32),
            pltpu.VMEM((1, rows + 16, depth), F32),
        ],
        7,
    )
    extra = along(extra, "gx", 1)
    back = along(back, "gx", -1)
    early_low = along(last, "gx", 1)
    ratio, weight = call(
        functools.partial(tables_kernel, group, layers),
        [diagonal],
        [(length + 1,) + plane, (4 * rounds + 1,) + plane],
    )
    marched = [melt_flow, low_x, high_x, thermal_state, powder_flag, low_y, high_y]
    padded = pltpu.VMEM((4, rows + 16, depth), F32)
    one_padded = pltpu.VMEM((1, rows + 16, depth), F32)
    (star,) = call(
        march_kernel, marched + [weight], [(3, layers) + plane], [padded], loose=1, flops=3 << 27
    )
    (partial,) = call(
        transform_kernel,
        [star, left, right],
        [(layers,) + plane],
        [pltpu.VMEM((rows + 16, depth), F32)],
        flops=1 << 27,
    )
    source, message = call(
        functools.partial(source_kernel, group, length),
        [
            melt_flow, low_x, thermal_state, extra, back, low_y, partial, left, right, table_z,
            edge, ratio,
        ],
        [(layers,) + plane, (2 * rows, depth)],
        [one_padded, pltpu.VMEM((layers, depth), F32)],
    )
    faces, late = call(
        functools.partial(faces_kernel, group, length),
        [source, ratio, weight, edge, thermal_state, early_low],
        [(2 * length + 8, depth), (2,) + plane],
        [pltpu.VMEM((max(length, layers + 1),) + plane, F32)],
        loose=1,
    )
    alone = blocks == 1
    early_high = along(late, "gx", -1)
    warmed, token = call(
        heat_kernel,
        [
            spot_lateral_a_cell, spot_lateral_b_cell, thermal_state, early_low, early_high,
            low_y, high_y, melt_flow,
        ],
        [(layers,) + plane, (8, depth)],
        [one_padded],
        scalars=2,
        flops=1 << 28,
    )
    sums = jnp.zeros((2,) + plane, F32)
    for turn in range(rounds - 1):
        message, sums, head, tail = call(
            functools.partial(merge_kernel, turn, group, length),
            [
                message, swapped(message, 1 << turn), faces, swapped(faces, 1 << turn),
                sums, weight,
            ],
            [(2 * rows + length + 8, depth), (2,) + plane, line, line],
        )
        if turn + 2 < rounds:
            rest = message[2 * rows + length :]
            message, faces = message[: 2 * rows], jnp.concatenate([head, tail, rest], 0)
    bit = group >> 1
    other = swapped(message, bit)
    rim = [
        swapped(tail, 0, 1), swapped(tail, bit, 1), swapped(head, 0, -1), swapped(head, bit, -1)
    ]
    outer = []
    scratch = [pltpu.VMEM((length + 1,) + plane, F32)]
    if not alone:
        (ends,) = call(
            functools.partial(close_kernel, rounds - 1, group, length),
            [message, other, sums, weight, ratio],
            [(2,) + plane],
        )
        outer = [jnp.stack([along(ends[0], "gx", group), along(ends[1], "gx", -group)])]
    operands = [source, message, other, sums] + rim
    operands += [weight, ratio, edge] + outer + [token]

    def coarse(*refs):
        coarse_kernel(rounds - 1, group, length, alone, *refs[:4], refs[4:8], *refs[8:])

    precond, image, report, faces = call(
        coarse,
        operands,
        [
            (layers + 1,) + plane, (layers + 1,) + plane, (2 * length + 8, depth),
            (3 * length, depth),
        ],
        scratch + [pltpu.VMEM((2,) + plane, F32)],
        loose=1,
    )
    if blocks > 1:
        onward = along(image[0], "gx", -1)
        at_end = position(group) == group - 1
        image = image.at[layers].set(jnp.where(at_end, onward, image[layers]))
        upper = along(report[:length], "gy", -1)
        crossing = jnp.sum(onward * image[layers - 1])
        crossing = crossing + jnp.sum(upper * report[length : 2 * length])
        numbers = report[2 * length :].at[3].set(2.0 * crossing)
        numbers = lax.psum(jnp.where(at_end, numbers, 0.0), "gx")
        report = report.at[2 * length :].set(numbers)
    reports = {0: report}
    for by in sorted(range(1, count_y), key=lambda by: (by == 2, by)):
        pairs = [(i, i ^ by if count_y == 4 else (i + by) % count_y) for i in range(count_y)]
        reports[by] = lax.ppermute(report, "gy", pairs)
    reports = [reports[by] for by in range(count_y)]
    precond, image = call(
        physical_kernel,
        [precond, image, left, right],
        [(layers + 1,) + plane, (layers + 1,) + plane],
    )
    flow, pressure = call(
        functools.partial(project_kernel, group, length, blocks > 1),
        [star, precond, image, faces, table_z] + reports,
        [(3, layers) + plane, (layers,) + plane],
        [
            pltpu.VMEM((layers + 1,) + plane, F32),
            pltpu.VMEM((rows + 8 + length, depth), F32),
        ],
    )
    return (flow, warmed, pressure)


def solution(mesh):
    placed = (
        P(None, ("runs", "gx"), "gy", None),
        P(("runs", "gx"), "gy", None),
        P(("runs", "gx"), "gy", None),
        P("runs"),
        P("runs"),
    )
    return jax.shard_map(
        per_device,
        mesh=mesh,
        in_specs=placed,
        out_specs=(
            P(None, ("runs", "gx"), "gy", None),
            P(("runs", "gx"), "gy", None),
            P(("runs", "gx"), "gy", None),
        ),
        check_vma=False,
    )
```
